32 devices in a mesh: ctx: 8 (over y, x, core), tp: 4 (over z).
Axes of the slice: x: 2, y: 2, z: 4, core: 2. Of those that a mesh axis runs over, the one named last changes fastest.
Arguments:
- hidden_in: bfloat16 [4096, 2048], P('ctx'), may hold values from -6 to 6
- cotangent: bfloat16 [4096, 2048], P('ctx'), may hold values from -6 to 6
- gain_attn: float32 [2048], replicated, may hold values from 0.5 to 1.5
- qkv_weight: bfloat16 [2048, 3, 2048], P(None, None, 'tp'), may hold values from -0.125 to 0.125
- qkv_bias: float32 [3, 2048], P(None, 'tp'), may hold values from -1.25 to 1.25
- out_weight: bfloat16 [2048, 2048], P('tp'), may hold values from -1 to 1
- gain_ffn: float32 [2048], replicated, may hold values from 0.5 to 1.5
- router_weight: bfloat16 [2048, 16], replicated, may hold values from -0.0625 to 0.0625
- routes: int32 [4096, 4], P('ctx'), may hold values from 0 to 15, all different within a row; in each aligned block of 512 rows (0 to 511, 512 to 1023, ...) at most 192 rows name the same one
- shared_gate: bfloat16 [2048], replicated, may hold values from -0.125 to 0.125
- shared_in: bfloat16 [2048, 2, 5632], P('ctx', None, 'tp'), may hold values from -0.125 to 0.125
- shared_out: bfloat16 [5632, 2048], P('tp', 'ctx'), may hold values from -0.078125 to 0.078125
- expert_in: bfloat16 [16, 2048, 2, 1408], P('ctx', None, None, 'tp'), may hold values from -0.125 to 0.125
- expert_out: bfloat16 [16, 1408, 2048], P('ctx', 'tp'), may hold values from -2.5 to 2.5
Outputs:
- block_out: bfloat16 [4096, 2048], P('ctx')
- grad_input: float32 [4096, 2048], P('ctx')
- grad_gain_attn: float32 [2048], replicated
- grad_qkv_weight: float32 [2048, 3, 2048], P(None, None, 'tp')
- grad_qkv_bias: float32 [3, 2048], P(None, 'tp')
- grad_out_weight: float32 [2048, 2048], P('tp')
- grad_gain_ffn: float32 [2048], replicated
- grad_router: float32 [2048, 16], replicated
- grad_shared_gate: float32 [2048], replicated
- grad_shared_in: float32 [2048, 2, 5632], P('ctx', None, 'tp')
- grad_shared_out: float32 [5632, 2048], P('tp', 'ctx')
- grad_expert_in: float32 [16, 2048, 2, 1408], P('ctx', None, None, 'tp')
- grad_expert_out: float32 [16, 1408, 2048], P('ctx', 'tp')
The draws below stay inside these ranges and needn't reach their ends.
Inputs may be any that keep to these rules, and one draw needn't show every extreme that they name: `routes`: each token names 4 different experts. Among the 512 tokens of one index of ctx (rows r * 512 to (r + 1) * 512 - 1) no expert is named more than 192 times, a bound that some block reaches.
All inputs are finite; a program needn't handle non-finite values.
Results may differ from the reference program's by a relative error of at most 0.03.
Values may be sent and summed in bfloat16 or wider, within the bound.
No kernel may reach another device: no remote copies, remote signals or barrier semaphores. Data moves between devices by JAX's collectives and lax.ppermute only.
A program may use at most 448 MiB of HBM per device.

```python
import math
import jax
import jax.numpy as jnp
import numpy as np
from jax import lax

D = 2048
HEADS = 16
HD = 128
FFE = 1408
FFS = 5632
TOP = 4
SEQ = 4096
EXPERTS = 16
TOK_DEV = 512
CAP = 192
N_CTX = 8


def levels(stream_key, extent, pieces, least, high):
    def one(axis_at, blocks):
        draws = jax.random.uniform(jax.random.fold_in(jax.random.fold_in(stream_key, 6), axis_at), (blocks,), jnp.float32, least / len(pieces), high / len(pieces))
        return jnp.repeat(jnp.exp(draws), extent[axis_at] // blocks).reshape((-1,) + (1,) * (len(extent) - axis_at - 1))

    factor_of = one(*pieces[0])
    for cut in pieces[1:]:
        factor_of = factor_of * one(*cut)
    return factor_of


def deal_out(rng, own, number, rows, amount, top, reach, skew):
    order = jax.random.permutation(rng, amount)
    crowded, common = load_shares(amount, rows * top, reach, skew, True), load_shares(amount, rows * top, reach, skew, False)
    places = jnp.arange(amount)

    def named(sizes, turn):
        used = int((sizes > 0).sum())
        fixed = max(1, used // 4)
        shifted = fixed + (places - fixed + turn * (used - fixed)) % max(1, amount - fixed)
        return jnp.zeros((amount,), jnp.int32).at[order[jnp.where(places < fixed, places, shifted)]].set(jnp.asarray(sizes, jnp.int32))

    sizes = jnp.where(number % 4 == 0, named(crowded, number // 4), named(common, number - number // 4 - 1))
    mixed = jax.random.permutation(jax.random.fold_in(own, 3), amount)
    source_of, taker = mixed[0:amount // 2 * 2:2], mixed[1:amount // 2 * 2:2]
    room = jnp.minimum(sizes[source_of] - 1, reach - sizes[taker]) // 2
    room = jnp.where((source_of == order[0]) | (taker == order[0]) | (sizes[taker] == 0), 0, jnp.maximum(room, 0))
    shifted = jax.random.randint(jax.random.fold_in(own, 4), (amount // 2,), 0, 1 << 20) % (room + 1)
    sizes = sizes.at[source_of].add(-shifted).at[taker].add(shifted)
    labels = jnp.searchsorted(jnp.cumsum(sizes), jnp.arange(rows * top), side="right").astype(jnp.int32)
    listing = labels.reshape(top, rows).T
    listing = listing[jax.random.permutation(jax.random.fold_in(own, 1), rows)]
    turn = jax.random.randint(jax.random.fold_in(own, 2), (rows, 1), 0, top)
    return jnp.take_along_axis(listing, (jnp.arange(top)[None, :] + turn) % top, axis=1)


def load_shares(count, total, most, skew, full):
    weights = [(1 << 20) // math.isqrt(standing ** skew) + 1 for standing in range(1, count + 1)]
    largest = most if full else min(most, max(-(-total // count), total * weights[0] // sum(weights)))
    least = 1 if total - largest >= count - 1 else 0
    holding, spare = [largest] + [least] * (count - 1), total - largest - least * (count - 1)
    while spare > 0:
        candidates = [i for i in range(1, count) if holding[i] < largest] or [i for i in range(1, count) if holding[i] < most]
        pool, remaining = sum([weights[i] for i in candidates]), spare
        for i in candidates:
            addition = min(most - holding[i], max(1, remaining * weights[i] // pool), spare)
            holding[i] = holding[i] + addition
            spare = spare - addition
    return np.array(holding)


def noise(stream_key, extent, spread, most, pieces=(), kind=jnp.bfloat16):
    level = levels(stream_key, extent, pieces, -0.22, 0.18) if pieces else 1.0
    array = jax.random.normal(stream_key, extent, jnp.float32) * spread * level
    return jnp.minimum(jnp.maximum(array, -most), most).astype(kind)


def setup_inputs(seed: int = 0) -> dict:
    splits = jax.random.split(jax.random.key(seed), 15)
    hidden_in = noise(splits[0], (SEQ, D), 1.0, 6.0, ((0, 8),))
    cotangent = noise(splits[1], (SEQ, D), 1.0, 6.0, ((0, 8),))
    gain_attn = jnp.clip(1.0 + 0.1 * jax.random.normal(splits[2], (D,), jnp.float32), 0.5, 1.5)
    qkv_weight = noise(splits[3], (D, 3, HEADS * HD), D ** -0.5, 0.125, ((2, 4),))
    qkv_bias = noise(splits[4], (3, HEADS * HD), 0.2, 1.25, ((1, 4),), jnp.float32)
    out_weight = noise(splits[5], (HEADS * HD, D), (HEADS * HD // 64) ** -0.5, 1.0, ((0, 4),))
    gain_ffn = jnp.clip(1.0 + 0.1 * jax.random.normal(splits[6], (D,), jnp.float32), 0.5, 1.5)
    router_weight = noise(splits[7], (D, EXPERTS), (4 * D) ** -0.5, 0.0625)
    routes_keys = jax.random.split(jax.random.fold_in(splits[8], 1), SEQ // TOK_DEV)
    routes_turns = jax.random.permutation(jax.random.fold_in(splits[8], 3), SEQ // TOK_DEV)
    routes = jax.vmap(lambda own, number: deal_out(jax.random.fold_in(splits[8], 2), own, number, TOK_DEV, EXPERTS, TOP, CAP, 2))(routes_keys, routes_turns).reshape((SEQ, TOP))
    shared_gate = noise(splits[9], (D,), D ** -0.5, 0.125)
    shared_in = noise(splits[10], (D, 2, FFS), D ** -0.5, 0.125, ((0, 8), (2, 4)))
    shared_out = noise(splits[11], (FFS, D), FFS ** -0.5, 0.078125, ((0, 4), (1, 8)))
    expert_in = noise(splits[12], (EXPERTS, D, 2, FFE), D ** -0.5, 0.125, ((0, 8), (3, 4)))
    expert_out = noise(splits[13], (EXPERTS, FFE, D), (max(FFE // 256, 1)) ** -0.5, 2.5, ((0, 8), (1, 4)))
    return dict(hidden_in=hidden_in, cotangent=cotangent, gain_attn=gain_attn, qkv_weight=qkv_weight, qkv_bias=qkv_bias, out_weight=out_weight, gain_ffn=gain_ffn, router_weight=router_weight, routes=routes, shared_gate=shared_gate, shared_in=shared_in, shared_out=shared_out, expert_in=expert_in, expert_out=expert_out)


EPS = 1e-06
THETA = 1000000.0
HIGH = lax.Precision.HIGHEST
NEG = -1e+30

@jax.custom_vjp
def low(v):
    return lax.optimization_barrier(v.astype(jnp.bfloat16)).astype(jnp.float32)

@jax.custom_vjp
def low_back(v):
    return v

def low_keep(v):
    return (low(v), None)

def low_pass(kept, grad):
    return (grad,)

def back_keep(v):
    return (v, None)

def back_low(kept, grad):
    return (low(grad),)
low.defvjp(low_keep, low_pass)
low_back.defvjp(back_keep, back_low)

def rms_scale(values, gain):
    return values * lax.rsqrt(lax.optimization_barrier(jnp.mean(values * values, axis=-1, keepdims=True)) + EPS) * gain

def rotary_tables(positions, width):
    half_width = width // 2
    freqs = THETA ** (-(jnp.arange(half_width, dtype=jnp.float32) * 2.0) / width)
    angles = positions.astype(jnp.float32)[:, None] * freqs[None, :]
    return (jnp.cos(angles), jnp.sin(angles))

def rotate(values, cosine, sine):
    half_width = values.shape[-1] // 2
    first = values[..., :half_width]
    second = values[..., half_width:]
    cos_b = cosine[:, None, :]
    sin_b = sine[:, None, :]
    return jnp.concatenate([first * cos_b - second * sin_b, second * cos_b + first * sin_b], axis=-1)

def swiglu(pair):
    return jax.nn.silu(pair[..., 0, :]) * pair[..., 1, :]

def routing_tables(routes):
    flat_e = routes.reshape(-1).astype(jnp.int32)
    flat_t = (jnp.arange(SEQ * TOP, dtype=jnp.int32) // TOP).astype(jnp.int32)
    onehot = (flat_e[:, None] == jnp.arange(EXPERTS, dtype=jnp.int32)[None, :]).astype(jnp.int32)
    ranks = jnp.cumsum(onehot.reshape(N_CTX, TOK_DEV * TOP, EXPERTS), axis=1).reshape(SEQ * TOP, EXPERTS)
    slot_of = lax.optimization_barrier(jnp.sum(onehot * (ranks - 1), axis=1)).astype(jnp.int32)
    row_of = (flat_t // TOK_DEV * CAP + slot_of).astype(jnp.int32)
    token_table = jnp.zeros((EXPERTS, N_CTX * CAP), jnp.int32).at[flat_e, row_of].set(flat_t)
    valid_table = jnp.zeros((EXPERTS, N_CTX * CAP), jnp.float32).at[flat_e, row_of].set(1.0)
    return (flat_e, row_of, token_table, valid_table)

def reference(hidden_in, cotangent, gain_attn, qkv_weight, qkv_bias, out_weight, gain_ffn, router_weight, routes, shared_gate, shared_in, shared_out, expert_in, expert_out):
    flat_e, row_of, token_table, valid_table = routing_tables(routes)
    cosine, sine = rotary_tables(jnp.arange(SEQ, dtype=jnp.int32), HD)
    block = math.gcd(SEQ, 512)
    starts = (jnp.arange(SEQ // block, dtype=jnp.int32) * block).astype(jnp.int32)
    key_pos = jnp.arange(SEQ, dtype=jnp.int32)
    score_scale = 1.0 / math.sqrt(HD)

    def forward(x_in, g_one, w_qkv, b_qkv, w_out, g_two, w_router, w_sgate, w_sin, w_sout, w_ein, w_eout):
        x_one = low(rms_scale(x_in, g_one))
        raw = low_back(jnp.einsum('td,dcf->tcf', x_one, w_qkv, precision=HIGH) + b_qkv[None])
        shaped = raw.reshape(SEQ, 3, HEADS, HD)
        query = low(rotate(shaped[:, 0], cosine, sine))
        key_rows = low(rotate(shaped[:, 1], cosine, sine))
        value_rows = low(shaped[:, 2])

        def attend(start):
            block_query = lax.dynamic_slice_in_dim(query, start, block, 0)
            scores = low_back(jnp.einsum('qhd,khd->hqk', block_query, key_rows, precision=HIGH) * score_scale)
            query_pos = start + jnp.arange(block, dtype=jnp.int32)
            allowed = key_pos[None, :] <= query_pos[:, None]
            weights = low(jax.nn.softmax(jnp.where(allowed[None], scores, NEG), axis=-1))
            return jnp.einsum('hqk,khd->qhd', weights, value_rows, precision=HIGH)
        attended = lax.map(jax.checkpoint(attend), starts).reshape(SEQ, HEADS * HD)
        att = low_back(low(attended))
        hidden = x_in + low_back(jnp.dot(att, w_out, precision=HIGH))
        x_two = low(rms_scale(hidden, g_two))
        router_probs = jax.nn.softmax(jnp.dot(x_two, w_router, precision=HIGH), axis=-1)
        gate_vals = jnp.take_along_axis(router_probs, routes, axis=1)
        shared_weight = jax.nn.sigmoid(jnp.dot(x_two, w_sgate, precision=HIGH))
        shared_pair = low_back(jnp.einsum('td,dcf->tcf', x_two, w_sin, precision=HIGH))
        shared_res = low_back(jnp.dot(low(swiglu(shared_pair)), w_sout, precision=HIGH))
        gate_table = jnp.zeros((EXPERTS, N_CTX * CAP), jnp.float32).at[flat_e, row_of].set(gate_vals.reshape(-1))

        def expert_step(mixed, items):
            rows_idx, valid, gate_col, w_in, w_down = items
            rows = x_two[rows_idx] * valid[:, None]
            pair = low_back(jnp.einsum('rd,dcf->rcf', rows, w_in, precision=HIGH))
            result = low_back(jnp.dot(low(swiglu(pair)), w_down, precision=HIGH))
            return (mixed.at[rows_idx].add(gate_col[:, None] * result), None)
        routed, _ = lax.scan(jax.checkpoint(expert_step), jnp.zeros((SEQ, D), jnp.float32), (token_table, valid_table, gate_table, w_ein, w_eout))
        return hidden + routed + shared_weight[:, None] * shared_res
    inputs = (hidden_in.astype(jnp.float32), gain_attn.astype(jnp.float32), qkv_weight.astype(jnp.float32), qkv_bias.astype(jnp.float32), out_weight.astype(jnp.float32), gain_ffn.astype(jnp.float32), router_weight.astype(jnp.float32), shared_gate.astype(jnp.float32), shared_in.astype(jnp.float32), shared_out.astype(jnp.float32), expert_in.astype(jnp.float32), expert_out.astype(jnp.float32))
    block_out, pullback = jax.vjp(forward, *inputs)
    grads = pullback(cotangent.astype(jnp.float32))
    return (block_out.astype(jnp.bfloat16), grads[0], grads[1], grads[2], grads[3], grads[4], grads[5], grads[6], grads[7], grads[8], grads[9], grads[10], grads[11])
```

```python
import functools
import math

import jax
import jax.numpy as jnp
from jax import lax
from jax.experimental import pallas as pl
from jax.experimental.pallas import tpu as pltpu
from jax.sharding import PartitionSpec as P

HD = 128
EPS = 1e-06
THETA = 1000000.0
NEG = -1e30
F32 = jnp.float32
BF16 = jnp.bfloat16


def rotary_tables(positions, width):
    half_width = width // 2
    freqs = THETA ** (-(jnp.arange(half_width, dtype=F32) * 2.0) / width)
    angles = positions.astype(F32)[:, None] * freqs[None, :]
    return (jnp.cos(angles), jnp.sin(angles))


def rotate(values, cosine, sine):
    half_width = values.shape[-1] // 2
    first, second = values[..., :half_width], values[..., half_width:]
    return jnp.concatenate(
        [first * cosine - second * sine, second * cosine + first * sine], axis=-1
    )


def dot(a, b, dims):
    return lax.dot_general(a, b, dims, preferred_element_type=F32)


def swap(value, bits):
    count = lax.axis_size("ctx")
    return lax.ppermute(value, "ctx", [(i, i ^ bits) for i in range(count)])


def relative(natural):
    count = natural.shape[0]
    order = jnp.arange(count, dtype=jnp.int32) ^ lax.axis_index("ctx")
    return natural[order]


def gather_ctx(own):
    count = lax.axis_size("ctx")
    if count != 8:
        whole = relative(lax.all_gather(own, "ctx", axis=0))
        return [whole[j] for j in range(count)]
    half = own.shape[0] // 2
    b1 = swap(own, 1)
    b2, b4 = swap(own, 2), swap(own, 4)
    b3, b5 = swap(b2, 1), swap(b4, 1)
    b6 = jnp.concatenate([swap(b4[:half], 2), swap(b2[half:], 4)], axis=0)
    return [own, b1, b2, b3, b4, b5, b6, swap(b6, 1)]


def scatter_ctx(parts):
    count = lax.axis_size("ctx")
    if count != 8:
        natural = relative(jnp.stack(parts))
        flat = natural.reshape((-1,) + natural.shape[2:])
        return lax.psum_scatter(flat, "ctx", scatter_dimension=0, tiled=True).astype(F32)
    half = parts[0].shape[0] // 2
    pair = [parts[j].astype(F32) + swap(parts[j ^ 1], 1).astype(F32) for j in (6, 2, 4, 0)]
    q6 = pair[0].astype(BF16)
    via_x, via_y = swap(q6[:half], 2), swap(q6[half:], 4)
    r2 = swap(pair[1][:half].astype(BF16), 2)
    r4 = swap(pair[2][half:].astype(BF16), 4)
    r4a = swap((pair[2][:half] + via_x.astype(F32)).astype(BF16), 4)
    r2b = swap((pair[1][half:] + via_y.astype(F32)).astype(BF16), 2)
    low = r2.astype(F32) + r4a.astype(F32)
    high = r2b.astype(F32) + r4.astype(F32)
    return pair[3] + jnp.concatenate([low, high], axis=0)


def sum_ctx(value):
    count = lax.axis_size("ctx")
    rows = value.shape[0] // count
    place = lax.axis_index("ctx")
    low = value.astype(BF16)
    parts = [
        lax.dynamic_slice_in_dim(low, (place ^ j) * rows, rows, 0) for j in range(count)
    ]
    own = scatter_ctx(parts).astype(BF16)
    return relative(jnp.stack(gather_ctx(own))).reshape(value.shape).astype(F32)


def gather_tp_rows(own):
    half = own.shape[0] // 2
    core = lax.axis_index("ctx") % 2
    mine = lax.all_gather(lax.dynamic_slice_in_dim(own, core * half, half, 0), "tp", axis=0)
    other = swap(mine, 1)
    first = jnp.where(core == 0, mine, other)
    second = jnp.where(core == 0, other, mine)
    return jnp.concatenate([first, second], axis=1).reshape((-1,) + own.shape[1:])


NT = (((1,), (1,)), ((), ()))
NN = (((1,), (0,)), ((), ()))
TN = (((0,), (0,)), ((), ()))
VMEM_LIMIT = 60 * 1024 * 1024


def attend_kernel(factor, count, place_ref, q_ref, *refs):
    kv_refs, (att_ref, lse_ref, kv, sems) = refs[:count], refs[count:]
    copies = [pltpu.make_async_copy(kv_refs[j], kv.at[j], sems.at[j]) for j in range(count)]
    for copy in copies:
        copy.start()
    for copy in copies:
        copy.wait()
    place = place_ref[0]
    heads, tokens, _ = q_ref.shape

    def one_head(head, _):
        query = q_ref[head]

        def scores(j):
            return dot(kv[j, 0, head], query, NT) * factor

        key_at = lax.broadcasted_iota(jnp.int32, (tokens, tokens), 0)
        query_at = lax.broadcasted_iota(jnp.int32, (tokens, tokens), 1)
        first = jnp.where(key_at <= query_at, scores(0), NEG)
        top = jnp.max(first, axis=0, keepdims=True)
        exps = jnp.exp2(first - top)
        total = jnp.sum(exps, axis=0, keepdims=True)
        acc = dot(kv[0, 1, head], exps.astype(BF16), TN)

        def earlier(i, carry):
            top, total, acc = carry
            j = place ^ i
            now = scores(j)
            higher = jnp.maximum(top, jnp.max(now, axis=0, keepdims=True))
            exps = jnp.exp2(now - higher)
            keep = jnp.exp2(top - higher)
            total = total * keep + jnp.sum(exps, axis=0, keepdims=True)
            acc = acc * keep + dot(kv[j, 1, head], exps.astype(BF16), TN)
            return higher, total, acc

        top, total, acc = lax.fori_loop(0, place, earlier, (top, total, acc))
        att_ref[head] = (acc / total).T
        lse_ref[head] = jnp.broadcast_to(top + jnp.log2(total), lse_ref.shape[1:])
        return 0

    lax.fori_loop(0, heads, one_head, 0)


def attend(place, query, kv_blocks):
    heads, tokens, size = query.shape
    count = len(kv_blocks)
    factor = math.log2(math.e) / math.sqrt(size)
    flops = 4 * count * heads * tokens * tokens * size
    return pl.pallas_call(
        functools.partial(attend_kernel, factor, count),
        out_shape=(
            jax.ShapeDtypeStruct((heads, tokens, size), F32),
            jax.ShapeDtypeStruct((heads, 8, tokens), F32),
        ),
        in_specs=[
            pl.BlockSpec(memory_space=pltpu.SMEM),
            pl.BlockSpec(memory_space=pltpu.VMEM),
        ]
        + [pl.BlockSpec(memory_space=pl.ANY)] * count,
        out_specs=(pl.BlockSpec(memory_space=pltpu.VMEM),) * 2,
        scratch_shapes=[
            pltpu.VMEM((count, 2, heads, tokens, size), BF16),
            pltpu.SemaphoreType.DMA((count,)),
        ],
        compiler_params=pltpu.CompilerParams(vmem_limit_bytes=VMEM_LIMIT),
        cost_estimate=pl.CostEstimate(
            flops=flops, bytes_accessed=count * heads * tokens * size * 4, transcendentals=0
        ),
        name="attend",
    )(place.reshape(1), query, *kv_blocks)


def attend_back_kernel(factor, scale, count, place_ref, q_ref, do_ref, lse_ref, delta_ref, *refs):
    kv_refs, (dq_ref, dkv_ref, kv, dkv, dq, sems, out_sems) = refs[:count], refs[count:]
    copies = [pltpu.make_async_copy(kv_refs[j], kv.at[j], sems.at[j]) for j in range(count)]
    for copy in copies:
        copy.start()
    for copy in copies:
        copy.wait()
    place = place_ref[0]
    heads, tokens, _ = q_ref.shape

    def out_copy(j):
        return pltpu.make_async_copy(dkv.at[j], dkv_ref.at[j], out_sems.at[j])

    def one_block(j, masked):
        def one_head(head, _):
            query, do = q_ref[head], do_ref[head]
            key, value = kv[j, 0, head], kv[j, 1, head]
            scores = dot(key, query, NT) * factor
            probs = jnp.exp2(scores - lse_ref[head, :1])
            if masked:
                key_at = lax.broadcasted_iota(jnp.int32, (tokens, tokens), 0)
                query_at = lax.broadcasted_iota(jnp.int32, (tokens, tokens), 1)
                probs = jnp.where(key_at <= query_at, probs, 0.0)
            dprob = dot(value, do, NT)
            dscore = (probs * (dprob - delta_ref[head, :1])).astype(BF16)
            dkv[j, 0, head] = (dot(dscore, query, NN) * scale).astype(BF16)
            dkv[j, 1, head] = dot(probs.astype(BF16), do, NN).astype(BF16)
            part = dot(key, dscore, TN)
            dq[head] = part if masked else dq[head] + part
            return 0

        lax.fori_loop(0, heads, one_head, 0)
        out_copy(j).start()

    one_block(0, True)

    def earlier(i, _):
        one_block(place ^ i, False)
        return 0

    def later(i, _):
        j = place ^ i
        dkv[j] = jnp.zeros(dkv.shape[1:], BF16)
        out_copy(j).start()
        return 0

    lax.fori_loop(0, place, earlier, 0)
    lax.fori_loop(place + 1, count, later, 0)
    for head in range(heads):
        dq_ref[head] = dq[head].T * scale
    for j in range(count):
        out_copy(j).wait()


def attend_back(place, query, do, lse, delta, kv_blocks):
    heads, tokens, size = query.shape
    count = len(kv_blocks)
    scale = 1.0 / math.sqrt(size)
    factor = math.log2(math.e) * scale
    return pl.pallas_call(
        functools.partial(attend_back_kernel, factor, scale, count),
        out_shape=(
            jax.ShapeDtypeStruct((heads, tokens, size), F32),
            jax.ShapeDtypeStruct((count, 2, heads, tokens, size), BF16),
        ),
        in_specs=[pl.BlockSpec(memory_space=pltpu.SMEM)]
        + [pl.BlockSpec(memory_space=pltpu.VMEM)] * 4
        + [pl.BlockSpec(memory_space=pl.ANY)] * count,
        out_specs=(pl.BlockSpec(memory_space=pltpu.VMEM), pl.BlockSpec(memory_space=pl.ANY)),
        scratch_shapes=[
            pltpu.VMEM((count, 2, heads, tokens, size), BF16),
            pltpu.VMEM((count, 2, heads, tokens, size), BF16),
            pltpu.VMEM((heads, size, tokens), F32),
            pltpu.SemaphoreType.DMA((count,)),
            pltpu.SemaphoreType.DMA((count,)),
        ],
        compiler_params=pltpu.CompilerParams(vmem_limit_bytes=VMEM_LIMIT),
        cost_estimate=pl.CostEstimate(
            flops=10 * count * heads * tokens * tokens * size,
            bytes_accessed=count * heads * tokens * size * 8,
            transcendentals=0,
        ),
        name="attend_back",
    )(place.reshape(1), query, do, lse, delta, *kv_blocks)


def swiglu_back(rows_x, rows_g, gate, w_one, w_two, w_out):
    one, two = dot(rows_x, w_one, NT), dot(rows_x, w_two, NT)
    dact = dot(rows_g, w_out, NT)
    sig = 1.0 / (1.0 + jnp.exp(-one))
    silu = one * sig
    act = silu * two
    prod = act * dact
    dgate = gate * dact
    d_one = (dgate * two * sig * (1.0 + one * (1.0 - sig))).astype(BF16)
    d_two = (dgate * silu).astype(BF16)
    return (gate * act).astype(BF16), d_one, d_two, prod


def split_low(value):
    high = value.astype(BF16)
    return high, (value - high.astype(F32)).astype(BF16)


def experts_kernel(group, local, experts, given, first_ref, *refs):
    x_refs, g_refs, refs = refs[:group], refs[group : 2 * group], refs[2 * group :]
    (slot_row, slot_col, w_in, w_out, w_shared, w_router), refs = refs[:6], refs[6 + given :]
    out_refs, dx_refs, refs = refs[:group], refs[group : 2 * group], refs[2 * group :]
    (rows_x_ref, rows_g_ref, act_ref, dpair_ref, sact_ref, sdpair_ref, dl_ref) = refs[:7]
    (xs, gs, outs, dxs, res, drow, probs, dl, in_sems, out_sems) = refs[7:]
    block, phase = pl.program_id(0), pl.program_id(1)
    tokens, width = xs.shape[1:]
    capacity = rows_x_ref.shape[2]

    def load(b):
        return (
            pltpu.make_async_copy(x_refs[b], xs.at[b], in_sems.at[0, b]),
            pltpu.make_async_copy(g_refs[b], gs.at[b], in_sems.at[1, b]),
        )

    def store(b):
        return (
            pltpu.make_async_copy(outs.at[b], out_refs[b], out_sems.at[0, b]),
            pltpu.make_async_copy(dxs.at[b], dx_refs[b], out_sems.at[1, b]),
        )

    @pl.when((block == 0) & (phase == 0))
    def _():
        for b in range(group):
            for copy in load(b):
                copy.start()

    for b in range(group):

        @pl.when((block == b) & (phase == 0))
        def _():
            for copy in load(b):
                copy.wait()

    x, g = xs[block], gs[block]
    row_at = lax.broadcasted_iota(jnp.int32, dl.shape, 0)

    @pl.when(phase == 0)
    def _():
        logits = dot(w_router[...], x, NT)
        shown = jnp.where(row_at < experts, logits, NEG)
        exps = jnp.exp(shown - jnp.max(shown, axis=0, keepdims=True))
        soft = exps / jnp.sum(exps, axis=0, keepdims=True)
        probs[...] = jnp.where(row_at == experts, 1.0 / (1.0 + jnp.exp(-logits)), soft)
        dl[...] = jnp.zeros_like(dl)

    @pl.when(phase < local)
    def _():
        chosen = row_at == first_ref[0] + phase
        own = jnp.sum(jnp.where(chosen, probs[...], 0.0), axis=0, keepdims=True)
        slot_at = lax.broadcasted_iota(jnp.int32, (capacity, tokens), 0)
        hits = slot_at == slot_row[0, pl.ds(phase, 1), :]
        picks = jnp.where(hits, 1.0, 0.0).astype(BF16)
        gate = jnp.sum(jnp.where(hits, own, 0.0), axis=1, keepdims=True)
        rows_x = dot(picks, x, NN).astype(BF16)
        rows_g = dot(picks, g, NN).astype(BF16)
        act, d_one, d_two, prod = swiglu_back(
            rows_x, rows_g, gate, w_in[0, 0], w_in[0, 1], w_out[0]
        )
        rows_x_ref[0, 0] = rows_x
        rows_g_ref[0, 0] = rows_g
        act_ref[0, 0] = act
        dpair_ref[0, 0, 0] = d_one
        dpair_ref[0, 0, 1] = d_two
        row_dot = jnp.sum(prod, axis=1, keepdims=True)
        weighted = jnp.sum(jnp.where(hits, row_dot, 0.0), axis=0, keepdims=True) * own
        is_expert = row_at < experts
        dl[...] += weighted * (
            jnp.where(chosen, 1.0, 0.0) - jnp.where(is_expert, probs[...], 0.0)
        )
        res[phase] = dot(act, w_out[0], NN).astype(BF16)
        drow[phase] = (dot(d_one, w_in[0, 0], NN) + dot(d_two, w_in[0, 1], NN)).astype(BF16)

    @pl.when(phase == local)
    def _():
        columns = dot(x, w_router[...], NT)
        lane = lax.broadcasted_iota(jnp.int32, columns.shape, 1)
        logit = jnp.sum(jnp.where(lane == experts, columns, 0.0), axis=1, keepdims=True)
        gate = 1.0 / (1.0 + jnp.exp(-logit))
        act, d_one, d_two, prod = swiglu_back(x, g, gate, w_shared[0], w_shared[1], w_shared[2])
        sact_ref[0] = act
        sdpair_ref[0, 0] = d_one
        sdpair_ref[0, 1] = d_two
        ones = jnp.ones((dl.shape[0], prod.shape[1]), BF16)
        high, low = split_low(prod)
        dots = dot(ones, high, NT) + dot(ones, low, NT)
        dl[...] += jnp.where(row_at == experts, dots * probs[...] * (1.0 - probs[...]), 0.0)
        high, low = split_low(dl[...])
        dl_ref[0, 0] = high
        dl_ref[0, 1] = low
        total = dot(act, w_shared[2], NN)
        dtotal = dot(d_one, w_shared[0], NN) + dot(d_two, w_shared[1], NN)
        dtotal += dot(high, w_router[...], TN) + dot(low, w_router[...], TN)
        slot_at = lax.broadcasted_iota(jnp.int32, (tokens, capacity), 1)
        for e in range(local):
            picks = jnp.where(slot_at == slot_col[0, :, e : e + 1], 1.0, 0.0).astype(BF16)
            total += dot(picks, res[e], NN)
            dtotal += dot(picks, drow[e], NN)
        outs[block] = total.astype(BF16)
        dxs[block] = dtotal.astype(BF16)
        for b in range(group):

            @pl.when(block == b)
            def _():
                for copy in store(b):
                    copy.start()

        @pl.when(block == group - 1)
        def _():
            for b in range(group):
                for copy in store(b):
                    copy.wait()


def run_experts(at, first, x_group, g_group, slot_rows, slot_cols, w_in, w_out, w_shared, w_router, kept):
    given = kept if at else []
    group = len(x_group)
    tokens, width = x_group[0].shape
    local, units = w_out.shape[:2]
    share = w_shared.shape[1]
    padded = w_router.shape[0]
    experts = padded_experts(local)
    capacity = kept[0].shape[2]
    last = lambda p: jnp.minimum(p, local - 1)
    any_spec = pl.BlockSpec(memory_space=pl.ANY)
    block = jax.ShapeDtypeStruct((tokens, width), BF16)
    flops = group * 2 * tokens * width * (
        local * capacity * 4
        + 9 * share
        + local * capacity * units * 6 // tokens
    )
    results = pl.pallas_call(
        functools.partial(experts_kernel, group, local, experts, len(given)),
        grid=(group, local + 1),
        out_shape=(block,) * (2 * group)
        + tuple(jax.ShapeDtypeStruct(k.shape, k.dtype) for k in kept),
        in_specs=[pl.BlockSpec(memory_space=pltpu.SMEM)]
        + [any_spec] * (2 * group)
        + [
            pl.BlockSpec((1, local, tokens), lambda b, p: (at + b, 0, 0)),
            pl.BlockSpec((1, tokens, local), lambda b, p: (at + b, 0, 0)),
            pl.BlockSpec((1, 2, units, width), lambda b, p: (last(p), 0, 0, 0)),
            pl.BlockSpec((1, units, width), lambda b, p: (last(p), 0, 0)),
            pl.BlockSpec((3, share, width), lambda b, p: (0, 0, 0)),
            pl.BlockSpec((padded, width), lambda b, p: (0, 0)),
        ]
        + [any_spec] * len(given),
        out_specs=(any_spec,) * (2 * group)
        + (
            pl.BlockSpec((1, 1, capacity, width), lambda b, p: (at + b, last(p), 0, 0)),
            pl.BlockSpec((1, 1, capacity, width), lambda b, p: (at + b, last(p), 0, 0)),
            pl.BlockSpec((1, 1, capacity, units), lambda b, p: (at + b, last(p), 0, 0)),
            pl.BlockSpec((1, 1, 2, capacity, units), lambda b, p: (at + b, last(p), 0, 0, 0)),
            pl.BlockSpec((1, tokens, share), lambda b, p: (at + b, 0, 0)),
            pl.BlockSpec((1, 2, tokens, share), lambda b, p: (at + b, 0, 0, 0)),
            pl.BlockSpec((1, 2, padded, tokens), lambda b, p: (at + b, 0, 0, 0)),
        ),
        input_output_aliases={7 + 2 * group + i: 2 * group + i for i in range(len(given))},
        scratch_shapes=[
            pltpu.VMEM((group, tokens, width), BF16),
            pltpu.VMEM((group, tokens, width), BF16),
            pltpu.VMEM((group, tokens, width), BF16),
            pltpu.VMEM((group, tokens, width), BF16),
            pltpu.VMEM((local, capacity, width), BF16),
            pltpu.VMEM((local, capacity, width), BF16),
            pltpu.VMEM((padded, tokens), F32),
            pltpu.VMEM((padded, tokens), F32),
            pltpu.SemaphoreType.DMA((2, group)),
            pltpu.SemaphoreType.DMA((2, group)),
        ],
        compiler_params=pltpu.CompilerParams(vmem_limit_bytes=VMEM_LIMIT),
        cost_estimate=pl.CostEstimate(flops=flops, bytes_accessed=20 * 2**20 * group, transcendentals=0),
        name="run_experts",
    )(first.reshape(1), *x_group, *g_group, slot_rows, slot_cols, w_in, w_out, w_shared, w_router, *given)
    return results[:group], results[group : 2 * group], results[2 * group :]


def padded_experts(local):
    return local * lax.axis_size("ctx")


def shared_grads_kernel(count, *refs):
    x_refs, g_refs, refs = refs[:count], refs[count : 2 * count], refs[2 * count :]
    (sact, sdpair, dl, grads_ref, router_ref, xs, gs, grads, router, sems) = refs
    at = pl.program_id(0)
    slot = lax.rem(at, 2)

    def load(j, into):
        return (
            pltpu.make_async_copy(x_refs[j], xs.at[into], sems.at[0, into]),
            pltpu.make_async_copy(g_refs[j], gs.at[into], sems.at[1, into]),
        )

    @pl.when(at == 0)
    def _():
        for copy in load(0, 0):
            copy.start()
        grads[...] = jnp.zeros_like(grads)
        router[...] = jnp.zeros_like(router)

    for j in range(1, count):

        @pl.when(at == j - 1)
        def _():
            for copy in load(j, j % 2):
                copy.start()

    for copy in load(0, slot):
        copy.wait()
    x, g = xs[slot], gs[slot]
    grads[0] += dot(sdpair[0, 0], x, TN)
    grads[1] += dot(sdpair[0, 1], x, TN)
    grads[2] += dot(sact[0], g, TN)
    router[...] += dot(dl[0, 0], x, NN) + dot(dl[0, 1], x, NN)

    @pl.when(at == count - 1)
    def _():
        grads_ref[...] = grads[...].astype(BF16)
        router_ref[...] = router[...]


def shared_grads(x_blocks, g_blocks, sact, sdpair, dl):
    count = len(x_blocks)
    tokens, width = x_blocks[0].shape
    share, padded = sact.shape[2], dl.shape[2]
    any_spec = pl.BlockSpec(memory_space=pl.ANY)
    return pl.pallas_call(
        functools.partial(shared_grads_kernel, count),
        grid=(count,),
        out_shape=(
            jax.ShapeDtypeStruct((3, share, width), BF16),
            jax.ShapeDtypeStruct((padded, width), F32),
        ),
        in_specs=[any_spec] * (2 * count)
        + [
            pl.BlockSpec((1, tokens, share), lambda j: (j, 0, 0)),
            pl.BlockSpec((1, 2, tokens, share), lambda j: (j, 0, 0, 0)),
            pl.BlockSpec((1, 2, padded, tokens), lambda j: (j, 0, 0, 0)),
        ],
        out_specs=(
            pl.BlockSpec((3, share, width), lambda j: (0, 0, 0)),
            pl.BlockSpec((padded, width), lambda j: (0, 0)),
        ),
        scratch_shapes=[
            pltpu.VMEM((2, tokens, width), BF16),
            pltpu.VMEM((2, tokens, width), BF16),
            pltpu.VMEM((3, share, width), F32),
            pltpu.VMEM((padded, width), F32),
            pltpu.SemaphoreType.DMA((2, 2)),
        ],
        compiler_params=pltpu.CompilerParams(vmem_limit_bytes=VMEM_LIMIT),
        cost_estimate=pl.CostEstimate(
            flops=6 * count * tokens * width * share,
            bytes_accessed=4 * count * tokens * width,
            transcendentals=0,
        ),
        name="shared_grads",
    )(*x_blocks, *g_blocks, sact, sdpair, dl)


def on_device(
    hidden_in,
    cotangent,
    gain_attn,
    qkv_weight,
    qkv_bias,
    out_weight,
    gain_ffn,
    router_weight,
    routes,
    shared_gate,
    shared_in,
    shared_out,
    expert_in,
    expert_out,
):
    tokens, width = hidden_in.shape
    ctx_count = lax.axis_size("ctx")
    heads_local = qkv_weight.shape[2] // HD
    local = expert_in.shape[0]
    experts = local * ctx_count
    top_count = routes.shape[1]
    capacity = 3 * tokens * top_count // (2 * experts)
    place = lax.axis_index("ctx")
    order = jnp.arange(ctx_count, dtype=jnp.int32) ^ place
    score_scale = 1.0 / math.sqrt(HD)
    query_pos = place * tokens + jnp.arange(tokens, dtype=jnp.int32)
    cosine, sine = rotary_tables(query_pos, HD)

    x_full = hidden_in.astype(F32)
    inv_one = lax.rsqrt(jnp.mean(x_full * x_full, axis=-1, keepdims=True) + EPS)
    normed_one = x_full * inv_one
    x_one = (normed_one * gain_attn).astype(BF16)
    projected = (
        jnp.einsum("td,dcf->ctf", x_one, qkv_weight, preferred_element_type=F32)
        + qkv_bias[:, None]
    )
    shaped = projected.reshape(3, tokens, heads_local, HD).transpose(0, 2, 1, 3)
    query = rotate(shaped[0], cosine, sine).astype(BF16)
    key_local = rotate(shaped[1], cosine, sine).astype(BF16)
    value_local = shaped[2].astype(BF16)
    kv_blocks = gather_ctx(jnp.stack([key_local, value_local]))
    g_blocks = gather_ctx(cotangent)

    share = shared_out.shape[0] // ctx_count
    piece = shared_out.shape[1]
    shared_send = jnp.concatenate(
        [
            shared_in.transpose(1, 2, 0).reshape(2, ctx_count, share, piece),
            shared_out.reshape(1, ctx_count, share, piece),
        ],
        axis=0,
    ).transpose(1, 0, 2, 3)
    shared_w = (
        lax.all_to_all(shared_send, "ctx", split_axis=0, concat_axis=0, tiled=True)
        .transpose(1, 2, 0, 3)
        .reshape(3, share, width)
    )
    out_full = gather_tp_rows(out_weight)

    routes_all = jnp.stack(gather_ctx(routes))
    own_experts = place * local + jnp.arange(local, dtype=jnp.int32)
    hit = jnp.any(routes_all[:, None] == own_experts[None, :, None, None], axis=-1)
    rank = jnp.cumsum(hit.astype(jnp.int32), axis=-1) - 1
    slot_rows = jnp.where(hit, rank, -1)
    slot_cols = slot_rows.transpose(0, 2, 1)
    padded = -(-(experts + 1) // 8) * 8
    w_router = jnp.concatenate(
        [
            router_weight.T,
            shared_gate[None],
            jnp.zeros((padded - experts - 1, width), BF16),
        ],
        axis=0,
    )
    w_in = expert_in.transpose(0, 2, 3, 1)

    attended, lse = attend(place, query, kv_blocks)
    att = attended.astype(BF16).transpose(1, 0, 2).reshape(tokens, heads_local * HD)
    att_all = lax.all_gather(att, "tp", axis=0)
    hidden = x_full + jnp.einsum(
        "ptf,pfd->td",
        att_all,
        out_full.reshape(att_all.shape[0], -1, width),
        preferred_element_type=F32,
    )
    inv_two = lax.rsqrt(jnp.mean(hidden * hidden, axis=-1, keepdims=True) + EPS)
    normed_two = hidden * inv_two
    x_two = (normed_two * gain_ffn).astype(BF16)

    x_blocks = gather_ctx(x_two)
    units, group = expert_out.shape[1], 2
    kept = [
        jax.ShapeDtypeStruct((ctx_count,) + shape, BF16)
        for shape in (
            (local, capacity, width),
            (local, capacity, width),
            (local, capacity, units),
            (local, 2, capacity, units),
            (tokens, share),
            (2, tokens, share),
            (2, padded, tokens),
        )
    ]
    outs, dxs = [], []
    for at in range(0, ctx_count, group):
        out, dx, kept = run_experts(
            at,
            place * local,
            x_blocks[at : at + group],
            g_blocks[at : at + group],
            slot_rows,
            slot_cols,
            w_in,
            expert_out,
            shared_w,
            w_router,
            kept,
        )
        outs += out
        dxs += dx
    grad_x_part = scatter_ctx(dxs)
    out_part = scatter_ctx(outs)
    rows_x, rows_g, act_low, dpair, s_act, s_dpair, low_logits = kept
    grad_expert_in = jnp.einsum("becd,bevcf->edvf", rows_x, dpair, preferred_element_type=F32)
    grad_expert_out = jnp.einsum("becf,becd->efd", act_low, rows_g, preferred_element_type=F32)
    shared_low, router_part = shared_grads(x_blocks, g_blocks, s_act, s_dpair, low_logits)
    shared_back = lax.all_to_all(
        shared_low.reshape(3, share, ctx_count, piece).transpose(2, 0, 1, 3),
        "ctx",
        split_axis=0,
        concat_axis=0,
        tiled=True,
    ).astype(F32)
    grad_shared_in = shared_back[:, :2].transpose(3, 1, 0, 2).reshape(shared_in.shape)
    grad_shared_out = shared_back[:, 2].reshape(shared_out.shape)

    summed = lax.psum(grad_x_part.astype(BF16), "tp").astype(F32)
    ffn_full = lax.psum(out_part.astype(BF16), "tp").astype(F32)
    grad_y = cotangent.astype(F32)
    grad_normed_two = summed * gain_ffn
    gain_ffn_part = jnp.sum(grad_x_part * normed_two, axis=0)
    grad_hidden = grad_y + inv_two * (
        grad_normed_two
        - normed_two * jnp.mean(grad_normed_two * normed_two, axis=-1, keepdims=True)
    )
    grad_hidden_low = grad_hidden.astype(BF16)
    out_weight_part = dot(att, grad_hidden_low, (((0,), (0,)), ((), ())))
    grad_att = (
        dot(grad_hidden_low, out_weight, (((1,), (1,)), ((), ())))
        .astype(BF16)
        .reshape(tokens, heads_local, HD)
        .transpose(1, 0, 2)
    )
    out_weight_grad = sum_ctx(out_weight_part)

    delta = jnp.sum(grad_att.astype(F32) * attended, axis=-1)
    delta = jnp.broadcast_to(delta[:, None], lse.shape)
    grad_query, grad_pairs = attend_back(place, query, grad_att, lse, delta, kv_blocks)
    grad_kv = scatter_ctx([grad_pairs[j] for j in range(ctx_count)])
    grad_raw = jnp.stack(
        [
            rotate(grad_query, cosine, -sine),
            rotate(grad_kv[0], cosine, -sine),
            grad_kv[1],
        ]
    ).astype(BF16)
    grad_raw = grad_raw.transpose(2, 0, 1, 3).reshape(tokens, 3, heads_local * HD)
    qkv_part = jnp.einsum("td,tcf->dcf", x_one, grad_raw, preferred_element_type=F32)
    bias_part = jnp.sum(grad_raw.astype(F32), axis=0)
    grad_x_one_part = jnp.einsum(
        "tcf,dcf->td", grad_raw, qkv_weight, preferred_element_type=F32
    )
    qkv_grad = sum_ctx(qkv_part.reshape(width, -1)).reshape(qkv_part.shape)
    grad_x_one_part, ffn_full = lax.optimization_barrier((grad_x_one_part, ffn_full))
    grad_x_one = lax.psum(grad_x_one_part.astype(BF16), "tp").astype(F32)
    grad_normed_one = grad_x_one * gain_attn
    gain_attn_part = jnp.sum(grad_x_one_part * normed_one, axis=0)
    grad_input = grad_hidden + inv_one * (
        grad_normed_one
        - normed_one * jnp.mean(grad_normed_one * normed_one, axis=-1, keepdims=True)
    )
    block_out = (hidden + ffn_full).astype(BF16)
    bias_grad = lax.psum(bias_part, "ctx")
    gain_attn_grad, gain_ffn_grad, router_both = lax.psum(
        (gain_attn_part, gain_ffn_part, router_part), ("ctx", "tp")
    )
    return (
        block_out,
        grad_input,
        gain_attn_grad,
        qkv_grad,
        bias_grad,
        out_weight_grad,
        gain_ffn_grad,
        router_both[:experts].T,
        router_both[experts],
        grad_shared_in,
        grad_shared_out,
        grad_expert_in,
        grad_expert_out,
    )


def solution(mesh):
    return jax.shard_map(
        on_device,
        mesh=mesh,
        in_specs=(
            P("ctx", None),
            P("ctx", None),
            P(),
            P(None, None, "tp"),
            P(None, "tp"),
            P("tp", None),
            P(),
            P(),
            P("ctx", None),
            P(),
            P("ctx", None, "tp"),
            P("tp", "ctx"),
            P("ctx", None, None, "tp"),
            P("ctx", "tp", None),
        ),
        out_specs=(
            P("ctx", None),
            P("ctx", None),
            P(),
            P(None, None, "tp"),
            P(None, "tp"),
            P("tp", None),
            P(),
            P(),
            P(),
            P("ctx", None, "tp"),
            P("tp", "ctx"),
            P("ctx", None, None, "tp"),
            P("ctx", "tp", None),
        ),
        check_vma=False,
    )
```

```python
import functools
import math

import jax
import jax.numpy as jnp
from jax import lax
from jax.experimental import pallas as pl
from jax.experimental.pallas import tpu as pltpu
from jax.sharding import PartitionSpec as P

HD = 128
EPS = 1e-06
THETA = 1000000.0
NEG = -1e30
F32 = jnp.float32
BF16 = jnp.bfloat16


def rotary_tables(positions, width):
    half_width = width // 2
    freqs = THETA ** (-(jnp.arange(half_width, dtype=F32) * 2.0) / width)
    angles = positions.astype(F32)[:, None] * freqs[None, :]
    return (jnp.cos(angles), jnp.sin(angles))


def rotate(values, cosine, sine):
    half_width = values.shape[-1] // 2
    first, second = values[..., :half_width], values[..., half_width:]
    return jnp.concatenate(
        [first * cosine - second * sine, second * cosine + first * sine], axis=-1
    )


def dot(a, b, dims):
    return lax.dot_general(a, b, dims, preferred_element_type=F32)


def swap(value, bits):
    count = lax.axis_size("ctx")
    return lax.ppermute(value, "ctx", [(i, i ^ bits) for i in range(count)])


def relative(natural):
    count = natural.shape[0]
    order = jnp.arange(count, dtype=jnp.int32) ^ lax.axis_index("ctx")
    return natural[order]


def after(value, *others):
    return lax.optimization_barrier((value,) + others)[0]


def gather_start(own):
    if lax.axis_size("ctx") != 8:
        return relative(lax.all_gather(own, "ctx", axis=0))
    return [own, swap(own, 1), swap(own, 2), swap(own, 4)]


def gather_end(got, *others):
    if lax.axis_size("ctx") != 8:
        return [got[j] for j in range(lax.axis_size("ctx"))]
    own, b1, b2, b4 = got
    if others:
        b2, b4 = lax.optimization_barrier((b2, b4) + others)[:2]
    half = own.shape[0] // 2
    via_x, via_y = swap(b4[:half], 2), swap(b2[half:], 4)
    b3, b5 = swap(b2, 1), swap(b4, 1)
    b6 = jnp.concatenate([via_x, via_y], axis=0)
    return [own, b1, b2, b3, b4, b5, b6, swap(b6, 1)]


def gather_ctx(own, *others):
    return gather_end(gather_start(own), *others)


def scatter_ctx(parts):
    count = lax.axis_size("ctx")
    if count != 8:
        natural = relative(jnp.stack(parts))
        flat = natural.reshape((-1,) + natural.shape[2:])
        return lax.psum_scatter(flat, "ctx", scatter_dimension=0, tiled=True).astype(F32)
    half = parts[0].shape[0] // 2
    pair = {j: parts[j].astype(F32) + swap(parts[j ^ 1], 1).astype(F32) for j in (2, 4, 6, 0)}
    r2 = swap(pair[2][:half].astype(BF16), 2)
    r4 = swap(pair[4][half:].astype(BF16), 4)
    q6 = pair[6].astype(BF16)
    via_x, via_y = swap(q6[:half], 2), swap(q6[half:], 4)
    r4a = swap((pair[4][:half] + via_x.astype(F32)).astype(BF16), 4)
    r2b = swap((pair[2][half:] + via_y.astype(F32)).astype(BF16), 2)
    low = r2.astype(F32) + r4a.astype(F32)
    high = r2b.astype(F32) + r4.astype(F32)
    return pair[0] + jnp.concatenate([low, high], axis=0)


def sum_ctx(parts):
    return gather_ctx(scatter_ctx(parts).astype(BF16))


def shards(value):
    count = lax.axis_size("ctx")
    rows = value.shape[0] // count
    place = lax.axis_index("ctx")
    return [lax.dynamic_slice_in_dim(value, (place ^ j) * rows, rows, 0) for j in range(count)]


def along(value, step):
    count = lax.axis_size("tp")
    return lax.ppermute(
        value, "tp", [(i, i + step) for i in range(count) if 0 <= i + step < count]
    )


def gather_tp(own):
    count = lax.axis_size("tp")
    at = lax.axis_index("tp")
    ups, downs = [own], [own]
    for _ in range(count - 1):
        ups.append(along(ups[-1], 1))
        downs.append(along(downs[-1], -1))
    return [own] + [jnp.where(at >= k, ups[k], downs[count - k]) for k in range(1, count)]


def sum_tp(value):
    count = lax.axis_size("tp")
    at = lax.axis_index("tp")
    rows = value.shape[0] // count

    def piece(which):
        which = jnp.clip(which, 0, count - 1)
        return lax.dynamic_slice_in_dim(value, which * rows, rows, 0)

    up = piece(at + count - 1)
    down = piece(at - count + 1)
    for step in range(1, count):
        got_up = along(up.astype(BF16), 1).astype(F32)
        got_down = along(down.astype(BF16), -1).astype(F32)
        up = piece(at + count - 1 - step) + jnp.where(at + count - 1 - step < count, got_up, 0.0)
        down = piece(at - count + 1 + step) + jnp.where(at - count + 1 + step >= 0, got_down, 0.0)
    total = up + down - piece(at)
    blocks = gather_tp(total.astype(BF16))
    whole = jnp.zeros(value.shape, BF16)
    for k in range(count):
        start = lax.rem(at - k + count, count) * rows
        whole = lax.dynamic_update_slice_in_dim(whole, blocks[k], start, 0)
    return whole.astype(F32)


def gather_tp_rows(own):
    half = own.shape[0] // 2
    core = lax.axis_index("ctx") % 2
    mine = lax.all_gather(lax.dynamic_slice_in_dim(own, core * half, half, 0), "tp", axis=0)
    other = swap(mine, 1)
    first = jnp.where(core == 0, mine, other)
    second = jnp.where(core == 0, other, mine)
    return jnp.concatenate([first, second], axis=1)


NT = (((1,), (1,)), ((), ()))
NN = (((1,), (0,)), ((), ()))
TN = (((0,), (0,)), ((), ()))
VMEM_LIMIT = 60 * 1024 * 1024


def attend_kernel(factor, count, place_ref, q_ref, *refs):
    kv_refs, (att_ref, lse_ref, kv, sems) = refs[:count], refs[count:]
    copies = [pltpu.make_async_copy(kv_refs[j], kv.at[j], sems.at[j]) for j in range(count)]
    for copy in copies:
        copy.start()
    for copy in copies:
        copy.wait()
    place = place_ref[0]
    heads, tokens, _ = q_ref.shape

    def one_head(head, _):
        query = q_ref[head]

        def scores(j):
            return dot(kv[j, 0, head], query, NT) * factor

        key_at = lax.broadcasted_iota(jnp.int32, (tokens, tokens), 0)
        query_at = lax.broadcasted_iota(jnp.int32, (tokens, tokens), 1)
        first = jnp.where(key_at <= query_at, scores(0), NEG)
        top = jnp.max(first, axis=0, keepdims=True)
        exps = jnp.exp2(first - top)
        total = jnp.sum(exps, axis=0, keepdims=True)
        acc = dot(kv[0, 1, head], exps.astype(BF16), TN)

        def earlier(i, carry):
            top, total, acc = carry
            j = place ^ i
            now = scores(j)
            higher = jnp.maximum(top, jnp.max(now, axis=0, keepdims=True))
            exps = jnp.exp2(now - higher)
            keep = jnp.exp2(top - higher)
            total = total * keep + jnp.sum(exps, axis=0, keepdims=True)
            acc = acc * keep + dot(kv[j, 1, head], exps.astype(BF16), TN)
            return higher, total, acc

        top, total, acc = lax.fori_loop(0, place, earlier, (top, total, acc))
        att_ref[head] = (acc / total).T
        lse_ref[head] = jnp.broadcast_to(top + jnp.log2(total), lse_ref.shape[1:])
        return 0

    lax.fori_loop(0, heads, one_head, 0)


def attend(place, query, kv_blocks):
    heads, tokens, size = query.shape
    count = len(kv_blocks)
    factor = math.log2(math.e) / math.sqrt(size)
    flops = 4 * count * heads * tokens * tokens * size
    return pl.pallas_call(
        functools.partial(attend_kernel, factor, count),
        out_shape=(
            jax.ShapeDtypeStruct((heads, tokens, size), F32),
            jax.ShapeDtypeStruct((heads, 8, tokens), F32),
        ),
        in_specs=[
            pl.BlockSpec(memory_space=pltpu.SMEM),
            pl.BlockSpec(memory_space=pltpu.VMEM),
        ]
        + [pl.BlockSpec(memory_space=pl.ANY)] * count,
        out_specs=(pl.BlockSpec(memory_space=pltpu.VMEM),) * 2,
        scratch_shapes=[
            pltpu.VMEM((count, 2, heads, tokens, size), BF16),
            pltpu.SemaphoreType.DMA((count,)),
        ],
        compiler_params=pltpu.CompilerParams(vmem_limit_bytes=VMEM_LIMIT),
        cost_estimate=pl.CostEstimate(
            flops=flops, bytes_accessed=count * heads * tokens * size * 4, transcendentals=0
        ),
        name="attend",
    )(place.reshape(1), query, *kv_blocks)


def attend_back_kernel(factor, scale, count, place_ref, q_ref, do_ref, lse_ref, delta_ref, *refs):
    kv_refs, (dq_ref, dkv_ref, kv, dkv, dq, sems, out_sems) = refs[:count], refs[count:]
    copies = [pltpu.make_async_copy(kv_refs[j], kv.at[j], sems.at[j]) for j in range(count)]
    for copy in copies:
        copy.start()
    for copy in copies:
        copy.wait()
    place = place_ref[0]
    heads, tokens, _ = q_ref.shape

    def out_copy(j):
        return pltpu.make_async_copy(dkv.at[j], dkv_ref.at[j], out_sems.at[j])

    def one_block(j, masked):
        def one_head(head, _):
            query, do = q_ref[head], do_ref[head]
            key, value = kv[j, 0, head], kv[j, 1, head]
            scores = dot(key, query, NT) * factor
            probs = jnp.exp2(scores - lse_ref[head, :1])
            if masked:
                key_at = lax.broadcasted_iota(jnp.int32, (tokens, tokens), 0)
                query_at = lax.broadcasted_iota(jnp.int32, (tokens, tokens), 1)
                probs = jnp.where(key_at <= query_at, probs, 0.0)
            dprob = dot(value, do, NT)
            dscore = (probs * (dprob - delta_ref[head, :1])).astype(BF16)
            dkv[j, 0, head] = (dot(dscore, query, NN) * scale).astype(BF16)
            dkv[j, 1, head] = dot(probs.astype(BF16), do, NN).astype(BF16)
            part = dot(key, dscore, TN)
            dq[head] = part if masked else dq[head] + part
            return 0

        lax.fori_loop(0, heads, one_head, 0)
        out_copy(j).start()

    one_block(0, True)

    def earlier(i, _):
        one_block(place ^ i, False)
        return 0

    def later(i, _):
        j = place ^ i
        dkv[j] = jnp.zeros(dkv.shape[1:], BF16)
        out_copy(j).start()
        return 0

    lax.fori_loop(0, place, earlier, 0)
    lax.fori_loop(place + 1, count, later, 0)
    for head in range(heads):
        dq_ref[head] = dq[head].T * scale
    for j in range(count):
        out_copy(j).wait()


def attend_back(place, query, do, lse, delta, kv_blocks):
    heads, tokens, size = query.shape
    count = len(kv_blocks)
    scale = 1.0 / math.sqrt(size)
    factor = math.log2(math.e) * scale
    return pl.pallas_call(
        functools.partial(attend_back_kernel, factor, scale, count),
        out_shape=(
            jax.ShapeDtypeStruct((heads, tokens, size), F32),
            jax.ShapeDtypeStruct((count, 2, heads, tokens, size), BF16),
        ),
        in_specs=[pl.BlockSpec(memory_space=pltpu.SMEM)]
        + [pl.BlockSpec(memory_space=pltpu.VMEM)] * 4
        + [pl.BlockSpec(memory_space=pl.ANY)] * count,
        out_specs=(pl.BlockSpec(memory_space=pltpu.VMEM), pl.BlockSpec(memory_space=pl.ANY)),
        scratch_shapes=[
            pltpu.VMEM((count, 2, heads, tokens, size), BF16),
            pltpu.VMEM((count, 2, heads, tokens, size), BF16),
            pltpu.VMEM((heads, size, tokens), F32),
            pltpu.SemaphoreType.DMA((count,)),
            pltpu.SemaphoreType.DMA((count,)),
        ],
        compiler_params=pltpu.CompilerParams(vmem_limit_bytes=VMEM_LIMIT),
        cost_estimate=pl.CostEstimate(
            flops=10 * count * heads * tokens * tokens * size,
            bytes_accessed=count * heads * tokens * size * 8,
            transcendentals=0,
        ),
        name="attend_back",
    )(place.reshape(1), query, do, lse, delta, *kv_blocks)


def swiglu_back(rows_x, rows_g, gate, w_one, w_two, w_out):
    one, two = dot(rows_x, w_one, NT), dot(rows_x, w_two, NT)
    dact = dot(rows_g, w_out, NT)
    sig = 1.0 / (1.0 + jnp.exp(-one))
    silu = one * sig
    act = silu * two
    prod = act * dact
    dgate = gate * dact
    d_one = (dgate * two * sig * (1.0 + one * (1.0 - sig))).astype(BF16)
    d_two = (dgate * silu).astype(BF16)
    return (gate * act).astype(BF16), d_one, d_two, prod


def split_low(value):
    high = value.astype(BF16)
    return high, (value - high.astype(F32)).astype(BF16)


def experts_kernel(group, local, experts, given, first_ref, *refs):
    x_refs, g_refs, refs = refs[:group], refs[group : 2 * group], refs[2 * group :]
    (slot_row, slot_col, w_in, w_out, w_shared, w_router), refs = refs[:6], refs[6 + given :]
    dx_refs, refs = refs[:group], refs[group:]
    (rows_x_ref, rows_g_ref, act_ref, dpair_ref, sact_ref, sdpair_ref, dl_ref) = refs[:7]
    (xs, gs, dxs, left, right, probs, dl, in_sems, out_sems) = refs[7:]
    phase = pl.program_id(0)
    tokens, width = xs.shape[1:]
    capacity = rows_x_ref.shape[2]
    wide = local * capacity
    units = act_ref.shape[3]
    share = sact_ref.shape[2]
    row_at = lax.broadcasted_iota(jnp.int32, probs.shape[1:], 0)

    def load(which, b):
        refs, into = ((x_refs, xs), (g_refs, gs))[which]
        return pltpu.make_async_copy(refs[b], into.at[b], in_sems.at[which, b])

    def store(b):
        return pltpu.make_async_copy(dxs.at[b], dx_refs[b], out_sems.at[b])

    @pl.when(phase == 0)
    def _():
        for b in range(group):
            load(0, b).start()
            load(1, b).start()
        for b in range(group):
            slot_at = lax.broadcasted_iota(jnp.int32, (capacity, tokens), 0)
            picks = jnp.concatenate(
                [
                    jnp.where(slot_at == slot_row[b, e : e + 1, :], 1.0, 0.0).astype(BF16)
                    for e in range(local)
                ],
                axis=0,
            )
            load(0, b).wait()
            logits = dot(w_router[...], xs[b], NT)
            shown = jnp.where(row_at < experts, logits, NEG)
            exps = jnp.exp(shown - jnp.max(shown, axis=0, keepdims=True))
            soft = exps / jnp.sum(exps, axis=0, keepdims=True)
            probs[b] = jnp.where(row_at == experts, 1.0 / (1.0 + jnp.exp(-logits)), soft)
            dl[b] = jnp.zeros(dl.shape[1:], F32)
            rows = dot(picks, xs[b], NN).astype(BF16)
            for e in range(local):
                rows_x_ref[e, b] = rows[e * capacity : (e + 1) * capacity]
            load(1, b).wait()
            rows = dot(picks, gs[b], NN).astype(BF16)
            for e in range(local):
                rows_g_ref[e, b] = rows[e * capacity : (e + 1) * capacity]

    for e in range(local):

        @pl.when(phase == e)
        def _():
            chosen = row_at == first_ref[0] + e
            is_expert = row_at < experts
            hits, gates, owns = [], [], []
            slot_at = lax.broadcasted_iota(jnp.int32, (capacity, tokens), 0)
            for b in range(group):
                own = jnp.sum(jnp.where(chosen, probs[b], 0.0), axis=0, keepdims=True)
                hit = slot_at == slot_row[b, e : e + 1, :]
                gates.append(jnp.sum(jnp.where(hit, own, 0.0), axis=1, keepdims=True))
                hits.append(hit)
                owns.append(own)
            rows_x = rows_x_ref[e].reshape(group * capacity, width)
            rows_g = rows_g_ref[e].reshape(group * capacity, width)
            act, d_one, d_two, prod = swiglu_back(
                rows_x, rows_g, jnp.concatenate(gates, axis=0), w_in[0, 0], w_in[0, 1], w_out[0]
            )
            act_ref[e] = act[:, :units].reshape(group, capacity, units)
            dpair_ref[e, 0] = d_one[:, :units].reshape(group, capacity, units)
            dpair_ref[e, 1] = d_two[:, :units].reshape(group, capacity, units)
            row_dot = jnp.sum(prod, axis=1, keepdims=True)
            drow = (dot(d_one, w_in[0, 0], NN) + dot(d_two, w_in[0, 1], NN)).astype(BF16)
            for b in range(group):
                at = slice(b * capacity, (b + 1) * capacity)
                found = jnp.sum(jnp.where(hits[b], row_dot[at], 0.0), axis=0, keepdims=True)
                dl[b] += (found * owns[b]) * (
                    jnp.where(chosen, 1.0, 0.0) - jnp.where(is_expert, probs[b], 0.0)
                )
                right[b, e * capacity : (e + 1) * capacity] = drow[at]

    @pl.when(phase == local)
    def _():
        x = xs[...].reshape(group * tokens, width)
        g = gs[...].reshape(group * tokens, width)
        columns = dot(x, w_router[...], NT)
        lane = lax.broadcasted_iota(jnp.int32, columns.shape, 1)
        logit = jnp.sum(jnp.where(lane == experts, columns, 0.0), axis=1, keepdims=True)
        gate = 1.0 / (1.0 + jnp.exp(-logit))
        act, d_one, d_two, prod = swiglu_back(x, g, gate, w_shared[0], w_shared[1], w_shared[2])
        sact_ref[...] = act.reshape(group, tokens, share)
        sdpair_ref[:, 0] = d_one.reshape(group, tokens, share)
        sdpair_ref[:, 1] = d_two.reshape(group, tokens, share)
        ones = jnp.ones((dl.shape[1], share), BF16)
        slot_at = lax.broadcasted_iota(jnp.int32, (tokens, capacity), 1)
        for b in range(group):
            at = slice(b * tokens, (b + 1) * tokens)
            high, low = split_low(prod[at])
            dots = dot(ones, high, NT) + dot(ones, low, NT)
            change = dl[b] + jnp.where(row_at == experts, dots * probs[b] * (1.0 - probs[b]), 0.0)
            high, low = split_low(change)
            dl_ref[b, 0] = high
            dl_ref[b, 1] = low
            for e in range(local):
                picks = jnp.where(slot_at == slot_col[b, :, e : e + 1], 1.0, 0.0).astype(BF16)
                left[b, :, e * capacity : (e + 1) * capacity] = picks
            left[b, :, wide : wide + share] = d_one[at]
            left[b, :, wide + share : wide + 2 * share] = d_two[at]
            right[b, wide : wide + share] = w_shared[0]
            right[b, wide + share : wide + 2 * share] = w_shared[1]
            total = dot(left[b], right[b], NN)
            total += dot(high, w_router[...], TN) + dot(low, w_router[...], TN)
            dxs[b] = total.astype(BF16)
            store(b).start()
        for b in range(group):
            store(b).wait()


def run_experts(at, experts, first, x_group, g_group, slot_rows, slot_cols, w_in, w_out, w_shared, w_router, kept):
    given = kept if at else []
    group = len(x_group)
    tokens, width = x_group[0].shape
    local, padded_units = w_out.shape[:2]
    share = w_shared.shape[1]
    padded = w_router.shape[0]
    capacity, units = kept[2].shape[2:]
    last = lambda p: jnp.minimum(p, local - 1)
    any_spec = pl.BlockSpec(memory_space=pl.ANY)
    block = jax.ShapeDtypeStruct((tokens, width), BF16)
    deep = local * capacity + 2 * share
    flops = group * 2 * tokens * width * (local * capacity * 3 + 5 * share) + (
        group * 2 * width * local * capacity * units * 5
    )
    step = at // group
    results = pl.pallas_call(
        functools.partial(experts_kernel, group, local, experts, len(given)),
        grid=(local + 1,),
        out_shape=(block,) * group + tuple(jax.ShapeDtypeStruct(k.shape, k.dtype) for k in kept),
        in_specs=[pl.BlockSpec(memory_space=pltpu.SMEM)]
        + [any_spec] * (2 * group)
        + [
            pl.BlockSpec((group, local, tokens), lambda p: (step, 0, 0)),
            pl.BlockSpec((group, tokens, local), lambda p: (step, 0, 0)),
            pl.BlockSpec((1, 2, padded_units, width), lambda p: (last(p), 0, 0, 0)),
            pl.BlockSpec((1, padded_units, width), lambda p: (last(p), 0, 0)),
            pl.BlockSpec((3, share, width), lambda p: (0, 0, 0)),
            pl.BlockSpec((padded, width), lambda p: (0, 0)),
        ]
        + [any_spec] * len(given),
        out_specs=(any_spec,) * group
        + (
            pl.BlockSpec((local, group, capacity, width), lambda p: (0, step, 0, 0)),
            pl.BlockSpec((local, group, capacity, width), lambda p: (0, step, 0, 0)),
            pl.BlockSpec((local, group, capacity, units), lambda p: (0, step, 0, 0)),
            pl.BlockSpec((local, 2, group, capacity, units), lambda p: (0, 0, step, 0, 0)),
            pl.BlockSpec((group, tokens, share), lambda p: (step, 0, 0)),
            pl.BlockSpec((group, 2, tokens, share), lambda p: (step, 0, 0, 0)),
            pl.BlockSpec((group, 2, padded, tokens), lambda p: (step, 0, 0, 0)),
        ),
        input_output_aliases={7 + 2 * group + i: group + i for i in range(len(given))},
        scratch_shapes=[
            pltpu.VMEM((group, tokens, width), BF16),
            pltpu.VMEM((group, tokens, width), BF16),
            pltpu.VMEM((group, tokens, width), BF16),
            pltpu.VMEM((group, tokens, deep), BF16),
            pltpu.VMEM((group, deep, width), BF16),
            pltpu.VMEM((group, padded, tokens), F32),
            pltpu.VMEM((group, padded, tokens), F32),
            pltpu.SemaphoreType.DMA((2, group)),
            pltpu.SemaphoreType.DMA((group,)),
        ],
        compiler_params=pltpu.CompilerParams(vmem_limit_bytes=VMEM_LIMIT),
        cost_estimate=pl.CostEstimate(flops=flops, bytes_accessed=20 * 2**20 * group, transcendentals=0),
        name="run_experts",
    )(first.reshape(1), *x_group, *g_group, slot_rows, slot_cols, w_in, w_out, w_shared, w_router, *given)
    return results[:group], results[group:]


def outputs_kernel(group, count, local, act, slot_col, sact, w_out, w_shared, *refs):
    out_refs, (outs, left, right, sems) = refs[:count], refs[count:]
    step = pl.program_id(0)
    slot = lax.rem(step, 2)
    capacity, units = act.shape[2:]
    tokens, share = sact.shape[1:]
    wide = local * capacity

    def store(at, b, into):
        return pltpu.make_async_copy(outs.at[into, b], out_refs[at * group + b], sems.at[into, b])

    @pl.when(step >= 2)
    def _():
        for b in range(group):
            store(0, b, slot).wait()

    for e in range(local):
        rows = dot(act[e].reshape(group * capacity, units), w_out[e], NN).astype(BF16)
        for b in range(group):
            right[b, e * capacity : (e + 1) * capacity] = rows[b * capacity : (b + 1) * capacity]
    slot_at = lax.broadcasted_iota(jnp.int32, (tokens, capacity), 1)
    for b in range(group):
        for e in range(local):
            picks = jnp.where(slot_at == slot_col[b, :, e : e + 1], 1.0, 0.0).astype(BF16)
            left[b, :, e * capacity : (e + 1) * capacity] = picks
        left[b, :, wide : wide + share] = sact[b]
        right[b, wide : wide + share] = w_shared[0]
        outs[slot, b] = dot(left[b], right[b], NN).astype(BF16)
    for at in range(count // group):

        @pl.when(step == at)
        def _():
            for b in range(group):
                store(at, b, at % 2).start()

    @pl.when(step == count // group - 1)
    def _():
        for b in range(group):
            for into in range(2):
                store(0, b, into).wait()


def run_outputs(act, slot_cols, sact, w_out, w_shared):
    local, count, capacity, units = act.shape
    tokens, share = sact.shape[1:]
    width = w_out.shape[2]
    group = 2
    deep = local * capacity + share
    return pl.pallas_call(
        functools.partial(outputs_kernel, group, count, local),
        grid=(count // group,),
        out_shape=(jax.ShapeDtypeStruct((tokens, width), BF16),) * count,
        in_specs=[
            pl.BlockSpec((local, group, capacity, units), lambda i: (0, i, 0, 0)),
            pl.BlockSpec((group, tokens, local), lambda i: (i, 0, 0)),
            pl.BlockSpec((group, tokens, share), lambda i: (i, 0, 0)),
            pl.BlockSpec((local, units, width), lambda i: (0, 0, 0)),
            pl.BlockSpec((1, share, width), lambda i: (2, 0, 0)),
        ],
        out_specs=(pl.BlockSpec(memory_space=pl.ANY),) * count,
        scratch_shapes=[
            pltpu.VMEM((2, group, tokens, width), BF16),
            pltpu.VMEM((group, tokens, deep), BF16),
            pltpu.VMEM((group, deep, width), BF16),
            pltpu.SemaphoreType.DMA((2, group)),
        ],
        compiler_params=pltpu.CompilerParams(vmem_limit_bytes=VMEM_LIMIT),
        cost_estimate=pl.CostEstimate(
            flops=count * 2 * width * (local * capacity * (units + tokens) + tokens * share),
            bytes_accessed=30 * 2**20,
            transcendentals=0,
        ),
        name="run_outputs",
    )(act, slot_cols, sact, w_out, w_shared)


def assemble_kernel(plan, place_ref, *refs):
    total = sum(count for count, _, _ in plan)
    block_refs, (out_ref, low, wide, in_sems, out_sems) = refs[:total], refs[total:]
    place = place_ref[0]
    steps, at = [], 0
    for count, rows, base in plan:
        for j in range(count):
            steps.append((at + j, rows, base + (place ^ j) * rows))
        at += count

    def load(i):
        which, rows, _ = steps[i]
        return pltpu.make_async_copy(
            block_refs[which].at[pl.ds(0, rows)], low.at[i % 2, pl.ds(0, rows)], in_sems.at[i % 2]
        )

    def store(i):
        _, rows, start = steps[i]
        return pltpu.make_async_copy(
            wide.at[i % 2, pl.ds(0, rows)],
            out_ref.at[pl.ds(pl.multiple_of(start, 8), rows)],
            out_sems.at[i % 2],
        )

    load(0).start()
    for i, (_, rows, _) in enumerate(steps):
        if i + 1 < len(steps):
            load(i + 1).start()
        load(i).wait()
        if i >= 2:
            store(i - 2).wait()
        wide[i % 2, :rows] = low[i % 2, :rows].astype(F32)
        store(i).start()
    for i in range(max(0, len(steps) - 2), len(steps)):
        store(i).wait()


def assemble(place, lists):
    plan, base = [], 0
    for blocks, rows in lists:
        plan.append((len(blocks), rows, base))
        base += len(blocks) * rows
    width = lists[0][0][0].shape[1]
    most = max(rows for _, rows in lists)
    flat = [b for blocks, _ in lists for b in blocks]
    return pl.pallas_call(
        functools.partial(assemble_kernel, plan),
        out_shape=jax.ShapeDtypeStruct((base, width), F32),
        in_specs=[pl.BlockSpec(memory_space=pltpu.SMEM)]
        + [pl.BlockSpec(memory_space=pl.ANY)] * len(flat),
        out_specs=pl.BlockSpec(memory_space=pl.ANY),
        scratch_shapes=[
            pltpu.VMEM((2, most, width), BF16),
            pltpu.VMEM((2, most, width), F32),
            pltpu.SemaphoreType.DMA((2,)),
            pltpu.SemaphoreType.DMA((2,)),
        ],
        compiler_params=pltpu.CompilerParams(vmem_limit_bytes=VMEM_LIMIT),
        cost_estimate=pl.CostEstimate(flops=0, bytes_accessed=6 * base * width, transcendentals=0),
        name="assemble",
    )(place.reshape(1), *flat)


def shared_grads_kernel(count, *refs):
    x_refs, g_refs, refs = refs[:count], refs[count : 2 * count], refs[2 * count :]
    (sact, sdpair, dl, grads_ref, router_ref, xs, gs, grads, router, sems) = refs
    at = pl.program_id(0)
    slot = lax.rem(at, 2)

    def load(j, into):
        return (
            pltpu.make_async_copy(x_refs[j], xs.at[into], sems.at[0, into]),
            pltpu.make_async_copy(g_refs[j], gs.at[into], sems.at[1, into]),
        )

    @pl.when(at == 0)
    def _():
        for copy in load(0, 0):
            copy.start()
        grads[...] = jnp.zeros_like(grads)
        router[...] = jnp.zeros_like(router)

    for j in range(1, count):

        @pl.when(at == j - 1)
        def _():
            for copy in load(j, j % 2):
                copy.start()

    for copy in load(0, slot):
        copy.wait()
    x, g = xs[slot], gs[slot]
    grads[0] += dot(sdpair[0, 0], x, TN)
    grads[1] += dot(sdpair[0, 1], x, TN)
    grads[2] += dot(sact[0], g, TN)
    router[...] += dot(dl[0, 0], x, NN) + dot(dl[0, 1], x, NN)

    @pl.when(at == count - 1)
    def _():
        grads_ref[...] = grads[...].astype(BF16)
        router_ref[...] = router[...]


def shared_grads(x_blocks, g_blocks, sact, sdpair, dl):
    count = len(x_blocks)
    tokens, width = x_blocks[0].shape
    share, padded = sact.shape[2], dl.shape[2]
    any_spec = pl.BlockSpec(memory_space=pl.ANY)
    return pl.pallas_call(
        functools.partial(shared_grads_kernel, count),
        grid=(count,),
        out_shape=(
            jax.ShapeDtypeStruct((3, share, width), BF16),
            jax.ShapeDtypeStruct((padded, width), F32),
        ),
        in_specs=[any_spec] * (2 * count)
        + [
            pl.BlockSpec((1, tokens, share), lambda j: (j, 0, 0)),
            pl.BlockSpec((1, 2, tokens, share), lambda j: (j, 0, 0, 0)),
            pl.BlockSpec((1, 2, padded, tokens), lambda j: (j, 0, 0, 0)),
        ],
        out_specs=(
            pl.BlockSpec((3, share, width), lambda j: (0, 0, 0)),
            pl.BlockSpec((padded, width), lambda j: (0, 0)),
        ),
        scratch_shapes=[
            pltpu.VMEM((2, tokens, width), BF16),
            pltpu.VMEM((2, tokens, width), BF16),
            pltpu.VMEM((3, share, width), F32),
            pltpu.VMEM((padded, width), F32),
            pltpu.SemaphoreType.DMA((2, 2)),
        ],
        compiler_params=pltpu.CompilerParams(vmem_limit_bytes=VMEM_LIMIT),
        cost_estimate=pl.CostEstimate(
            flops=6 * count * tokens * width * share,
            bytes_accessed=4 * count * tokens * width,
            transcendentals=0,
        ),
        name="shared_grads",
    )(*x_blocks, *g_blocks, sact, sdpair, dl)


def on_device(
    hidden_in,
    cotangent,
    gain_attn,
    qkv_weight,
    qkv_bias,
    out_weight,
    gain_ffn,
    router_weight,
    routes,
    shared_gate,
    shared_in,
    shared_out,
    expert_in,
    expert_out,
):
    tokens, width = hidden_in.shape
    ctx_count = lax.axis_size("ctx")
    heads_local = qkv_weight.shape[2] // HD
    local = expert_in.shape[0]
    experts = local * ctx_count
    top_count = routes.shape[1]
    capacity = 3 * tokens * top_count // (2 * experts)
    place = lax.axis_index("ctx")
    order = jnp.arange(ctx_count, dtype=jnp.int32) ^ place
    score_scale = 1.0 / math.sqrt(HD)
    query_pos = place * tokens + jnp.arange(tokens, dtype=jnp.int32)
    cosine, sine = rotary_tables(query_pos, HD)

    x_full = hidden_in.astype(F32)
    inv_one = lax.rsqrt(jnp.mean(x_full * x_full, axis=-1, keepdims=True) + EPS)
    normed_one = x_full * inv_one
    x_one = (normed_one * gain_attn).astype(BF16)
    projected = (
        jnp.einsum("td,dcf->ctf", x_one, qkv_weight, preferred_element_type=F32)
        + qkv_bias[:, None]
    )
    shaped = projected.reshape(3, tokens, heads_local, HD).transpose(0, 2, 1, 3)
    query = rotate(shaped[0], cosine, sine).astype(BF16)
    key_local = rotate(shaped[1], cosine, sine).astype(BF16)
    value_local = shaped[2].astype(BF16)
    routes_got = gather_ctx(routes)
    kv_local = after(jnp.stack([key_local, value_local]), routes_got[7 % ctx_count])
    kv_blocks = gather_ctx(kv_local)
    g_blocks = gather_ctx(after(cotangent, kv_blocks[6 % ctx_count]))

    share = shared_out.shape[0] // ctx_count
    piece = shared_out.shape[1]
    shared_send = jnp.concatenate(
        [
            shared_in.transpose(1, 2, 0).reshape(2, ctx_count, share, piece),
            shared_out.reshape(1, ctx_count, share, piece),
        ],
        axis=0,
    ).transpose(1, 0, 2, 3)
    shared_w = (
        lax.all_to_all(shared_send, "ctx", split_axis=0, concat_axis=0, tiled=True)
        .transpose(1, 2, 0, 3)
        .reshape(3, share, width)
    )
    out_full = gather_tp_rows(out_weight)

    routes_all = jnp.stack(routes_got)
    own_experts = place * local + jnp.arange(local, dtype=jnp.int32)
    hit = jnp.any(routes_all[:, None] == own_experts[None, :, None, None], axis=-1)
    rank = jnp.cumsum(hit.astype(jnp.int32), axis=-1) - 1
    slot_rows = jnp.where(hit, rank, -1)
    slot_cols = slot_rows.transpose(0, 2, 1)
    padded = -(-(experts + 1) // 8) * 8
    w_router = jnp.concatenate(
        [
            router_weight.T,
            shared_gate[None],
            jnp.zeros((padded - experts - 1, width), BF16),
        ],
        axis=0,
    )
    w_in = expert_in.transpose(0, 2, 3, 1)

    attended, lse = attend(place, query, kv_blocks)
    att = attended.astype(BF16).transpose(1, 0, 2).reshape(tokens, heads_local * HD)
    tp_at, tp_count = lax.axis_index("tp"), lax.axis_size("tp")
    hidden = x_full
    for k, block in enumerate(gather_tp(att)):
        rows = lax.dynamic_index_in_dim(
            out_full, lax.rem(tp_at - k + tp_count, tp_count), 0, keepdims=False
        )
        hidden = hidden + dot(block, rows, NN)
    inv_two = lax.rsqrt(jnp.mean(hidden * hidden, axis=-1, keepdims=True) + EPS)
    normed_two = hidden * inv_two
    x_two = (normed_two * gain_ffn).astype(BF16)

    units, group = expert_out.shape[1], 2
    kept = [
        jax.ShapeDtypeStruct(shape, BF16)
        for shape in (
            (local, ctx_count, capacity, width),
            (local, ctx_count, capacity, width),
            (local, ctx_count, capacity, units),
            (local, 2, ctx_count, capacity, units),
            (ctx_count, tokens, share),
            (ctx_count, 2, tokens, share),
            (ctx_count, 2, padded, tokens),
        )
    ]
    extra = -units % 128
    w_in = jnp.pad(w_in, ((0, 0), (0, 0), (0, extra), (0, 0)))
    w_out = jnp.pad(expert_out, ((0, 0), (0, extra), (0, 0)))
    got = gather_start(x_two)
    x_blocks = [got[0], got[1]]
    dxs = []
    for at in range(0, ctx_count, group):
        dx, kept = run_experts(
            at,
            experts,
            place * local,
            x_blocks[at : at + group],
            g_blocks[at : at + group],
            slot_rows,
            slot_cols,
            w_in,
            w_out,
            shared_w,
            w_router,
            kept,
        )
        dxs += dx
        if at == 0:
            x_blocks = gather_end(got, dx[0])
    rows_x, rows_g, act_low, dpair, s_act, s_dpair, low_logits = kept
    grad_x_part = scatter_ctx(dxs)
    outs = run_outputs(act_low, slot_cols, s_act, expert_out, shared_w)
    outs = lax.optimization_barrier(tuple(outs) + (grad_x_part,))[:ctx_count]
    out_part = scatter_ctx(outs)
    grad_expert_in = jnp.einsum("ebcd,evbcf->edvf", rows_x, dpair, preferred_element_type=F32)
    grad_expert_out = jnp.einsum("ebcf,ebcd->efd", act_low, rows_g, preferred_element_type=F32)
    shared_low, router_part = shared_grads(x_blocks, g_blocks, s_act, s_dpair, low_logits)
    shared_back = lax.all_to_all(
        shared_low.reshape(3, share, ctx_count, piece).transpose(2, 0, 1, 3),
        "ctx",
        split_axis=0,
        concat_axis=0,
        tiled=True,
    ).astype(F32)
    grad_shared_in = shared_back[:, :2].transpose(3, 1, 0, 2).reshape(shared_in.shape)
    grad_shared_out = shared_back[:, 2].reshape(shared_out.shape)

    summed = sum_tp(grad_x_part)
    ffn_full = lax.psum(after(out_part.astype(BF16), summed), "tp").astype(F32)
    grad_y = cotangent.astype(F32)
    grad_normed_two = summed * gain_ffn
    gain_ffn_part = jnp.sum(grad_x_part * normed_two, axis=0)
    grad_hidden = grad_y + inv_two * (
        grad_normed_two
        - normed_two * jnp.mean(grad_normed_two * normed_two, axis=-1, keepdims=True)
    )
    grad_hidden_low = grad_hidden.astype(BF16)
    out_weight_part = dot(att, grad_hidden_low, (((0,), (0,)), ((), ())))
    grad_att = (
        dot(grad_hidden_low, out_weight, (((1,), (1,)), ((), ())))
        .astype(BF16)
        .reshape(tokens, heads_local, HD)
        .transpose(1, 0, 2)
    )
    small = lax.psum(jnp.concatenate([router_part, gain_ffn_part[None]], axis=0), "tp")
    spare = 16 * ctx_count
    small = jnp.pad(small, ((0, spare - padded - 1), (0, 0))).astype(BF16)
    first_sums = sum_ctx(
        [
            jnp.concatenate([a, b], axis=0)
            for a, b in zip(shards(out_weight_part.astype(BF16)), shards(small))
        ]
    )
    out_rows = out_weight.shape[0] // ctx_count
    out_weight_grad = assemble(place, [(first_sums, out_rows)])
    small = relative(jnp.stack([b[out_rows:] for b in first_sums])).reshape(spare, width)
    small = small.astype(F32)

    delta = jnp.sum(grad_att.astype(F32) * attended, axis=-1)
    delta = jnp.broadcast_to(delta[:, None], lse.shape)
    grad_query, grad_pairs = attend_back(place, query, grad_att, lse, delta, kv_blocks)
    grad_kv = scatter_ctx([grad_pairs[j] for j in range(ctx_count)])
    def raw_part(value):
        return value.astype(BF16).transpose(1, 0, 2).reshape(tokens, heads_local * HD)

    raw = [
        raw_part(rotate(grad_query, cosine, -sine)),
        raw_part(rotate(grad_kv[0], cosine, -sine)),
        raw_part(grad_kv[1]),
    ]
    grad_x_one_part = sum(
        dot(raw[c], qkv_weight[:, c], NT) for c in range(3)
    )
    grad_x_one = sum_tp(grad_x_one_part)
    gain_attn_part = jnp.sum(grad_x_one_part * normed_one, axis=0)
    gain_sum = gain_attn_part
    bits = 1
    while bits < tp_count:
        gain_sum = gain_sum + lax.ppermute(gain_sum, "tp", [(i, i ^ bits) for i in range(tp_count)])
        bits *= 2
    head_width = heads_local * HD
    gain_rows = width // head_width
    ends = jnp.concatenate(
        [jnp.sum(r.astype(F32), axis=0)[None] for r in raw] + [gain_sum.reshape(gain_rows, -1)], axis=0
    )
    ends = jnp.pad(ends, ((0, spare - 3 - gain_rows), (0, 0))).astype(BF16)
    query_part = dot(x_one, raw[0], TN).astype(BF16)
    pair_part = jnp.concatenate([dot(x_one, raw[1], TN), dot(x_one, raw[2], TN)], axis=0).astype(BF16)
    query_sums = sum_ctx(shards(query_part))
    pair_sums = sum_ctx(
        [jnp.concatenate([a, b], axis=0) for a, b in zip(shards(pair_part), shards(ends))]
    )
    q_rows = width // ctx_count
    qkv_grad = assemble(place, [(query_sums, q_rows), (pair_sums, 2 * q_rows)])
    qkv_grad = qkv_grad.reshape(3, width, head_width).transpose(1, 0, 2)
    ends = relative(jnp.stack([b[2 * q_rows :] for b in pair_sums])).reshape(spare, head_width)
    ends = ends.astype(F32)
    grad_normed_one = grad_x_one * gain_attn
    grad_input = grad_hidden + inv_one * (
        grad_normed_one
        - normed_one * jnp.mean(grad_normed_one * normed_one, axis=-1, keepdims=True)
    )
    block_out = (hidden + ffn_full).astype(BF16)
    return (
        block_out,
        grad_input,
        ends[3 : 3 + gain_rows].reshape(-1),
        qkv_grad,
        ends[:3],
        out_weight_grad,
        small[padded],
        small[:experts].T,
        small[experts],
        grad_shared_in,
        grad_shared_out,
        grad_expert_in,
        grad_expert_out,
    )


def solution(mesh):
    return jax.shard_map(
        on_device,
        mesh=mesh,
        in_specs=(
            P("ctx", None),
            P("ctx", None),
            P(),
            P(None, None, "tp"),
            P(None, "tp"),
            P("tp", None),
            P(),
            P(),
            P("ctx", None),
            P(),
            P("ctx", None, "tp"),
            P("tp", "ctx"),
            P("ctx", None, None, "tp"),
            P("ctx", "tp", None),
        ),
        out_specs=(
            P("ctx", None),
            P("ctx", None),
            P(),
            P(None, None, "tp"),
            P(None, "tp"),
            P("tp", None),
            P(),
            P(),
            P(),
            P("ctx", None, "tp"),
            P("tp", "ctx"),
            P("ctx", None, None, "tp"),
            P("ctx", "tp", None),
        ),
        check_vma=False,
    )
```

```python
import functools
import math

import jax
import jax.numpy as jnp
from jax import lax
from jax.experimental import pallas as pl
from jax.experimental.pallas import tpu as pltpu
from jax.sharding import PartitionSpec as P

HD = 128
EPS = 1e-06
THETA = 1000000.0
NEG = -1e30
F32 = jnp.float32
BF16 = jnp.bfloat16


def rotary_tables(positions, width):
    half_width = width // 2
    freqs = THETA ** (-(jnp.arange(half_width, dtype=F32) * 2.0) / width)
    angles = positions.astype(F32)[:, None] * freqs[None, :]
    return (jnp.cos(angles), jnp.sin(angles))


def rotate(values, cosine, sine):
    half_width = values.shape[-1] // 2
    first, second = values[..., :half_width], values[..., half_width:]
    return jnp.concatenate(
        [first * cosine - second * sine, second * cosine + first * sine], axis=-1
    )


def dot(a, b, dims):
    return lax.dot_general(a, b, dims, preferred_element_type=F32)


def swap(value, bits):
    count = lax.axis_size("ctx")
    return lax.ppermute(value, "ctx", [(i, i ^ bits) for i in range(count)])


def relative(natural):
    count = natural.shape[0]
    order = jnp.arange(count, dtype=jnp.int32) ^ lax.axis_index("ctx")
    return natural[order]


def nothing_kernel(*refs):
    pass


def after(values, *others):
    single = not isinstance(values, (list, tuple))
    values = [values] if single else list(values)
    any_spec = pl.BlockSpec(memory_space=pl.ANY)
    results = pl.pallas_call(
        nothing_kernel,
        out_shape=[jax.ShapeDtypeStruct(v.shape, v.dtype) for v in values],
        in_specs=[any_spec] * (len(values) + len(others)),
        out_specs=[any_spec] * len(values),
        input_output_aliases={i: i for i in range(len(values))},
        name="after",
    )(*values, *others)
    return results[0] if single else results


def gather_start(own):
    if lax.axis_size("ctx") != 8:
        return relative(lax.all_gather(own, "ctx", axis=0))
    return [own, swap(own, 1), swap(own, 2), swap(own, 4)]


def gather_end(got, *others):
    if lax.axis_size("ctx") != 8:
        return [got[j] for j in range(lax.axis_size("ctx"))]
    own, b1, b2, b4 = got
    if others:
        b2, b4 = after((b2, b4), *others)
    half = own.shape[0] // 2
    via_x, via_y = swap(b4[:half], 2), swap(b2[half:], 4)
    b3, b5 = swap(b2, 1), swap(b4, 1)
    b6 = jnp.concatenate([via_x, via_y], axis=0)
    return [own, b1, b2, b3, b4, b5, b6, swap(b6, 1)]


def gather_ctx(own, *others):
    return gather_end(gather_start(own), *others)


def scatter_ctx(parts):
    count = lax.axis_size("ctx")
    if count != 8:
        natural = relative(jnp.stack(parts))
        flat = natural.reshape((-1,) + natural.shape[2:])
        return lax.psum_scatter(flat, "ctx", scatter_dimension=0, tiled=True).astype(F32)
    half = parts[0].shape[0] // 2
    pair = {j: parts[j].astype(F32) + swap(parts[j ^ 1], 1).astype(F32) for j in (2, 4, 6, 0)}
    r2 = swap(pair[2][:half].astype(BF16), 2)
    r4 = swap(pair[4][half:].astype(BF16), 4)
    q6 = pair[6].astype(BF16)
    via_x, via_y = swap(q6[:half], 2), swap(q6[half:], 4)
    r4a = swap((pair[4][:half] + via_x.astype(F32)).astype(BF16), 4)
    r2b = swap((pair[2][half:] + via_y.astype(F32)).astype(BF16), 2)
    low = r2.astype(F32) + r4a.astype(F32)
    high = r2b.astype(F32) + r4.astype(F32)
    return pair[0] + jnp.concatenate([low, high], axis=0)


def sum_ctx(parts):
    return gather_ctx(scatter_ctx(parts).astype(BF16))


def shards(value):
    count = lax.axis_size("ctx")
    rows = value.shape[0] // count
    place = lax.axis_index("ctx")
    return [lax.dynamic_slice_in_dim(value, (place ^ j) * rows, rows, 0) for j in range(count)]


def gather_tp(own):
    count = lax.axis_size("tp")
    return [own] + [
        lax.ppermute(own, "tp", [(i, i ^ k) for i in range(count)]) for k in range(1, count)
    ]


NT = (((1,), (1,)), ((), ()))
NN = (((1,), (0,)), ((), ()))
TN = (((0,), (0,)), ((), ()))
VMEM_LIMIT = 60 * 1024 * 1024


def attend_kernel(factor, count, place_ref, q_ref, *refs):
    kv_refs, (att_ref, lse_ref, kv, sems) = refs[:count], refs[count:]
    copies = [pltpu.make_async_copy(kv_refs[j], kv.at[j], sems.at[j]) for j in range(count)]
    for copy in copies:
        copy.start()
    for copy in copies:
        copy.wait()
    place = place_ref[0]
    heads, tokens, _ = q_ref.shape

    def one_head(head, _):
        query = q_ref[head]

        def scores(j):
            return dot(kv[j, 0, head], query, NT) * factor

        key_at = lax.broadcasted_iota(jnp.int32, (tokens, tokens), 0)
        query_at = lax.broadcasted_iota(jnp.int32, (tokens, tokens), 1)
        first = jnp.where(key_at <= query_at, scores(0), NEG)
        top = jnp.max(first, axis=0, keepdims=True)
        exps = jnp.exp2(first - top)
        total = jnp.sum(exps, axis=0, keepdims=True)
        acc = dot(kv[0, 1, head], exps.astype(BF16), TN)

        def earlier(i, carry):
            top, total, acc = carry
            j = place ^ i
            now = scores(j)
            higher = jnp.maximum(top, jnp.max(now, axis=0, keepdims=True))
            exps = jnp.exp2(now - higher)
            keep = jnp.exp2(top - higher)
            total = total * keep + jnp.sum(exps, axis=0, keepdims=True)
            acc = acc * keep + dot(kv[j, 1, head], exps.astype(BF16), TN)
            return higher, total, acc

        top, total, acc = lax.fori_loop(0, place, earlier, (top, total, acc))
        att_ref[head] = (acc / total).T
        lse_ref[head] = jnp.broadcast_to(top + jnp.log2(total), lse_ref.shape[1:])
        return 0

    lax.fori_loop(0, heads, one_head, 0)


def attend(place, query, kv_blocks):
    heads, tokens, size = query.shape
    count = len(kv_blocks)
    factor = math.log2(math.e) / math.sqrt(size)
    flops = 4 * count * heads * tokens * tokens * size
    return pl.pallas_call(
        functools.partial(attend_kernel, factor, count),
        out_shape=(
            jax.ShapeDtypeStruct((heads, tokens, size), F32),
            jax.ShapeDtypeStruct((heads, 8, tokens), F32),
        ),
        in_specs=[
            pl.BlockSpec(memory_space=pltpu.SMEM),
            pl.BlockSpec(memory_space=pltpu.VMEM),
        ]
        + [pl.BlockSpec(memory_space=pl.ANY)] * count,
        out_specs=(pl.BlockSpec(memory_space=pltpu.VMEM),) * 2,
        scratch_shapes=[
            pltpu.VMEM((count, 2, heads, tokens, size), BF16),
            pltpu.SemaphoreType.DMA((count,)),
        ],
        compiler_params=pltpu.CompilerParams(vmem_limit_bytes=VMEM_LIMIT),
        cost_estimate=pl.CostEstimate(
            flops=flops, bytes_accessed=count * heads * tokens * size * 4, transcendentals=0
        ),
        name="attend",
    )(place.reshape(1), query, *kv_blocks)


def attend_back_kernel(factor, scale, count, place_ref, q_ref, do_ref, lse_ref, delta_ref, *refs):
    kv_refs, (dq_ref, dkv_ref, kv, dkv, dq, sems, out_sems) = refs[:count], refs[count:]
    copies = [pltpu.make_async_copy(kv_refs[j], kv.at[j], sems.at[j]) for j in range(count)]
    for copy in copies:
        copy.start()
    for copy in copies:
        copy.wait()
    place = place_ref[0]
    heads, tokens, _ = q_ref.shape

    def out_copy(j):
        return pltpu.make_async_copy(dkv.at[j], dkv_ref.at[j], out_sems.at[j])

    def one_block(j, masked):
        def one_head(head, _):
            query, do = q_ref[head], do_ref[head]
            key, value = kv[j, 0, head], kv[j, 1, head]
            scores = dot(key, query, NT) * factor
            probs = jnp.exp2(scores - lse_ref[head, :1])
            if masked:
                key_at = lax.broadcasted_iota(jnp.int32, (tokens, tokens), 0)
                query_at = lax.broadcasted_iota(jnp.int32, (tokens, tokens), 1)
                probs = jnp.where(key_at <= query_at, probs, 0.0)
            dprob = dot(value, do, NT)
            dscore = (probs * (dprob - delta_ref[head, :1])).astype(BF16)
            dkv[j, 0, head] = (dot(dscore, query, NN) * scale).astype(BF16)
            dkv[j, 1, head] = dot(probs.astype(BF16), do, NN).astype(BF16)
            part = dot(key, dscore, TN)
            dq[head] = part if masked else dq[head] + part
            return 0

        lax.fori_loop(0, heads, one_head, 0)
        out_copy(j).start()

    one_block(0, True)

    def earlier(i, _):
        one_block(place ^ i, False)
        return 0

    def later(i, _):
        j = place ^ i
        dkv[j] = jnp.zeros(dkv.shape[1:], BF16)
        out_copy(j).start()
        return 0

    lax.fori_loop(0, place, earlier, 0)
    lax.fori_loop(place + 1, count, later, 0)
    for head in range(heads):
        dq_ref[head] = dq[head].T * scale
    for j in range(count):
        out_copy(j).wait()


def attend_back(place, query, do, lse, delta, kv_blocks):
    heads, tokens, size = query.shape
    count = len(kv_blocks)
    scale = 1.0 / math.sqrt(size)
    factor = math.log2(math.e) * scale
    return pl.pallas_call(
        functools.partial(attend_back_kernel, factor, scale, count),
        out_shape=(
            jax.ShapeDtypeStruct((heads, tokens, size), F32),
            jax.ShapeDtypeStruct((count, 2, heads, tokens, size), BF16),
        ),
        in_specs=[pl.BlockSpec(memory_space=pltpu.SMEM)]
        + [pl.BlockSpec(memory_space=pltpu.VMEM)] * 4
        + [pl.BlockSpec(memory_space=pl.ANY)] * count,
        out_specs=(pl.BlockSpec(memory_space=pltpu.VMEM), pl.BlockSpec(memory_space=pl.ANY)),
        scratch_shapes=[
            pltpu.VMEM((count, 2, heads, tokens, size), BF16),
            pltpu.VMEM((count, 2, heads, tokens, size), BF16),
            pltpu.VMEM((heads, size, tokens), F32),
            pltpu.SemaphoreType.DMA((count,)),
            pltpu.SemaphoreType.DMA((count,)),
        ],
        compiler_params=pltpu.CompilerParams(vmem_limit_bytes=VMEM_LIMIT),
        cost_estimate=pl.CostEstimate(
            flops=10 * count * heads * tokens * tokens * size,
            bytes_accessed=count * heads * tokens * size * 8,
            transcendentals=0,
        ),
        name="attend_back",
    )(place.reshape(1), query, do, lse, delta, *kv_blocks)


def swiglu_back(one, two, dact, gate):
    sig = 1.0 / (1.0 + jnp.exp(-one))
    silu = one * sig
    act = silu * two
    prod = act * dact
    dgate = gate * dact
    d_one = (dgate * two * sig * (1.0 + one * (1.0 - sig))).astype(BF16)
    d_two = (dgate * silu).astype(BF16)
    return (gate * act).astype(BF16), d_one, d_two, prod


def experts_kernel(at, group, local, experts, given, first_ref, *refs):
    x_refs, g_refs, refs = refs[:group], refs[group : 2 * group], refs[2 * group :]
    (slot_row, slot_col, w_router, w_first, w_in, w_out, w_shared), refs = refs[:7], refs[7 + given :]
    dx_refs, refs = refs[:group], refs[group:]
    kept_refs, refs = refs[:7], refs[7:]
    (xs, gs, first_w, in_w, out_w, shared_w, dxs, left, right, sems, out_sems), stage = refs[:11], refs[11:]
    rows_x, rows_g, act_s, dpair_s, sact_s, sdpair_s, dl_s = stage
    tokens, width = xs.shape[1:]
    capacity, units = act_s.shape[2:]
    wide = local * capacity
    share = sact_s.shape[2]
    third = first_w.shape[0] - 128
    second = third // 2
    padded = w_router.shape[0]

    loads = [pltpu.make_async_copy(x_refs[b], xs.at[b], sems.at[b]) for b in range(group)]
    loads.append(pltpu.make_async_copy(w_first, first_w, sems.at[group]))
    loads += [
        pltpu.make_async_copy(g_refs[b], gs.at[b], sems.at[group + 1 + b]) for b in range(group)
    ]
    more = [
        pltpu.make_async_copy(w_in.at[e], in_w.at[e], sems.at[2 * group + 1 + 2 * e])
        for e in range(local)
    ]
    more_out = [
        pltpu.make_async_copy(w_out.at[e], out_w.at[e], sems.at[2 * group + 2 + 2 * e])
        for e in range(local)
    ]
    last = pltpu.make_async_copy(w_shared, shared_w, sems.at[2 * group + 1 + 2 * local])
    for copy in loads[: group + 1]:
        copy.start()

    sent = []

    def send(copy):
        copy.start()
        sent.append(copy)

    for copy in loads[: group + 1]:
        copy.wait()
    for copy in loads[group + 1 :] + [more[0], more_out[0]]:
        copy.start()
    x = xs[...].reshape(group * tokens, width)
    fore = dot(x, first_w[...], NT)
    s_one, s_two = fore[:, :share], fore[:, second : second + share]
    s_gate = 1.0 / (1.0 + jnp.exp(-fore[:, third + experts : third + experts + 1]))
    row_at = lax.broadcasted_iota(jnp.int32, (padded, tokens), 0)
    slot_at = lax.broadcasted_iota(jnp.int32, (capacity, tokens), 0)
    probs, change, hits = [], [], []
    for b in range(group):
        logits = fore[b * tokens : (b + 1) * tokens, third:].T[:padded]
        shown = jnp.where(row_at < experts, logits, NEG)
        exps = jnp.exp(shown - jnp.max(shown, axis=0, keepdims=True))
        soft = exps / jnp.sum(exps, axis=0, keepdims=True)
        probs.append(jnp.where(row_at == experts, 1.0 / (1.0 + jnp.exp(-logits)), soft))
        change.append(jnp.zeros((padded, tokens), F32))
        picks = jnp.concatenate(
            [
                jnp.where(slot_at == slot_row[b, e : e + 1, :], 1.0, 0.0).astype(BF16)
                for e in range(local)
            ],
            axis=0,
        )
        rows = dot(picks, xs[b], NN).astype(BF16)
        for e in range(local):
            rows_x[e, b] = rows[e * capacity : (e + 1) * capacity]
        loads[group + 1 + b].wait()
        if b == group - 1:
            for e in range(1, local):
                more[e].start()
                more_out[e].start()
            last.start()
        rows = dot(picks, gs[b], NN).astype(BF16)
        for e in range(local):
            rows_g[e, b] = rows[e * capacity : (e + 1) * capacity]
    def send_all(i, lead):
        for e in range(lead):
            send(
                pltpu.make_async_copy(
                    stage[i].at[e], kept_refs[i].at[e, pl.ds(at, group)], out_sems.at[i, e]
                )
            )

    send_all(0, local)
    send_all(1, local)
    is_expert = row_at < experts
    for e in range(local):
        chosen = row_at == first_ref[0] + e
        gates, owns, hits = [], [], []
        for b in range(group):
            own = jnp.sum(jnp.where(chosen, probs[b], 0.0), axis=0, keepdims=True)
            hit = slot_at == slot_row[b, e : e + 1, :]
            gates.append(jnp.sum(jnp.where(hit, own, 0.0), axis=1, keepdims=True))
            owns.append(own)
            hits.append(hit)
        more[e].wait()
        pair = dot(rows_x[e].reshape(group * capacity, width), in_w[e], NT)
        most = pair.shape[1] // 2
        more_out[e].wait()
        dact = dot(rows_g[e].reshape(group * capacity, width), out_w[e], NT)
        act, d_one, d_two, prod = swiglu_back(
            pair[:, :most], pair[:, most:], dact, jnp.concatenate(gates, axis=0)
        )
        act_s[e] = act[:, :units].reshape(group, capacity, units)
        dpair_s[2 * e] = d_one[:, :units].reshape(group, capacity, units)
        dpair_s[2 * e + 1] = d_two[:, :units].reshape(group, capacity, units)
        row_dot = jnp.sum(prod, axis=1, keepdims=True)
        drow = dot(jnp.concatenate([d_one, d_two], axis=1), in_w[e], NN).astype(BF16)
        for b in range(group):
            rows = slice(b * capacity, (b + 1) * capacity)
            found = jnp.sum(jnp.where(hits[b], row_dot[rows], 0.0), axis=0, keepdims=True)
            change[b] += (found * owns[b]) * (
                jnp.where(chosen, 1.0, 0.0) - jnp.where(is_expert, probs[b], 0.0)
            )
            right[b, e * capacity : (e + 1) * capacity] = drow[rows]
    send_all(2, local)
    send_all(3, 2 * local)
    last.wait()
    g = gs[...].reshape(group * tokens, width)
    s_dact = dot(g, shared_w[...], NT)
    act, d_one, d_two, prod = swiglu_back(s_one, s_two, s_dact, s_gate)
    sact_s[...] = act.reshape(group, tokens, share)
    sdpair_s[:, 0] = d_one.reshape(group, tokens, share)
    sdpair_s[:, 1] = d_two.reshape(group, tokens, share)
    dslogit = jnp.sum(prod, axis=1, keepdims=True) * s_gate * (1.0 - s_gate)
    lane_at = lax.broadcasted_iota(jnp.int32, (tokens, 128), 1)
    rest = jnp.zeros((128 - padded, tokens), F32)
    deep = wide + 2 * share
    column_at = lax.broadcasted_iota(jnp.int32, (tokens, capacity), 1)
    stores = []
    for b in range(group):
        rows = slice(b * tokens, (b + 1) * tokens)
        columns = jnp.concatenate([change[b], rest], axis=0).T
        columns = jnp.where(lane_at == experts, dslogit[rows], columns)[:, :padded].astype(BF16)
        dl_s[b] = columns
        left[b, :, deep : deep + padded] = columns
        right[b, deep : deep + padded] = w_router[...]
        for e in range(local):
            picks = jnp.where(column_at == slot_col[b, :, e : e + 1], 1.0, 0.0).astype(BF16)
            left[b, :, e * capacity : (e + 1) * capacity] = picks
        left[b, :, wide : wide + share] = d_one[rows]
        left[b, :, wide + share : wide + 2 * share] = d_two[rows]
        right[b, wide : wide + share] = first_w[:share]
        right[b, wide + share : wide + 2 * share] = first_w[second : second + share]
        dxs[b] = dot(left[b], right[b], NN).astype(BF16)
        send(pltpu.make_async_copy(dxs.at[b], dx_refs[b], out_sems.at[7, b]))
    for i in range(4, 7):
        send(pltpu.make_async_copy(stage[i], kept_refs[i].at[pl.ds(at, group)], out_sems.at[i, 0]))
    for copy in sent:
        copy.wait()


def run_experts(at, experts, first, x_group, g_group, slot_rows, slot_cols, weights, kept):
    given = kept if at else []
    group = len(x_group)
    tokens, width = x_group[0].shape
    w_router, w_first, w_in, w_out, w_shared = weights
    local, padded_units = w_out.shape[:2]
    share = w_shared.shape[0]
    padded = w_router.shape[0]
    capacity, units = kept[2].shape[2:]
    any_spec = pl.BlockSpec(memory_space=pl.ANY)
    block = jax.ShapeDtypeStruct((tokens, width), BF16)
    deep = local * capacity + 2 * share + padded
    flops = group * 2 * tokens * width * (local * capacity * 3 + 5 * share) + (
        group * 2 * width * local * capacity * units * 5
    )
    step = at // group
    results = pl.pallas_call(
        functools.partial(experts_kernel, at, group, local, experts, len(given)),
        grid=(1,),
        out_shape=(block,) * group + tuple(jax.ShapeDtypeStruct(k.shape, k.dtype) for k in kept),
        in_specs=[pl.BlockSpec(memory_space=pltpu.SMEM)]
        + [any_spec] * (2 * group)
        + [
            pl.BlockSpec((group, local, tokens), lambda i: (step, 0, 0)),
            pl.BlockSpec((group, tokens, local), lambda i: (step, 0, 0)),
            pl.BlockSpec((padded, width), lambda i: (0, 0)),
        ]
        + [any_spec] * (4 + len(given)),
        out_specs=(any_spec,) * (group + len(kept)),
        input_output_aliases={8 + 2 * group + i: group + i for i in range(len(given))},
        scratch_shapes=[
            pltpu.VMEM((group, tokens, width), BF16),
            pltpu.VMEM((group, tokens, width), BF16),
            pltpu.VMEM(w_first.shape, BF16),
            pltpu.VMEM(w_in.shape, BF16),
            pltpu.VMEM(w_out.shape, BF16),
            pltpu.VMEM(w_shared.shape, BF16),
            pltpu.VMEM((group, tokens, width), BF16),
            pltpu.VMEM((group, tokens, deep), BF16),
            pltpu.VMEM((group, deep, width), BF16),
            pltpu.SemaphoreType.DMA((2 * group + 2 + 2 * local,)),
            pltpu.SemaphoreType.DMA((8, max(2 * local, group))),
        ]
        + [
            pltpu.VMEM(k.shape[:1] + (group,) + k.shape[2:], BF16) for k in kept[:4]
        ]
        + [pltpu.VMEM((group,) + k.shape[1:], BF16) for k in kept[4:]],
        compiler_params=pltpu.CompilerParams(vmem_limit_bytes=VMEM_LIMIT),
        cost_estimate=pl.CostEstimate(flops=flops, bytes_accessed=20 * 2**20 * group, transcendentals=0),
        name="run_experts",
    )(first.reshape(1), *x_group, *g_group, slot_rows, slot_cols, *weights, *given)
    return results[:group], results[group:]


def outputs_kernel(group, count, local, act, slot_col, sact, w_out, w_shared, *refs):
    out_refs, (outs, left, right, sems) = refs[:count], refs[count:]
    step = pl.program_id(0)
    slot = lax.rem(step, 2)
    capacity, units = act.shape[2:]
    tokens, share = sact.shape[1:]
    wide = local * capacity

    def store(at, b, into):
        return pltpu.make_async_copy(outs.at[into, b], out_refs[at * group + b], sems.at[into, b])

    @pl.when(step >= 2)
    def _():
        for b in range(group):
            store(0, b, slot).wait()

    for e in range(local):
        rows = dot(act[e].reshape(group * capacity, units), w_out[e], NN).astype(BF16)
        for b in range(group):
            right[b, e * capacity : (e + 1) * capacity] = rows[b * capacity : (b + 1) * capacity]
    slot_at = lax.broadcasted_iota(jnp.int32, (tokens, capacity), 1)
    for b in range(group):
        for e in range(local):
            picks = jnp.where(slot_at == slot_col[b, :, e : e + 1], 1.0, 0.0).astype(BF16)
            left[b, :, e * capacity : (e + 1) * capacity] = picks
        left[b, :, wide : wide + share] = sact[b]
        right[b, wide : wide + share] = w_shared[0]
        outs[slot, b] = dot(left[b], right[b], NN).astype(BF16)
    for at in range(count // group):

        @pl.when(step == at)
        def _():
            for b in range(group):
                store(at, b, at % 2).start()

    @pl.when(step == count // group - 1)
    def _():
        for b in range(group):
            for into in range(2):
                store(0, b, into).wait()


def run_outputs(act, slot_cols, sact, w_out, w_shared):
    local, count, capacity, units = act.shape
    tokens, share = sact.shape[1:]
    width = w_out.shape[2]
    group = 2
    deep = local * capacity + share
    return pl.pallas_call(
        functools.partial(outputs_kernel, group, count, local),
        grid=(count // group,),
        out_shape=(jax.ShapeDtypeStruct((tokens, width), BF16),) * count,
        in_specs=[
            pl.BlockSpec((local, group, capacity, units), lambda i: (0, i, 0, 0)),
            pl.BlockSpec((group, tokens, local), lambda i: (i, 0, 0)),
            pl.BlockSpec((group, tokens, share), lambda i: (i, 0, 0)),
            pl.BlockSpec((local, units, width), lambda i: (0, 0, 0)),
            pl.BlockSpec((1, share, width), lambda i: (2, 0, 0)),
        ],
        out_specs=(pl.BlockSpec(memory_space=pl.ANY),) * count,
        scratch_shapes=[
            pltpu.VMEM((2, group, tokens, width), BF16),
            pltpu.VMEM((group, tokens, deep), BF16),
            pltpu.VMEM((group, deep, width), BF16),
            pltpu.SemaphoreType.DMA((2, group)),
        ],
        compiler_params=pltpu.CompilerParams(vmem_limit_bytes=VMEM_LIMIT),
        cost_estimate=pl.CostEstimate(
            flops=count * 2 * width * (local * capacity * (units + tokens) + tokens * share),
            bytes_accessed=30 * 2**20,
            transcendentals=0,
        ),
        name="run_outputs",
    )(act, slot_cols, sact, w_out, w_shared)


def assemble_kernel(plan, place_ref, *refs):
    total = sum(count for count, _, _, _ in plan)
    block_refs, (out_ref, low, wide, in_sems, out_sems) = refs[:total], refs[total:]
    place = place_ref[0]
    steps, at = [], 0
    for count, skip, rows, base in plan:
        for j in range(count):
            steps.append((at + j, skip, rows, base + (place ^ j) * rows))
        at += count

    def load(i):
        which, skip, rows, _ = steps[i]
        return pltpu.make_async_copy(
            block_refs[which].at[pl.ds(skip, rows)], low.at[i % 2, pl.ds(0, rows)], in_sems.at[i % 2]
        )

    def store(i):
        _, _, rows, start = steps[i]
        return pltpu.make_async_copy(
            wide.at[i % 2, pl.ds(0, rows)],
            out_ref.at[pl.ds(pl.multiple_of(start, 8), rows)],
            out_sems.at[i % 2],
        )

    load(0).start()
    for i, (_, _, rows, _) in enumerate(steps):
        if i + 1 < len(steps):
            load(i + 1).start()
        load(i).wait()
        if i >= 2:
            store(i - 2).wait()
        wide[i % 2, :rows] = low[i % 2, :rows].astype(F32)
        store(i).start()
    for i in range(max(0, len(steps) - 2), len(steps)):
        store(i).wait()


def assemble(place, lists):
    plan, base = [], 0
    for blocks, skip, rows in lists:
        plan.append((len(blocks), skip, rows, base))
        base += len(blocks) * rows
    width = lists[0][0][0].shape[1]
    most = max(rows for _, _, rows in lists)
    flat = [b for blocks, _, _ in lists for b in blocks]
    return pl.pallas_call(
        functools.partial(assemble_kernel, plan),
        out_shape=jax.ShapeDtypeStruct((base, width), F32),
        in_specs=[pl.BlockSpec(memory_space=pltpu.SMEM)]
        + [pl.BlockSpec(memory_space=pl.ANY)] * len(flat),
        out_specs=pl.BlockSpec(memory_space=pl.ANY),
        scratch_shapes=[
            pltpu.VMEM((2, most, width), BF16),
            pltpu.VMEM((2, most, width), F32),
            pltpu.SemaphoreType.DMA((2,)),
            pltpu.SemaphoreType.DMA((2,)),
        ],
        compiler_params=pltpu.CompilerParams(vmem_limit_bytes=VMEM_LIMIT),
        cost_estimate=pl.CostEstimate(flops=0, bytes_accessed=6 * base * width, transcendentals=0),
        name="assemble",
    )(place.reshape(1), *flat)


def shared_grads_kernel(count, *refs):
    x_refs, g_refs, refs = refs[:count], refs[count : 2 * count], refs[2 * count :]
    (sact, sdpair, dl, grads_ref, router_ref, xs, gs, grads, router, sems) = refs
    at = pl.program_id(0)
    slot = lax.rem(at, 2)

    def load(j, into):
        return (
            pltpu.make_async_copy(x_refs[j], xs.at[into], sems.at[0, into]),
            pltpu.make_async_copy(g_refs[j], gs.at[into], sems.at[1, into]),
        )

    @pl.when(at == 0)
    def _():
        for copy in load(0, 0):
            copy.start()
        grads[...] = jnp.zeros_like(grads)
        router[...] = jnp.zeros_like(router)

    for j in range(1, count):

        @pl.when(at == j - 1)
        def _():
            for copy in load(j, j % 2):
                copy.start()

    for copy in load(0, slot):
        copy.wait()
    x, g = xs[slot], gs[slot]
    grads[0] += dot(sdpair[0, 0], x, TN)
    grads[1] += dot(sdpair[0, 1], x, TN)
    grads[2] += dot(sact[0], g, TN)
    router[...] += dot(dl[0], x, TN)

    @pl.when(at == count - 1)
    def _():
        grads_ref[...] = grads[...].astype(BF16)
        router_ref[...] = router[...]


def shared_grads(x_blocks, g_blocks, sact, sdpair, dl):
    count = len(x_blocks)
    tokens, width = x_blocks[0].shape
    share, padded = sact.shape[2], dl.shape[2]
    any_spec = pl.BlockSpec(memory_space=pl.ANY)
    return pl.pallas_call(
        functools.partial(shared_grads_kernel, count),
        grid=(count,),
        out_shape=(
            jax.ShapeDtypeStruct((3, share, width), BF16),
            jax.ShapeDtypeStruct((padded, width), F32),
        ),
        in_specs=[any_spec] * (2 * count)
        + [
            pl.BlockSpec((1, tokens, share), lambda j: (j, 0, 0)),
            pl.BlockSpec((1, 2, tokens, share), lambda j: (j, 0, 0, 0)),
            pl.BlockSpec((1, tokens, padded), lambda j: (j, 0, 0)),
        ],
        out_specs=(
            pl.BlockSpec((3, share, width), lambda j: (0, 0, 0)),
            pl.BlockSpec((padded, width), lambda j: (0, 0)),
        ),
        scratch_shapes=[
            pltpu.VMEM((2, tokens, width), BF16),
            pltpu.VMEM((2, tokens, width), BF16),
            pltpu.VMEM((3, share, width), F32),
            pltpu.VMEM((padded, width), F32),
            pltpu.SemaphoreType.DMA((2, 2)),
        ],
        compiler_params=pltpu.CompilerParams(vmem_limit_bytes=VMEM_LIMIT),
        cost_estimate=pl.CostEstimate(
            flops=6 * count * tokens * width * share,
            bytes_accessed=4 * count * tokens * width,
            transcendentals=0,
        ),
        name="shared_grads",
    )(*x_blocks, *g_blocks, sact, sdpair, dl)


def on_device(
    hidden_in,
    cotangent,
    gain_attn,
    qkv_weight,
    qkv_bias,
    out_weight,
    gain_ffn,
    router_weight,
    routes,
    shared_gate,
    shared_in,
    shared_out,
    expert_in,
    expert_out,
):
    tokens, width = hidden_in.shape
    ctx_count = lax.axis_size("ctx")
    heads_local = qkv_weight.shape[2] // HD
    local = expert_in.shape[0]
    experts = local * ctx_count
    top_count = routes.shape[1]
    capacity = 3 * tokens * top_count // (2 * experts)
    place = lax.axis_index("ctx")
    order = jnp.arange(ctx_count, dtype=jnp.int32) ^ place
    score_scale = 1.0 / math.sqrt(HD)
    query_pos = place * tokens + jnp.arange(tokens, dtype=jnp.int32)
    cosine, sine = rotary_tables(query_pos, HD)

    x_full = hidden_in.astype(F32)
    inv_one = lax.rsqrt(jnp.mean(x_full * x_full, axis=-1, keepdims=True) + EPS)
    normed_one = x_full * inv_one
    x_one = (normed_one * gain_attn).astype(BF16)
    projected = (
        jnp.einsum("td,dcf->ctf", x_one, qkv_weight, preferred_element_type=F32)
        + qkv_bias[:, None]
    )
    shaped = projected.reshape(3, tokens, heads_local, HD).transpose(0, 2, 1, 3)
    query = rotate(shaped[0], cosine, sine).astype(BF16)
    key_local = rotate(shaped[1], cosine, sine).astype(BF16)
    value_local = shaped[2].astype(BF16)
    routes_got = gather_ctx(routes)
    kv_local = jnp.stack([key_local, value_local])
    kv_blocks = gather_ctx(kv_local)
    g_blocks = gather_ctx(after(cotangent, kv_blocks[6 % ctx_count]))

    share = shared_out.shape[0] // ctx_count
    piece = shared_out.shape[1]
    shared_send = jnp.concatenate(
        [
            shared_in.transpose(1, 2, 0).reshape(2, ctx_count, share, piece),
            shared_out.reshape(1, ctx_count, share, piece),
        ],
        axis=0,
    ).transpose(1, 0, 2, 3)
    shared_w = (
        lax.all_to_all(shared_send, "ctx", split_axis=0, concat_axis=0, tiled=True)
        .transpose(1, 2, 0, 3)
        .reshape(3, share, width)
    )
    half_rows = out_weight.shape[0] // 2
    core = place % 2
    out_mine = gather_tp(lax.dynamic_slice_in_dim(out_weight, core * half_rows, half_rows, 0))
    out_mine = jnp.concatenate(out_mine, axis=0)

    routes_all = jnp.stack(routes_got)
    own_experts = place * local + jnp.arange(local, dtype=jnp.int32)
    hit = jnp.any(routes_all[:, None] == own_experts[None, :, None, None], axis=-1)
    rank = jnp.cumsum(hit.astype(jnp.int32), axis=-1) - 1
    slot_rows = jnp.where(hit, rank, -1)
    slot_cols = slot_rows.transpose(0, 2, 1)
    padded = -(-(experts + 1) // 8) * 8
    w_router = jnp.concatenate(
        [
            router_weight.T,
            shared_gate[None],
            jnp.zeros((padded - experts - 1, width), BF16),
        ],
        axis=0,
    )
    w_in = expert_in.transpose(0, 2, 3, 1)

    attended, lse = attend(place, query, kv_blocks)
    att = attended.astype(BF16).transpose(1, 0, 2).reshape(tokens, heads_local * HD)
    out_other = swap(after(out_mine, attended), 1)
    att_all = gather_tp(att)
    att_low = jnp.concatenate([a[:, :half_rows] for a in att_all], axis=1)
    att_high = jnp.concatenate([a[:, half_rows:] for a in att_all], axis=1)
    out_low = jnp.where(core == 0, out_mine, out_other)
    out_high = jnp.where(core == 0, out_other, out_mine)
    hidden = x_full + dot(
        jnp.concatenate([att_low, att_high], axis=1),
        jnp.concatenate([out_low, out_high], axis=0),
        NN,
    )
    inv_two = lax.rsqrt(jnp.mean(hidden * hidden, axis=-1, keepdims=True) + EPS)
    normed_two = hidden * inv_two
    x_two = (normed_two * gain_ffn).astype(BF16)

    units, group = expert_out.shape[1], 2
    kept = [
        jax.ShapeDtypeStruct(shape, BF16)
        for shape in (
            (local, ctx_count, capacity, width),
            (local, ctx_count, capacity, width),
            (local, ctx_count, capacity, units),
            (2 * local, ctx_count, capacity, units),
            (ctx_count, tokens, share),
            (ctx_count, 2, tokens, share),
            (ctx_count, tokens, padded),
        )
    ]
    extra = -units % 128
    w_in = jnp.pad(w_in, ((0, 0), (0, 0), (0, extra), (0, 0)))
    w_in = w_in.reshape(local, 2 * (units + extra), width)
    w_out = jnp.pad(expert_out, ((0, 0), (0, extra), (0, 0)))
    half = -(-share // 64) * 64
    gap = jnp.zeros((half - share, width), BF16)
    w_first = jnp.concatenate(
        [shared_w[0], gap, shared_w[1], gap, w_router, jnp.zeros((128 - padded, width), BF16)], axis=0
    )
    weights = (w_router, w_first, w_in, w_out, shared_w[2])
    got = gather_start(x_two)
    x_blocks = [got[0], got[1]]
    dxs = []
    for at in range(0, ctx_count, group):
        dx, kept = run_experts(
            at,
            experts,
            place * local,
            x_blocks[at : at + group],
            g_blocks[at : at + group],
            slot_rows,
            slot_cols,
            weights,
            kept,
        )
        dxs += dx
        if at == 0:
            x_blocks = gather_end(got, dx[0])
    rows_x, rows_g, act_low, dpair, s_act, s_dpair, low_logits = kept
    grad_x_part = scatter_ctx(dxs)
    outs = run_outputs(act_low, slot_cols, s_act, expert_out, shared_w)
    outs = after(outs, grad_x_part)
    out_part = scatter_ctx(outs)
    dpair = dpair.reshape(local, 2, ctx_count, capacity, units)
    grad_expert_in = jnp.einsum("ebcd,evbcf->edvf", rows_x, dpair, preferred_element_type=F32)
    grad_expert_out = jnp.einsum("ebcf,ebcd->efd", act_low, rows_g, preferred_element_type=F32)
    shared_low, router_part = shared_grads(x_blocks, g_blocks, s_act, s_dpair, low_logits)
    shared_back = lax.all_to_all(
        shared_low.reshape(3, share, ctx_count, piece).transpose(2, 0, 1, 3),
        "ctx",
        split_axis=0,
        concat_axis=0,
        tiled=True,
    ).astype(F32)
    grad_shared_in = shared_back[:, :2].transpose(3, 1, 0, 2).reshape(shared_in.shape)
    grad_shared_out = shared_back[:, 2].reshape(shared_out.shape)

    summed = lax.psum(grad_x_part.astype(BF16), "tp").astype(F32)
    ffn_full = lax.psum(after(out_part.astype(BF16), summed), "tp").astype(F32)
    grad_y = cotangent.astype(F32)
    grad_normed_two = summed * gain_ffn
    gain_ffn_part = jnp.sum(grad_x_part * normed_two, axis=0)
    grad_hidden = grad_y + inv_two * (
        grad_normed_two
        - normed_two * jnp.mean(grad_normed_two * normed_two, axis=-1, keepdims=True)
    )
    grad_hidden_low = grad_hidden.astype(BF16)
    out_weight_part = dot(att, grad_hidden_low, (((0,), (0,)), ((), ())))
    grad_att = (
        dot(grad_hidden_low, out_weight, (((1,), (1,)), ((), ())))
        .astype(BF16)
        .reshape(tokens, heads_local, HD)
        .transpose(1, 0, 2)
    )
    small = jnp.concatenate([router_part, gain_ffn_part[None]], axis=0)
    small = lax.psum(small, ("ctx", "tp"))
    delta = jnp.sum(grad_att.astype(F32) * attended, axis=-1)
    delta = jnp.broadcast_to(delta[:, None], lse.shape)
    grad_query, grad_pairs = attend_back(place, query, grad_att, lse, delta, kv_blocks)
    grad_kv = scatter_ctx([grad_pairs[j] for j in range(ctx_count)])
    def raw_part(value):
        return value.astype(BF16).transpose(1, 0, 2).reshape(tokens, heads_local * HD)

    raw = [
        raw_part(rotate(grad_query, cosine, -sine)),
        raw_part(rotate(grad_kv[0], cosine, -sine)),
        raw_part(grad_kv[1]),
    ]
    grad_x_one_part = sum(
        dot(raw[c], qkv_weight[:, c], NT) for c in range(3)
    )
    grad_x_one = lax.psum(after(grad_x_one_part.astype(BF16), ffn_full), "tp").astype(F32)
    gain_attn_part = jnp.sum(grad_x_one_part * normed_one, axis=0)
    gain_sum = gain_attn_part
    tp_count, bits = lax.axis_size("tp"), 1
    while bits < tp_count:
        gain_sum = gain_sum + lax.ppermute(gain_sum, "tp", [(i, i ^ bits) for i in range(tp_count)])
        bits *= 2
    head_width = heads_local * HD
    spare = 16 * ctx_count
    gain_rows = width // head_width
    ends = jnp.concatenate(
        [jnp.sum(r.astype(F32), axis=0)[None] for r in raw] + [gain_sum.reshape(gain_rows, -1)], axis=0
    )
    ends = jnp.pad(ends, ((0, spare - 3 - gain_rows), (0, 0))).astype(BF16)
    query_part = after(dot(x_one, raw[0], TN).astype(BF16), grad_kv)
    pair_part = jnp.concatenate([dot(x_one, raw[1], TN), dot(x_one, raw[2], TN)], axis=0).astype(BF16)
    spread = lambda v: v.astype(BF16).reshape(-1, head_width)
    first_parts = [
        jnp.concatenate([a, b], axis=0)
        for a, b in zip(shards(query_part), shards(spread(out_weight_part)))
    ]
    first_sums = sum_ctx(first_parts)
    pair_sums = sum_ctx(
        [jnp.concatenate([a, b], axis=0) for a, b in zip(shards(pair_part), shards(ends))]
    )
    q_rows = width // ctx_count
    qkv_grad = assemble(place, [(first_sums, 0, q_rows), (pair_sums, 0, 2 * q_rows)])
    qkv_grad = qkv_grad.reshape(3, width, head_width).transpose(1, 0, 2)
    out_rows = first_sums[0].shape[0] - q_rows
    out_weight_grad = assemble(place, [(first_sums, q_rows, out_rows)]).reshape(out_weight.shape)
    ends = relative(jnp.stack([b[2 * q_rows :] for b in pair_sums])).reshape(spare, head_width)
    ends = ends.astype(F32)
    grad_normed_one = grad_x_one * gain_attn
    grad_input = grad_hidden + inv_one * (
        grad_normed_one
        - normed_one * jnp.mean(grad_normed_one * normed_one, axis=-1, keepdims=True)
    )
    block_out = (hidden + after(ffn_full, grad_kv)).astype(BF16)
    return (
        block_out,
        grad_input,
        ends[3 : 3 + gain_rows].reshape(-1),
        qkv_grad,
        ends[:3],
        out_weight_grad,
        small[padded],
        small[:experts].T,
        small[experts],
        grad_shared_in,
        grad_shared_out,
        grad_expert_in,
        grad_expert_out,
    )


def solution(mesh):
    return jax.shard_map(
        on_device,
        mesh=mesh,
        in_specs=(
            P("ctx", None),
            P("ctx", None),
            P(),
            P(None, None, "tp"),
            P(None, "tp"),
            P("tp", None),
            P(),
            P(),
            P("ctx", None),
            P(),
            P("ctx", None, "tp"),
            P("tp", "ctx"),
            P("ctx", None, None, "tp"),
            P("ctx", "tp", None),
        ),
        out_specs=(
            P("ctx", None),
            P("ctx", None),
            P(),
            P(None, None, "tp"),
            P(None, "tp"),
            P("tp", None),
            P(),
            P(),
            P(),
            P("ctx", None, "tp"),
            P("tp", "ctx"),
            P("ctx", None, None, "tp"),
            P("ctx", "tp", None),
        ),
        check_vma=False,
    )
```

```python
import functools
import math

import jax
import jax.numpy as jnp
from jax import lax
from jax.experimental import pallas as pl
from jax.experimental.pallas import tpu as pltpu
from jax.sharding import PartitionSpec as P

HD = 128
EPS = 1e-06
THETA = 1000000.0
NEG = -1e30
F32 = jnp.float32
BF16 = jnp.bfloat16


def rotary_tables(positions, width):
    half_width = width // 2
    freqs = THETA ** (-(jnp.arange(half_width, dtype=F32) * 2.0) / width)
    angles = positions.astype(F32)[:, None] * freqs[None, :]
    return (jnp.cos(angles), jnp.sin(angles))


def rotate(values, cosine, sine):
    half_width = values.shape[-1] // 2
    first, second = values[..., :half_width], values[..., half_width:]
    return jnp.concatenate(
        [first * cosine - second * sine, second * cosine + first * sine], axis=-1
    )


def dot(a, b, dims):
    return lax.dot_general(a, b, dims, preferred_element_type=F32)


def swap(value, bits):
    count = lax.axis_size("ctx")
    return lax.ppermute(value, "ctx", [(i, i ^ bits) for i in range(count)])


def relative(natural):
    count = natural.shape[0]
    order = jnp.arange(count, dtype=jnp.int32) ^ lax.axis_index("ctx")
    return natural[order]


def nothing_kernel(*refs):
    pass


def after(values, *others):
    single = not isinstance(values, (list, tuple))
    values = [values] if single else list(values)
    any_spec = pl.BlockSpec(memory_space=pl.ANY)
    results = pl.pallas_call(
        nothing_kernel,
        out_shape=[jax.ShapeDtypeStruct(v.shape, v.dtype) for v in values],
        in_specs=[any_spec] * (len(values) + len(others)),
        out_specs=[any_spec] * len(values),
        input_output_aliases={i: i for i in range(len(values))},
        name="after",
    )(*values, *others)
    return results[0] if single else results


def gather_start(own):
    if lax.axis_size("ctx") != 8:
        return relative(lax.all_gather(own, "ctx", axis=0))
    return [own, swap(own, 1), swap(own, 2), swap(own, 4)]


def gather_end(got, *others):
    if lax.axis_size("ctx") != 8:
        return [got[j] for j in range(lax.axis_size("ctx"))]
    own, b1, b2, b4 = got
    if others:
        b2, b4 = after((b2, b4), *others)
    half = own.shape[0] // 2
    via_x, via_y = swap(b4[:half], 2), swap(b2[half:], 4)
    b3, b5 = swap(b2, 1), swap(b4, 1)
    b6 = jnp.concatenate([via_x, via_y], axis=0)
    return [own, b1, b2, b3, b4, b5, b6, swap(b6, 1)]


def gather_ctx(own, *others):
    return gather_end(gather_start(own), *others)


def pair_sum(parts, j):
    return parts[j].astype(F32) + swap(parts[j ^ 1], 1).astype(F32)


def scatter_ctx(parts, early=None):
    count = lax.axis_size("ctx")
    if count != 8:
        natural = relative(jnp.stack(parts))
        flat = natural.reshape((-1,) + natural.shape[2:])
        return lax.psum_scatter(flat, "ctx", scatter_dimension=0, tiled=True).astype(F32)
    half = parts[0].shape[0] // 2
    pair = {j: pair_sum(parts, j) for j in (2, 4, 6, 0) if j != 2 or early is None}
    if early is None:
        early = (pair[2], pair[2][:half].astype(BF16))
    pair[2] = early[0]
    r2 = swap(early[1], 2)
    r4 = swap(pair[4][half:].astype(BF16), 4)
    q6 = pair[6].astype(BF16)
    via_x, via_y = swap(q6[:half], 2), swap(q6[half:], 4)
    r4a = swap((pair[4][:half] + via_x.astype(F32)).astype(BF16), 4)
    r2b = swap((pair[2][half:] + via_y.astype(F32)).astype(BF16), 2)
    low = r2.astype(F32) + r4a.astype(F32)
    high = r2b.astype(F32) + r4.astype(F32)
    return pair[0] + jnp.concatenate([low, high], axis=0)


def sum_ctx(parts, *others):
    own = scatter_ctx(parts).astype(BF16)
    return gather_ctx(after(own, *others) if others else own)


def shards(value):
    count = lax.axis_size("ctx")
    rows = value.shape[0] // count
    place = lax.axis_index("ctx")
    return [lax.dynamic_slice_in_dim(value, (place ^ j) * rows, rows, 0) for j in range(count)]


def gather_tp(own):
    count = lax.axis_size("tp")
    return [own] + [
        lax.ppermute(own, "tp", [(i, i ^ k) for i in range(count)]) for k in range(1, count)
    ]


NT = (((1,), (1,)), ((), ()))
NN = (((1,), (0,)), ((), ()))
TN = (((0,), (0,)), ((), ()))
VMEM_LIMIT = 60 * 1024 * 1024


def sum_tp(value, *others):
    count, at = lax.axis_size("tp"), lax.axis_index("tp")
    pieces = value.astype(BF16).reshape(count, -1, value.shape[1])
    got = lax.all_to_all(pieces, "tp", split_axis=0, concat_axis=0, tiled=True)
    if others:
        got = after(got, *others)
    total = jnp.sum(got.astype(F32), axis=0).astype(BF16)
    blocks = jnp.stack(gather_tp(total))
    return blocks[jnp.arange(count, dtype=jnp.int32) ^ at].reshape(value.shape), total


def sum_tp_small(value):
    count, bits = lax.axis_size("tp"), 1
    while bits < count:
        value = value + lax.ppermute(value, "tp", [(i, i ^ bits) for i in range(count)])
        bits *= 2
    return value


def attend_kernel(factor, count, place_ref, q_ref, *refs):
    kv_refs, (att_ref, lse_ref, kv, sems) = refs[:count], refs[count:]
    rows = kv.shape[2]
    copies = [
        pltpu.make_async_copy(kv_refs[j].at[:, pl.ds(0, rows)], kv.at[j], sems.at[j])
        for j in range(count)
    ]
    for copy in copies:
        copy.start()
    for copy in copies:
        copy.wait()
    place = place_ref[0]
    heads, tokens, _ = q_ref.shape

    def one_head(head, _):
        query = q_ref[head]
        here = pl.ds(pl.multiple_of(head * tokens, tokens), tokens)

        def scores(j):
            return dot(kv[j, 0, here], query, NT) * factor

        key_at = lax.broadcasted_iota(jnp.int32, (tokens, tokens), 0)
        query_at = lax.broadcasted_iota(jnp.int32, (tokens, tokens), 1)
        first = jnp.where(key_at <= query_at, scores(0), NEG)
        top = jnp.max(first, axis=0, keepdims=True)
        exps = jnp.exp2(first - top)
        total = jnp.sum(exps, axis=0, keepdims=True)
        acc = dot(kv[0, 1, here], exps.astype(BF16), TN)

        def earlier(i, carry):
            top, total, acc = carry
            j = place ^ i
            now = scores(j)
            higher = jnp.maximum(top, jnp.max(now, axis=0, keepdims=True))
            exps = jnp.exp2(now - higher)
            keep = jnp.exp2(top - higher)
            total = total * keep + jnp.sum(exps, axis=0, keepdims=True)
            acc = acc * keep + dot(kv[j, 1, here], exps.astype(BF16), TN)
            return higher, total, acc

        top, total, acc = lax.fori_loop(0, place, earlier, (top, total, acc))
        att_ref[head] = (acc / total).T
        lse_ref[head] = jnp.broadcast_to(top + jnp.log2(total), lse_ref.shape[1:])
        return 0

    lax.fori_loop(0, heads, one_head, 0)


def attend(place, query, kv_blocks):
    heads, tokens, size = query.shape
    count = len(kv_blocks)
    factor = math.log2(math.e) / math.sqrt(size)
    flops = 4 * count * heads * tokens * tokens * size
    return pl.pallas_call(
        functools.partial(attend_kernel, factor, count),
        out_shape=(
            jax.ShapeDtypeStruct((heads, tokens, size), F32),
            jax.ShapeDtypeStruct((heads, 8, tokens), F32),
        ),
        in_specs=[
            pl.BlockSpec(memory_space=pltpu.SMEM),
            pl.BlockSpec(memory_space=pltpu.VMEM),
        ]
        + [pl.BlockSpec(memory_space=pl.ANY)] * count,
        out_specs=(pl.BlockSpec(memory_space=pltpu.VMEM),) * 2,
        scratch_shapes=[
            pltpu.VMEM((count, 2, heads * tokens, size), BF16),
            pltpu.SemaphoreType.DMA((count,)),
        ],
        compiler_params=pltpu.CompilerParams(vmem_limit_bytes=VMEM_LIMIT),
        cost_estimate=pl.CostEstimate(
            flops=flops // 16, bytes_accessed=2**20, transcendentals=0
        ),
        name="attend",
    )(place.reshape(1), query, *kv_blocks)


def attend_back_kernel(factor, scale, count, place_ref, q_ref, do_ref, lse_ref, delta_ref, *refs):
    kv_refs, (dq_ref, dkv_ref, kv, dkv, dq, sems, out_sems) = refs[:count], refs[count:]
    rows = kv.shape[2]
    copies = [
        pltpu.make_async_copy(kv_refs[j].at[:, pl.ds(0, rows)], kv.at[j], sems.at[j])
        for j in range(count)
    ]
    for copy in copies:
        copy.start()
    for copy in copies:
        copy.wait()
    place = place_ref[0]
    heads, tokens, _ = q_ref.shape

    def out_copy(j):
        return pltpu.make_async_copy(dkv.at[j], dkv_ref.at[j], out_sems.at[j])

    def one_block(j, masked):
        def one_head(head, _):
            query, do = q_ref[head], do_ref[head]
            here = pl.ds(pl.multiple_of(head * tokens, tokens), tokens)
            key, value = kv[j, 0, here], kv[j, 1, here]
            scores = dot(key, query, NT) * factor
            probs = jnp.exp2(scores - lse_ref[head, :1])
            if masked:
                key_at = lax.broadcasted_iota(jnp.int32, (tokens, tokens), 0)
                query_at = lax.broadcasted_iota(jnp.int32, (tokens, tokens), 1)
                probs = jnp.where(key_at <= query_at, probs, 0.0)
            dprob = dot(value, do, NT)
            dscore = (probs * (dprob - delta_ref[head, :1])).astype(BF16)
            dkv[j, 0, head] = (dot(dscore, query, NN) * scale).astype(BF16)
            dkv[j, 1, head] = dot(probs.astype(BF16), do, NN).astype(BF16)
            part = dot(key, dscore, TN)
            dq[head] = part if masked else dq[head] + part
            return 0

        lax.fori_loop(0, heads, one_head, 0)
        out_copy(j).start()

    one_block(0, True)

    def earlier(i, _):
        one_block(place ^ i, False)
        return 0

    def later(i, _):
        j = place ^ i
        dkv[j] = jnp.zeros(dkv.shape[1:], BF16)
        out_copy(j).start()
        return 0

    lax.fori_loop(0, place, earlier, 0)
    lax.fori_loop(place + 1, count, later, 0)
    for head in range(heads):
        dq_ref[head] = dq[head].T * scale
    for j in range(count):
        out_copy(j).wait()


def attend_back(place, query, do, lse, delta, kv_blocks):
    heads, tokens, size = query.shape
    count = len(kv_blocks)
    scale = 1.0 / math.sqrt(size)
    factor = math.log2(math.e) * scale
    return pl.pallas_call(
        functools.partial(attend_back_kernel, factor, scale, count),
        out_shape=(
            jax.ShapeDtypeStruct((heads, tokens, size), F32),
            jax.ShapeDtypeStruct((count, 2, heads, tokens, size), BF16),
        ),
        in_specs=[pl.BlockSpec(memory_space=pltpu.SMEM)]
        + [pl.BlockSpec(memory_space=pltpu.VMEM)] * 4
        + [pl.BlockSpec(memory_space=pl.ANY)] * count,
        out_specs=(pl.BlockSpec(memory_space=pltpu.VMEM), pl.BlockSpec(memory_space=pl.ANY)),
        scratch_shapes=[
            pltpu.VMEM((count, 2, heads * tokens, size), BF16),
            pltpu.VMEM((count, 2, heads, tokens, size), BF16),
            pltpu.VMEM((heads, size, tokens), F32),
            pltpu.SemaphoreType.DMA((count,)),
            pltpu.SemaphoreType.DMA((count,)),
        ],
        compiler_params=pltpu.CompilerParams(vmem_limit_bytes=VMEM_LIMIT),
        cost_estimate=pl.CostEstimate(
            flops=count * heads * tokens * tokens * size,
            bytes_accessed=2**20,
            transcendentals=0,
        ),
        name="attend_back",
    )(place.reshape(1), query, do, lse, delta, *kv_blocks)


def swiglu_back(one, two, dact, gate):
    sig = 1.0 / (1.0 + jnp.exp(-one))
    silu = one * sig
    act = silu * two
    prod = act * dact
    dgate = gate * dact
    d_one = (dgate * two * sig * (1.0 + one * (1.0 - sig))).astype(BF16)
    d_two = (dgate * silu).astype(BF16)
    return (gate * act).astype(BF16), d_one, d_two, prod


def experts_kernel(at, group, local, experts, given, first_ref, *refs):
    x_refs, g_refs, refs = refs[:group], refs[group : 2 * group], refs[2 * group :]
    (slot_row, slot_col, w_router, w_first, w_in, w_out, w_shared), refs = refs[:7], refs[7 + given :]
    dx_refs, refs = refs[:group], refs[group:]
    kept_refs, refs = refs[:7], refs[7:]
    (xs, gs, first_w, in_w, out_w, shared_w, dxs, left, right, sems, out_sems), stage = refs[:11], refs[11:]
    rows_x, rows_g, act_s, dpair_s, sact_s, sdpair_s, dl_s = stage
    tokens, width = xs.shape[1:]
    capacity, units = act_s.shape[2:]
    wide = local * capacity
    share = sact_s.shape[2]
    third = first_w.shape[0] - 128
    second = third // 2
    padded = w_router.shape[0]

    loads = [pltpu.make_async_copy(x_refs[b], xs.at[b], sems.at[b]) for b in range(group)]
    loads.append(pltpu.make_async_copy(w_first, first_w, sems.at[group]))
    loads += [
        pltpu.make_async_copy(g_refs[b], gs.at[b], sems.at[group + 1 + b]) for b in range(group)
    ]
    more = [
        pltpu.make_async_copy(w_in.at[e], in_w.at[e], sems.at[2 * group + 1 + 2 * e])
        for e in range(local)
    ]
    more_out = [
        pltpu.make_async_copy(w_out.at[e], out_w.at[e], sems.at[2 * group + 2 + 2 * e])
        for e in range(local)
    ]
    last = pltpu.make_async_copy(w_shared, shared_w, sems.at[2 * group + 1 + 2 * local])
    for copy in loads[: group + 1]:
        copy.start()

    sent = []

    def send(copy):
        copy.start()
        sent.append(copy)

    for copy in loads[: group + 1]:
        copy.wait()
    for copy in loads[group + 1 :] + [more[0], more_out[0]]:
        copy.start()
    x = xs[...].reshape(group * tokens, width)
    fore = dot(x, first_w[...], NT)
    s_one, s_two = fore[:, :share], fore[:, second : second + share]
    s_gate = 1.0 / (1.0 + jnp.exp(-fore[:, third + experts : third + experts + 1]))
    row_at = lax.broadcasted_iota(jnp.int32, (padded, tokens), 0)
    slot_at = lax.broadcasted_iota(jnp.int32, (capacity, tokens), 0)
    probs, change, hits = [], [], []
    for b in range(group):
        logits = fore[b * tokens : (b + 1) * tokens, third:].T[:padded]
        shown = jnp.where(row_at < experts, logits, NEG)
        exps = jnp.exp(shown - jnp.max(shown, axis=0, keepdims=True))
        soft = exps / jnp.sum(exps, axis=0, keepdims=True)
        probs.append(jnp.where(row_at == experts, 1.0 / (1.0 + jnp.exp(-logits)), soft))
        change.append(jnp.zeros((padded, tokens), F32))
        picks = jnp.concatenate(
            [
                jnp.where(slot_at == slot_row[b, e : e + 1, :], 1.0, 0.0).astype(BF16)
                for e in range(local)
            ],
            axis=0,
        )
        rows = dot(picks, xs[b], NN).astype(BF16)
        for e in range(local):
            rows_x[e, b] = rows[e * capacity : (e + 1) * capacity]
        loads[group + 1 + b].wait()
        if b == group - 1:
            for e in range(1, local):
                more[e].start()
                more_out[e].start()
            last.start()
        rows = dot(picks, gs[b], NN).astype(BF16)
        for e in range(local):
            rows_g[e, b] = rows[e * capacity : (e + 1) * capacity]
    def send_all(i, lead):
        for e in range(lead):
            send(
                pltpu.make_async_copy(
                    stage[i].at[e], kept_refs[i].at[e, pl.ds(at, group)], out_sems.at[i, e]
                )
            )

    send_all(0, local)
    send_all(1, local)
    is_expert = row_at < experts
    for e in range(local):
        chosen = row_at == first_ref[0] + e
        gates, owns, hits = [], [], []
        for b in range(group):
            own = jnp.sum(jnp.where(chosen, probs[b], 0.0), axis=0, keepdims=True)
            hit = slot_at == slot_row[b, e : e + 1, :]
            gates.append(jnp.sum(jnp.where(hit, own, 0.0), axis=1, keepdims=True))
            owns.append(own)
            hits.append(hit)
        more[e].wait()
        pair = dot(rows_x[e].reshape(group * capacity, width), in_w[e], NT)
        most = pair.shape[1] // 2
        more_out[e].wait()
        dact = dot(rows_g[e].reshape(group * capacity, width), out_w[e], NT)
        act, d_one, d_two, prod = swiglu_back(
            pair[:, :most], pair[:, most:], dact, jnp.concatenate(gates, axis=0)
        )
        act_s[e] = act[:, :units].reshape(group, capacity, units)
        dpair_s[2 * e] = d_one[:, :units].reshape(group, capacity, units)
        dpair_s[2 * e + 1] = d_two[:, :units].reshape(group, capacity, units)
        row_dot = jnp.sum(prod, axis=1, keepdims=True)
        drow = dot(jnp.concatenate([d_one, d_two], axis=1), in_w[e], NN).astype(BF16)
        for b in range(group):
            rows = slice(b * capacity, (b + 1) * capacity)
            found = jnp.sum(jnp.where(hits[b], row_dot[rows], 0.0), axis=0, keepdims=True)
            change[b] += (found * owns[b]) * (
                jnp.where(chosen, 1.0, 0.0) - jnp.where(is_expert, probs[b], 0.0)
            )
            right[b, e * capacity : (e + 1) * capacity] = drow[rows]
    send_all(2, local)
    send_all(3, 2 * local)
    last.wait()
    g = gs[...].reshape(group * tokens, width)
    s_dact = dot(g, shared_w[...], NT)
    act, d_one, d_two, prod = swiglu_back(s_one, s_two, s_dact, s_gate)
    sact_s[...] = act.reshape(group, tokens, share)
    sdpair_s[:, 0] = d_one.reshape(group, tokens, share)
    sdpair_s[:, 1] = d_two.reshape(group, tokens, share)
    dslogit = jnp.sum(prod, axis=1, keepdims=True) * s_gate * (1.0 - s_gate)
    lane_at = lax.broadcasted_iota(jnp.int32, (tokens, 128), 1)
    rest = jnp.zeros((128 - padded, tokens), F32)
    deep = wide + 2 * share
    column_at = lax.broadcasted_iota(jnp.int32, (tokens, capacity), 1)
    stores = []
    for b in range(group):
        rows = slice(b * tokens, (b + 1) * tokens)
        columns = jnp.concatenate([change[b], rest], axis=0).T
        columns = jnp.where(lane_at == experts, dslogit[rows], columns)[:, :padded].astype(BF16)
        dl_s[b] = columns
        left[b, :, deep : deep + padded] = columns
        right[b, deep : deep + padded] = w_router[...]
        for e in range(local):
            picks = jnp.where(column_at == slot_col[b, :, e : e + 1], 1.0, 0.0).astype(BF16)
            left[b, :, e * capacity : (e + 1) * capacity] = picks
        left[b, :, wide : wide + share] = d_one[rows]
        left[b, :, wide + share : wide + 2 * share] = d_two[rows]
        right[b, wide : wide + share] = first_w[:share]
        right[b, wide + share : wide + 2 * share] = first_w[second : second + share]
        dxs[b] = dot(left[b], right[b], NN).astype(BF16)
        send(pltpu.make_async_copy(dxs.at[b], dx_refs[b], out_sems.at[7, b]))
    for i in range(4, 7):
        send(pltpu.make_async_copy(stage[i], kept_refs[i].at[pl.ds(at, group)], out_sems.at[i, 0]))
    for copy in sent:
        copy.wait()


def run_experts(at, experts, first, x_group, g_group, slot_rows, slot_cols, weights, kept):
    given = kept if at else []
    group = len(x_group)
    tokens, width = x_group[0].shape
    w_router, w_first, w_in, w_out, w_shared = weights
    local, padded_units = w_out.shape[:2]
    share = w_shared.shape[0]
    padded = w_router.shape[0]
    capacity, units = kept[2].shape[2:]
    any_spec = pl.BlockSpec(memory_space=pl.ANY)
    block = jax.ShapeDtypeStruct((tokens, width), BF16)
    deep = local * capacity + 2 * share + padded
    flops = group * 2 * tokens * width * (local * capacity * 3 + 5 * share) + (
        group * 2 * width * local * capacity * units * 5
    )
    step = at // group
    results = pl.pallas_call(
        functools.partial(experts_kernel, at, group, local, experts, len(given)),
        grid=(1,),
        out_shape=(block,) * group + tuple(jax.ShapeDtypeStruct(k.shape, k.dtype) for k in kept),
        in_specs=[pl.BlockSpec(memory_space=pltpu.SMEM)]
        + [any_spec] * (2 * group)
        + [
            pl.BlockSpec((group, local, tokens), lambda i: (step, 0, 0)),
            pl.BlockSpec((group, tokens, local), lambda i: (step, 0, 0)),
            pl.BlockSpec((padded, width), lambda i: (0, 0)),
        ]
        + [any_spec] * (4 + len(given)),
        out_specs=(any_spec,) * (group + len(kept)),
        input_output_aliases={8 + 2 * group + i: group + i for i in range(len(given))},
        scratch_shapes=[
            pltpu.VMEM((group, tokens, width), BF16),
            pltpu.VMEM((group, tokens, width), BF16),
            pltpu.VMEM(w_first.shape, BF16),
            pltpu.VMEM(w_in.shape, BF16),
            pltpu.VMEM(w_out.shape, BF16),
            pltpu.VMEM(w_shared.shape, BF16),
            pltpu.VMEM((group, tokens, width), BF16),
            pltpu.VMEM((group, tokens, deep), BF16),
            pltpu.VMEM((group, deep, width), BF16),
            pltpu.SemaphoreType.DMA((2 * group + 2 + 2 * local,)),
            pltpu.SemaphoreType.DMA((8, max(2 * local, group))),
        ]
        + [
            pltpu.VMEM(k.shape[:1] + (group,) + k.shape[2:], BF16) for k in kept[:4]
        ]
        + [pltpu.VMEM((group,) + k.shape[1:], BF16) for k in kept[4:]],
        compiler_params=pltpu.CompilerParams(vmem_limit_bytes=VMEM_LIMIT),
        cost_estimate=pl.CostEstimate(flops=flops // 16, bytes_accessed=2**20, transcendentals=0),
        name="run_experts",
    )(first.reshape(1), *x_group, *g_group, slot_rows, slot_cols, *weights, *given)
    return results[:group], results[group:]


def outputs_kernel(group, count, local, act, slot_col, sact, w_out, w_shared, *refs):
    out_refs, (outs, left, right, sems) = refs[:count], refs[count:]
    step = pl.program_id(0)
    slot = lax.rem(step, 2)
    capacity, units = act.shape[2:]
    tokens, share = sact.shape[1:]
    wide = local * capacity

    def store(at, b, into):
        return pltpu.make_async_copy(outs.at[into, b], out_refs[at * group + b], sems.at[into, b])

    @pl.when(step >= 2)
    def _():
        for b in range(group):
            store(0, b, slot).wait()

    for e in range(local):
        rows = dot(act[e].reshape(group * capacity, units), w_out[e], NN).astype(BF16)
        for b in range(group):
            right[b, e * capacity : (e + 1) * capacity] = rows[b * capacity : (b + 1) * capacity]
    slot_at = lax.broadcasted_iota(jnp.int32, (tokens, capacity), 1)
    for b in range(group):
        for e in range(local):
            picks = jnp.where(slot_at == slot_col[b, :, e : e + 1], 1.0, 0.0).astype(BF16)
            left[b, :, e * capacity : (e + 1) * capacity] = picks
        left[b, :, wide : wide + share] = sact[b]
        right[b, wide : wide + share] = w_shared[0]
        outs[slot, b] = dot(left[b], right[b], NN).astype(BF16)
    for at in range(count // group):

        @pl.when(step == at)
        def _():
            for b in range(group):
                store(at, b, at % 2).start()

    @pl.when(step == count // group - 1)
    def _():
        for b in range(group):
            for into in range(2):
                store(0, b, into).wait()


def run_outputs(act, slot_cols, sact, w_out, w_shared):
    local, count, capacity, units = act.shape
    tokens, share = sact.shape[1:]
    width = w_out.shape[2]
    group = 2
    deep = local * capacity + share
    return pl.pallas_call(
        functools.partial(outputs_kernel, group, count, local),
        grid=(count // group,),
        out_shape=(jax.ShapeDtypeStruct((tokens, width), BF16),) * count,
        in_specs=[
            pl.BlockSpec((local, group, capacity, units), lambda i: (0, i, 0, 0)),
            pl.BlockSpec((group, tokens, local), lambda i: (i, 0, 0)),
            pl.BlockSpec((group, tokens, share), lambda i: (i, 0, 0)),
            pl.BlockSpec((local, units, width), lambda i: (0, 0, 0)),
            pl.BlockSpec((1, share, width), lambda i: (2, 0, 0)),
        ],
        out_specs=(pl.BlockSpec(memory_space=pl.ANY),) * count,
        scratch_shapes=[
            pltpu.VMEM((2, group, tokens, width), BF16),
            pltpu.VMEM((group, tokens, deep), BF16),
            pltpu.VMEM((group, deep, width), BF16),
            pltpu.SemaphoreType.DMA((2, group)),
        ],
        compiler_params=pltpu.CompilerParams(vmem_limit_bytes=VMEM_LIMIT),
        cost_estimate=pl.CostEstimate(
            flops=count * width // 8 * (local * capacity * (units + tokens) + tokens * share),
            bytes_accessed=2**20,
            transcendentals=0,
        ),
        name="run_outputs",
    )(act, slot_cols, sact, w_out, w_shared)


def assemble_kernel(plan, place_ref, *refs):
    total = sum(count for count, _, _, _ in plan)
    block_refs, (out_ref, low, wide, in_sems, out_sems) = refs[:total], refs[total:]
    place = place_ref[0]
    steps, at = [], 0
    for count, skip, rows, base in plan:
        for j in range(count):
            steps.append((at + j, skip, rows, base + (place ^ j) * rows))
        at += count

    def load(i):
        which, skip, rows, _ = steps[i]
        return pltpu.make_async_copy(
            block_refs[which].at[pl.ds(skip, rows)], low.at[i % 2, pl.ds(0, rows)], in_sems.at[i % 2]
        )

    def store(i):
        _, _, rows, start = steps[i]
        return pltpu.make_async_copy(
            wide.at[i % 2, pl.ds(0, rows)],
            out_ref.at[pl.ds(pl.multiple_of(start, 8), rows)],
            out_sems.at[i % 2],
        )

    load(0).start()
    for i, (_, _, rows, _) in enumerate(steps):
        if i + 1 < len(steps):
            load(i + 1).start()
        load(i).wait()
        if i >= 2:
            store(i - 2).wait()
        wide[i % 2, :rows] = low[i % 2, :rows].astype(F32)
        store(i).start()
    for i in range(max(0, len(steps) - 2), len(steps)):
        store(i).wait()


def assemble(place, lists):
    plan, base = [], 0
    for blocks, skip, rows in lists:
        plan.append((len(blocks), skip, rows, base))
        base += len(blocks) * rows
    width = lists[0][0][0].shape[1]
    most = max(rows for _, _, rows in lists)
    flat = [b for blocks, _, _ in lists for b in blocks]
    return pl.pallas_call(
        functools.partial(assemble_kernel, plan),
        out_shape=jax.ShapeDtypeStruct((base, width), F32),
        in_specs=[pl.BlockSpec(memory_space=pltpu.SMEM)]
        + [pl.BlockSpec(memory_space=pl.ANY)] * len(flat),
        out_specs=pl.BlockSpec(memory_space=pl.ANY),
        scratch_shapes=[
            pltpu.VMEM((2, most, width), BF16),
            pltpu.VMEM((2, most, width), F32),
            pltpu.SemaphoreType.DMA((2,)),
            pltpu.SemaphoreType.DMA((2,)),
        ],
        compiler_params=pltpu.CompilerParams(vmem_limit_bytes=VMEM_LIMIT),
        cost_estimate=pl.CostEstimate(flops=0, bytes_accessed=6 * base * width, transcendentals=0),
        name="assemble",
    )(place.reshape(1), *flat)


def shared_grads_kernel(count, *refs):
    x_refs, g_refs, refs = refs[:count], refs[count : 2 * count], refs[2 * count :]
    (sact, sdpair, dl, grads_ref, router_ref, xs, gs, grads, router, sems) = refs
    at = pl.program_id(0)
    slot = lax.rem(at, 2)

    def load(j, into):
        return (
            pltpu.make_async_copy(x_refs[j], xs.at[into], sems.at[0, into]),
            pltpu.make_async_copy(g_refs[j], gs.at[into], sems.at[1, into]),
        )

    @pl.when(at == 0)
    def _():
        for copy in load(0, 0):
            copy.start()
        grads[...] = jnp.zeros_like(grads)
        router[...] = jnp.zeros_like(router)

    for j in range(1, count):

        @pl.when(at == j - 1)
        def _():
            for copy in load(j, j % 2):
                copy.start()

    for copy in load(0, slot):
        copy.wait()
    x, g = xs[slot], gs[slot]
    grads[0] += dot(sdpair[0, 0], x, TN)
    grads[1] += dot(sdpair[0, 1], x, TN)
    grads[2] += dot(sact[0], g, TN)
    router[...] += dot(dl[0], x, TN)

    @pl.when(at == count - 1)
    def _():
        grads_ref[...] = grads[...].astype(BF16)
        router_ref[...] = router[...]


def shared_grads(x_blocks, g_blocks, sact, sdpair, dl):
    count = len(x_blocks)
    tokens, width = x_blocks[0].shape
    share, padded = sact.shape[2], dl.shape[2]
    any_spec = pl.BlockSpec(memory_space=pl.ANY)
    return pl.pallas_call(
        functools.partial(shared_grads_kernel, count),
        grid=(count,),
        out_shape=(
            jax.ShapeDtypeStruct((3, share, width), BF16),
            jax.ShapeDtypeStruct((padded, width), F32),
        ),
        in_specs=[any_spec] * (2 * count)
        + [
            pl.BlockSpec((1, tokens, share), lambda j: (j, 0, 0)),
            pl.BlockSpec((1, 2, tokens, share), lambda j: (j, 0, 0, 0)),
            pl.BlockSpec((1, tokens, padded), lambda j: (j, 0, 0)),
        ],
        out_specs=(
            pl.BlockSpec((3, share, width), lambda j: (0, 0, 0)),
            pl.BlockSpec((padded, width), lambda j: (0, 0)),
        ),
        scratch_shapes=[
            pltpu.VMEM((2, tokens, width), BF16),
            pltpu.VMEM((2, tokens, width), BF16),
            pltpu.VMEM((3, share, width), F32),
            pltpu.VMEM((padded, width), F32),
            pltpu.SemaphoreType.DMA((2, 2)),
        ],
        compiler_params=pltpu.CompilerParams(vmem_limit_bytes=VMEM_LIMIT),
        cost_estimate=pl.CostEstimate(
            flops=count * tokens * width * share,
            bytes_accessed=2**20,
            transcendentals=0,
        ),
        name="shared_grads",
    )(*x_blocks, *g_blocks, sact, sdpair, dl)


def on_device(
    hidden_in,
    cotangent,
    gain_attn,
    qkv_weight,
    qkv_bias,
    out_weight,
    gain_ffn,
    router_weight,
    routes,
    shared_gate,
    shared_in,
    shared_out,
    expert_in,
    expert_out,
):
    tokens, width = hidden_in.shape
    ctx_count = lax.axis_size("ctx")
    heads_local = qkv_weight.shape[2] // HD
    local = expert_in.shape[0]
    experts = local * ctx_count
    top_count = routes.shape[1]
    capacity = 3 * tokens * top_count // (2 * experts)
    place = lax.axis_index("ctx")
    order = jnp.arange(ctx_count, dtype=jnp.int32) ^ place
    score_scale = 1.0 / math.sqrt(HD)
    query_pos = place * tokens + jnp.arange(tokens, dtype=jnp.int32)
    cosine, sine = rotary_tables(query_pos, HD)

    x_full = hidden_in.astype(F32)
    inv_one = lax.rsqrt(jnp.mean(x_full * x_full, axis=-1, keepdims=True) + EPS)
    normed_one = x_full * inv_one
    x_one = (normed_one * gain_attn).astype(BF16)
    projected = (
        jnp.einsum("td,dcf->ctf", x_one, qkv_weight, preferred_element_type=F32)
        + qkv_bias[:, None]
    )
    shaped = projected.reshape(3, tokens, heads_local, HD).transpose(0, 2, 1, 3)
    query = rotate(shaped[0], cosine, sine).astype(BF16)
    key_local = rotate(shaped[1], cosine, sine).astype(BF16)
    value_local = shaped[2].astype(BF16)
    kv_rows = heads_local * tokens
    route_rows = -(-tokens * top_count // HD)
    behind = jnp.pad(
        routes.astype(BF16).reshape(route_rows, HD), ((0, -route_rows % 16), (0, 0))
    )
    kv_local = jnp.stack(
        [
            jnp.concatenate([key_local.reshape(kv_rows, HD), behind], axis=0),
            jnp.concatenate([value_local.reshape(kv_rows, HD), behind], axis=0),
        ]
    )
    kv_got = gather_start(kv_local)
    kv_blocks = gather_end(kv_got)
    g_blocks = gather_ctx(after(cotangent, kv_blocks[6 % ctx_count]))

    share = shared_out.shape[0] // ctx_count
    piece = shared_out.shape[1]
    shared_send = jnp.concatenate(
        [
            shared_in.transpose(1, 2, 0).reshape(2, ctx_count, share, piece),
            shared_out.reshape(1, ctx_count, share, piece),
        ],
        axis=0,
    ).transpose(1, 0, 2, 3)
    shared_w = (
        lax.all_to_all(shared_send, "ctx", split_axis=0, concat_axis=0, tiled=True)
        .transpose(1, 2, 0, 3)
        .reshape(3, share, width)
    )
    half_rows = out_weight.shape[0] // 2
    core = place % 2
    out_mine = lax.all_gather(
        lax.dynamic_slice_in_dim(out_weight, core * half_rows, half_rows, 0), "tp", axis=0, tiled=True
    )

    routes_all = jnp.stack([b[0, kv_rows : kv_rows + route_rows] for b in kv_blocks])
    routes_all = routes_all.astype(jnp.int32).reshape(ctx_count, tokens, top_count)
    own_experts = place * local + jnp.arange(local, dtype=jnp.int32)
    hit = jnp.any(routes_all[:, None] == own_experts[None, :, None, None], axis=-1)
    rank = jnp.cumsum(hit.astype(jnp.int32), axis=-1) - 1
    slot_rows = jnp.where(hit, rank, -1)
    slot_cols = slot_rows.transpose(0, 2, 1)
    padded = -(-(experts + 1) // 8) * 8
    w_router = jnp.concatenate(
        [
            router_weight.T,
            shared_gate[None],
            jnp.zeros((padded - experts - 1, width), BF16),
        ],
        axis=0,
    )
    w_in = expert_in.transpose(0, 2, 3, 1)

    attended, lse = attend(place, query, kv_blocks)
    att = attended.astype(BF16).transpose(1, 0, 2).reshape(tokens, heads_local * HD)
    out_other = swap(after(out_mine, attended), 1)
    tp_count = lax.axis_size("tp")
    att_all = gather_tp(att)
    where_to = jnp.arange(tp_count, dtype=jnp.int32) ^ lax.axis_index("tp")
    att_all = jnp.stack(att_all)[where_to]
    att_low = jnp.concatenate([a[:, :half_rows] for a in att_all], axis=1)
    att_high = jnp.concatenate([a[:, half_rows:] for a in att_all], axis=1)
    out_low = jnp.where(core == 0, out_mine, out_other)
    out_high = jnp.where(core == 0, out_other, out_mine)
    hidden = x_full + dot(
        jnp.concatenate([att_low, att_high], axis=1),
        jnp.concatenate([out_low, out_high], axis=0),
        NN,
    )
    inv_two = lax.rsqrt(jnp.mean(hidden * hidden, axis=-1, keepdims=True) + EPS)
    normed_two = hidden * inv_two
    x_two = (normed_two * gain_ffn).astype(BF16)

    units, group = expert_out.shape[1], 2
    kept = [
        jax.ShapeDtypeStruct(shape, BF16)
        for shape in (
            (local, ctx_count, capacity, width),
            (local, ctx_count, capacity, width),
            (local, ctx_count, capacity, units),
            (2 * local, ctx_count, capacity, units),
            (ctx_count, tokens, share),
            (ctx_count, 2, tokens, share),
            (ctx_count, tokens, padded),
        )
    ]
    extra = -units % 128
    w_in = jnp.pad(w_in, ((0, 0), (0, 0), (0, extra), (0, 0)))
    w_in = w_in.reshape(local, 2 * (units + extra), width)
    w_out = jnp.pad(expert_out, ((0, 0), (0, extra), (0, 0)))
    half = -(-share // 64) * 64
    gap = jnp.zeros((half - share, width), BF16)
    w_first = jnp.concatenate(
        [shared_w[0], gap, shared_w[1], gap, w_router, jnp.zeros((128 - padded, width), BF16)], axis=0
    )
    weights = (w_router, w_first, w_in, w_out, shared_w[2])
    got = gather_start(x_two)
    x_blocks = [got[0], got[1]]
    dxs = []
    early = None
    for at in range(0, ctx_count, group):
        if at == 4 and ctx_count == 8:
            pair_two = pair_sum(dxs, 2)
            early = (pair_two, pair_two[: tokens // 2].astype(BF16))
        if at == 6 and ctx_count == 8:
            x_blocks[6] = after(x_blocks[6], early[1])
        dx, kept = run_experts(
            at,
            experts,
            place * local,
            x_blocks[at : at + group],
            g_blocks[at : at + group],
            slot_rows,
            slot_cols,
            weights,
            kept,
        )
        dxs += dx
        if at == 0:
            x_blocks = gather_end(got, dx[0])
    rows_x, rows_g, act_low, dpair, s_act, s_dpair, low_logits = kept
    grad_x_part = scatter_ctx(dxs, early)
    outs = run_outputs(act_low, slot_cols, s_act, expert_out, shared_w)
    outs = after(outs, grad_x_part)
    out_part = scatter_ctx(outs)
    dpair = dpair.reshape(local, 2, ctx_count, capacity, units)
    grad_expert_in = jnp.einsum("ebcd,evbcf->edvf", rows_x, dpair, preferred_element_type=F32)
    grad_expert_out = jnp.einsum("ebcf,ebcd->efd", act_low, rows_g, preferred_element_type=F32)
    shared_low, router_part = shared_grads(x_blocks, g_blocks, s_act, s_dpair, low_logits)
    shared_back = lax.all_to_all(
        shared_low.reshape(3, share, ctx_count, piece).transpose(2, 0, 1, 3),
        "ctx",
        split_axis=0,
        concat_axis=0,
        tiled=True,
    ).astype(F32)
    grad_shared_in = shared_back[:, :2].transpose(3, 1, 0, 2).reshape(shared_in.shape)
    grad_shared_out = shared_back[:, 2].reshape(shared_out.shape)

    summed = lax.psum(grad_x_part.astype(BF16), "tp")
    gain_ffn_part = jnp.sum(grad_x_part * normed_two, axis=0)
    small = sum_tp_small(jnp.concatenate([router_part, gain_ffn_part[None]], axis=0))
    summed = after(summed, out_part, shared_low, grad_expert_in, grad_expert_out, small)
    summed = summed.astype(F32)
    grad_y = cotangent.astype(F32)
    grad_normed_two = summed * gain_ffn
    grad_hidden = grad_y + inv_two * (
        grad_normed_two
        - normed_two * jnp.mean(grad_normed_two * normed_two, axis=-1, keepdims=True)
    )
    grad_hidden_low = grad_hidden.astype(BF16)
    out_weight_part = dot(att, grad_hidden_low, (((0,), (0,)), ((), ())))
    grad_att = (
        dot(grad_hidden_low, out_weight, (((1,), (1,)), ((), ())))
        .astype(BF16)
        .reshape(tokens, heads_local, HD)
        .transpose(1, 0, 2)
    )
    delta = jnp.sum(grad_att.astype(F32) * attended, axis=-1)
    delta = jnp.broadcast_to(delta[:, None], lse.shape)
    grad_query, grad_pairs = attend_back(place, query, grad_att, lse, delta, kv_blocks)
    ffn_low, _ = sum_tp(after(out_part, summed), grad_query)
    grad_kv = scatter_ctx([grad_pairs[j] for j in range(ctx_count)])
    grad_kv = after(grad_kv, ffn_low)

    def raw_part(value):
        return value.astype(BF16).transpose(1, 0, 2).reshape(tokens, heads_local * HD)

    raw = [
        raw_part(rotate(grad_query, cosine, -sine)),
        raw_part(rotate(grad_kv[0], cosine, -sine)),
        raw_part(grad_kv[1]),
    ]
    grad_x_one_part = sum(
        dot(raw[c], qkv_weight[:, c], NT) for c in range(3)
    )
    grad_x_one, half_way = sum_tp(grad_x_one_part)
    gain_attn_part = jnp.sum(grad_x_one_part * normed_one, axis=0)
    gain_sum = sum_tp_small(gain_attn_part[None])
    head_width = heads_local * HD
    gain_rows = width // head_width
    ends = jnp.concatenate(
        [jnp.sum(r.astype(F32), axis=0)[None] for r in raw]
        + [gain_sum.reshape(gain_rows, -1), small.reshape((padded + 1) * gain_rows, -1)],
        axis=0,
    )
    ends = jnp.pad(ends, ((0, -ends.shape[0] % (16 * ctx_count)), (0, 0))).astype(BF16)
    query_part = after(dot(x_one, raw[0], TN).astype(BF16), grad_kv)
    pair_part = jnp.concatenate([dot(x_one, raw[1], TN), dot(x_one, raw[2], TN)], axis=0).astype(BF16)
    spread = lambda v: v.astype(BF16).reshape(-1, head_width)
    sums = sum_ctx(
        [
            jnp.concatenate(list(parts), axis=0)
            for parts in zip(
                *[shards(v) for v in (query_part, pair_part, spread(out_weight_part), ends)]
            )
        ],
        half_way,
    )
    q_rows = width // ctx_count
    qkv_grad = assemble(place, [(sums, 0, q_rows), (sums, q_rows, 2 * q_rows)])
    qkv_grad = qkv_grad.reshape(3, width, head_width).transpose(1, 0, 2)
    out_rows = out_weight.size // head_width // ctx_count
    out_weight_grad = assemble(place, [(sums, 3 * q_rows, out_rows)]).reshape(out_weight.shape)
    ends = relative(jnp.stack([b[3 * q_rows + out_rows :] for b in sums]))
    ends = ends.reshape(-1, head_width).astype(F32)
    small = ends[3 + gain_rows : 3 + (padded + 2) * gain_rows].reshape(padded + 1, width)
    grad_x_one = after(grad_x_one, sums[2]).astype(F32)
    grad_normed_one = grad_x_one * gain_attn
    grad_input = grad_hidden + inv_one * (
        grad_normed_one
        - normed_one * jnp.mean(grad_normed_one * normed_one, axis=-1, keepdims=True)
    )
    block_out = (hidden + ffn_low.astype(F32)).astype(BF16)
    return (
        block_out,
        grad_input,
        ends[3 : 3 + gain_rows].reshape(-1),
        qkv_grad,
        ends[:3],
        out_weight_grad,
        small[padded],
        small[:experts].T,
        small[experts],
        grad_shared_in,
        grad_shared_out,
        grad_expert_in,
        grad_expert_out,
    )


def solution(mesh):
    return jax.shard_map(
        on_device,
        mesh=mesh,
        in_specs=(
            P("ctx", None),
            P("ctx", None),
            P(),
            P(None, None, "tp"),
            P(None, "tp"),
            P("tp", None),
            P(),
            P(),
            P("ctx", None),
            P(),
            P("ctx", None, "tp"),
            P("tp", "ctx"),
            P("ctx", None, None, "tp"),
            P("ctx", "tp", None),
        ),
        out_specs=(
            P("ctx", None),
            P("ctx", None),
            P(),
            P(None, None, "tp"),
            P(None, "tp"),
            P("tp", None),
            P(),
            P(),
            P(),
            P("ctx", None, "tp"),
            P("tp", "ctx"),
            P("ctx", None, None, "tp"),
            P("ctx", "tp", None),
        ),
        check_vma=False,
    )
```

```python
import functools
import math

import jax
import jax.numpy as jnp
from jax import lax
from jax.experimental import pallas as pl
from jax.experimental.pallas import tpu as pltpu
from jax.sharding import PartitionSpec as P

HD = 128
EPS = 1e-06
THETA = 1000000.0
NEG = -1e30
F32 = jnp.float32
BF16 = jnp.bfloat16


def rotary_tables(positions, width):
    half_width = width // 2
    freqs = THETA ** (-(jnp.arange(half_width, dtype=F32) * 2.0) / width)
    angles = positions.astype(F32)[:, None] * freqs[None, :]
    return (jnp.cos(angles), jnp.sin(angles))


def rotate(values, cosine, sine):
    half_width = values.shape[-1] // 2
    first, second = values[..., :half_width], values[..., half_width:]
    return jnp.concatenate(
        [first * cosine - second * sine, second * cosine + first * sine], axis=-1
    )


def dot(a, b, dims):
    return lax.dot_general(a, b, dims, preferred_element_type=F32)


def swap(value, bits):
    count = lax.axis_size("ctx")
    return lax.ppermute(value, "ctx", [(i, i ^ bits) for i in range(count)])


def relative(natural):
    count = natural.shape[0]
    order = jnp.arange(count, dtype=jnp.int32) ^ lax.axis_index("ctx")
    return natural[order]


def nothing_kernel(*refs):
    pass


def after(values, *others):
    single = not isinstance(values, (list, tuple))
    values = [values] if single else list(values)
    any_spec = pl.BlockSpec(memory_space=pl.ANY)
    results = pl.pallas_call(
        nothing_kernel,
        out_shape=[jax.ShapeDtypeStruct(v.shape, v.dtype) for v in values],
        in_specs=[any_spec] * (len(values) + len(others)),
        out_specs=[any_spec] * len(values),
        input_output_aliases={i: i for i in range(len(values))},
        name="after",
    )(*values, *others)
    return results[0] if single else results


def gather_start(own):
    if lax.axis_size("ctx") != 8:
        return relative(lax.all_gather(own, "ctx", axis=0))
    return [own, swap(own, 1), swap(own, 2), swap(own, 4)]


def gather_end(got, *others):
    if lax.axis_size("ctx") != 8:
        return [got[j] for j in range(lax.axis_size("ctx"))]
    own, b1, b2, b4 = got
    if others:
        b2, b4 = after((b2, b4), *others)
    half = own.shape[0] // 2
    via_x, via_y = swap(b4[:half], 2), swap(b2[half:], 4)
    b3, b5 = swap(b2, 1), swap(b4, 1)
    b6 = jnp.concatenate([via_x, via_y], axis=0)
    return [own, b1, b2, b3, b4, b5, b6, swap(b6, 1)]


def gather_ctx(own, *others):
    return gather_end(gather_start(own), *others)


def pair_sum(parts, j):
    return parts[j].astype(F32) + swap(parts[j ^ 1], 1).astype(F32)


def scatter_ctx(parts, early=None, late=None):
    count = lax.axis_size("ctx")
    if count != 8:
        natural = relative(jnp.stack(parts))
        flat = natural.reshape((-1,) + natural.shape[2:])
        return lax.psum_scatter(flat, "ctx", scatter_dimension=0, tiled=True).astype(F32)
    half = parts[0].shape[0] // 2
    pair = {j: pair_sum(parts, j) for j in (2, 4, 6, 0) if j != 2 or early is None}
    if early is None:
        early = (pair[2], pair[2][:half].astype(BF16))
    pair[2] = early[0]
    r2 = swap(early[1], 2)
    r4 = swap(pair[4][half:].astype(BF16), 4)
    q6 = pair[6].astype(BF16)
    via_x, via_y = swap(q6[:half], 2), swap(q6[half:], 4)
    r4a = (pair[4][:half] + via_x.astype(F32)).astype(BF16)
    r2b = (pair[2][half:] + via_y.astype(F32)).astype(BF16)
    if late is not None:
        r4a, r2b = after((r4a, r2b), late)
    r4a, r2b = swap(r4a, 4), swap(r2b, 2)
    low = r2.astype(F32) + r4a.astype(F32)
    high = r2b.astype(F32) + r4.astype(F32)
    return pair[0] + jnp.concatenate([low, high], axis=0)


def sum_ctx(parts, *others):
    own = scatter_ctx(parts).astype(BF16)
    return gather_ctx(after(own, *others) if others else own)


def shards(value):
    count = lax.axis_size("ctx")
    rows = value.shape[0] // count
    place = lax.axis_index("ctx")
    return [lax.dynamic_slice_in_dim(value, (place ^ j) * rows, rows, 0) for j in range(count)]


def gather_tp(own):
    count = lax.axis_size("tp")
    return [own] + [
        lax.ppermute(own, "tp", [(i, i ^ k) for i in range(count)]) for k in range(1, count)
    ]


NT = (((1,), (1,)), ((), ()))
NN = (((1,), (0,)), ((), ()))
TN = (((0,), (0,)), ((), ()))
VMEM_LIMIT = 60 * 1024 * 1024


def sum_tp(value, *others):
    count, at = lax.axis_size("tp"), lax.axis_index("tp")
    pieces = value.astype(BF16).reshape(count, -1, value.shape[1])
    got = lax.all_to_all(pieces, "tp", split_axis=0, concat_axis=0, tiled=True)
    if others:
        got = after(got, *others)
    total = jnp.sum(got.astype(F32), axis=0).astype(BF16)
    blocks = jnp.stack(gather_tp(total))
    return blocks[jnp.arange(count, dtype=jnp.int32) ^ at].reshape(value.shape), total


def sum_tp_small(value):
    count, bits = lax.axis_size("tp"), 1
    while bits < count:
        value = value + lax.ppermute(value, "tp", [(i, i ^ bits) for i in range(count)])
        bits *= 2
    return value


def attend_kernel(factor, count, place_ref, q_ref, *refs):
    kv_refs, (att_ref, lse_ref, kv, sems) = refs[:count], refs[count:]
    rows = kv.shape[2]
    copies = [
        pltpu.make_async_copy(kv_refs[j].at[:, pl.ds(0, rows)], kv.at[j], sems.at[j])
        for j in range(count)
    ]
    for copy in copies:
        copy.start()
    for copy in copies:
        copy.wait()
    place = place_ref[0]
    heads, tokens, _ = q_ref.shape

    def one_head(head, _):
        query = q_ref[head]
        here = pl.ds(pl.multiple_of(head * tokens, tokens), tokens)

        def scores(j):
            return dot(kv[j, 0, here], query, NT) * factor

        key_at = lax.broadcasted_iota(jnp.int32, (tokens, tokens), 0)
        query_at = lax.broadcasted_iota(jnp.int32, (tokens, tokens), 1)
        first = jnp.where(key_at <= query_at, scores(0), NEG)
        top = jnp.max(first, axis=0, keepdims=True)
        exps = jnp.exp2(first - top)
        total = jnp.sum(exps, axis=0, keepdims=True)
        acc = dot(kv[0, 1, here], exps.astype(BF16), TN)

        def earlier(i, carry):
            top, total, acc = carry
            j = place ^ i
            now = scores(j)
            higher = jnp.maximum(top, jnp.max(now, axis=0, keepdims=True))
            exps = jnp.exp2(now - higher)
            keep = jnp.exp2(top - higher)
            total = total * keep + jnp.sum(exps, axis=0, keepdims=True)
            acc = acc * keep + dot(kv[j, 1, here], exps.astype(BF16), TN)
            return higher, total, acc

        top, total, acc = lax.fori_loop(0, place, earlier, (top, total, acc))
        att_ref[head] = (acc / total).T
        lse_ref[head] = jnp.broadcast_to(top + jnp.log2(total), lse_ref.shape[1:])
        return 0

    lax.fori_loop(0, heads, one_head, 0)


def attend(place, query, kv_blocks):
    heads, tokens, size = query.shape
    count = len(kv_blocks)
    factor = math.log2(math.e) / math.sqrt(size)
    flops = 4 * count * heads * tokens * tokens * size
    return pl.pallas_call(
        functools.partial(attend_kernel, factor, count),
        out_shape=(
            jax.ShapeDtypeStruct((heads, tokens, size), F32),
            jax.ShapeDtypeStruct((heads, 8, tokens), F32),
        ),
        in_specs=[
            pl.BlockSpec(memory_space=pltpu.SMEM),
            pl.BlockSpec(memory_space=pltpu.VMEM),
        ]
        + [pl.BlockSpec(memory_space=pl.ANY)] * count,
        out_specs=(pl.BlockSpec(memory_space=pltpu.VMEM),) * 2,
        scratch_shapes=[
            pltpu.VMEM((count, 2, heads * tokens, size), BF16),
            pltpu.SemaphoreType.DMA((count,)),
        ],
        compiler_params=pltpu.CompilerParams(vmem_limit_bytes=VMEM_LIMIT),
        cost_estimate=pl.CostEstimate(
            flops=flops // 16, bytes_accessed=2**20, transcendentals=0
        ),
        name="attend",
    )(place.reshape(1), query, *kv_blocks)


def attend_back_kernel(factor, scale, count, place_ref, q_ref, do_ref, lse_ref, delta_ref, *refs):
    kv_refs, (dq_ref, dkv_ref, kv, dkv, dq, sems, out_sems) = refs[:count], refs[count:]
    rows = kv.shape[2]
    copies = [
        pltpu.make_async_copy(kv_refs[j].at[:, pl.ds(0, rows)], kv.at[j], sems.at[j])
        for j in range(count)
    ]
    for copy in copies:
        copy.start()
    for copy in copies:
        copy.wait()
    place = place_ref[0]
    heads, tokens, _ = q_ref.shape

    def out_copy(j):
        return pltpu.make_async_copy(dkv.at[j], dkv_ref.at[j], out_sems.at[j])

    def one_block(j, masked):
        def one_head(head, _):
            query, do = q_ref[head], do_ref[head]
            here = pl.ds(pl.multiple_of(head * tokens, tokens), tokens)
            key, value = kv[j, 0, here], kv[j, 1, here]
            scores = dot(key, query, NT) * factor
            probs = jnp.exp2(scores - lse_ref[head, :1])
            if masked:
                key_at = lax.broadcasted_iota(jnp.int32, (tokens, tokens), 0)
                query_at = lax.broadcasted_iota(jnp.int32, (tokens, tokens), 1)
                probs = jnp.where(key_at <= query_at, probs, 0.0)
            dprob = dot(value, do, NT)
            dscore = (probs * (dprob - delta_ref[head, :1])).astype(BF16)
            dkv[j, 0, head] = (dot(dscore, query, NN) * scale).astype(BF16)
            dkv[j, 1, head] = dot(probs.astype(BF16), do, NN).astype(BF16)
            part = dot(key, dscore, TN)
            dq[head] = part if masked else dq[head] + part
            return 0

        lax.fori_loop(0, heads, one_head, 0)
        out_copy(j).start()

    one_block(0, True)

    def earlier(i, _):
        one_block(place ^ i, False)
        return 0

    def later(i, _):
        j = place ^ i
        dkv[j] = jnp.zeros(dkv.shape[1:], BF16)
        out_copy(j).start()
        return 0

    lax.fori_loop(0, place, earlier, 0)
    lax.fori_loop(place + 1, count, later, 0)
    for head in range(heads):
        dq_ref[head] = dq[head].T * scale
    for j in range(count):
        out_copy(j).wait()


def attend_back(place, query, do, lse, delta, kv_blocks):
    heads, tokens, size = query.shape
    count = len(kv_blocks)
    scale = 1.0 / math.sqrt(size)
    factor = math.log2(math.e) * scale
    return pl.pallas_call(
        functools.partial(attend_back_kernel, factor, scale, count),
        out_shape=(
            jax.ShapeDtypeStruct((heads, tokens, size), F32),
            jax.ShapeDtypeStruct((count, 2, heads, tokens, size), BF16),
        ),
        in_specs=[pl.BlockSpec(memory_space=pltpu.SMEM)]
        + [pl.BlockSpec(memory_space=pltpu.VMEM)] * 4
        + [pl.BlockSpec(memory_space=pl.ANY)] * count,
        out_specs=(pl.BlockSpec(memory_space=pltpu.VMEM), pl.BlockSpec(memory_space=pl.ANY)),
        scratch_shapes=[
            pltpu.VMEM((count, 2, heads * tokens, size), BF16),
            pltpu.VMEM((count, 2, heads, tokens, size), BF16),
            pltpu.VMEM((heads, size, tokens), F32),
            pltpu.SemaphoreType.DMA((count,)),
            pltpu.SemaphoreType.DMA((count,)),
        ],
        compiler_params=pltpu.CompilerParams(vmem_limit_bytes=VMEM_LIMIT),
        cost_estimate=pl.CostEstimate(
            flops=count * heads * tokens * tokens * size,
            bytes_accessed=2**20,
            transcendentals=0,
        ),
        name="attend_back",
    )(place.reshape(1), query, do, lse, delta, *kv_blocks)


def swiglu_back(one, two, dact, gate):
    sig = 1.0 / (1.0 + jnp.exp(-one))
    silu = one * sig
    act = silu * two
    prod = act * dact
    dgate = gate * dact
    d_one = (dgate * two * sig * (1.0 + one * (1.0 - sig))).astype(BF16)
    d_two = (dgate * silu).astype(BF16)
    return (gate * act).astype(BF16), d_one, d_two, prod


def experts_kernel(at, group, local, experts, given, first_ref, *refs):
    x_refs, g_refs, refs = refs[:group], refs[group : 2 * group], refs[2 * group :]
    (slot_row, slot_col, w_router, w_in, w_out, w_shared), refs = refs[:6], refs[6 + given :]
    dx_refs, refs = refs[:group], refs[group:]
    kept_refs, refs = refs[:7], refs[7:]
    (xs, gs, first_w, in_w, out_w, shared_w, dxs, left, right, sems, out_sems), stage = refs[:11], refs[11:]
    rows_x, rows_g, act_s, dpair_s, sact_s, sdpair_s, dl_s = stage
    tokens, width = xs.shape[1:]
    capacity, units = act_s.shape[2:]
    wide = local * capacity
    share = sact_s.shape[2]
    third = first_w.shape[0] - 128
    second = third // 2
    padded = w_router.shape[0]
    most = out_w.shape[1]

    loads = [pltpu.make_async_copy(x_refs[b], xs.at[b], sems.at[b]) for b in range(group)]
    fore_loads = [
        pltpu.make_async_copy(
            w_shared.at[c], first_w.at[pl.ds(c * second, share)], sems.at[2 * group + c]
        )
        for c in range(2)
    ]
    loads += [
        pltpu.make_async_copy(g_refs[b], gs.at[b], sems.at[group + b]) for b in range(group)
    ]
    base = 2 * group + 2
    more = [
        [
            pltpu.make_async_copy(
                w_in.at[e, c], in_w.at[e, pl.ds(c * most, units)], sems.at[base + 3 * e + c]
            )
            for c in range(2)
        ]
        + [
            pltpu.make_async_copy(
                w_out.at[e], out_w.at[e, pl.ds(0, units)], sems.at[base + 3 * e + 2]
            )
        ]
        for e in range(local)
    ]
    last = pltpu.make_async_copy(w_shared.at[2], shared_w, sems.at[base + 3 * local])
    for copy in loads[:group] + fore_loads:
        copy.start()
    first_w[third : third + padded] = w_router[...]
    first_w[third + padded :] = jnp.zeros((128 - padded, width), BF16)
    if second > share:
        for c in range(2):
            gap = jnp.zeros((second - share, width), BF16)
            first_w[c * second + share : (c + 1) * second] = gap
    if most > units:
        gap = jnp.zeros((most - units, width), BF16)
        for e in range(local):
            in_w[e, units:most] = gap
            in_w[e, most + units :] = gap
            out_w[e, units:] = gap

    sent = []

    def send(copy):
        copy.start()
        sent.append(copy)

    for copy in loads[:group] + fore_loads:
        copy.wait()
    for copy in loads[group:] + more[0]:
        copy.start()
    x = xs[...].reshape(group * tokens, width)
    fore = dot(x, first_w[...], NT)
    s_one, s_two = fore[:, :share], fore[:, second : second + share]
    s_gate = 1.0 / (1.0 + jnp.exp(-fore[:, third + experts : third + experts + 1]))
    row_at = lax.broadcasted_iota(jnp.int32, (padded, tokens), 0)
    slot_at = lax.broadcasted_iota(jnp.int32, (capacity, tokens), 0)
    probs, change, hits = [], [], []
    for b in range(group):
        logits = fore[b * tokens : (b + 1) * tokens, third:].T[:padded]
        shown = jnp.where(row_at < experts, logits, NEG)
        exps = jnp.exp(shown - jnp.max(shown, axis=0, keepdims=True))
        soft = exps / jnp.sum(exps, axis=0, keepdims=True)
        probs.append(jnp.where(row_at == experts, 1.0 / (1.0 + jnp.exp(-logits)), soft))
        change.append(jnp.zeros((padded, tokens), F32))
        picks = jnp.concatenate(
            [
                jnp.where(slot_at == slot_row[b, e : e + 1, :], 1.0, 0.0).astype(BF16)
                for e in range(local)
            ],
            axis=0,
        )
        rows = dot(picks, xs[b], NN).astype(BF16)
        for e in range(local):
            rows_x[e, b] = rows[e * capacity : (e + 1) * capacity]
        loads[group + b].wait()
        if b == group - 1:
            for e in range(1, local):
                for copy in more[e]:
                    copy.start()
            last.start()
        rows = dot(picks, gs[b], NN).astype(BF16)
        for e in range(local):
            rows_g[e, b] = rows[e * capacity : (e + 1) * capacity]
    def send_all(i, lead):
        for e in range(lead):
            send(
                pltpu.make_async_copy(
                    stage[i].at[e], kept_refs[i].at[e, pl.ds(at, group)], out_sems.at[i, e]
                )
            )

    send_all(0, local)
    send_all(1, local)
    is_expert = row_at < experts
    for e in range(local):
        chosen = row_at == first_ref[0] + e
        gates, owns, hits = [], [], []
        for b in range(group):
            own = jnp.sum(jnp.where(chosen, probs[b], 0.0), axis=0, keepdims=True)
            hit = slot_at == slot_row[b, e : e + 1, :]
            gates.append(jnp.sum(jnp.where(hit, own, 0.0), axis=1, keepdims=True))
            owns.append(own)
            hits.append(hit)
        for copy in more[e]:
            copy.wait()
        pair = dot(rows_x[e].reshape(group * capacity, width), in_w[e], NT)
        dact = dot(rows_g[e].reshape(group * capacity, width), out_w[e], NT)
        act, d_one, d_two, prod = swiglu_back(
            pair[:, :most], pair[:, most:], dact, jnp.concatenate(gates, axis=0)
        )
        act_s[e] = act[:, :units].reshape(group, capacity, units)
        dpair_s[2 * e] = d_one[:, :units].reshape(group, capacity, units)
        dpair_s[2 * e + 1] = d_two[:, :units].reshape(group, capacity, units)
        row_dot = jnp.sum(prod, axis=1, keepdims=True)
        drow = dot(jnp.concatenate([d_one, d_two], axis=1), in_w[e], NN).astype(BF16)
        for b in range(group):
            rows = slice(b * capacity, (b + 1) * capacity)
            found = jnp.sum(jnp.where(hits[b], row_dot[rows], 0.0), axis=0, keepdims=True)
            change[b] += (found * owns[b]) * (
                jnp.where(chosen, 1.0, 0.0) - jnp.where(is_expert, probs[b], 0.0)
            )
            right[b, e * capacity : (e + 1) * capacity] = drow[rows]
    send_all(2, local)
    send_all(3, 2 * local)
    last.wait()
    g = gs[...].reshape(group * tokens, width)
    s_dact = dot(g, shared_w[...], NT)
    act, d_one, d_two, prod = swiglu_back(s_one, s_two, s_dact, s_gate)
    sact_s[...] = act.reshape(group, tokens, share)
    sdpair_s[:, 0] = d_one.reshape(group, tokens, share)
    sdpair_s[:, 1] = d_two.reshape(group, tokens, share)
    dslogit = jnp.sum(prod, axis=1, keepdims=True) * s_gate * (1.0 - s_gate)
    lane_at = lax.broadcasted_iota(jnp.int32, (tokens, 128), 1)
    rest = jnp.zeros((128 - padded, tokens), F32)
    deep = wide + 2 * share
    column_at = lax.broadcasted_iota(jnp.int32, (tokens, capacity), 1)
    stores = []
    for b in range(group):
        rows = slice(b * tokens, (b + 1) * tokens)
        columns = jnp.concatenate([change[b], rest], axis=0).T
        columns = jnp.where(lane_at == experts, dslogit[rows], columns)[:, :padded].astype(BF16)
        dl_s[b] = columns
        left[b, :, deep : deep + padded] = columns
        right[b, deep : deep + padded] = w_router[...]
        for e in range(local):
            picks = jnp.where(column_at == slot_col[b, :, e : e + 1], 1.0, 0.0).astype(BF16)
            left[b, :, e * capacity : (e + 1) * capacity] = picks
        left[b, :, wide : wide + share] = d_one[rows]
        left[b, :, wide + share : wide + 2 * share] = d_two[rows]
        right[b, wide : wide + share] = first_w[:share]
        right[b, wide + share : wide + 2 * share] = first_w[second : second + share]
        dxs[b] = dot(left[b], right[b], NN).astype(BF16)
        send(pltpu.make_async_copy(dxs.at[b], dx_refs[b], out_sems.at[7, b]))
    for i in range(4, 7):
        send(pltpu.make_async_copy(stage[i], kept_refs[i].at[pl.ds(at, group)], out_sems.at[i, 0]))
    for copy in sent:
        copy.wait()


def run_experts(at, experts, first, x_group, g_group, slot_rows, slot_cols, weights, kept):
    given = kept if at else []
    group = len(x_group)
    tokens, width = x_group[0].shape
    w_router, w_in, w_out, w_shared = weights
    local = w_out.shape[0]
    share = w_shared.shape[1]
    padded = w_router.shape[0]
    capacity, units = kept[2].shape[2:]
    any_spec = pl.BlockSpec(memory_space=pl.ANY)
    block = jax.ShapeDtypeStruct((tokens, width), BF16)
    deep = local * capacity + 2 * share + padded
    flops = group * 2 * tokens * width * (local * capacity * 3 + 5 * share) + (
        group * 2 * width * local * capacity * units * 5
    )
    step = at // group
    wide_units = -(-units // 128) * 128
    fore = 2 * (-(-share // 64) * 64) + 128
    results = pl.pallas_call(
        functools.partial(experts_kernel, at, group, local, experts, len(given)),
        grid=(1,),
        out_shape=(block,) * group + tuple(jax.ShapeDtypeStruct(k.shape, k.dtype) for k in kept),
        in_specs=[pl.BlockSpec(memory_space=pltpu.SMEM)]
        + [any_spec] * (2 * group)
        + [
            pl.BlockSpec((group, local, tokens), lambda i: (step, 0, 0)),
            pl.BlockSpec((group, tokens, local), lambda i: (step, 0, 0)),
            pl.BlockSpec((padded, width), lambda i: (0, 0)),
        ]
        + [any_spec] * (3 + len(given)),
        out_specs=(any_spec,) * (group + len(kept)),
        input_output_aliases={7 + 2 * group + i: group + i for i in range(len(given))},
        scratch_shapes=[
            pltpu.VMEM((group, tokens, width), BF16),
            pltpu.VMEM((group, tokens, width), BF16),
            pltpu.VMEM((fore, width), BF16),
            pltpu.VMEM((local, 2 * wide_units, width), BF16),
            pltpu.VMEM((local, wide_units, width), BF16),
            pltpu.VMEM((share, width), BF16),
            pltpu.VMEM((group, tokens, width), BF16),
            pltpu.VMEM((group, tokens, deep), BF16),
            pltpu.VMEM((group, deep, width), BF16),
            pltpu.SemaphoreType.DMA((2 * group + 3 + 3 * local,)),
            pltpu.SemaphoreType.DMA((8, max(2 * local, group))),
        ]
        + [
            pltpu.VMEM(k.shape[:1] + (group,) + k.shape[2:], BF16) for k in kept[:4]
        ]
        + [pltpu.VMEM((group,) + k.shape[1:], BF16) for k in kept[4:]],
        compiler_params=pltpu.CompilerParams(vmem_limit_bytes=VMEM_LIMIT),
        cost_estimate=pl.CostEstimate(flops=flops // 16, bytes_accessed=2**20, transcendentals=0),
        name="run_experts",
    )(first.reshape(1), *x_group, *g_group, slot_rows, slot_cols, *weights, *given)
    return results[:group], results[group:]


def outputs_kernel(group, count, local, act, slot_col, sact, w_out, w_shared, *refs):
    out_refs, (outs, left, right, sems) = refs[:count], refs[count:]
    step = pl.program_id(0)
    slot = lax.rem(step, 2)
    capacity, units = act.shape[2:]
    tokens, share = sact.shape[1:]
    wide = local * capacity

    def store(at, b, into):
        return pltpu.make_async_copy(outs.at[into, b], out_refs[at * group + b], sems.at[into, b])

    @pl.when(step >= 2)
    def _():
        for b in range(group):
            store(0, b, slot).wait()

    for e in range(local):
        rows = dot(act[e].reshape(group * capacity, units), w_out[e], NN).astype(BF16)
        for b in range(group):
            right[b, e * capacity : (e + 1) * capacity] = rows[b * capacity : (b + 1) * capacity]
    slot_at = lax.broadcasted_iota(jnp.int32, (tokens, capacity), 1)
    for b in range(group):
        for e in range(local):
            picks = jnp.where(slot_at == slot_col[b, :, e : e + 1], 1.0, 0.0).astype(BF16)
            left[b, :, e * capacity : (e + 1) * capacity] = picks
        left[b, :, wide : wide + share] = sact[b]
        right[b, wide : wide + share] = w_shared[0]
        outs[slot, b] = dot(left[b], right[b], NN).astype(BF16)
    for at in range(count // group):

        @pl.when(step == at)
        def _():
            for b in range(group):
                store(at, b, at % 2).start()

    @pl.when(step == count // group - 1)
    def _():
        for b in range(group):
            for into in range(2):
                store(0, b, into).wait()


def expert_grads_kernel(rows_x, rows_g, act, dpair, in_ref, out_ref):
    rows = rows_x.shape[1] * rows_x.shape[2]
    x = rows_x[0].reshape(rows, -1)
    for c in range(2):
        in_ref[0, c] = dot(dpair[c].reshape(rows, -1), x, TN)
    out_ref[0] = dot(act[0].reshape(rows, -1), rows_g[0].reshape(rows, -1), TN)


def grads_of_experts(rows_x, rows_g, act, dpair):
    local, count, capacity, width = rows_x.shape
    units = act.shape[3]
    tile = min(width, 1024)
    return pl.pallas_call(
        expert_grads_kernel,
        grid=(local, width // tile),
        out_shape=(
            jax.ShapeDtypeStruct((local, 2, units, width), F32),
            jax.ShapeDtypeStruct((local, units, width), F32),
        ),
        in_specs=[
            pl.BlockSpec((1, count, capacity, tile), lambda e, i: (e, 0, 0, i)),
            pl.BlockSpec((1, count, capacity, tile), lambda e, i: (e, 0, 0, i)),
            pl.BlockSpec((1, count, capacity, units), lambda e, i: (e, 0, 0, 0)),
            pl.BlockSpec((2, count, capacity, units), lambda e, i: (e, 0, 0, 0)),
        ],
        out_specs=(
            pl.BlockSpec((1, 2, units, tile), lambda e, i: (e, 0, 0, i)),
            pl.BlockSpec((1, units, tile), lambda e, i: (e, 0, i)),
        ),
        compiler_params=pltpu.CompilerParams(vmem_limit_bytes=VMEM_LIMIT),
        cost_estimate=pl.CostEstimate(flops=0, bytes_accessed=2**20, transcendentals=0),
        name="grads_of_experts",
    )(rows_x, rows_g, act, dpair)


def run_outputs(act, slot_cols, sact, w_out, w_shared):
    local, count, capacity, units = act.shape
    tokens, share = sact.shape[1:]
    width = w_out.shape[2]
    group = 2
    deep = local * capacity + share
    return pl.pallas_call(
        functools.partial(outputs_kernel, group, count, local),
        grid=(count // group,),
        out_shape=(jax.ShapeDtypeStruct((tokens, width), BF16),) * count,
        in_specs=[
            pl.BlockSpec((local, group, capacity, units), lambda i: (0, i, 0, 0)),
            pl.BlockSpec((group, tokens, local), lambda i: (i, 0, 0)),
            pl.BlockSpec((group, tokens, share), lambda i: (i, 0, 0)),
            pl.BlockSpec((local, units, width), lambda i: (0, 0, 0)),
            pl.BlockSpec((1, share, width), lambda i: (2, 0, 0)),
        ],
        out_specs=(pl.BlockSpec(memory_space=pl.ANY),) * count,
        scratch_shapes=[
            pltpu.VMEM((2, group, tokens, width), BF16),
            pltpu.VMEM((group, tokens, deep), BF16),
            pltpu.VMEM((group, deep, width), BF16),
            pltpu.SemaphoreType.DMA((2, group)),
        ],
        compiler_params=pltpu.CompilerParams(vmem_limit_bytes=VMEM_LIMIT),
        cost_estimate=pl.CostEstimate(
            flops=count * width // 8 * (local * capacity * (units + tokens) + tokens * share),
            bytes_accessed=2**20,
            transcendentals=0,
        ),
        name="run_outputs",
    )(act, slot_cols, sact, w_out, w_shared)


def assemble_kernel(plan, count, place_ref, *refs):
    block_refs, refs = refs[:count], refs[count:]
    out_refs, (low, wide, in_sems, out_sems) = refs[:-4], refs[-4:]
    place = place_ref[0]

    def load(j):
        return pltpu.make_async_copy(block_refs[j], low.at[j % 2], in_sems.at[j % 2])

    def stores(j):
        return [
            pltpu.make_async_copy(
                wide.at[j % 2, pl.ds(first, rows)],
                out_refs[which].at[
                    pl.ds(pl.multiple_of(base + (place ^ j) * rows, 8), rows),
                    pl.ds(column, wide.shape[2]),
                ],
                out_sems.at[j % 2, i],
            )
            for i, (which, first, rows, base, column) in enumerate(plan)
        ]

    load(0).start()
    for j in range(count):
        if j + 1 < count:
            load(j + 1).start()
        load(j).wait()
        if j >= 2:
            for copy in stores(j - 2):
                copy.wait()
        wide[j % 2] = low[j % 2].astype(F32)
        for copy in stores(j):
            copy.start()
    for j in range(max(0, count - 2), count):
        for copy in stores(j):
            copy.wait()


def assemble(place, blocks, shapes, plan):
    count = len(blocks)
    rows, width = blocks[0].shape
    any_spec = pl.BlockSpec(memory_space=pl.ANY)
    return pl.pallas_call(
        functools.partial(assemble_kernel, plan, count),
        out_shape=[jax.ShapeDtypeStruct(shape, F32) for shape in shapes],
        in_specs=[pl.BlockSpec(memory_space=pltpu.SMEM)] + [any_spec] * count,
        out_specs=[any_spec] * len(shapes),
        scratch_shapes=[
            pltpu.VMEM((2, rows, width), BF16),
            pltpu.VMEM((2, rows, width), F32),
            pltpu.SemaphoreType.DMA((2,)),
            pltpu.SemaphoreType.DMA((2, len(plan))),
        ],
        compiler_params=pltpu.CompilerParams(vmem_limit_bytes=VMEM_LIMIT),
        cost_estimate=pl.CostEstimate(flops=0, bytes_accessed=2**20, transcendentals=0),
        name="assemble",
    )(place.reshape(1), *blocks)


def shared_grads_kernel(count, *refs):
    x_refs, g_refs, refs = refs[:count], refs[count : 2 * count], refs[2 * count :]
    (sact, sdpair, dl, grads_ref, router_ref, xs, gs, grads, router, sems) = refs
    at = pl.program_id(0)
    slot = lax.rem(at, 2)

    def load(j, into):
        return (
            pltpu.make_async_copy(x_refs[j], xs.at[into], sems.at[0, into]),
            pltpu.make_async_copy(g_refs[j], gs.at[into], sems.at[1, into]),
        )

    @pl.when(at == 0)
    def _():
        for copy in load(0, 0):
            copy.start()
        grads[...] = jnp.zeros_like(grads)
        router[...] = jnp.zeros_like(router)

    for j in range(1, count):

        @pl.when(at == j - 1)
        def _():
            for copy in load(j, j % 2):
                copy.start()

    for copy in load(0, slot):
        copy.wait()
    x, g = xs[slot], gs[slot]
    grads[0] += dot(sdpair[0, 0], x, TN)
    grads[1] += dot(sdpair[0, 1], x, TN)
    grads[2] += dot(sact[0], g, TN)
    router[...] += dot(dl[0], x, TN)

    @pl.when(at == count - 1)
    def _():
        grads_ref[...] = grads[...].astype(BF16)
        router_ref[...] = router[...]


def shared_grads(x_blocks, g_blocks, sact, sdpair, dl):
    count = len(x_blocks)
    tokens, width = x_blocks[0].shape
    share, padded = sact.shape[2], dl.shape[2]
    any_spec = pl.BlockSpec(memory_space=pl.ANY)
    return pl.pallas_call(
        functools.partial(shared_grads_kernel, count),
        grid=(count,),
        out_shape=(
            jax.ShapeDtypeStruct((3, share, width), BF16),
            jax.ShapeDtypeStruct((padded, width), F32),
        ),
        in_specs=[any_spec] * (2 * count)
        + [
            pl.BlockSpec((1, tokens, share), lambda j: (j, 0, 0)),
            pl.BlockSpec((1, 2, tokens, share), lambda j: (j, 0, 0, 0)),
            pl.BlockSpec((1, tokens, padded), lambda j: (j, 0, 0)),
        ],
        out_specs=(
            pl.BlockSpec((3, share, width), lambda j: (0, 0, 0)),
            pl.BlockSpec((padded, width), lambda j: (0, 0)),
        ),
        scratch_shapes=[
            pltpu.VMEM((2, tokens, width), BF16),
            pltpu.VMEM((2, tokens, width), BF16),
            pltpu.VMEM((3, share, width), F32),
            pltpu.VMEM((padded, width), F32),
            pltpu.SemaphoreType.DMA((2, 2)),
        ],
        compiler_params=pltpu.CompilerParams(vmem_limit_bytes=VMEM_LIMIT),
        cost_estimate=pl.CostEstimate(
            flops=count * tokens * width * share,
            bytes_accessed=2**20,
            transcendentals=0,
        ),
        name="shared_grads",
    )(*x_blocks, *g_blocks, sact, sdpair, dl)


def on_device(
    hidden_in,
    cotangent,
    gain_attn,
    qkv_weight,
    qkv_bias,
    out_weight,
    gain_ffn,
    router_weight,
    routes,
    shared_gate,
    shared_in,
    shared_out,
    expert_in,
    expert_out,
):
    tokens, width = hidden_in.shape
    ctx_count = lax.axis_size("ctx")
    heads_local = qkv_weight.shape[2] // HD
    local = expert_in.shape[0]
    experts = local * ctx_count
    top_count = routes.shape[1]
    capacity = 3 * tokens * top_count // (2 * experts)
    place = lax.axis_index("ctx")
    order = jnp.arange(ctx_count, dtype=jnp.int32) ^ place
    score_scale = 1.0 / math.sqrt(HD)
    query_pos = place * tokens + jnp.arange(tokens, dtype=jnp.int32)
    cosine, sine = rotary_tables(query_pos, HD)

    x_full = hidden_in.astype(F32)
    inv_one = lax.rsqrt(jnp.mean(x_full * x_full, axis=-1, keepdims=True) + EPS)
    normed_one = x_full * inv_one
    x_one = (normed_one * gain_attn).astype(BF16)
    projected = (
        jnp.einsum("td,dcf->ctf", x_one, qkv_weight, preferred_element_type=F32)
        + qkv_bias[:, None]
    )
    shaped = projected.reshape(3, tokens, heads_local, HD).transpose(0, 2, 1, 3)
    query = rotate(shaped[0], cosine, sine).astype(BF16)
    key_local = rotate(shaped[1], cosine, sine).astype(BF16)
    value_local = shaped[2].astype(BF16)
    kv_rows = heads_local * tokens
    route_rows = -(-tokens * top_count // HD)
    behind = jnp.pad(
        routes.T.astype(BF16).reshape(route_rows, HD), ((0, -route_rows % 16), (0, 0))
    )
    kv_local = jnp.stack(
        [
            jnp.concatenate([key_local.reshape(kv_rows, HD), behind], axis=0),
            jnp.concatenate([value_local.reshape(kv_rows, HD), behind], axis=0),
        ]
    )
    kv_got = gather_start(kv_local)
    kv_blocks = gather_end(kv_got)
    g_got = gather_start(after(cotangent, kv_blocks[6 % ctx_count]))

    share = shared_out.shape[0] // ctx_count
    piece = shared_out.shape[1]
    shared_send = jnp.concatenate(
        [
            shared_in.transpose(1, 2, 0).reshape(2, ctx_count, share, piece),
            shared_out.reshape(1, ctx_count, share, piece),
        ],
        axis=0,
    ).transpose(1, 0, 2, 3)
    shared_w = (
        lax.all_to_all(shared_send, "ctx", split_axis=0, concat_axis=0, tiled=True)
        .transpose(1, 2, 0, 3)
        .reshape(3, share, width)
    )
    whole_share = -(-share // 16) * 16
    if whole_share > share:
        shared_w = jnp.pad(shared_w, ((0, 0), (0, whole_share - share), (0, 0)))
    half_rows = out_weight.shape[0] // 2
    core = place % 2
    out_mine = lax.all_gather(
        lax.dynamic_slice_in_dim(out_weight, core * half_rows, half_rows, 0), "tp", axis=0, tiled=True
    )

    routes_all = jnp.stack([b[0, kv_rows : kv_rows + route_rows] for b in kv_blocks])
    routes_all = routes_all.reshape(ctx_count, 1, top_count, tokens)
    own_experts = (place * local + jnp.arange(local, dtype=jnp.int32)).astype(BF16)
    hit = jnp.any(routes_all == own_experts[None, :, None, None], axis=2)
    token_at = jnp.arange(tokens, dtype=jnp.int32)
    earlier = (token_at[:, None] <= token_at[None, :]).astype(BF16)
    rank = dot(hit.astype(BF16).reshape(-1, tokens), earlier, NN).reshape(hit.shape) - 1.0
    slot_rows = jnp.where(hit, rank, -1.0).astype(jnp.int32)
    slot_cols = slot_rows.transpose(0, 2, 1)
    padded = -(-(experts + 1) // 8) * 8
    w_router = jnp.concatenate(
        [
            router_weight.T,
            shared_gate[None],
            jnp.zeros((padded - experts - 1, width), BF16),
        ],
        axis=0,
    )
    w_in = expert_in.transpose(0, 2, 3, 1)

    attended, lse = attend(place, query, kv_blocks)
    att = attended.astype(BF16).transpose(1, 0, 2).reshape(tokens, heads_local * HD)
    out_other = swap(after(out_mine, attended), 1)
    tp_count = lax.axis_size("tp")
    att_all = gather_tp(att)
    where_to = jnp.arange(tp_count, dtype=jnp.int32) ^ lax.axis_index("tp")
    att_all = jnp.stack(att_all)[where_to]
    att_low = jnp.concatenate([a[:, :half_rows] for a in att_all], axis=1)
    att_high = jnp.concatenate([a[:, half_rows:] for a in att_all], axis=1)
    out_low = jnp.where(core == 0, out_mine, out_other)
    out_high = jnp.where(core == 0, out_other, out_mine)
    att_cat = jnp.concatenate([att_low, att_high], axis=1)
    g_blocks = gather_end(g_got)
    if ctx_count == 8:
        att_cat = after(att_cat, g_blocks[2], g_blocks[4])
    hidden = x_full + dot(
        att_cat,
        jnp.concatenate([out_low, out_high], axis=0),
        NN,
    )
    inv_two = lax.rsqrt(jnp.mean(hidden * hidden, axis=-1, keepdims=True) + EPS)
    normed_two = hidden * inv_two
    x_two = (normed_two * gain_ffn).astype(BF16)

    units, group = expert_out.shape[1], 2
    kept = [
        jax.ShapeDtypeStruct(shape, BF16)
        for shape in (
            (local, ctx_count, capacity, width),
            (local, ctx_count, capacity, width),
            (local, ctx_count, capacity, units),
            (2 * local, ctx_count, capacity, units),
            (ctx_count, tokens, whole_share),
            (ctx_count, 2, tokens, whole_share),
            (ctx_count, tokens, padded),
        )
    ]
    weights = (w_router, w_in, expert_out, shared_w)
    got = gather_start(x_two)
    x_blocks = [got[0], got[1]]
    if ctx_count == 8:
        x_blocks[1] = after(got[1], g_blocks[6])
    dxs = []
    early = None
    for at in range(0, ctx_count, group):
        if at == 4 and ctx_count == 8:
            pair_two = pair_sum(dxs, 2)
            early = (pair_two, pair_two[: tokens // 2].astype(BF16))
        if at == 6 and ctx_count == 8:
            x_blocks[6] = after(x_blocks[6], early[1])
        dx, kept = run_experts(
            at,
            experts,
            place * local,
            x_blocks[at : at + group],
            g_blocks[at : at + group],
            slot_rows,
            slot_cols,
            weights,
            kept,
        )
        dxs += dx
        if at == 0:
            x_blocks = x_blocks[:2] + gather_end(got, dx[0])[2:]
    grad_x_part = scatter_ctx(dxs, early)
    outs = run_outputs(kept[2], slot_cols, kept[4], expert_out, shared_w)
    grad_x_low = grad_x_part.astype(BF16)
    kept = after(kept, grad_x_low, outs[0])
    rows_x, rows_g, act_low, dpair, s_act, s_dpair, low_logits = kept
    expert_grads = grads_of_experts(rows_x, rows_g, act_low, dpair)
    grad_expert_in, grad_expert_out = expert_grads
    shared_low, router_part = shared_grads(x_blocks, g_blocks, s_act, s_dpair, low_logits)
    gain_ffn_part = jnp.sum(grad_x_part * normed_two, axis=0)
    small = sum_tp_small(jnp.concatenate([router_part, gain_ffn_part[None]], axis=0))
    out_part = scatter_ctx(after(outs, grad_x_low))
    summed, _ = sum_tp(grad_x_low)
    summed = after(summed, shared_low, small, *expert_grads, out_part)
    shared_back = lax.all_to_all(
        shared_low[:, :share].reshape(3, share, ctx_count, piece).transpose(2, 0, 1, 3),
        "ctx",
        split_axis=0,
        concat_axis=0,
        tiled=True,
    ).astype(F32)
    grad_shared_in = shared_back[:, :2].transpose(3, 1, 0, 2).reshape(shared_in.shape)
    grad_shared_out = shared_back[:, 2].reshape(shared_out.shape)

    summed = summed.astype(F32)
    grad_y = cotangent.astype(F32)
    grad_normed_two = summed * gain_ffn
    grad_hidden = grad_y + inv_two * (
        grad_normed_two
        - normed_two * jnp.mean(grad_normed_two * normed_two, axis=-1, keepdims=True)
    )
    grad_hidden_low = grad_hidden.astype(BF16)
    out_weight_part = dot(att, grad_hidden_low, (((0,), (0,)), ((), ())))
    grad_att = (
        dot(grad_hidden_low, out_weight, (((1,), (1,)), ((), ())))
        .astype(BF16)
        .reshape(tokens, heads_local, HD)
        .transpose(1, 0, 2)
    )
    delta = jnp.sum(grad_att.astype(F32) * attended, axis=-1)
    delta = jnp.broadcast_to(delta[:, None], lse.shape)
    grad_query, grad_pairs = attend_back(place, query, grad_att, lse, delta, kv_blocks)
    ffn_low, _ = sum_tp(out_part, grad_query)
    grad_kv = scatter_ctx([grad_pairs[j] for j in range(ctx_count)])
    grad_kv = after(grad_kv, ffn_low)
    def raw_part(value):
        return value.astype(BF16).transpose(1, 0, 2).reshape(tokens, heads_local * HD)

    raw = [
        raw_part(rotate(grad_query, cosine, -sine)),
        raw_part(rotate(grad_kv[0], cosine, -sine)),
        raw_part(grad_kv[1]),
    ]
    grad_x_one_part = jnp.einsum(
        "tcf,dcf->td", jnp.stack(raw, axis=1), qkv_weight, preferred_element_type=F32
    )
    grad_x_one, half_way = sum_tp(grad_x_one_part)
    gain_attn_part = jnp.sum(grad_x_one_part * normed_one, axis=0)
    gain_sum = sum_tp_small(gain_attn_part[None])
    head_width = heads_local * HD
    gain_rows = width // head_width
    ends = jnp.concatenate(
        [jnp.sum(r.astype(F32), axis=0)[None] for r in raw]
        + [gain_sum.reshape(gain_rows, -1), small.reshape((padded + 1) * gain_rows, -1)],
        axis=0,
    )
    ends = jnp.pad(ends, ((0, -ends.shape[0] % (16 * ctx_count)), (0, 0))).astype(BF16)
    query_part = after(dot(x_one, raw[0], TN).astype(BF16), grad_kv)
    pair_part = jnp.concatenate([dot(x_one, raw[1], TN), dot(x_one, raw[2], TN)], axis=0).astype(BF16)
    turns = width // head_width
    out_shards = [
        jnp.concatenate([s[:, k * head_width : (k + 1) * head_width] for k in range(turns)], axis=0)
        for s in shards(out_weight_part.astype(BF16))
    ]
    sums = sum_ctx(
        [
            jnp.concatenate(list(parts), axis=0)
            for parts in zip(shards(query_part), shards(pair_part), out_shards, shards(ends))
        ],
        half_way,
    )
    q_rows = width // ctx_count
    out_rows = out_weight.shape[0] // ctx_count
    plan = [(0, 0, q_rows, 0, 0), (0, q_rows, 2 * q_rows, width, 0)] + [
        (1, 3 * q_rows + k * out_rows, out_rows, 0, k * head_width) for k in range(turns)
    ]
    qkv_grad, out_weight_grad = assemble(
        place, sums, [(3 * width, head_width), out_weight.shape], plan
    )
    qkv_grad = qkv_grad.reshape(3, width, head_width).transpose(1, 0, 2)
    ends = relative(jnp.stack([b[3 * q_rows + turns * out_rows :] for b in sums]))
    ends = ends.reshape(-1, head_width).astype(F32)
    small = ends[3 + gain_rows : 3 + (padded + 2) * gain_rows].reshape(padded + 1, width)
    grad_x_one = after(grad_x_one, sums[2]).astype(F32)
    grad_normed_one = grad_x_one * gain_attn
    grad_input = grad_hidden + inv_one * (
        grad_normed_one
        - normed_one * jnp.mean(grad_normed_one * normed_one, axis=-1, keepdims=True)
    )
    block_out = (hidden + ffn_low.astype(F32)).astype(BF16)
    return (
        block_out,
        grad_input,
        ends[3 : 3 + gain_rows].reshape(-1),
        qkv_grad,
        ends[:3],
        out_weight_grad,
        small[padded],
        small[:experts].T,
        small[experts],
        grad_shared_in,
        grad_shared_out,
        grad_expert_in.transpose(0, 3, 1, 2),
        grad_expert_out,
    )


def solution(mesh):
    return jax.shard_map(
        on_device,
        mesh=mesh,
        in_specs=(
            P("ctx", None),
            P("ctx", None),
            P(),
            P(None, None, "tp"),
            P(None, "tp"),
            P("tp", None),
            P(),
            P(),
            P("ctx", None),
            P(),
            P("ctx", None, "tp"),
            P("tp", "ctx"),
            P("ctx", None, None, "tp"),
            P("ctx", "tp", None),
        ),
        out_specs=(
            P("ctx", None),
            P("ctx", None),
            P(),
            P(None, None, "tp"),
            P(None, "tp"),
            P("tp", None),
            P(),
            P(),
            P(),
            P("ctx", None, "tp"),
            P("tp", "ctx"),
            P("ctx", None, None, "tp"),
            P("ctx", "tp", None),
        ),
        check_vma=False,
    )
```

```python
import functools
import math

import jax
import jax.numpy as jnp
from jax import lax
from jax.experimental import pallas as pl
from jax.experimental.pallas import tpu as pltpu
from jax.sharding import PartitionSpec as P

HD = 128
EPS = 1e-06
THETA = 1000000.0
NEG = -1e30
F32 = jnp.float32
BF16 = jnp.bfloat16


def rotary_tables(positions, width):
    half_width = width // 2
    freqs = THETA ** (-(jnp.arange(half_width, dtype=F32) * 2.0) / width)
    angles = positions.astype(F32)[:, None] * freqs[None, :]
    return (jnp.cos(angles), jnp.sin(angles))


def rotate(values, cosine, sine):
    half_width = values.shape[-1] // 2
    first, second = values[..., :half_width], values[..., half_width:]
    return jnp.concatenate(
        [first * cosine - second * sine, second * cosine + first * sine], axis=-1
    )


def dot(a, b, dims):
    return lax.dot_general(a, b, dims, preferred_element_type=F32)


def swap(value, bits):
    count = lax.axis_size("ctx")
    return lax.ppermute(value, "ctx", [(i, i ^ bits) for i in range(count)])


def relative(natural):
    count = natural.shape[0]
    order = jnp.arange(count, dtype=jnp.int32) ^ lax.axis_index("ctx")
    return natural[order]


def nothing_kernel(*refs):
    pass


def after(values, *others):
    single = not isinstance(values, (list, tuple))
    values = [values] if single else list(values)
    any_spec = pl.BlockSpec(memory_space=pl.ANY)
    results = pl.pallas_call(
        nothing_kernel,
        out_shape=[jax.ShapeDtypeStruct(v.shape, v.dtype) for v in values],
        in_specs=[any_spec] * (len(values) + len(others)),
        out_specs=[any_spec] * len(values),
        input_output_aliases={i: i for i in range(len(values))},
        name="after",
    )(*values, *others)
    return results[0] if single else results


def gather_start(own):
    if lax.axis_size("ctx") != 8:
        return relative(lax.all_gather(own, "ctx", axis=0))
    return [own, swap(own, 1), swap(own, 2), swap(own, 4)]


def gather_end(got, *others):
    if lax.axis_size("ctx") != 8:
        return [got[j] for j in range(lax.axis_size("ctx"))]
    own, b1, b2, b4 = got
    if others:
        b2, b4 = after((b2, b4), *others)
    half = own.shape[0] // 2
    via_x, via_y = swap(b4[:half], 2), swap(b2[half:], 4)
    b3, b5 = swap(b2, 1), swap(b4, 1)
    b6 = jnp.concatenate([via_x, via_y], axis=0)
    return [own, b1, b2, b3, b4, b5, b6, swap(b6, 1)]


def gather_ctx(own, *others):
    return gather_end(gather_start(own), *others)


def pair_sum(parts, j):
    return parts[j].astype(F32) + swap(parts[j ^ 1], 1).astype(F32)


def scatter_ctx(parts, early=None):
    return scatter_end(scatter_start(parts, early))


def scatter_start(parts, early=None):
    if lax.axis_size("ctx") != 8:
        return [jnp.stack(parts)], None
    half = parts[0].shape[0] // 2
    pair = {j: pair_sum(parts, j) for j in (2, 4, 6, 0) if j != 2 or early is None}
    if early is None:
        early = (pair[2], pair[2][:half].astype(BF16))
    q6 = pair[6].astype(BF16)
    hops = [early[1], pair[4][half:].astype(BF16), q6[:half], q6[half:]]
    return hops, (early[0], pair[4], pair[0])


def scatter_end(started, *others):
    hops, stay = started
    if lax.axis_size("ctx") != 8:
        natural = relative(hops[0])
        flat = natural.reshape((-1,) + natural.shape[2:])
        return lax.psum_scatter(flat, "ctx", scatter_dimension=0, tiled=True).astype(F32)
    two, four, zero = stay
    half = two.shape[0] // 2
    r2, r4 = swap(hops[0], 2), swap(hops[1], 4)
    via_x, via_y = swap(hops[2], 2), swap(hops[3], 4)
    r4a = (four[:half] + via_x.astype(F32)).astype(BF16)
    r2b = (two[half:] + via_y.astype(F32)).astype(BF16)
    if others:
        r4a, r2b = after((r4a, r2b), *others)
    r4a, r2b = swap(r4a, 4), swap(r2b, 2)
    low = r2.astype(F32) + r4a.astype(F32)
    high = r2b.astype(F32) + r4.astype(F32)
    return zero + jnp.concatenate([low, high], axis=0)


def sum_ctx(parts, *others):
    return gather_ctx(scatter_end(scatter_start(parts), *others).astype(BF16))


def shards(value):
    count = lax.axis_size("ctx")
    rows = value.shape[0] // count
    place = lax.axis_index("ctx")
    return [lax.dynamic_slice_in_dim(value, (place ^ j) * rows, rows, 0) for j in range(count)]


def gather_tp(own):
    count = lax.axis_size("tp")
    return [own] + [
        lax.ppermute(own, "tp", [(i, i ^ k) for i in range(count)]) for k in range(1, count)
    ]


NT = (((1,), (1,)), ((), ()))
NN = (((1,), (0,)), ((), ()))
TN = (((0,), (0,)), ((), ()))
VMEM_LIMIT = 60 * 1024 * 1024


def sum_tp_start(value):
    pieces = value.astype(BF16).reshape(lax.axis_size("tp"), -1, value.shape[1])
    got = lax.all_to_all(pieces, "tp", split_axis=0, concat_axis=0, tiled=True)
    return jnp.sum(got.astype(F32), axis=0).astype(BF16)


def sum_tp_end(total):
    count, at = lax.axis_size("tp"), lax.axis_index("tp")
    blocks = jnp.stack(gather_tp(total))
    blocks = blocks[jnp.arange(count, dtype=jnp.int32) ^ at]
    return blocks.reshape(-1, total.shape[1])


def sum_tp_small(value):
    count, bits = lax.axis_size("tp"), 1
    while bits < count:
        value = value + lax.ppermute(value, "tp", [(i, i ^ bits) for i in range(count)])
        bits *= 2
    return value


def arrange_kernel(places, mine, other, out, sems):
    core, at = lax.rem(places[0], 2), places[1]
    copies = []
    for k in range(out.shape[0]):
        for i, (ref, half) in enumerate(((mine, core), (other, 1 - core))):
            copies.append(pltpu.make_async_copy(ref.at[at ^ k], out.at[k, half], sems.at[k, i]))
    for copy in copies:
        copy.start()
    for copy in copies:
        copy.wait()


def arrange(place, mine, other):
    count, rows, width = mine.shape
    any_spec = pl.BlockSpec(memory_space=pl.ANY)
    return pl.pallas_call(
        arrange_kernel,
        out_shape=jax.ShapeDtypeStruct((count, 2, rows, width), mine.dtype),
        in_specs=[pl.BlockSpec(memory_space=pltpu.SMEM), any_spec, any_spec],
        out_specs=any_spec,
        scratch_shapes=[pltpu.SemaphoreType.DMA((count, 2))],
        cost_estimate=pl.CostEstimate(flops=0, bytes_accessed=2**20, transcendentals=0),
        name="arrange",
    )(jnp.stack([place, lax.axis_index("tp")]), mine, other).reshape(-1, width)


def attend_kernel(factor, count, place_ref, q_ref, *refs):
    kv_refs, (att_ref, lse_ref, kv, sems) = refs[:count], refs[count:]
    rows = kv.shape[2]
    copies = [
        pltpu.make_async_copy(kv_refs[j].at[:, pl.ds(0, rows)], kv.at[j], sems.at[j])
        for j in range(count)
    ]
    for copy in copies:
        copy.start()
    for copy in copies:
        copy.wait()
    place = place_ref[0]
    heads, tokens, _ = q_ref.shape

    def one_head(head, _):
        query = q_ref[head]
        here = pl.ds(pl.multiple_of(head * tokens, tokens), tokens)

        def scores(j):
            return dot(kv[j, 0, here], query, NT) * factor

        key_at = lax.broadcasted_iota(jnp.int32, (tokens, tokens), 0)
        query_at = lax.broadcasted_iota(jnp.int32, (tokens, tokens), 1)
        first = jnp.where(key_at <= query_at, scores(0), NEG)
        top = jnp.max(first, axis=0, keepdims=True)
        exps = jnp.exp2(first - top)
        total = jnp.sum(exps, axis=0, keepdims=True)
        acc = dot(kv[0, 1, here], exps.astype(BF16), TN)

        def earlier(i, carry):
            top, total, acc = carry
            j = place ^ i
            now = scores(j)
            higher = jnp.maximum(top, jnp.max(now, axis=0, keepdims=True))
            exps = jnp.exp2(now - higher)
            keep = jnp.exp2(top - higher)
            total = total * keep + jnp.sum(exps, axis=0, keepdims=True)
            acc = acc * keep + dot(kv[j, 1, here], exps.astype(BF16), TN)
            return higher, total, acc

        top, total, acc = lax.fori_loop(0, place, earlier, (top, total, acc))
        att_ref[head] = (acc / total).T
        lse_ref[head] = jnp.broadcast_to(top + jnp.log2(total), lse_ref.shape[1:])
        return 0

    lax.fori_loop(0, heads, one_head, 0)


def attend(place, query, kv_blocks):
    heads, tokens, size = query.shape
    count = len(kv_blocks)
    factor = math.log2(math.e) / math.sqrt(size)
    flops = 4 * count * heads * tokens * tokens * size
    return pl.pallas_call(
        functools.partial(attend_kernel, factor, count),
        out_shape=(
            jax.ShapeDtypeStruct((heads, tokens, size), F32),
            jax.ShapeDtypeStruct((heads, 8, tokens), F32),
        ),
        in_specs=[
            pl.BlockSpec(memory_space=pltpu.SMEM),
            pl.BlockSpec(memory_space=pltpu.VMEM),
        ]
        + [pl.BlockSpec(memory_space=pl.ANY)] * count,
        out_specs=(pl.BlockSpec(memory_space=pltpu.VMEM),) * 2,
        scratch_shapes=[
            pltpu.VMEM((count, 2, heads * tokens, size), BF16),
            pltpu.SemaphoreType.DMA((count,)),
        ],
        compiler_params=pltpu.CompilerParams(vmem_limit_bytes=VMEM_LIMIT),
        cost_estimate=pl.CostEstimate(
            flops=flops // 16, bytes_accessed=2**20, transcendentals=0
        ),
        name="attend",
    )(place.reshape(1), query, *kv_blocks)


def attend_back_kernel(factor, scale, count, place_ref, q_ref, do_ref, lse_ref, delta_ref, *refs):
    kv_refs, (dq_ref, dkv_ref, kv, dkv, dq, sems, out_sems) = refs[:count], refs[count:]
    rows = kv.shape[2]
    copies = [
        pltpu.make_async_copy(kv_refs[j].at[:, pl.ds(0, rows)], kv.at[j], sems.at[j])
        for j in range(count)
    ]
    for copy in copies:
        copy.start()
    for copy in copies:
        copy.wait()
    place = place_ref[0]
    heads, tokens, _ = q_ref.shape

    def out_copy(j):
        return pltpu.make_async_copy(dkv.at[j], dkv_ref.at[j], out_sems.at[j])

    def one_block(j, masked):
        def one_head(head, _):
            query, do = q_ref[head], do_ref[head]
            here = pl.ds(pl.multiple_of(head * tokens, tokens), tokens)
            key, value = kv[j, 0, here], kv[j, 1, here]
            scores = dot(key, query, NT) * factor
            probs = jnp.exp2(scores - lse_ref[head, :1])
            if masked:
                key_at = lax.broadcasted_iota(jnp.int32, (tokens, tokens), 0)
                query_at = lax.broadcasted_iota(jnp.int32, (tokens, tokens), 1)
                probs = jnp.where(key_at <= query_at, probs, 0.0)
            dprob = dot(value, do, NT)
            dscore = (probs * (dprob - delta_ref[head, :1])).astype(BF16)
            dkv[j, 0, head] = (dot(dscore, query, NN) * scale).astype(BF16)
            dkv[j, 1, head] = dot(probs.astype(BF16), do, NN).astype(BF16)
            part = dot(key, dscore, TN)
            dq[head] = part if masked else dq[head] + part
            return 0

        lax.fori_loop(0, heads, one_head, 0)
        out_copy(j).start()

    one_block(0, True)

    def earlier(i, _):
        one_block(place ^ i, False)
        return 0

    def later(i, _):
        j = place ^ i
        dkv[j] = jnp.zeros(dkv.shape[1:], BF16)
        out_copy(j).start()
        return 0

    lax.fori_loop(0, place, earlier, 0)
    lax.fori_loop(place + 1, count, later, 0)
    for head in range(heads):
        dq_ref[head] = dq[head].T * scale
    for j in range(count):
        out_copy(j).wait()


def attend_back(place, query, do, lse, delta, kv_blocks):
    heads, tokens, size = query.shape
    count = len(kv_blocks)
    scale = 1.0 / math.sqrt(size)
    factor = math.log2(math.e) * scale
    return pl.pallas_call(
        functools.partial(attend_back_kernel, factor, scale, count),
        out_shape=(
            jax.ShapeDtypeStruct((heads, tokens, size), F32),
            jax.ShapeDtypeStruct((count, 2, heads, tokens, size), BF16),
        ),
        in_specs=[pl.BlockSpec(memory_space=pltpu.SMEM)]
        + [pl.BlockSpec(memory_space=pltpu.VMEM)] * 4
        + [pl.BlockSpec(memory_space=pl.ANY)] * count,
        out_specs=(pl.BlockSpec(memory_space=pltpu.VMEM), pl.BlockSpec(memory_space=pl.ANY)),
        scratch_shapes=[
            pltpu.VMEM((count, 2, heads * tokens, size), BF16),
            pltpu.VMEM((count, 2, heads, tokens, size), BF16),
            pltpu.VMEM((heads, size, tokens), F32),
            pltpu.SemaphoreType.DMA((count,)),
            pltpu.SemaphoreType.DMA((count,)),
        ],
        compiler_params=pltpu.CompilerParams(vmem_limit_bytes=VMEM_LIMIT),
        cost_estimate=pl.CostEstimate(
            flops=count * heads * tokens * tokens * size,
            bytes_accessed=2**20,
            transcendentals=0,
        ),
        name="attend_back",
    )(place.reshape(1), query, do, lse, delta, *kv_blocks)


def swiglu_back(one, two, dact, gate):
    sig = 1.0 / (1.0 + jnp.exp(-one))
    silu = one * sig
    act = silu * two
    prod = act * dact
    dgate = gate * dact
    d_one = (dgate * two * sig * (1.0 + one * (1.0 - sig))).astype(BF16)
    d_two = (dgate * silu).astype(BF16)
    return (gate * act).astype(BF16), d_one, d_two, prod


def experts_kernel(at, group, local, experts, given, first_ref, *refs):
    x_refs, g_refs, refs = refs[:group], refs[group : 2 * group], refs[2 * group :]
    (slot_row, slot_col, w_router, w_in, w_out, w_shared), refs = refs[:6], refs[6 + given :]
    dx_refs, refs = refs[:group], refs[group:]
    kept_refs, refs = refs[:7], refs[7:]
    (xs, gs, first_w, in_w, out_w, shared_w, dxs, left, right, sems, out_sems), stage = refs[:11], refs[11:]
    rows_x, rows_g, act_s, dpair_s, sact_s, sdpair_s, dl_s = stage
    tokens, width = xs.shape[1:]
    capacity, units = act_s.shape[2:]
    wide = local * capacity
    share = sact_s.shape[2]
    third = first_w.shape[0] - 128
    second = third // 2
    padded = w_router.shape[0]
    most = out_w.shape[1]

    loads = [pltpu.make_async_copy(x_refs[b], xs.at[b], sems.at[b]) for b in range(group)]
    fore_loads = [
        pltpu.make_async_copy(
            w_shared.at[c], first_w.at[pl.ds(c * second, share)], sems.at[2 * group + c]
        )
        for c in range(2)
    ]
    loads += [
        pltpu.make_async_copy(g_refs[b], gs.at[b], sems.at[group + b]) for b in range(group)
    ]
    base = 2 * group + 2
    more = [
        [
            pltpu.make_async_copy(
                w_in.at[e, c], in_w.at[e, pl.ds(c * most, units)], sems.at[base + 3 * e + c]
            )
            for c in range(2)
        ]
        + [
            pltpu.make_async_copy(
                w_out.at[e], out_w.at[e, pl.ds(0, units)], sems.at[base + 3 * e + 2]
            )
        ]
        for e in range(local)
    ]
    last = pltpu.make_async_copy(w_shared.at[2], shared_w, sems.at[base + 3 * local])
    for copy in loads[:group] + fore_loads:
        copy.start()
    first_w[third : third + padded] = w_router[...]
    first_w[third + padded :] = jnp.zeros((128 - padded, width), BF16)
    if second > share:
        for c in range(2):
            gap = jnp.zeros((second - share, width), BF16)
            first_w[c * second + share : (c + 1) * second] = gap
    if most > units:
        gap = jnp.zeros((most - units, width), BF16)
        for e in range(local):
            in_w[e, units:most] = gap
            in_w[e, most + units :] = gap
            out_w[e, units:] = gap

    sent = []

    def send(copy):
        copy.start()
        sent.append(copy)

    for copy in loads[:group] + fore_loads:
        copy.wait()
    for copy in loads[group:] + more[0]:
        copy.start()
    x = xs[...].reshape(group * tokens, width)
    fore = dot(x, first_w[...], NT)
    s_one, s_two = fore[:, :share], fore[:, second : second + share]
    s_gate = 1.0 / (1.0 + jnp.exp(-fore[:, third + experts : third + experts + 1]))
    row_at = lax.broadcasted_iota(jnp.int32, (padded, tokens), 0)
    slot_at = lax.broadcasted_iota(jnp.int32, (capacity, tokens), 0)
    probs, change, hits = [], [], []
    for b in range(group):
        logits = fore[b * tokens : (b + 1) * tokens, third:].T[:padded]
        shown = jnp.where(row_at < experts, logits, NEG)
        exps = jnp.exp(shown - jnp.max(shown, axis=0, keepdims=True))
        soft = exps / jnp.sum(exps, axis=0, keepdims=True)
        probs.append(jnp.where(row_at == experts, 1.0 / (1.0 + jnp.exp(-logits)), soft))
        change.append(jnp.zeros((padded, tokens), F32))
        picks = jnp.concatenate(
            [
                jnp.where(slot_at == slot_row[b, e : e + 1, :], 1.0, 0.0).astype(BF16)
                for e in range(local)
            ],
            axis=0,
        )
        rows = dot(picks, xs[b], NN).astype(BF16)
        for e in range(local):
            rows_x[e, b] = rows[e * capacity : (e + 1) * capacity]
        loads[group + b].wait()
        if b == group - 1:
            for e in range(1, local):
                for copy in more[e]:
                    copy.start()
            last.start()
        rows = dot(picks, gs[b], NN).astype(BF16)
        for e in range(local):
            rows_g[e, b] = rows[e * capacity : (e + 1) * capacity]
    def send_all(i, lead):
        for e in range(lead):
            send(
                pltpu.make_async_copy(
                    stage[i].at[e], kept_refs[i].at[e, pl.ds(at, group)], out_sems.at[i, e]
                )
            )

    send_all(0, local)
    send_all(1, local)
    is_expert = row_at < experts
    for e in range(local):
        chosen = row_at == first_ref[0] + e
        gates, owns, hits = [], [], []
        for b in range(group):
            own = jnp.sum(jnp.where(chosen, probs[b], 0.0), axis=0, keepdims=True)
            hit = slot_at == slot_row[b, e : e + 1, :]
            gates.append(jnp.sum(jnp.where(hit, own, 0.0), axis=1, keepdims=True))
            owns.append(own)
            hits.append(hit)
        for copy in more[e]:
            copy.wait()
        pair = dot(rows_x[e].reshape(group * capacity, width), in_w[e], NT)
        dact = dot(rows_g[e].reshape(group * capacity, width), out_w[e], NT)
        act, d_one, d_two, prod = swiglu_back(
            pair[:, :most], pair[:, most:], dact, jnp.concatenate(gates, axis=0)
        )
        act_s[e] = act[:, :units].reshape(group, capacity, units)
        dpair_s[2 * e] = d_one[:, :units].reshape(group, capacity, units)
        dpair_s[2 * e + 1] = d_two[:, :units].reshape(group, capacity, units)
        row_dot = jnp.sum(prod, axis=1, keepdims=True)
        drow = dot(jnp.concatenate([d_one, d_two], axis=1), in_w[e], NN).astype(BF16)
        for b in range(group):
            rows = slice(b * capacity, (b + 1) * capacity)
            found = jnp.sum(jnp.where(hits[b], row_dot[rows], 0.0), axis=0, keepdims=True)
            change[b] += (found * owns[b]) * (
                jnp.where(chosen, 1.0, 0.0) - jnp.where(is_expert, probs[b], 0.0)
            )
            right[b, e * capacity : (e + 1) * capacity] = drow[rows]
    send_all(2, local)
    send_all(3, 2 * local)
    last.wait()
    g = gs[...].reshape(group * tokens, width)
    s_dact = dot(g, shared_w[...], NT)
    act, d_one, d_two, prod = swiglu_back(s_one, s_two, s_dact, s_gate)
    sact_s[...] = act.reshape(group, tokens, share)
    sdpair_s[:, 0] = d_one.reshape(group, tokens, share)
    sdpair_s[:, 1] = d_two.reshape(group, tokens, share)
    dslogit = jnp.sum(prod, axis=1, keepdims=True) * s_gate * (1.0 - s_gate)
    lane_at = lax.broadcasted_iota(jnp.int32, (tokens, 128), 1)
    rest = jnp.zeros((128 - padded, tokens), F32)
    deep = wide + 2 * share
    column_at = lax.broadcasted_iota(jnp.int32, (tokens, capacity), 1)
    stores = []
    for b in range(group):
        rows = slice(b * tokens, (b + 1) * tokens)
        columns = jnp.concatenate([change[b], rest], axis=0).T
        columns = jnp.where(lane_at == experts, dslogit[rows], columns)[:, :padded].astype(BF16)
        dl_s[b] = columns
        left[b, :, deep : deep + padded] = columns
        right[b, deep : deep + padded] = w_router[...]
        for e in range(local):
            picks = jnp.where(column_at == slot_col[b, :, e : e + 1], 1.0, 0.0).astype(BF16)
            left[b, :, e * capacity : (e + 1) * capacity] = picks
        left[b, :, wide : wide + share] = d_one[rows]
        left[b, :, wide + share : wide + 2 * share] = d_two[rows]
        right[b, wide : wide + share] = first_w[:share]
        right[b, wide + share : wide + 2 * share] = first_w[second : second + share]
        dxs[b] = dot(left[b], right[b], NN).astype(BF16)
        send(pltpu.make_async_copy(dxs.at[b], dx_refs[b], out_sems.at[7, b]))
    for i in range(4, 7):
        send(pltpu.make_async_copy(stage[i], kept_refs[i].at[pl.ds(at, group)], out_sems.at[i, 0]))
    for copy in sent:
        copy.wait()


def run_experts(at, experts, first, x_group, g_group, slot_rows, slot_cols, weights, kept):
    given = kept if at else []
    group = len(x_group)
    tokens, width = x_group[0].shape
    w_router, w_in, w_out, w_shared = weights
    local = w_out.shape[0]
    share = w_shared.shape[1]
    padded = w_router.shape[0]
    capacity, units = kept[2].shape[2:]
    any_spec = pl.BlockSpec(memory_space=pl.ANY)
    block = jax.ShapeDtypeStruct((tokens, width), BF16)
    deep = local * capacity + 2 * share + padded
    flops = group * 2 * tokens * width * (local * capacity * 3 + 5 * share) + (
        group * 2 * width * local * capacity * units * 5
    )
    step = at // group
    wide_units = -(-units // 128) * 128
    fore = 2 * (-(-share // 64) * 64) + 128
    results = pl.pallas_call(
        functools.partial(experts_kernel, at, group, local, experts, len(given)),
        grid=(1,),
        out_shape=(block,) * group + tuple(jax.ShapeDtypeStruct(k.shape, k.dtype) for k in kept),
        in_specs=[pl.BlockSpec(memory_space=pltpu.SMEM)]
        + [any_spec] * (2 * group)
        + [
            pl.BlockSpec((group, local, tokens), lambda i: (step, 0, 0)),
            pl.BlockSpec((group, tokens, local), lambda i: (step, 0, 0)),
            pl.BlockSpec((padded, width), lambda i: (0, 0)),
        ]
        + [any_spec] * (3 + len(given)),
        out_specs=(any_spec,) * (group + len(kept)),
        input_output_aliases={7 + 2 * group + i: group + i for i in range(len(given))},
        scratch_shapes=[
            pltpu.VMEM((group, tokens, width), BF16),
            pltpu.VMEM((group, tokens, width), BF16),
            pltpu.VMEM((fore, width), BF16),
            pltpu.VMEM((local, 2 * wide_units, width), BF16),
            pltpu.VMEM((local, wide_units, width), BF16),
            pltpu.VMEM((share, width), BF16),
            pltpu.VMEM((group, tokens, width), BF16),
            pltpu.VMEM((group, tokens, deep), BF16),
            pltpu.VMEM((group, deep, width), BF16),
            pltpu.SemaphoreType.DMA((2 * group + 3 + 3 * local,)),
            pltpu.SemaphoreType.DMA((8, max(2 * local, group))),
        ]
        + [
            pltpu.VMEM(k.shape[:1] + (group,) + k.shape[2:], BF16) for k in kept[:4]
        ]
        + [pltpu.VMEM((group,) + k.shape[1:], BF16) for k in kept[4:]],
        compiler_params=pltpu.CompilerParams(vmem_limit_bytes=VMEM_LIMIT),
        cost_estimate=pl.CostEstimate(flops=flops // 16, bytes_accessed=2**20, transcendentals=0),
        name="run_experts",
    )(first.reshape(1), *x_group, *g_group, slot_rows, slot_cols, *weights, *given)
    return results[:group], results[group:]


def outputs_kernel(group, count, local, act, slot_col, sact, w_out, w_shared, *refs):
    out_refs, (outs, left, right, sems) = refs[:count], refs[count:]
    step = pl.program_id(0)
    slot = lax.rem(step, 2)
    capacity, units = act.shape[2:]
    tokens, share = sact.shape[1:]
    wide = local * capacity

    def store(at, b, into):
        return pltpu.make_async_copy(outs.at[into, b], out_refs[at * group + b], sems.at[into, b])

    @pl.when(step >= 2)
    def _():
        for b in range(group):
            store(0, b, slot).wait()

    for e in range(local):
        rows = dot(act[e].reshape(group * capacity, units), w_out[e], NN).astype(BF16)
        for b in range(group):
            right[b, e * capacity : (e + 1) * capacity] = rows[b * capacity : (b + 1) * capacity]
    slot_at = lax.broadcasted_iota(jnp.int32, (tokens, capacity), 1)
    for b in range(group):
        for e in range(local):
            picks = jnp.where(slot_at == slot_col[b, :, e : e + 1], 1.0, 0.0).astype(BF16)
            left[b, :, e * capacity : (e + 1) * capacity] = picks
        left[b, :, wide : wide + share] = sact[b]
        right[b, wide : wide + share] = w_shared[0]
        outs[slot, b] = dot(left[b], right[b], NN).astype(BF16)
    for at in range(count // group):

        @pl.when(step == at)
        def _():
            for b in range(group):
                store(at, b, at % 2).start()

    @pl.when(step == count // group - 1)
    def _():
        for b in range(group):
            for into in range(2):
                store(0, b, into).wait()


def expert_grads_kernel(rows_x, rows_g, act, dpair, in_ref, out_ref):
    rows = rows_x.shape[1] * rows_x.shape[2]
    x = rows_x[0].reshape(rows, -1)
    for c in range(2):
        in_ref[0, c] = dot(dpair[c].reshape(rows, -1), x, TN)
    out_ref[0] = dot(act[0].reshape(rows, -1), rows_g[0].reshape(rows, -1), TN)


def grads_of_experts(rows_x, rows_g, act, dpair):
    local, count, capacity, width = rows_x.shape
    units = act.shape[3]
    tile = min(width, 1024)
    return pl.pallas_call(
        expert_grads_kernel,
        grid=(local, width // tile),
        out_shape=(
            jax.ShapeDtypeStruct((local, 2, units, width), F32),
            jax.ShapeDtypeStruct((local, units, width), F32),
        ),
        in_specs=[
            pl.BlockSpec((1, count, capacity, tile), lambda e, i: (e, 0, 0, i)),
            pl.BlockSpec((1, count, capacity, tile), lambda e, i: (e, 0, 0, i)),
            pl.BlockSpec((1, count, capacity, units), lambda e, i: (e, 0, 0, 0)),
            pl.BlockSpec((2, count, capacity, units), lambda e, i: (e, 0, 0, 0)),
        ],
        out_specs=(
            pl.BlockSpec((1, 2, units, tile), lambda e, i: (e, 0, 0, i)),
            pl.BlockSpec((1, units, tile), lambda e, i: (e, 0, i)),
        ),
        compiler_params=pltpu.CompilerParams(vmem_limit_bytes=VMEM_LIMIT),
        cost_estimate=pl.CostEstimate(flops=0, bytes_accessed=2**20, transcendentals=0),
        name="grads_of_experts",
    )(rows_x, rows_g, act, dpair)


def run_outputs(act, slot_cols, sact, w_out, w_shared):
    local, count, capacity, units = act.shape
    tokens, share = sact.shape[1:]
    width = w_out.shape[2]
    group = 2
    deep = local * capacity + share
    return pl.pallas_call(
        functools.partial(outputs_kernel, group, count, local),
        grid=(count // group,),
        out_shape=(jax.ShapeDtypeStruct((tokens, width), BF16),) * count,
        in_specs=[
            pl.BlockSpec((local, group, capacity, units), lambda i: (0, i, 0, 0)),
            pl.BlockSpec((group, tokens, local), lambda i: (i, 0, 0)),
            pl.BlockSpec((group, tokens, share), lambda i: (i, 0, 0)),
            pl.BlockSpec((local, units, width), lambda i: (0, 0, 0)),
            pl.BlockSpec((1, share, width), lambda i: (2, 0, 0)),
        ],
        out_specs=(pl.BlockSpec(memory_space=pl.ANY),) * count,
        scratch_shapes=[
            pltpu.VMEM((2, group, tokens, width), BF16),
            pltpu.VMEM((group, tokens, deep), BF16),
            pltpu.VMEM((group, deep, width), BF16),
            pltpu.SemaphoreType.DMA((2, group)),
        ],
        compiler_params=pltpu.CompilerParams(vmem_limit_bytes=VMEM_LIMIT),
        cost_estimate=pl.CostEstimate(
            flops=count * width // 8 * (local * capacity * (units + tokens) + tokens * share),
            bytes_accessed=2**20,
            transcendentals=0,
        ),
        name="run_outputs",
    )(act, slot_cols, sact, w_out, w_shared)


def assemble_kernel(plan, count, place_ref, *refs):
    block_refs, refs = refs[:count], refs[count:]
    out_refs, (low, wide, in_sems, out_sems) = refs[:-4], refs[-4:]
    place = place_ref[0]

    def load(j):
        return pltpu.make_async_copy(block_refs[j], low.at[j % 2], in_sems.at[j % 2])

    def stores(j):
        return [
            pltpu.make_async_copy(
                wide.at[j % 2, pl.ds(first, rows)],
                out_refs[which].at[
                    pl.ds(pl.multiple_of(base + (place ^ j) * rows, 8), rows),
                    pl.ds(column, wide.shape[2]),
                ],
                out_sems.at[j % 2, i],
            )
            for i, (which, first, rows, base, column) in enumerate(plan)
        ]

    load(0).start()
    for j in range(count):
        if j + 1 < count:
            load(j + 1).start()
        load(j).wait()
        if j >= 2:
            for copy in stores(j - 2):
                copy.wait()
        wide[j % 2] = low[j % 2].astype(F32)
        for copy in stores(j):
            copy.start()
    for j in range(max(0, count - 2), count):
        for copy in stores(j):
            copy.wait()


def assemble(place, blocks, shapes, plan):
    count = len(blocks)
    rows, width = blocks[0].shape
    any_spec = pl.BlockSpec(memory_space=pl.ANY)
    return pl.pallas_call(
        functools.partial(assemble_kernel, plan, count),
        out_shape=[jax.ShapeDtypeStruct(shape, F32) for shape in shapes],
        in_specs=[pl.BlockSpec(memory_space=pltpu.SMEM)] + [any_spec] * count,
        out_specs=[any_spec] * len(shapes),
        scratch_shapes=[
            pltpu.VMEM((2, rows, width), BF16),
            pltpu.VMEM((2, rows, width), F32),
            pltpu.SemaphoreType.DMA((2,)),
            pltpu.SemaphoreType.DMA((2, len(plan))),
        ],
        compiler_params=pltpu.CompilerParams(vmem_limit_bytes=VMEM_LIMIT),
        cost_estimate=pl.CostEstimate(flops=0, bytes_accessed=2**20, transcendentals=0),
        name="assemble",
    )(place.reshape(1), *blocks)


def shared_grads_kernel(count, *refs):
    x_refs, g_refs, refs = refs[:count], refs[count : 2 * count], refs[2 * count :]
    (sact, sdpair, dl, grads_ref, router_ref, xs, gs, grads, router, sems) = refs
    at = pl.program_id(0)
    slot = lax.rem(at, 2)

    def load(j, into):
        return (
            pltpu.make_async_copy(x_refs[j], xs.at[into], sems.at[0, into]),
            pltpu.make_async_copy(g_refs[j], gs.at[into], sems.at[1, into]),
        )

    @pl.when(at == 0)
    def _():
        for copy in load(0, 0):
            copy.start()
        grads[...] = jnp.zeros_like(grads)
        router[...] = jnp.zeros_like(router)

    for j in range(1, count):

        @pl.when(at == j - 1)
        def _():
            for copy in load(j, j % 2):
                copy.start()

    for copy in load(0, slot):
        copy.wait()
    x, g = xs[slot], gs[slot]
    grads[0] += dot(sdpair[0, 0], x, TN)
    grads[1] += dot(sdpair[0, 1], x, TN)
    grads[2] += dot(sact[0], g, TN)
    router[...] += dot(dl[0], x, TN)

    @pl.when(at == count - 1)
    def _():
        grads_ref[...] = grads[...].astype(BF16)
        router_ref[...] = router[...]


def shared_grads(x_blocks, g_blocks, sact, sdpair, dl):
    count = len(x_blocks)
    tokens, width = x_blocks[0].shape
    share, padded = sact.shape[2], dl.shape[2]
    any_spec = pl.BlockSpec(memory_space=pl.ANY)
    return pl.pallas_call(
        functools.partial(shared_grads_kernel, count),
        grid=(count,),
        out_shape=(
            jax.ShapeDtypeStruct((3, share, width), BF16),
            jax.ShapeDtypeStruct((padded, width), F32),
        ),
        in_specs=[any_spec] * (2 * count)
        + [
            pl.BlockSpec((1, tokens, share), lambda j: (j, 0, 0)),
            pl.BlockSpec((1, 2, tokens, share), lambda j: (j, 0, 0, 0)),
            pl.BlockSpec((1, tokens, padded), lambda j: (j, 0, 0)),
        ],
        out_specs=(
            pl.BlockSpec((3, share, width), lambda j: (0, 0, 0)),
            pl.BlockSpec((padded, width), lambda j: (0, 0)),
        ),
        scratch_shapes=[
            pltpu.VMEM((2, tokens, width), BF16),
            pltpu.VMEM((2, tokens, width), BF16),
            pltpu.VMEM((3, share, width), F32),
            pltpu.VMEM((padded, width), F32),
            pltpu.SemaphoreType.DMA((2, 2)),
        ],
        compiler_params=pltpu.CompilerParams(vmem_limit_bytes=VMEM_LIMIT),
        cost_estimate=pl.CostEstimate(
            flops=count * tokens * width * share,
            bytes_accessed=2**20,
            transcendentals=0,
        ),
        name="shared_grads",
    )(*x_blocks, *g_blocks, sact, sdpair, dl)


def on_device(
    hidden_in,
    cotangent,
    gain_attn,
    qkv_weight,
    qkv_bias,
    out_weight,
    gain_ffn,
    router_weight,
    routes,
    shared_gate,
    shared_in,
    shared_out,
    expert_in,
    expert_out,
):
    tokens, width = hidden_in.shape
    ctx_count = lax.axis_size("ctx")
    heads_local = qkv_weight.shape[2] // HD
    local = expert_in.shape[0]
    experts = local * ctx_count
    top_count = routes.shape[1]
    capacity = 3 * tokens * top_count // (2 * experts)
    place = lax.axis_index("ctx")
    order = jnp.arange(ctx_count, dtype=jnp.int32) ^ place
    score_scale = 1.0 / math.sqrt(HD)
    query_pos = place * tokens + jnp.arange(tokens, dtype=jnp.int32)
    cosine, sine = rotary_tables(query_pos, HD)

    x_full = hidden_in.astype(F32)
    inv_one = lax.rsqrt(jnp.mean(x_full * x_full, axis=-1, keepdims=True) + EPS)
    normed_one = x_full * inv_one
    x_one = (normed_one * gain_attn).astype(BF16)
    projected = (
        jnp.einsum("td,dcf->ctf", x_one, qkv_weight, preferred_element_type=F32)
        + qkv_bias[:, None]
    )
    shaped = projected.reshape(3, tokens, heads_local, HD).transpose(0, 2, 1, 3)
    query = rotate(shaped[0], cosine, sine).astype(BF16)
    key_local = rotate(shaped[1], cosine, sine).astype(BF16)
    value_local = shaped[2].astype(BF16)
    kv_rows = heads_local * tokens
    route_rows = -(-tokens * top_count // HD)
    behind = jnp.pad(
        routes.T.astype(BF16).reshape(route_rows, HD), ((0, -route_rows % 16), (0, 0))
    )
    kv_local = jnp.stack(
        [
            jnp.concatenate([key_local.reshape(kv_rows, HD), behind], axis=0),
            jnp.concatenate([value_local.reshape(kv_rows, HD), behind], axis=0),
        ]
    )
    halves = ctx_count == 8
    half = tokens // 2
    if halves:
        g_early = [swap(cotangent[:half], 2), swap(cotangent[:half], 4)]
        kv_local = after(kv_local, *g_early)
    kv_blocks = gather_ctx(kv_local)
    if halves:
        rest = after(cotangent[half:], kv_blocks[6])
        g_late = [swap(rest, 2), swap(rest, 4)]
        g_pair = [jnp.concatenate(parts, axis=0) for parts in zip(g_early, g_late)]
    else:
        g_blocks = gather_ctx(cotangent)

    share = shared_out.shape[0] // ctx_count
    piece = shared_out.shape[1]
    shared_send = jnp.concatenate(
        [
            shared_in.transpose(1, 2, 0).reshape(2, ctx_count, share, piece),
            shared_out.reshape(1, ctx_count, share, piece),
        ],
        axis=0,
    ).transpose(1, 0, 2, 3)
    shared_w = (
        lax.all_to_all(shared_send, "ctx", split_axis=0, concat_axis=0, tiled=True)
        .transpose(1, 2, 0, 3)
        .reshape(3, share, width)
    )
    whole_share = -(-share // 16) * 16
    if whole_share > share:
        shared_w = jnp.pad(shared_w, ((0, 0), (0, whole_share - share), (0, 0)))
    half_rows = out_weight.shape[0] // 2
    core = place % 2
    out_mine = lax.all_gather(
        lax.dynamic_slice_in_dim(out_weight, core * half_rows, half_rows, 0), "tp", axis=0
    )

    routes_all = jnp.stack([b[0, kv_rows : kv_rows + route_rows] for b in kv_blocks])
    routes_all = routes_all.reshape(ctx_count, 1, top_count, tokens)
    own_experts = (place * local + jnp.arange(local, dtype=jnp.int32)).astype(BF16)
    hit = jnp.any(routes_all == own_experts[None, :, None, None], axis=2)
    token_at = jnp.arange(tokens, dtype=jnp.int32)
    earlier = (token_at[:, None] <= token_at[None, :]).astype(BF16)
    rank = dot(hit.astype(BF16).reshape(-1, tokens), earlier, NN).reshape(hit.shape) - 1.0
    slot_rows = jnp.where(hit, rank, -1.0).astype(jnp.int32)
    slot_cols = slot_rows.transpose(0, 2, 1)
    padded = -(-(experts + 1) // 8) * 8
    w_router = jnp.concatenate(
        [
            router_weight.T,
            shared_gate[None],
            jnp.zeros((padded - experts - 1, width), BF16),
        ],
        axis=0,
    )
    w_in = expert_in.transpose(0, 2, 3, 1)

    attended, lse = attend(place, after(query, shared_send), kv_blocks)
    att = attended.astype(BF16).transpose(1, 0, 2).reshape(tokens, heads_local * HD)
    att_all = jnp.concatenate(gather_tp(att), axis=1)
    out_mine = after(out_mine, attended)
    out_other = swap(out_mine, 1)
    out_full = arrange(place, out_mine, out_other)
    if halves:
        via_x, via_y = swap(g_early[1], 2), swap(g_late[0], 4)
        b6 = jnp.concatenate([via_x, via_y], axis=0)
        att_all = after(att_all, b6, shared_w, slot_rows, slot_cols, w_router, w_in)
        g_blocks = [cotangent, swap(cotangent, 1), g_pair[0], swap(g_pair[0], 1)]
        g_blocks += [g_pair[1], swap(g_pair[1], 1), b6, swap(b6, 1)]
    hidden = x_full + dot(att_all, out_full, NN)
    inv_two = lax.rsqrt(jnp.mean(hidden * hidden, axis=-1, keepdims=True) + EPS)
    normed_two = hidden * inv_two
    x_two = (normed_two * gain_ffn).astype(BF16)

    units, group = expert_out.shape[1], 2
    kept = [
        jax.ShapeDtypeStruct(shape, BF16)
        for shape in (
            (local, ctx_count, capacity, width),
            (local, ctx_count, capacity, width),
            (local, ctx_count, capacity, units),
            (2 * local, ctx_count, capacity, units),
            (ctx_count, tokens, whole_share),
            (ctx_count, 2, tokens, whole_share),
            (ctx_count, tokens, padded),
        )
    ]
    weights = (w_router, w_in, expert_out, shared_w)
    got = gather_start(x_two)
    x_blocks = [got[0], got[1]]
    dxs = []
    early = None
    for at in range(0, ctx_count, group):
        if at == 4 and ctx_count == 8:
            pair_two = pair_sum(dxs, 2)
            early = (pair_two, pair_two[: tokens // 2].astype(BF16))
        if at == 6 and ctx_count == 8:
            x_blocks[6] = after(x_blocks[6], early[1])
        dx, kept = run_experts(
            at,
            experts,
            place * local,
            x_blocks[at : at + group],
            g_blocks[at : at + group],
            slot_rows,
            slot_cols,
            weights,
            kept,
        )
        dxs += dx
        if at == 0:
            x_blocks = x_blocks[:2] + gather_end(got, dx[0])[2:]
    grad_x_part = scatter_ctx(dxs, early)
    outs = run_outputs(kept[2], slot_cols, kept[4], expert_out, shared_w)
    grad_x_low = grad_x_part.astype(BF16)
    out_hops, out_stay = scatter_start(after(outs, grad_x_low))
    kept = after(kept, *out_hops)
    rows_x, rows_g, act_low, dpair, s_act, s_dpair, low_logits = kept
    shared_low, router_part = shared_grads(x_blocks, g_blocks, s_act, s_dpair, low_logits)
    expert_grads = grads_of_experts(rows_x, rows_g, act_low, dpair)
    grad_expert_in, grad_expert_out = expert_grads
    gain_ffn_part = jnp.sum(grad_x_part * normed_two, axis=0)
    small = sum_tp_small(jnp.concatenate([router_part, gain_ffn_part[None]], axis=0))
    out_part = scatter_end((out_hops, out_stay))
    shared_back = lax.all_to_all(
        shared_low[:, :share].reshape(3, share, ctx_count, piece).transpose(2, 0, 1, 3),
        "ctx",
        split_axis=0,
        concat_axis=0,
        tiled=True,
    )
    summed = sum_tp_end(sum_tp_start(grad_x_low))
    summed = after(summed, shared_back, small, *expert_grads, out_part)
    shared_back = shared_back.astype(F32)
    grad_shared_in = shared_back[:, :2].transpose(3, 1, 0, 2).reshape(shared_in.shape)
    grad_shared_out = shared_back[:, 2].reshape(shared_out.shape)

    summed = summed.astype(F32)
    grad_y = cotangent.astype(F32)
    grad_normed_two = summed * gain_ffn
    grad_hidden = grad_y + inv_two * (
        grad_normed_two
        - normed_two * jnp.mean(grad_normed_two * normed_two, axis=-1, keepdims=True)
    )
    grad_hidden_low = grad_hidden.astype(BF16)
    out_weight_part = dot(att, grad_hidden_low, (((0,), (0,)), ((), ())))
    grad_att = (
        dot(grad_hidden_low, out_weight, (((1,), (1,)), ((), ())))
        .astype(BF16)
        .reshape(tokens, heads_local, HD)
        .transpose(1, 0, 2)
    )
    delta = jnp.sum(grad_att.astype(F32) * attended, axis=-1)
    delta = jnp.broadcast_to(delta[:, None], lse.shape)
    grad_query, grad_pairs = attend_back(place, query, grad_att, lse, delta, kv_blocks)
    ffn_total = sum_tp_start(out_part)
    grad_pairs = after(grad_pairs, ffn_total)
    ffn_low = sum_tp_end(after(ffn_total, grad_query))
    grad_kv = scatter_ctx([grad_pairs[j] for j in range(ctx_count)])
    grad_kv = after(grad_kv, ffn_low)

    def raw_part(value):
        return value.astype(BF16).transpose(1, 0, 2).reshape(tokens, heads_local * HD)

    raw = [
        raw_part(rotate(grad_query, cosine, -sine)),
        raw_part(rotate(grad_kv[0], cosine, -sine)),
        raw_part(grad_kv[1]),
    ]
    grad_x_one_part = jnp.einsum(
        "tcf,dcf->td", jnp.stack(raw, axis=1), qkv_weight, preferred_element_type=F32
    )
    grad_x_low = grad_x_one_part.astype(BF16)
    half_way = sum_tp_start(grad_x_low)
    grad_x_one = sum_tp_end(half_way)
    x_one = after(x_one, grad_x_low)
    gain_attn_part = jnp.sum(grad_x_one_part * normed_one, axis=0)
    gain_sum = sum_tp_small(gain_attn_part[None])
    head_width = heads_local * HD
    gain_rows = width // head_width
    ends = jnp.concatenate(
        [jnp.sum(r.astype(F32), axis=0)[None] for r in raw]
        + [gain_sum.reshape(gain_rows, -1), small.reshape((padded + 1) * gain_rows, -1)],
        axis=0,
    )
    ends = jnp.pad(ends, ((0, -ends.shape[0] % (16 * ctx_count)), (0, 0))).astype(BF16)
    query_part = after(dot(x_one, raw[0], TN).astype(BF16), grad_kv)
    pair_part = jnp.concatenate([dot(x_one, raw[1], TN), dot(x_one, raw[2], TN)], axis=0).astype(BF16)
    turns = width // head_width
    out_shards = [
        jnp.concatenate([s[:, k * head_width : (k + 1) * head_width] for k in range(turns)], axis=0)
        for s in shards(out_weight_part.astype(BF16))
    ]
    sums = sum_ctx(
        [
            jnp.concatenate(list(parts), axis=0)
            for parts in zip(shards(query_part), shards(pair_part), out_shards, shards(ends))
        ],
        half_way,
    )
    q_rows = width // ctx_count
    out_rows = out_weight.shape[0] // ctx_count
    plan = [(0, 0, q_rows, 0, 0), (0, q_rows, 2 * q_rows, width, 0)] + [
        (1, 3 * q_rows + k * out_rows, out_rows, 0, k * head_width) for k in range(turns)
    ]
    qkv_grad, out_weight_grad = assemble(
        place, sums, [(3 * width, head_width), out_weight.shape], plan
    )
    qkv_grad = qkv_grad.reshape(3, width, head_width).transpose(1, 0, 2)
    ends = relative(jnp.stack([b[3 * q_rows + turns * out_rows :] for b in sums]))
    ends = ends.reshape(-1, head_width).astype(F32)
    small = ends[3 + gain_rows : 3 + (padded + 2) * gain_rows].reshape(padded + 1, width)
    grad_x_one = after(grad_x_one, sums[2]).astype(F32)
    grad_normed_one = grad_x_one * gain_attn
    grad_input = grad_hidden + inv_one * (
        grad_normed_one
        - normed_one * jnp.mean(grad_normed_one * normed_one, axis=-1, keepdims=True)
    )
    block_out = (hidden + ffn_low.astype(F32)).astype(BF16)
    return (
        block_out,
        grad_input,
        ends[3 : 3 + gain_rows].reshape(-1),
        qkv_grad,
        ends[:3],
        out_weight_grad,
        small[padded],
        small[:experts].T,
        small[experts],
        grad_shared_in,
        grad_shared_out,
        grad_expert_in.transpose(0, 3, 1, 2),
        grad_expert_out,
    )


def solution(mesh):
    return jax.shard_map(
        on_device,
        mesh=mesh,
        in_specs=(
            P("ctx", None),
            P("ctx", None),
            P(),
            P(None, None, "tp"),
            P(None, "tp"),
            P("tp", None),
            P(),
            P(),
            P("ctx", None),
            P(),
            P("ctx", None, "tp"),
            P("tp", "ctx"),
            P("ctx", None, None, "tp"),
            P("ctx", "tp", None),
        ),
        out_specs=(
            P("ctx", None),
            P("ctx", None),
            P(),
            P(None, None, "tp"),
            P(None, "tp"),
            P("tp", None),
            P(),
            P(),
            P(),
            P("ctx", None, "tp"),
            P("tp", "ctx"),
            P("ctx", None, None, "tp"),
            P("ctx", "tp", None),
        ),
        check_vma=False,
    )
```

```python
import functools
import math

import jax
import jax.numpy as jnp
from jax import lax
from jax.experimental import pallas as pl
from jax.experimental.pallas import tpu as pltpu
from jax.sharding import PartitionSpec as P

HD = 128
EPS = 1e-06
THETA = 1000000.0
NEG = -1e30
F32 = jnp.float32
BF16 = jnp.bfloat16


def rotary_tables(positions, width):
    half_width = width // 2
    freqs = THETA ** (-(jnp.arange(half_width, dtype=F32) * 2.0) / width)
    angles = positions.astype(F32)[:, None] * freqs[None, :]
    return (jnp.cos(angles), jnp.sin(angles))


def rotate(values, cosine, sine):
    half_width = values.shape[-1] // 2
    first, second = values[..., :half_width], values[..., half_width:]
    return jnp.concatenate(
        [first * cosine - second * sine, second * cosine + first * sine], axis=-1
    )


def dot(a, b, dims):
    return lax.dot_general(a, b, dims, preferred_element_type=F32)


def swap(value, bits):
    count = lax.axis_size("ctx")
    return lax.ppermute(value, "ctx", [(i, i ^ bits) for i in range(count)])


def relative(natural):
    count = natural.shape[0]
    order = jnp.arange(count, dtype=jnp.int32) ^ lax.axis_index("ctx")
    return natural[order]


def nothing_kernel(*refs):
    pass


def after(values, *others):
    single = not isinstance(values, (list, tuple))
    values = [values] if single else list(values)
    any_spec = pl.BlockSpec(memory_space=pl.ANY)
    results = pl.pallas_call(
        nothing_kernel,
        out_shape=[jax.ShapeDtypeStruct(v.shape, v.dtype) for v in values],
        in_specs=[any_spec] * (len(values) + len(others)),
        out_specs=[any_spec] * len(values),
        input_output_aliases={i: i for i in range(len(values))},
        name="after",
    )(*values, *others)
    return results[0] if single else results


def gather_start(own):
    if lax.axis_size("ctx") != 8:
        return relative(lax.all_gather(own, "ctx", axis=0))
    return [own, swap(own, 1), swap(own, 2), swap(own, 4)]


def gather_end(got, *others):
    if lax.axis_size("ctx") != 8:
        return [got[j] for j in range(lax.axis_size("ctx"))]
    own, b1, b2, b4 = got
    if others:
        b2, b4 = after((b2, b4), *others)
    half = own.shape[0] // 2
    via_x, via_y = swap(b4[:half], 2), swap(b2[half:], 4)
    b3, b5 = swap(b2, 1), swap(b4, 1)
    b6 = jnp.concatenate([via_x, via_y], axis=0)
    return [own, b1, b2, b3, b4, b5, b6, swap(b6, 1)]


def gather_ctx(own, *others):
    return gather_end(gather_start(own), *others)


def pair_sum(parts, j):
    return parts[j].astype(F32) + swap(parts[j ^ 1], 1).astype(F32)


def scatter_ctx(parts, early=None):
    return scatter_end(scatter_start(parts, early))


def scatter_start(parts, early=None):
    if lax.axis_size("ctx") != 8:
        return [jnp.stack(parts)], None
    half = parts[0].shape[0] // 2
    pair = {j: pair_sum(parts, j) for j in (2, 4, 6, 0) if j != 2 or early is None}
    if early is None:
        early = (pair[2], pair[2][:half].astype(BF16))
    q6 = pair[6].astype(BF16)
    hops = [early[1], pair[4][half:].astype(BF16), q6[:half], q6[half:]]
    return hops, (early[0], pair[4], pair[0])


def scatter_end(started, *others):
    hops, stay = started
    if lax.axis_size("ctx") != 8:
        natural = relative(hops[0])
        flat = natural.reshape((-1,) + natural.shape[2:])
        return lax.psum_scatter(flat, "ctx", scatter_dimension=0, tiled=True).astype(F32)
    two, four, zero = stay
    half = two.shape[0] // 2
    r2, r4 = swap(hops[0], 2), swap(hops[1], 4)
    via_x, via_y = swap(hops[2], 2), swap(hops[3], 4)
    r4a = (four[:half] + via_x.astype(F32)).astype(BF16)
    r2b = (two[half:] + via_y.astype(F32)).astype(BF16)
    if others:
        r4a, r2b = after((r4a, r2b), *others)
    r4a, r2b = swap(r4a, 4), swap(r2b, 2)
    low = r2.astype(F32) + r4a.astype(F32)
    high = r2b.astype(F32) + r4.astype(F32)
    return zero + jnp.concatenate([low, high], axis=0)


def sum_ctx(parts, *others):
    return gather_ctx(scatter_end(scatter_start(parts), *others).astype(BF16))


def shards(value):
    count = lax.axis_size("ctx")
    rows = value.shape[0] // count
    place = lax.axis_index("ctx")
    return [lax.dynamic_slice_in_dim(value, (place ^ j) * rows, rows, 0) for j in range(count)]


def gather_tp(own):
    count = lax.axis_size("tp")
    return [own] + [
        lax.ppermute(own, "tp", [(i, i ^ k) for i in range(count)]) for k in range(1, count)
    ]


NT = (((1,), (1,)), ((), ()))
NN = (((1,), (0,)), ((), ()))
TN = (((0,), (0,)), ((), ()))
VMEM_LIMIT = 60 * 1024 * 1024


def sum_tp_start(value):
    pieces = value.astype(BF16).reshape(lax.axis_size("tp"), -1, value.shape[1])
    got = lax.all_to_all(pieces, "tp", split_axis=0, concat_axis=0, tiled=True)
    return jnp.sum(got.astype(F32), axis=0).astype(BF16)


def sum_tp_end(total):
    count, at = lax.axis_size("tp"), lax.axis_index("tp")
    blocks = jnp.stack(gather_tp(total))
    blocks = blocks[jnp.arange(count, dtype=jnp.int32) ^ at]
    return blocks.reshape(-1, total.shape[1])


def sum_tp_small(value):
    count, bits = lax.axis_size("tp"), 1
    while bits < count:
        value = value + lax.ppermute(value, "tp", [(i, i ^ bits) for i in range(count)])
        bits *= 2
    return value


def arrange_kernel(places, mine, other, out):
    @pl.when(pl.program_id(1) == 0)
    def _():
        out[0, 0] = mine[0]

    @pl.when(pl.program_id(1) == 1)
    def _():
        out[0, 0] = other[0]


def arrange(place, mine, other):
    count, rows, width = mine.shape
    places = jnp.stack([place % 2, lax.axis_index("tp")])
    return pl.pallas_call(
        arrange_kernel,
        grid_spec=pltpu.PrefetchScalarGridSpec(
            num_scalar_prefetch=1,
            grid=(count, 2),
            in_specs=[pl.BlockSpec((1, rows, width), lambda k, i, p: (p[1] ^ k, 0, 0))] * 2,
            out_specs=pl.BlockSpec((1, 1, rows, width), lambda k, i, p: (k, p[0] ^ i, 0, 0)),
        ),
        out_shape=jax.ShapeDtypeStruct((count, 2, rows, width), mine.dtype),
        compiler_params=pltpu.CompilerParams(vmem_limit_bytes=VMEM_LIMIT),
        cost_estimate=pl.CostEstimate(flops=0, bytes_accessed=2**20, transcendentals=0),
        name="arrange",
    )(places, mine, other).reshape(-1, width)


def attend_kernel(factor, count, place_ref, q_ref, *refs):
    kv_refs, (att_ref, lse_ref, kv, sems) = refs[:count], refs[count:]
    rows = kv.shape[2]
    copies = [
        pltpu.make_async_copy(kv_refs[j].at[:, pl.ds(0, rows)], kv.at[j], sems.at[j])
        for j in range(count)
    ]
    for copy in copies:
        copy.start()
    for copy in copies:
        copy.wait()
    place = place_ref[0]
    heads, tokens, _ = q_ref.shape

    def one_head(head, _):
        query = q_ref[head]
        here = pl.ds(pl.multiple_of(head * tokens, tokens), tokens)

        def scores(j):
            return dot(kv[j, 0, here], query, NT) * factor

        key_at = lax.broadcasted_iota(jnp.int32, (tokens, tokens), 0)
        query_at = lax.broadcasted_iota(jnp.int32, (tokens, tokens), 1)
        first = jnp.where(key_at <= query_at, scores(0), NEG)
        top = jnp.max(first, axis=0, keepdims=True)
        exps = jnp.exp2(first - top)
        total = jnp.sum(exps, axis=0, keepdims=True)
        acc = dot(kv[0, 1, here], exps.astype(BF16), TN)

        def earlier(i, carry):
            top, total, acc = carry
            j = place ^ i
            now = scores(j)
            higher = jnp.maximum(top, jnp.max(now, axis=0, keepdims=True))
            exps = jnp.exp2(now - higher)
            keep = jnp.exp2(top - higher)
            total = total * keep + jnp.sum(exps, axis=0, keepdims=True)
            acc = acc * keep + dot(kv[j, 1, here], exps.astype(BF16), TN)
            return higher, total, acc

        top, total, acc = lax.fori_loop(0, place, earlier, (top, total, acc))
        att_ref[head] = (acc / total).T
        lse_ref[head] = jnp.broadcast_to(top + jnp.log2(total), lse_ref.shape[1:])
        return 0

    lax.fori_loop(0, heads, one_head, 0)


def attend(place, query, kv_blocks):
    heads, tokens, size = query.shape
    count = len(kv_blocks)
    factor = math.log2(math.e) / math.sqrt(size)
    flops = 4 * count * heads * tokens * tokens * size
    return pl.pallas_call(
        functools.partial(attend_kernel, factor, count),
        out_shape=(
            jax.ShapeDtypeStruct((heads, tokens, size), F32),
            jax.ShapeDtypeStruct((heads, 8, tokens), F32),
        ),
        in_specs=[
            pl.BlockSpec(memory_space=pltpu.SMEM),
            pl.BlockSpec(memory_space=pltpu.VMEM),
        ]
        + [pl.BlockSpec(memory_space=pl.ANY)] * count,
        out_specs=(pl.BlockSpec(memory_space=pltpu.VMEM),) * 2,
        scratch_shapes=[
            pltpu.VMEM((count, 2, heads * tokens, size), BF16),
            pltpu.SemaphoreType.DMA((count,)),
        ],
        compiler_params=pltpu.CompilerParams(vmem_limit_bytes=VMEM_LIMIT),
        cost_estimate=pl.CostEstimate(
            flops=flops // 16, bytes_accessed=2**20, transcendentals=0
        ),
        name="attend",
    )(place.reshape(1), query, *kv_blocks)


def attend_back_kernel(factor, scale, count, place_ref, q_ref, do_ref, lse_ref, delta_ref, *refs):
    kv_refs, (dq_ref, dkv_ref, kv, dkv, dq, sems, out_sems) = refs[:count], refs[count:]
    rows = kv.shape[2]
    copies = [
        pltpu.make_async_copy(kv_refs[j].at[:, pl.ds(0, rows)], kv.at[j], sems.at[j])
        for j in range(count)
    ]
    for copy in copies:
        copy.start()
    for copy in copies:
        copy.wait()
    place = place_ref[0]
    heads, tokens, _ = q_ref.shape

    def out_copy(j):
        return pltpu.make_async_copy(dkv.at[j], dkv_ref.at[j], out_sems.at[j])

    def one_block(j, masked):
        def one_head(head, _):
            query, do = q_ref[head], do_ref[head]
            here = pl.ds(pl.multiple_of(head * tokens, tokens), tokens)
            key, value = kv[j, 0, here], kv[j, 1, here]
            scores = dot(key, query, NT) * factor
            probs = jnp.exp2(scores - lse_ref[head, :1])
            if masked:
                key_at = lax.broadcasted_iota(jnp.int32, (tokens, tokens), 0)
                query_at = lax.broadcasted_iota(jnp.int32, (tokens, tokens), 1)
                probs = jnp.where(key_at <= query_at, probs, 0.0)
            dprob = dot(value, do, NT)
            dscore = (probs * (dprob - delta_ref[head, :1])).astype(BF16)
            dkv[j, 0, head] = (dot(dscore, query, NN) * scale).astype(BF16)
            dkv[j, 1, head] = dot(probs.astype(BF16), do, NN).astype(BF16)
            part = dot(key, dscore, TN)
            dq[head] = part if masked else dq[head] + part
            return 0

        lax.fori_loop(0, heads, one_head, 0)
        out_copy(j).start()

    one_block(0, True)

    def earlier(i, _):
        one_block(place ^ i, False)
        return 0

    def later(i, _):
        j = place ^ i
        dkv[j] = jnp.zeros(dkv.shape[1:], BF16)
        out_copy(j).start()
        return 0

    lax.fori_loop(0, place, earlier, 0)
    lax.fori_loop(place + 1, count, later, 0)
    for head in range(heads):
        dq_ref[head] = dq[head].T * scale
    for j in range(count):
        out_copy(j).wait()


def attend_back(place, query, do, lse, delta, kv_blocks):
    heads, tokens, size = query.shape
    count = len(kv_blocks)
    scale = 1.0 / math.sqrt(size)
    factor = math.log2(math.e) * scale
    return pl.pallas_call(
        functools.partial(attend_back_kernel, factor, scale, count),
        out_shape=(
            jax.ShapeDtypeStruct((heads, tokens, size), F32),
            jax.ShapeDtypeStruct((count, 2, heads, tokens, size), BF16),
        ),
        in_specs=[pl.BlockSpec(memory_space=pltpu.SMEM)]
        + [pl.BlockSpec(memory_space=pltpu.VMEM)] * 4
        + [pl.BlockSpec(memory_space=pl.ANY)] * count,
        out_specs=(pl.BlockSpec(memory_space=pltpu.VMEM), pl.BlockSpec(memory_space=pl.ANY)),
        scratch_shapes=[
            pltpu.VMEM((count, 2, heads * tokens, size), BF16),
            pltpu.VMEM((count, 2, heads, tokens, size), BF16),
            pltpu.VMEM((heads, size, tokens), F32),
            pltpu.SemaphoreType.DMA((count,)),
            pltpu.SemaphoreType.DMA((count,)),
        ],
        compiler_params=pltpu.CompilerParams(vmem_limit_bytes=VMEM_LIMIT),
        cost_estimate=pl.CostEstimate(
            flops=count * heads * tokens * tokens * size,
            bytes_accessed=2**20,
            transcendentals=0,
        ),
        name="attend_back",
    )(place.reshape(1), query, do, lse, delta, *kv_blocks)


def swiglu_back(one, two, dact, gate):
    sig = 1.0 / (1.0 + jnp.exp(-one))
    silu = one * sig
    act = silu * two
    prod = act * dact
    dgate = gate * dact
    d_one = (dgate * two * sig * (1.0 + one * (1.0 - sig))).astype(BF16)
    d_two = (dgate * silu).astype(BF16)
    return (gate * act).astype(BF16), d_one, d_two, prod


def experts_kernel(at, group, local, experts, given, place_ref, *refs):
    x_refs, g_all, refs = refs[:group], refs[group], refs[group + 1 :]
    (slot_row, slot_col, w_router, w_in, w_out, w_shared), refs = refs[:6], refs[6 + given :]
    dx_refs, refs = refs[:group], refs[group:]
    kept_refs, refs = refs[:7], refs[7:]
    (xs, gs, first_w, in_w, out_w, shared_w, dxs, left, right, sems, out_sems), stage = refs[:11], refs[11:]
    rows_x, rows_g, act_s, dpair_s, sact_s, sdpair_s, dl_s = stage
    tokens, width = xs.shape[1:]
    capacity, units = act_s.shape[2:]
    wide = local * capacity
    share = sact_s.shape[2]
    third = first_w.shape[0] - 128
    second = third // 2
    padded = w_router.shape[0]
    most = out_w.shape[1]

    loads = [pltpu.make_async_copy(x_refs[b], xs.at[b], sems.at[b]) for b in range(group)]
    fore_loads = [
        pltpu.make_async_copy(
            w_shared.at[c], first_w.at[pl.ds(c * second, share)], sems.at[2 * group + c]
        )
        for c in range(2)
    ]
    loads += [
        pltpu.make_async_copy(g_all.at[place_ref[0] ^ (at + b)], gs.at[b], sems.at[group + b])
        for b in range(group)
    ]
    base = 2 * group + 2
    more = [
        [
            pltpu.make_async_copy(
                w_in.at[e, c], in_w.at[e, pl.ds(c * most, units)], sems.at[base + 3 * e + c]
            )
            for c in range(2)
        ]
        + [
            pltpu.make_async_copy(
                w_out.at[e], out_w.at[e, pl.ds(0, units)], sems.at[base + 3 * e + 2]
            )
        ]
        for e in range(local)
    ]
    last = pltpu.make_async_copy(w_shared.at[2], shared_w, sems.at[base + 3 * local])
    for copy in loads[:group] + fore_loads:
        copy.start()
    first_w[third : third + padded] = w_router[...]
    first_w[third + padded :] = jnp.zeros((128 - padded, width), BF16)
    if second > share:
        for c in range(2):
            gap = jnp.zeros((second - share, width), BF16)
            first_w[c * second + share : (c + 1) * second] = gap
    if most > units:
        gap = jnp.zeros((most - units, width), BF16)
        for e in range(local):
            in_w[e, units:most] = gap
            in_w[e, most + units :] = gap
            out_w[e, units:] = gap

    sent = []

    def send(copy):
        copy.start()
        sent.append(copy)

    for copy in loads[:group] + fore_loads:
        copy.wait()
    for copy in loads[group:] + more[0]:
        copy.start()
    x = xs[...].reshape(group * tokens, width)
    fore = dot(x, first_w[...], NT)
    s_one, s_two = fore[:, :share], fore[:, second : second + share]
    s_gate = 1.0 / (1.0 + jnp.exp(-fore[:, third + experts : third + experts + 1]))
    row_at = lax.broadcasted_iota(jnp.int32, (padded, tokens), 0)
    slot_at = lax.broadcasted_iota(jnp.int32, (capacity, tokens), 0)
    probs, change, hits = [], [], []
    for b in range(group):
        logits = fore[b * tokens : (b + 1) * tokens, third:].T[:padded]
        shown = jnp.where(row_at < experts, logits, NEG)
        exps = jnp.exp(shown - jnp.max(shown, axis=0, keepdims=True))
        soft = exps / jnp.sum(exps, axis=0, keepdims=True)
        probs.append(jnp.where(row_at == experts, 1.0 / (1.0 + jnp.exp(-logits)), soft))
        change.append(jnp.zeros((padded, tokens), F32))
        picks = jnp.concatenate(
            [
                jnp.where(slot_at == slot_row[b, e : e + 1, :], 1.0, 0.0).astype(BF16)
                for e in range(local)
            ],
            axis=0,
        )
        rows = dot(picks, xs[b], NN).astype(BF16)
        for e in range(local):
            rows_x[e, b] = rows[e * capacity : (e + 1) * capacity]
        loads[group + b].wait()
        if b == group - 1:
            for e in range(1, local):
                for copy in more[e]:
                    copy.start()
            last.start()
        rows = dot(picks, gs[b], NN).astype(BF16)
        for e in range(local):
            rows_g[e, b] = rows[e * capacity : (e + 1) * capacity]
    def send_all(i, lead):
        for e in range(lead):
            send(
                pltpu.make_async_copy(
                    stage[i].at[e], kept_refs[i].at[e, pl.ds(at, group)], out_sems.at[i, e]
                )
            )

    send_all(0, local)
    send_all(1, local)
    is_expert = row_at < experts
    for e in range(local):
        chosen = row_at == place_ref[0] * local + e
        gates, owns, hits = [], [], []
        for b in range(group):
            own = jnp.sum(jnp.where(chosen, probs[b], 0.0), axis=0, keepdims=True)
            hit = slot_at == slot_row[b, e : e + 1, :]
            gates.append(jnp.sum(jnp.where(hit, own, 0.0), axis=1, keepdims=True))
            owns.append(own)
            hits.append(hit)
        for copy in more[e]:
            copy.wait()
        pair = dot(rows_x[e].reshape(group * capacity, width), in_w[e], NT)
        dact = dot(rows_g[e].reshape(group * capacity, width), out_w[e], NT)
        act, d_one, d_two, prod = swiglu_back(
            pair[:, :most], pair[:, most:], dact, jnp.concatenate(gates, axis=0)
        )
        act_s[e] = act[:, :units].reshape(group, capacity, units)
        dpair_s[2 * e] = d_one[:, :units].reshape(group, capacity, units)
        dpair_s[2 * e + 1] = d_two[:, :units].reshape(group, capacity, units)
        row_dot = jnp.sum(prod, axis=1, keepdims=True)
        drow = dot(jnp.concatenate([d_one, d_two], axis=1), in_w[e], NN).astype(BF16)
        for b in range(group):
            rows = slice(b * capacity, (b + 1) * capacity)
            found = jnp.sum(jnp.where(hits[b], row_dot[rows], 0.0), axis=0, keepdims=True)
            change[b] += (found * owns[b]) * (
                jnp.where(chosen, 1.0, 0.0) - jnp.where(is_expert, probs[b], 0.0)
            )
            right[b, e * capacity : (e + 1) * capacity] = drow[rows]
    send_all(2, local)
    send_all(3, 2 * local)
    last.wait()
    g = gs[...].reshape(group * tokens, width)
    s_dact = dot(g, shared_w[...], NT)
    act, d_one, d_two, prod = swiglu_back(s_one, s_two, s_dact, s_gate)
    sact_s[...] = act.reshape(group, tokens, share)
    sdpair_s[:, 0] = d_one.reshape(group, tokens, share)
    sdpair_s[:, 1] = d_two.reshape(group, tokens, share)
    dslogit = jnp.sum(prod, axis=1, keepdims=True) * s_gate * (1.0 - s_gate)
    lane_at = lax.broadcasted_iota(jnp.int32, (tokens, 128), 1)
    rest = jnp.zeros((128 - padded, tokens), F32)
    deep = wide + 2 * share
    column_at = lax.broadcasted_iota(jnp.int32, (tokens, capacity), 1)
    stores = []
    for b in range(group):
        rows = slice(b * tokens, (b + 1) * tokens)
        columns = jnp.concatenate([change[b], rest], axis=0).T
        columns = jnp.where(lane_at == experts, dslogit[rows], columns)[:, :padded].astype(BF16)
        dl_s[b] = columns
        left[b, :, deep : deep + padded] = columns
        right[b, deep : deep + padded] = w_router[...]
        for e in range(local):
            picks = jnp.where(column_at == slot_col[b, :, e : e + 1], 1.0, 0.0).astype(BF16)
            left[b, :, e * capacity : (e + 1) * capacity] = picks
        left[b, :, wide : wide + share] = d_one[rows]
        left[b, :, wide + share : wide + 2 * share] = d_two[rows]
        right[b, wide : wide + share] = first_w[:share]
        right[b, wide + share : wide + 2 * share] = first_w[second : second + share]
        dxs[b] = dot(left[b], right[b], NN).astype(BF16)
        send(pltpu.make_async_copy(dxs.at[b], dx_refs[b], out_sems.at[7, b]))
    for i in range(4, 7):
        send(pltpu.make_async_copy(stage[i], kept_refs[i].at[pl.ds(at, group)], out_sems.at[i, 0]))
    for copy in sent:
        copy.wait()


def run_experts(at, experts, place, x_group, g_all, slot_rows, slot_cols, weights, kept):
    given = kept if at else []
    group = len(x_group)
    tokens, width = x_group[0].shape
    w_router, w_in, w_out, w_shared = weights
    local = w_out.shape[0]
    share = w_shared.shape[1]
    padded = w_router.shape[0]
    capacity, units = kept[2].shape[2:]
    any_spec = pl.BlockSpec(memory_space=pl.ANY)
    block = jax.ShapeDtypeStruct((tokens, width), BF16)
    deep = local * capacity + 2 * share + padded
    flops = group * 2 * tokens * width * (local * capacity * 3 + 5 * share) + (
        group * 2 * width * local * capacity * units * 5
    )
    step = at // group
    wide_units = -(-units // 128) * 128
    fore = 2 * (-(-share // 64) * 64) + 128
    results = pl.pallas_call(
        functools.partial(experts_kernel, at, group, local, experts, len(given)),
        grid=(1,),
        out_shape=(block,) * group + tuple(jax.ShapeDtypeStruct(k.shape, k.dtype) for k in kept),
        in_specs=[pl.BlockSpec(memory_space=pltpu.SMEM)]
        + [any_spec] * (group + 1)
        + [
            pl.BlockSpec((group, local, tokens), lambda i: (step, 0, 0)),
            pl.BlockSpec((group, tokens, local), lambda i: (step, 0, 0)),
            pl.BlockSpec((padded, width), lambda i: (0, 0)),
        ]
        + [any_spec] * (3 + len(given)),
        out_specs=(any_spec,) * (group + len(kept)),
        input_output_aliases={8 + group + i: group + i for i in range(len(given))},
        scratch_shapes=[
            pltpu.VMEM((group, tokens, width), BF16),
            pltpu.VMEM((group, tokens, width), BF16),
            pltpu.VMEM((fore, width), BF16),
            pltpu.VMEM((local, 2 * wide_units, width), BF16),
            pltpu.VMEM((local, wide_units, width), BF16),
            pltpu.VMEM((share, width), BF16),
            pltpu.VMEM((group, tokens, width), BF16),
            pltpu.VMEM((group, tokens, deep), BF16),
            pltpu.VMEM((group, deep, width), BF16),
            pltpu.SemaphoreType.DMA((2 * group + 3 + 3 * local,)),
            pltpu.SemaphoreType.DMA((8, max(2 * local, group))),
        ]
        + [
            pltpu.VMEM(k.shape[:1] + (group,) + k.shape[2:], BF16) for k in kept[:4]
        ]
        + [pltpu.VMEM((group,) + k.shape[1:], BF16) for k in kept[4:]],
        compiler_params=pltpu.CompilerParams(vmem_limit_bytes=VMEM_LIMIT),
        cost_estimate=pl.CostEstimate(flops=flops // 16, bytes_accessed=2**20, transcendentals=0),
        name="run_experts",
    )(place.reshape(1), *x_group, g_all, slot_rows, slot_cols, *weights, *given)
    return results[:group], results[group:]


def outputs_kernel(group, count, local, act, slot_col, sact, w_out, w_shared, *refs):
    out_refs, (outs, left, right, sems) = refs[:count], refs[count:]
    step = pl.program_id(0)
    slot = lax.rem(step, 2)
    capacity, units = act.shape[2:]
    tokens, share = sact.shape[1:]
    wide = local * capacity

    def store(at, b, into):
        return pltpu.make_async_copy(outs.at[into, b], out_refs[at * group + b], sems.at[into, b])

    @pl.when(step >= 2)
    def _():
        for b in range(group):
            store(0, b, slot).wait()

    for e in range(local):
        rows = dot(act[e].reshape(group * capacity, units), w_out[e], NN).astype(BF16)
        for b in range(group):
            right[b, e * capacity : (e + 1) * capacity] = rows[b * capacity : (b + 1) * capacity]
    slot_at = lax.broadcasted_iota(jnp.int32, (tokens, capacity), 1)
    for b in range(group):
        for e in range(local):
            picks = jnp.where(slot_at == slot_col[b, :, e : e + 1], 1.0, 0.0).astype(BF16)
            left[b, :, e * capacity : (e + 1) * capacity] = picks
        left[b, :, wide : wide + share] = sact[b]
        right[b, wide : wide + share] = w_shared[0]
        outs[slot, b] = dot(left[b], right[b], NN).astype(BF16)
    for at in range(count // group):

        @pl.when(step == at)
        def _():
            for b in range(group):
                store(at, b, at % 2).start()

    @pl.when(step == count // group - 1)
    def _():
        for b in range(group):
            for into in range(2):
                store(0, b, into).wait()


def expert_grads_kernel(rows_x, rows_g, act, dpair, in_ref, out_ref):
    rows = rows_x.shape[1] * rows_x.shape[2]
    x = rows_x[0].reshape(rows, -1)
    for c in range(2):
        in_ref[0, c] = dot(dpair[c].reshape(rows, -1), x, TN)
    out_ref[0] = dot(act[0].reshape(rows, -1), rows_g[0].reshape(rows, -1), TN)


def grads_of_experts(rows_x, rows_g, act, dpair):
    local, count, capacity, width = rows_x.shape
    units = act.shape[3]
    tile = min(width, 1024)
    return pl.pallas_call(
        expert_grads_kernel,
        grid=(local, width // tile),
        out_shape=(
            jax.ShapeDtypeStruct((local, 2, units, width), F32),
            jax.ShapeDtypeStruct((local, units, width), F32),
        ),
        in_specs=[
            pl.BlockSpec((1, count, capacity, tile), lambda e, i: (e, 0, 0, i)),
            pl.BlockSpec((1, count, capacity, tile), lambda e, i: (e, 0, 0, i)),
            pl.BlockSpec((1, count, capacity, units), lambda e, i: (e, 0, 0, 0)),
            pl.BlockSpec((2, count, capacity, units), lambda e, i: (e, 0, 0, 0)),
        ],
        out_specs=(
            pl.BlockSpec((1, 2, units, tile), lambda e, i: (e, 0, 0, i)),
            pl.BlockSpec((1, units, tile), lambda e, i: (e, 0, i)),
        ),
        compiler_params=pltpu.CompilerParams(vmem_limit_bytes=VMEM_LIMIT),
        cost_estimate=pl.CostEstimate(flops=0, bytes_accessed=2**20, transcendentals=0),
        name="grads_of_experts",
    )(rows_x, rows_g, act, dpair)


def run_outputs(act, slot_cols, sact, w_out, w_shared):
    local, count, capacity, units = act.shape
    tokens, share = sact.shape[1:]
    width = w_out.shape[2]
    group = 2
    deep = local * capacity + share
    return pl.pallas_call(
        functools.partial(outputs_kernel, group, count, local),
        grid=(count // group,),
        out_shape=(jax.ShapeDtypeStruct((tokens, width), BF16),) * count,
        in_specs=[
            pl.BlockSpec((local, group, capacity, units), lambda i: (0, i, 0, 0)),
            pl.BlockSpec((group, tokens, local), lambda i: (i, 0, 0)),
            pl.BlockSpec((group, tokens, share), lambda i: (i, 0, 0)),
            pl.BlockSpec((local, units, width), lambda i: (0, 0, 0)),
            pl.BlockSpec((1, share, width), lambda i: (2, 0, 0)),
        ],
        out_specs=(pl.BlockSpec(memory_space=pl.ANY),) * count,
        scratch_shapes=[
            pltpu.VMEM((2, group, tokens, width), BF16),
            pltpu.VMEM((group, tokens, deep), BF16),
            pltpu.VMEM((group, deep, width), BF16),
            pltpu.SemaphoreType.DMA((2, group)),
        ],
        compiler_params=pltpu.CompilerParams(vmem_limit_bytes=VMEM_LIMIT),
        cost_estimate=pl.CostEstimate(
            flops=count * width // 8 * (local * capacity * (units + tokens) + tokens * share),
            bytes_accessed=2**20,
            transcendentals=0,
        ),
        name="run_outputs",
    )(act, slot_cols, sact, w_out, w_shared)


def assemble_kernel(plan, count, place_ref, *refs):
    block_refs, refs = refs[:count], refs[count:]
    out_refs, (low, wide, in_sems, out_sems) = refs[:-4], refs[-4:]
    place = place_ref[0]

    def load(j):
        return pltpu.make_async_copy(block_refs[j], low.at[j % 2], in_sems.at[j % 2])

    def stores(j):
        return [
            pltpu.make_async_copy(
                wide.at[j % 2, pl.ds(first, rows)],
                out_refs[which].at[
                    pl.ds(pl.multiple_of(base + (place ^ j) * rows, 8), rows),
                    pl.ds(column, wide.shape[2]),
                ],
                out_sems.at[j % 2, i],
            )
            for i, (which, first, rows, base, column) in enumerate(plan)
        ]

    load(0).start()
    for j in range(count):
        if j + 1 < count:
            load(j + 1).start()
        load(j).wait()
        if j >= 2:
            for copy in stores(j - 2):
                copy.wait()
        wide[j % 2] = low[j % 2].astype(F32)
        for copy in stores(j):
            copy.start()
    for j in range(max(0, count - 2), count):
        for copy in stores(j):
            copy.wait()


def assemble(place, blocks, shapes, plan):
    count = len(blocks)
    rows, width = blocks[0].shape
    any_spec = pl.BlockSpec(memory_space=pl.ANY)
    return pl.pallas_call(
        functools.partial(assemble_kernel, plan, count),
        out_shape=[jax.ShapeDtypeStruct(shape, F32) for shape in shapes],
        in_specs=[pl.BlockSpec(memory_space=pltpu.SMEM)] + [any_spec] * count,
        out_specs=[any_spec] * len(shapes),
        scratch_shapes=[
            pltpu.VMEM((2, rows, width), BF16),
            pltpu.VMEM((2, rows, width), F32),
            pltpu.SemaphoreType.DMA((2,)),
            pltpu.SemaphoreType.DMA((2, len(plan))),
        ],
        compiler_params=pltpu.CompilerParams(vmem_limit_bytes=VMEM_LIMIT),
        cost_estimate=pl.CostEstimate(flops=0, bytes_accessed=2**20, transcendentals=0),
        name="assemble",
    )(place.reshape(1), *blocks)


def shared_grads_kernel(count, place_ref, *refs):
    x_refs, g_all, refs = refs[:count], refs[count], refs[count + 1 :]
    (sact, sdpair, dl, grads_ref, router_ref, xs, gs, grads, router, sems) = refs
    at = pl.program_id(0)
    slot = lax.rem(at, 2)

    def load(j, into):
        return (
            pltpu.make_async_copy(x_refs[j], xs.at[into], sems.at[0, into]),
            pltpu.make_async_copy(g_all.at[place_ref[0] ^ j], gs.at[into], sems.at[1, into]),
        )

    @pl.when(at == 0)
    def _():
        for copy in load(0, 0):
            copy.start()
        grads[...] = jnp.zeros_like(grads)
        router[...] = jnp.zeros_like(router)

    for j in range(1, count):

        @pl.when(at == j - 1)
        def _():
            for copy in load(j, j % 2):
                copy.start()

    for copy in load(0, slot):
        copy.wait()
    x, g = xs[slot], gs[slot]
    grads[0] += dot(sdpair[0, 0], x, TN)
    grads[1] += dot(sdpair[0, 1], x, TN)
    grads[2] += dot(sact[0], g, TN)
    router[...] += dot(dl[0], x, TN)

    @pl.when(at == count - 1)
    def _():
        grads_ref[...] = grads[...].astype(BF16)
        router_ref[...] = router[...]


def shared_grads(place, x_blocks, g_all, sact, sdpair, dl):
    count = len(x_blocks)
    tokens, width = x_blocks[0].shape
    share, padded = sact.shape[2], dl.shape[2]
    any_spec = pl.BlockSpec(memory_space=pl.ANY)
    return pl.pallas_call(
        functools.partial(shared_grads_kernel, count),
        grid=(count,),
        out_shape=(
            jax.ShapeDtypeStruct((3, share, width), BF16),
            jax.ShapeDtypeStruct((padded, width), F32),
        ),
        in_specs=[pl.BlockSpec(memory_space=pltpu.SMEM)]
        + [any_spec] * (count + 1)
        + [
            pl.BlockSpec((1, tokens, share), lambda j: (j, 0, 0)),
            pl.BlockSpec((1, 2, tokens, share), lambda j: (j, 0, 0, 0)),
            pl.BlockSpec((1, tokens, padded), lambda j: (j, 0, 0)),
        ],
        out_specs=(
            pl.BlockSpec((3, share, width), lambda j: (0, 0, 0)),
            pl.BlockSpec((padded, width), lambda j: (0, 0)),
        ),
        scratch_shapes=[
            pltpu.VMEM((2, tokens, width), BF16),
            pltpu.VMEM((2, tokens, width), BF16),
            pltpu.VMEM((3, share, width), F32),
            pltpu.VMEM((padded, width), F32),
            pltpu.SemaphoreType.DMA((2, 2)),
        ],
        compiler_params=pltpu.CompilerParams(vmem_limit_bytes=VMEM_LIMIT),
        cost_estimate=pl.CostEstimate(
            flops=count * tokens * width * share,
            bytes_accessed=2**20,
            transcendentals=0,
        ),
        name="shared_grads",
    )(place.reshape(1), *x_blocks, g_all, sact, sdpair, dl)


def on_device(
    hidden_in,
    cotangent,
    gain_attn,
    qkv_weight,
    qkv_bias,
    out_weight,
    gain_ffn,
    router_weight,
    routes,
    shared_gate,
    shared_in,
    shared_out,
    expert_in,
    expert_out,
):
    tokens, width = hidden_in.shape
    ctx_count = lax.axis_size("ctx")
    heads_local = qkv_weight.shape[2] // HD
    local = expert_in.shape[0]
    experts = local * ctx_count
    top_count = routes.shape[1]
    capacity = 3 * tokens * top_count // (2 * experts)
    place = lax.axis_index("ctx")
    order = jnp.arange(ctx_count, dtype=jnp.int32) ^ place
    score_scale = 1.0 / math.sqrt(HD)
    query_pos = place * tokens + jnp.arange(tokens, dtype=jnp.int32)
    cosine, sine = rotary_tables(query_pos, HD)

    x_full = hidden_in.astype(F32)
    inv_one = lax.rsqrt(jnp.mean(x_full * x_full, axis=-1, keepdims=True) + EPS)
    normed_one = x_full * inv_one
    x_one = (normed_one * gain_attn).astype(BF16)
    projected = (
        jnp.einsum("td,dcf->ctf", x_one, qkv_weight, preferred_element_type=F32)
        + qkv_bias[:, None]
    )
    shaped = projected.reshape(3, tokens, heads_local, HD).transpose(0, 2, 1, 3)
    query = rotate(shaped[0], cosine, sine).astype(BF16)
    key_local = rotate(shaped[1], cosine, sine).astype(BF16)
    value_local = shaped[2].astype(BF16)
    kv_rows = heads_local * tokens
    route_rows = -(-tokens * top_count // HD)
    behind = jnp.pad(
        routes.T.astype(BF16).reshape(route_rows, HD), ((0, -route_rows % 16), (0, 0))
    )
    kv_local = jnp.stack(
        [
            jnp.concatenate([key_local.reshape(kv_rows, HD), behind], axis=0),
            jnp.concatenate([value_local.reshape(kv_rows, HD), behind], axis=0),
        ]
    )
    kv_got = gather_start(kv_local)
    kv_blocks = gather_end(kv_got)
    hops = kv_got[2:4] if ctx_count == 8 else [kv_local]
    g_all = lax.all_gather(after(cotangent, *hops), "ctx", axis=0)

    share = shared_out.shape[0] // ctx_count
    piece = shared_out.shape[1]
    shared_send = jnp.concatenate(
        [
            shared_in.transpose(1, 2, 0).reshape(2, ctx_count, share, piece),
            shared_out.reshape(1, ctx_count, share, piece),
        ],
        axis=0,
    ).transpose(1, 0, 2, 3)
    shared_w = (
        lax.all_to_all(shared_send, "ctx", split_axis=0, concat_axis=0, tiled=True)
        .transpose(1, 2, 0, 3)
        .reshape(3, share, width)
    )
    whole_share = -(-share // 16) * 16
    if whole_share > share:
        shared_w = jnp.pad(shared_w, ((0, 0), (0, whole_share - share), (0, 0)))
    half_rows = out_weight.shape[0] // 2
    core = place % 2
    out_mine = lax.all_gather(
        lax.dynamic_slice_in_dim(out_weight, core * half_rows, half_rows, 0), "tp", axis=0
    )

    routes_all = jnp.stack([b[0, kv_rows : kv_rows + route_rows] for b in kv_blocks])
    routes_all = routes_all.reshape(ctx_count, 1, top_count, tokens)
    own_experts = (place * local + jnp.arange(local, dtype=jnp.int32)).astype(BF16)
    hit = jnp.any(routes_all == own_experts[None, :, None, None], axis=2)
    token_at = jnp.arange(tokens, dtype=jnp.int32)
    earlier = (token_at[:, None] <= token_at[None, :]).astype(BF16)
    rank = dot(hit.astype(BF16).reshape(-1, tokens), earlier, NN).reshape(hit.shape) - 1.0
    slot_rows = jnp.where(hit, rank, -1.0).astype(jnp.int32)
    slot_cols = slot_rows.transpose(0, 2, 1)
    padded = -(-(experts + 1) // 8) * 8
    w_router = jnp.concatenate(
        [
            router_weight.T,
            shared_gate[None],
            jnp.zeros((padded - experts - 1, width), BF16),
        ],
        axis=0,
    )
    w_in = expert_in.transpose(0, 2, 3, 1)

    attended, lse = attend(place, after(query, shared_send), kv_blocks)
    att = attended.astype(BF16).transpose(1, 0, 2).reshape(tokens, heads_local * HD)
    att_all = jnp.concatenate(gather_tp(att), axis=1)
    out_mine = after(out_mine, attended)
    out_other = swap(out_mine, 1)
    out_full = arrange(place, out_mine, out_other)
    att_all = after(att_all, shared_w, slot_rows, slot_cols, w_router, w_in)
    hidden = x_full + dot(att_all, out_full, NN)
    inv_two = lax.rsqrt(jnp.mean(hidden * hidden, axis=-1, keepdims=True) + EPS)
    normed_two = hidden * inv_two
    x_two = (normed_two * gain_ffn).astype(BF16)

    units, group = expert_out.shape[1], 2
    kept = [
        jax.ShapeDtypeStruct(shape, BF16)
        for shape in (
            (local, ctx_count, capacity, width),
            (local, ctx_count, capacity, width),
            (local, ctx_count, capacity, units),
            (2 * local, ctx_count, capacity, units),
            (ctx_count, tokens, whole_share),
            (ctx_count, 2, tokens, whole_share),
            (ctx_count, tokens, padded),
        )
    ]
    weights = (w_router, w_in, expert_out, shared_w)
    got = gather_start(x_two)
    x_blocks = [got[0], got[1]]
    dxs = []
    early = None
    for at in range(0, ctx_count, group):
        if at == 4 and ctx_count == 8:
            pair_two = pair_sum(dxs, 2)
            early = (pair_two, pair_two[: tokens // 2].astype(BF16))
        if at == 6 and ctx_count == 8:
            x_blocks[6] = after(x_blocks[6], early[1])
        dx, kept = run_experts(
            at,
            experts,
            place,
            x_blocks[at : at + group],
            g_all,
            slot_rows,
            slot_cols,
            weights,
            kept,
        )
        dxs += dx
        if at == 0:
            x_blocks = x_blocks[:2] + gather_end(got, dx[0])[2:]
    grad_x_part = scatter_ctx(dxs, early)
    outs = run_outputs(kept[2], slot_cols, kept[4], expert_out, shared_w)
    grad_x_low = grad_x_part.astype(BF16)
    out_hops, out_stay = scatter_start(after(outs, grad_x_low))
    kept = after(kept, grad_x_low, outs[0])
    rows_x, rows_g, act_low, dpair, s_act, s_dpair, low_logits = kept
    shared_low, router_part = shared_grads(place, x_blocks, g_all, s_act, s_dpair, low_logits)
    expert_grads = grads_of_experts(rows_x, rows_g, act_low, dpair)
    grad_expert_in, grad_expert_out = expert_grads
    gain_ffn_part = jnp.sum(grad_x_part * normed_two, axis=0)
    small = jnp.concatenate([router_part, gain_ffn_part[None]], axis=0).astype(BF16)
    small_rows = padded + 1
    half = tokens // 2
    second = jnp.concatenate(
        [grad_x_low[half:], jnp.pad(small, ((0, -small_rows % 16), (0, 0)))], axis=0
    )
    first = lax.psum(grad_x_low[:half], "tp")
    out_part = scatter_end((out_hops, out_stay), first)
    second = lax.psum(after(second, first), "tp")
    small = second[half : half + small_rows].astype(F32)
    shared_back = lax.all_to_all(
        shared_low[:, :share].reshape(3, share, ctx_count, piece).transpose(2, 0, 1, 3),
        "ctx",
        split_axis=0,
        concat_axis=0,
        tiled=True,
    )
    summed = jnp.concatenate([first, second[:half]], axis=0)
    summed = after(summed, shared_back, *expert_grads, out_part)
    shared_back = shared_back.astype(F32)
    grad_shared_in = shared_back[:, :2].transpose(3, 1, 0, 2).reshape(shared_in.shape)
    grad_shared_out = shared_back[:, 2].reshape(shared_out.shape)

    summed = summed.astype(F32)
    grad_y = cotangent.astype(F32)
    grad_normed_two = summed * gain_ffn
    grad_hidden = grad_y + inv_two * (
        grad_normed_two
        - normed_two * jnp.mean(grad_normed_two * normed_two, axis=-1, keepdims=True)
    )
    grad_hidden_low = grad_hidden.astype(BF16)
    out_weight_part = dot(att, grad_hidden_low, (((0,), (0,)), ((), ())))
    grad_att = (
        dot(grad_hidden_low, out_weight, (((1,), (1,)), ((), ())))
        .astype(BF16)
        .reshape(tokens, heads_local, HD)
        .transpose(1, 0, 2)
    )
    delta = jnp.sum(grad_att.astype(F32) * attended, axis=-1)
    delta = jnp.broadcast_to(delta[:, None], lse.shape)
    grad_query, grad_pairs = attend_back(place, query, grad_att, lse, delta, kv_blocks)
    ffn_total = sum_tp_start(out_part)
    grad_pairs = after(grad_pairs, ffn_total)
    ffn_low = sum_tp_end(after(ffn_total, grad_query))
    grad_kv = scatter_ctx([grad_pairs[j] for j in range(ctx_count)])
    grad_kv = after(grad_kv, ffn_low)

    def raw_part(value):
        return value.astype(BF16).transpose(1, 0, 2).reshape(tokens, heads_local * HD)

    raw = [
        raw_part(rotate(grad_query, cosine, -sine)),
        raw_part(rotate(grad_kv[0], cosine, -sine)),
        raw_part(grad_kv[1]),
    ]
    grad_x_one_part = jnp.einsum(
        "tcf,dcf->td", jnp.stack(raw, axis=1), qkv_weight, preferred_element_type=F32
    )
    grad_x_low = grad_x_one_part.astype(BF16)
    half_way = sum_tp_start(grad_x_low)
    grad_x_one = sum_tp_end(half_way)
    x_one = after(x_one, grad_x_low)
    gain_attn_part = jnp.sum(grad_x_one_part * normed_one, axis=0)
    gain_sum = sum_tp_small(gain_attn_part[None])
    head_width = heads_local * HD
    gain_rows = width // head_width
    ends = jnp.concatenate(
        [jnp.sum(r.astype(F32), axis=0)[None] for r in raw]
        + [gain_sum.reshape(gain_rows, -1), small.reshape((padded + 1) * gain_rows, -1)],
        axis=0,
    )
    ends = jnp.pad(ends, ((0, -ends.shape[0] % (16 * ctx_count)), (0, 0))).astype(BF16)
    query_part = after(dot(x_one, raw[0], TN).astype(BF16), grad_kv)
    pair_part = jnp.concatenate([dot(x_one, raw[1], TN), dot(x_one, raw[2], TN)], axis=0).astype(BF16)
    turns = width // head_width
    out_shards = [
        jnp.concatenate([s[:, k * head_width : (k + 1) * head_width] for k in range(turns)], axis=0)
        for s in shards(out_weight_part.astype(BF16))
    ]
    sums = sum_ctx(
        [
            jnp.concatenate(list(parts), axis=0)
            for parts in zip(shards(query_part), shards(pair_part), out_shards, shards(ends))
        ],
        half_way,
    )
    q_rows = width // ctx_count
    out_rows = out_weight.shape[0] // ctx_count
    plan = [(0, 0, q_rows, 0, 0), (0, q_rows, 2 * q_rows, width, 0)] + [
        (1, 3 * q_rows + k * out_rows, out_rows, 0, k * head_width) for k in range(turns)
    ]
    qkv_grad, out_weight_grad = assemble(
        place, sums, [(3 * width, head_width), out_weight.shape], plan
    )
    qkv_grad = qkv_grad.reshape(3, width, head_width).transpose(1, 0, 2)
    ends = relative(jnp.stack([b[3 * q_rows + turns * out_rows :] for b in sums]))
    ends = ends.reshape(-1, head_width).astype(F32)
    small = ends[3 + gain_rows : 3 + (padded + 2) * gain_rows].reshape(padded + 1, width)
    grad_x_one = after(grad_x_one, sums[2]).astype(F32)
    grad_normed_one = grad_x_one * gain_attn
    grad_input = grad_hidden + inv_one * (
        grad_normed_one
        - normed_one * jnp.mean(grad_normed_one * normed_one, axis=-1, keepdims=True)
    )
    block_out = (hidden + ffn_low.astype(F32)).astype(BF16)
    return (
        block_out,
        grad_input,
        ends[3 : 3 + gain_rows].reshape(-1),
        qkv_grad,
        ends[:3],
        out_weight_grad,
        small[padded],
        small[:experts].T,
        small[experts],
        grad_shared_in,
        grad_shared_out,
        grad_expert_in.transpose(0, 3, 1, 2),
        grad_expert_out,
    )


def solution(mesh):
    return jax.shard_map(
        on_device,
        mesh=mesh,
        in_specs=(
            P("ctx", None),
            P("ctx", None),
            P(),
            P(None, None, "tp"),
            P(None, "tp"),
            P("tp", None),
            P(),
            P(),
            P("ctx", None),
            P(),
            P("ctx", None, "tp"),
            P("tp", "ctx"),
            P("ctx", None, None, "tp"),
            P("ctx", "tp", None),
        ),
        out_specs=(
            P("ctx", None),
            P("ctx", None),
            P(),
            P(None, None, "tp"),
            P(None, "tp"),
            P("tp", None),
            P(),
            P(),
            P(),
            P("ctx", None, "tp"),
            P("tp", "ctx"),
            P("ctx", None, None, "tp"),
            P("ctx", "tp", None),
        ),
        check_vma=False,
    )
```

```python
import functools
import math

import jax
import jax.numpy as jnp
from jax import lax
from jax.experimental import pallas as pl
from jax.experimental.pallas import tpu as pltpu
from jax.sharding import PartitionSpec as P

HD = 128
EPS = 1e-06
THETA = 1000000.0
NEG = -1e30
F32 = jnp.float32
BF16 = jnp.bfloat16


def rotary_tables(positions, width):
    half_width = width // 2
    freqs = THETA ** (-(jnp.arange(half_width, dtype=F32) * 2.0) / width)
    angles = positions.astype(F32)[:, None] * freqs[None, :]
    return (jnp.cos(angles), jnp.sin(angles))


def rotate(values, cosine, sine):
    half_width = values.shape[-1] // 2
    first, second = values[..., :half_width], values[..., half_width:]
    return jnp.concatenate(
        [first * cosine - second * sine, second * cosine + first * sine], axis=-1
    )


def dot(a, b, dims):
    return lax.dot_general(a, b, dims, preferred_element_type=F32)


def swap(value, bits):
    count = lax.axis_size("ctx")
    return lax.ppermute(value, "ctx", [(i, i ^ bits) for i in range(count)])


def relative(natural):
    count = natural.shape[0]
    order = jnp.arange(count, dtype=jnp.int32) ^ lax.axis_index("ctx")
    return natural[order]


def nothing_kernel(*refs):
    pass


def after(values, *others):
    single = not isinstance(values, (list, tuple))
    values = [values] if single else list(values)
    any_spec = pl.BlockSpec(memory_space=pl.ANY)
    results = pl.pallas_call(
        nothing_kernel,
        out_shape=[jax.ShapeDtypeStruct(v.shape, v.dtype) for v in values],
        in_specs=[any_spec] * (len(values) + len(others)),
        out_specs=[any_spec] * len(values),
        input_output_aliases={i: i for i in range(len(values))},
        name="after",
    )(*values, *others)
    return results[0] if single else results


def gather_start(own):
    if lax.axis_size("ctx") != 8:
        return relative(lax.all_gather(own, "ctx", axis=0))
    return [own, swap(own, 1), swap(own, 2), swap(own, 4)]


def gather_end(got, *others):
    if lax.axis_size("ctx") != 8:
        return [got[j] for j in range(lax.axis_size("ctx"))]
    own, b1, b2, b4 = got
    if others:
        b2, b4 = after((b2, b4), *others)
    half = own.shape[0] // 2
    via_x, via_y = swap(b4[:half], 2), swap(b2[half:], 4)
    b3, b5 = swap(b2, 1), swap(b4, 1)
    b6 = jnp.concatenate([via_x, via_y], axis=0)
    return [own, b1, b2, b3, b4, b5, b6, swap(b6, 1)]


def gather_ctx(own, *others):
    return gather_end(gather_start(own), *others)


def pair_sum(parts, j):
    return parts[j].astype(F32) + swap(parts[j ^ 1], 1).astype(F32)


def scatter_ctx(parts, early=None):
    return scatter_end(scatter_start(parts, early))


def scatter_start(parts, early=None):
    if lax.axis_size("ctx") != 8:
        return [jnp.stack(parts)], None
    half = parts[0].shape[0] // 2
    pair = {j: pair_sum(parts, j) for j in (2, 4, 6, 0) if j != 2 or early is None}
    if early is None:
        early = (pair[2], pair[2][:half].astype(BF16))
    q6 = pair[6].astype(BF16)
    hops = [early[1], pair[4][half:].astype(BF16), q6[:half], q6[half:]]
    return hops, (early[0], pair[4], pair[0])


def scatter_end(started, *others):
    hops, stay = started
    if lax.axis_size("ctx") != 8:
        natural = relative(hops[0])
        flat = natural.reshape((-1,) + natural.shape[2:])
        return lax.psum_scatter(flat, "ctx", scatter_dimension=0, tiled=True).astype(F32)
    two, four, zero = stay
    half = two.shape[0] // 2
    r2, r4 = swap(hops[0], 2), swap(hops[1], 4)
    via_x, via_y = swap(hops[2], 2), swap(hops[3], 4)
    r4a = (four[:half] + via_x.astype(F32)).astype(BF16)
    r2b = (two[half:] + via_y.astype(F32)).astype(BF16)
    if others:
        r4a, r2b = after((r4a, r2b), *others)
    r4a, r2b = swap(r4a, 4), swap(r2b, 2)
    low = r2.astype(F32) + r4a.astype(F32)
    high = r2b.astype(F32) + r4.astype(F32)
    return zero + jnp.concatenate([low, high], axis=0)


def sum_ctx(parts, *others):
    return gather_ctx(scatter_end(scatter_start(parts), *others).astype(BF16))


def shards(value):
    count = lax.axis_size("ctx")
    rows = value.shape[0] // count
    place = lax.axis_index("ctx")
    return [lax.dynamic_slice_in_dim(value, (place ^ j) * rows, rows, 0) for j in range(count)]


def gather_tp(own):
    count = lax.axis_size("tp")
    return [own] + [
        lax.ppermute(own, "tp", [(i, i ^ k) for i in range(count)]) for k in range(1, count)
    ]


NT = (((1,), (1,)), ((), ()))
NN = (((1,), (0,)), ((), ()))
TN = (((0,), (0,)), ((), ()))
VMEM_LIMIT = 60 * 1024 * 1024


def sum_tp_start(value):
    pieces = value.astype(BF16).reshape(lax.axis_size("tp"), -1, value.shape[1])
    got = lax.all_to_all(pieces, "tp", split_axis=0, concat_axis=0, tiled=True)
    return jnp.sum(got.astype(F32), axis=0).astype(BF16)


def sum_tp_end(total):
    count, at = lax.axis_size("tp"), lax.axis_index("tp")
    blocks = jnp.stack(gather_tp(total))
    blocks = blocks[jnp.arange(count, dtype=jnp.int32) ^ at]
    return blocks.reshape(-1, total.shape[1])


def sum_tp_small(value):
    count, bits = lax.axis_size("tp"), 1
    while bits < count:
        value = value + lax.ppermute(value, "tp", [(i, i ^ bits) for i in range(count)])
        bits *= 2
    return value


def arrange_kernel(places, mine, other, out):
    @pl.when(pl.program_id(1) == 0)
    def _():
        out[0, 0] = mine[0]

    @pl.when(pl.program_id(1) == 1)
    def _():
        out[0, 0] = other[0]


def arrange(place, mine, other):
    count, rows, width = mine.shape
    places = jnp.stack([place % 2, lax.axis_index("tp")])
    return pl.pallas_call(
        arrange_kernel,
        grid_spec=pltpu.PrefetchScalarGridSpec(
            num_scalar_prefetch=1,
            grid=(count, 2),
            in_specs=[pl.BlockSpec((1, rows, width), lambda k, i, p: (p[1] ^ k, 0, 0))] * 2,
            out_specs=pl.BlockSpec((1, 1, rows, width), lambda k, i, p: (k, p[0] ^ i, 0, 0)),
        ),
        out_shape=jax.ShapeDtypeStruct((count, 2, rows, width), mine.dtype),
        compiler_params=pltpu.CompilerParams(vmem_limit_bytes=VMEM_LIMIT),
        cost_estimate=pl.CostEstimate(flops=0, bytes_accessed=2**20, transcendentals=0),
        name="arrange",
    )(places, mine, other).reshape(-1, width)


def attend_kernel(factor, count, place_ref, q_ref, *refs):
    kv_refs, (att_ref, lse_ref, kv, sems) = refs[:count], refs[count:]
    rows = kv.shape[2]
    copies = [
        pltpu.make_async_copy(kv_refs[j].at[:, pl.ds(0, rows)], kv.at[j], sems.at[j])
        for j in range(count)
    ]
    for copy in copies:
        copy.start()
    for copy in copies:
        copy.wait()
    place = place_ref[0]
    heads, tokens, _ = q_ref.shape

    def one_head(head, _):
        query = q_ref[head]
        here = pl.ds(pl.multiple_of(head * tokens, tokens), tokens)

        def scores(j):
            return dot(kv[j, 0, here], query, NT) * factor

        key_at = lax.broadcasted_iota(jnp.int32, (tokens, tokens), 0)
        query_at = lax.broadcasted_iota(jnp.int32, (tokens, tokens), 1)
        first = jnp.where(key_at <= query_at, scores(0), NEG)
        top = jnp.max(first, axis=0, keepdims=True)
        exps = jnp.exp2(first - top)
        total = jnp.sum(exps, axis=0, keepdims=True)
        acc = dot(kv[0, 1, here], exps.astype(BF16), TN)

        def earlier(i, carry):
            top, total, acc = carry
            j = place ^ i
            now = scores(j)
            higher = jnp.maximum(top, jnp.max(now, axis=0, keepdims=True))
            exps = jnp.exp2(now - higher)
            keep = jnp.exp2(top - higher)
            total = total * keep + jnp.sum(exps, axis=0, keepdims=True)
            acc = acc * keep + dot(kv[j, 1, here], exps.astype(BF16), TN)
            return higher, total, acc

        top, total, acc = lax.fori_loop(0, place, earlier, (top, total, acc))
        att_ref[head] = (acc / total).T
        lse_ref[head] = jnp.broadcast_to(top + jnp.log2(total), lse_ref.shape[1:])
        return 0

    lax.fori_loop(0, heads, one_head, 0)


def attend(place, query, kv_blocks):
    heads, tokens, size = query.shape
    count = len(kv_blocks)
    factor = math.log2(math.e) / math.sqrt(size)
    flops = 4 * count * heads * tokens * tokens * size
    return pl.pallas_call(
        functools.partial(attend_kernel, factor, count),
        out_shape=(
            jax.ShapeDtypeStruct((heads, tokens, size), F32),
            jax.ShapeDtypeStruct((heads, 8, tokens), F32),
        ),
        in_specs=[
            pl.BlockSpec(memory_space=pltpu.SMEM),
            pl.BlockSpec(memory_space=pltpu.VMEM),
        ]
        + [pl.BlockSpec(memory_space=pl.ANY)] * count,
        out_specs=(pl.BlockSpec(memory_space=pltpu.VMEM),) * 2,
        scratch_shapes=[
            pltpu.VMEM((count, 2, heads * tokens, size), BF16),
            pltpu.SemaphoreType.DMA((count,)),
        ],
        compiler_params=pltpu.CompilerParams(vmem_limit_bytes=VMEM_LIMIT),
        cost_estimate=pl.CostEstimate(
            flops=flops // 16, bytes_accessed=2**20, transcendentals=0
        ),
        name="attend",
    )(place.reshape(1), query, *kv_blocks)


def attend_back_kernel(factor, scale, count, place_ref, q_ref, do_ref, lse_ref, delta_ref, *refs):
    kv_refs, (dq_ref, dkv_ref, kv, dkv, dq, sems, out_sems) = refs[:count], refs[count:]
    rows = kv.shape[2]
    copies = [
        pltpu.make_async_copy(kv_refs[j].at[:, pl.ds(0, rows)], kv.at[j], sems.at[j])
        for j in range(count)
    ]
    for copy in copies:
        copy.start()
    for copy in copies:
        copy.wait()
    place = place_ref[0]
    heads, tokens, _ = q_ref.shape

    def out_copy(j):
        return pltpu.make_async_copy(dkv.at[j], dkv_ref.at[j], out_sems.at[j])

    def one_block(j, masked):
        def one_head(head, _):
            query, do = q_ref[head], do_ref[head]
            here = pl.ds(pl.multiple_of(head * tokens, tokens), tokens)
            key, value = kv[j, 0, here], kv[j, 1, here]
            scores = dot(key, query, NT) * factor
            probs = jnp.exp2(scores - lse_ref[head, :1])
            if masked:
                key_at = lax.broadcasted_iota(jnp.int32, (tokens, tokens), 0)
                query_at = lax.broadcasted_iota(jnp.int32, (tokens, tokens), 1)
                probs = jnp.where(key_at <= query_at, probs, 0.0)
            dprob = dot(value, do, NT)
            dscore = (probs * (dprob - delta_ref[head, :1])).astype(BF16)
            dkv[j, 0, head] = (dot(dscore, query, NN) * scale).astype(BF16)
            dkv[j, 1, head] = dot(probs.astype(BF16), do, NN).astype(BF16)
            part = dot(key, dscore, TN)
            dq[head] = part if masked else dq[head] + part
            return 0

        lax.fori_loop(0, heads, one_head, 0)
        out_copy(j).start()

    one_block(0, True)

    def earlier(i, _):
        one_block(place ^ i, False)
        return 0

    def later(i, _):
        j = place ^ i
        dkv[j] = jnp.zeros(dkv.shape[1:], BF16)
        out_copy(j).start()
        return 0

    lax.fori_loop(0, place, earlier, 0)
    lax.fori_loop(place + 1, count, later, 0)
    for head in range(heads):
        dq_ref[head] = dq[head].T * scale
    for j in range(count):
        out_copy(j).wait()


def attend_back(place, query, do, lse, delta, kv_blocks):
    heads, tokens, size = query.shape
    count = len(kv_blocks)
    scale = 1.0 / math.sqrt(size)
    factor = math.log2(math.e) * scale
    return pl.pallas_call(
        functools.partial(attend_back_kernel, factor, scale, count),
        out_shape=(
            jax.ShapeDtypeStruct((heads, tokens, size), F32),
            jax.ShapeDtypeStruct((count, 2, heads, tokens, size), BF16),
        ),
        in_specs=[pl.BlockSpec(memory_space=pltpu.SMEM)]
        + [pl.BlockSpec(memory_space=pltpu.VMEM)] * 4
        + [pl.BlockSpec(memory_space=pl.ANY)] * count,
        out_specs=(pl.BlockSpec(memory_space=pltpu.VMEM), pl.BlockSpec(memory_space=pl.ANY)),
        scratch_shapes=[
            pltpu.VMEM((count, 2, heads * tokens, size), BF16),
            pltpu.VMEM((count, 2, heads, tokens, size), BF16),
            pltpu.VMEM((heads, size, tokens), F32),
            pltpu.SemaphoreType.DMA((count,)),
            pltpu.SemaphoreType.DMA((count,)),
        ],
        compiler_params=pltpu.CompilerParams(vmem_limit_bytes=VMEM_LIMIT),
        cost_estimate=pl.CostEstimate(
            flops=count * heads * tokens * tokens * size,
            bytes_accessed=2**20,
            transcendentals=0,
        ),
        name="attend_back",
    )(place.reshape(1), query, do, lse, delta, *kv_blocks)


def swiglu_back(one, two, dact, gate):
    sig = 1.0 / (1.0 + jnp.exp(-one))
    silu = one * sig
    act = silu * two
    prod = act * dact
    dgate = gate * dact
    d_one = (dgate * two * sig * (1.0 + one * (1.0 - sig))).astype(BF16)
    d_two = (dgate * silu).astype(BF16)
    return (gate * act).astype(BF16), d_one, d_two, prod


def experts_kernel(at, group, local, experts, given, place_ref, *refs):
    x_refs, g_all, refs = refs[:group], refs[group], refs[group + 1 :]
    (slot_row, slot_col, w_router, w_in, w_out, w_shared), refs = refs[:6], refs[6 + given :]
    dx_refs, refs = refs[:group], refs[group:]
    kept_refs, refs = refs[:7], refs[7:]
    (xs, gs, first_w, in_w, out_w, shared_w, dxs, left, right, sems, out_sems), stage = refs[:11], refs[11:]
    rows_x, rows_g, act_s, dpair_s, sact_s, sdpair_s, dl_s = stage
    tokens, width = xs.shape[1:]
    capacity, units = act_s.shape[2:]
    wide = local * capacity
    share = sact_s.shape[2]
    third = first_w.shape[0] - 128
    second = third // 2
    padded = w_router.shape[0]
    most = out_w.shape[1]

    loads = [pltpu.make_async_copy(x_refs[b], xs.at[b], sems.at[b]) for b in range(group)]
    fore_loads = [
        pltpu.make_async_copy(
            w_shared.at[c], first_w.at[pl.ds(c * second, share)], sems.at[2 * group + c]
        )
        for c in range(2)
    ]
    loads += [
        pltpu.make_async_copy(g_all.at[place_ref[0] ^ (at + b)], gs.at[b], sems.at[group + b])
        for b in range(group)
    ]
    base = 2 * group + 2
    more = [
        [
            pltpu.make_async_copy(
                w_in.at[e, c], in_w.at[e, pl.ds(c * most, units)], sems.at[base + 3 * e + c]
            )
            for c in range(2)
        ]
        + [
            pltpu.make_async_copy(
                w_out.at[e], out_w.at[e, pl.ds(0, units)], sems.at[base + 3 * e + 2]
            )
        ]
        for e in range(local)
    ]
    last = pltpu.make_async_copy(w_shared.at[2], shared_w, sems.at[base + 3 * local])
    for copy in loads[:group] + fore_loads:
        copy.start()
    first_w[third : third + padded] = w_router[...]
    first_w[third + padded :] = jnp.zeros((128 - padded, width), BF16)
    if second > share:
        for c in range(2):
            gap = jnp.zeros((second - share, width), BF16)
            first_w[c * second + share : (c + 1) * second] = gap
    if most > units:
        gap = jnp.zeros((most - units, width), BF16)
        for e in range(local):
            in_w[e, units:most] = gap
            in_w[e, most + units :] = gap
            out_w[e, units:] = gap

    sent = []

    def send(copy):
        copy.start()
        sent.append(copy)

    for copy in loads[:group] + fore_loads:
        copy.wait()
    for copy in loads[group:] + more[0]:
        copy.start()
    x = xs[...].reshape(group * tokens, width)
    fore = dot(x, first_w[...], NT)
    s_one, s_two = fore[:, :share], fore[:, second : second + share]
    s_gate = 1.0 / (1.0 + jnp.exp(-fore[:, third + experts : third + experts + 1]))
    row_at = lax.broadcasted_iota(jnp.int32, (padded, tokens), 0)
    slot_at = lax.broadcasted_iota(jnp.int32, (capacity, tokens), 0)
    probs, change, hits = [], [], []
    for b in range(group):
        logits = fore[b * tokens : (b + 1) * tokens, third:].T[:padded]
        shown = jnp.where(row_at < experts, logits, NEG)
        exps = jnp.exp(shown - jnp.max(shown, axis=0, keepdims=True))
        soft = exps / jnp.sum(exps, axis=0, keepdims=True)
        probs.append(jnp.where(row_at == experts, 1.0 / (1.0 + jnp.exp(-logits)), soft))
        change.append(jnp.zeros((padded, tokens), F32))
        picks = jnp.concatenate(
            [
                jnp.where(slot_at == slot_row[b, e : e + 1, :], 1.0, 0.0).astype(BF16)
                for e in range(local)
            ],
            axis=0,
        )
        rows = dot(picks, xs[b], NN).astype(BF16)
        for e in range(local):
            rows_x[e, b] = rows[e * capacity : (e + 1) * capacity]
        loads[group + b].wait()
        if b == group - 1:
            for e in range(1, local):
                for copy in more[e]:
                    copy.start()
            last.start()
        rows = dot(picks, gs[b], NN).astype(BF16)
        for e in range(local):
            rows_g[e, b] = rows[e * capacity : (e + 1) * capacity]
    def send_all(i, lead):
        for e in range(lead):
            send(
                pltpu.make_async_copy(
                    stage[i].at[e], kept_refs[i].at[e, pl.ds(at, group)], out_sems.at[i, e]
                )
            )

    send_all(0, local)
    send_all(1, local)
    is_expert = row_at < experts
    for e in range(local):
        chosen = row_at == place_ref[0] * local + e
        gates, owns, hits = [], [], []
        for b in range(group):
            own = jnp.sum(jnp.where(chosen, probs[b], 0.0), axis=0, keepdims=True)
            hit = slot_at == slot_row[b, e : e + 1, :]
            gates.append(jnp.sum(jnp.where(hit, own, 0.0), axis=1, keepdims=True))
            owns.append(own)
            hits.append(hit)
        for copy in more[e]:
            copy.wait()
        pair = dot(rows_x[e].reshape(group * capacity, width), in_w[e], NT)
        dact = dot(rows_g[e].reshape(group * capacity, width), out_w[e], NT)
        act, d_one, d_two, prod = swiglu_back(
            pair[:, :most], pair[:, most:], dact, jnp.concatenate(gates, axis=0)
        )
        act_s[e] = act[:, :units].reshape(group, capacity, units)
        dpair_s[2 * e] = d_one[:, :units].reshape(group, capacity, units)
        dpair_s[2 * e + 1] = d_two[:, :units].reshape(group, capacity, units)
        row_dot = jnp.sum(prod, axis=1, keepdims=True)
        drow = dot(jnp.concatenate([d_one, d_two], axis=1), in_w[e], NN).astype(BF16)
        for b in range(group):
            rows = slice(b * capacity, (b + 1) * capacity)
            found = jnp.sum(jnp.where(hits[b], row_dot[rows], 0.0), axis=0, keepdims=True)
            change[b] += (found * owns[b]) * (
                jnp.where(chosen, 1.0, 0.0) - jnp.where(is_expert, probs[b], 0.0)
            )
            right[b, e * capacity : (e + 1) * capacity] = drow[rows]
    send_all(2, local)
    send_all(3, 2 * local)
    last.wait()
    g = gs[...].reshape(group * tokens, width)
    s_dact = dot(g, shared_w[...], NT)
    act, d_one, d_two, prod = swiglu_back(s_one, s_two, s_dact, s_gate)
    sact_s[...] = act.reshape(group, tokens, share)
    sdpair_s[:, 0] = d_one.reshape(group, tokens, share)
    sdpair_s[:, 1] = d_two.reshape(group, tokens, share)
    dslogit = jnp.sum(prod, axis=1, keepdims=True) * s_gate * (1.0 - s_gate)
    lane_at = lax.broadcasted_iota(jnp.int32, (tokens, 128), 1)
    rest = jnp.zeros((128 - padded, tokens), F32)
    deep = wide + 2 * share
    column_at = lax.broadcasted_iota(jnp.int32, (tokens, capacity), 1)
    stores = []
    for b in range(group):
        rows = slice(b * tokens, (b + 1) * tokens)
        columns = jnp.concatenate([change[b], rest], axis=0).T
        columns = jnp.where(lane_at == experts, dslogit[rows], columns)[:, :padded].astype(BF16)
        dl_s[b] = columns
        left[b, :, deep : deep + padded] = columns
        right[b, deep : deep + padded] = w_router[...]
        for e in range(local):
            picks = jnp.where(column_at == slot_col[b, :, e : e + 1], 1.0, 0.0).astype(BF16)
            left[b, :, e * capacity : (e + 1) * capacity] = picks
        left[b, :, wide : wide + share] = d_one[rows]
        left[b, :, wide + share : wide + 2 * share] = d_two[rows]
        right[b, wide : wide + share] = first_w[:share]
        right[b, wide + share : wide + 2 * share] = first_w[second : second + share]
        dxs[b] = dot(left[b], right[b], NN).astype(BF16)
        send(pltpu.make_async_copy(dxs.at[b], dx_refs[b], out_sems.at[7, b]))
    for i in range(4, 7):
        send(pltpu.make_async_copy(stage[i], kept_refs[i].at[pl.ds(at, group)], out_sems.at[i, 0]))
    for copy in sent:
        copy.wait()


def run_experts(at, experts, place, x_group, g_all, slot_rows, slot_cols, weights, kept):
    given = kept if at else []
    group = len(x_group)
    tokens, width = x_group[0].shape
    w_router, w_in, w_out, w_shared = weights
    local = w_out.shape[0]
    share = w_shared.shape[1]
    padded = w_router.shape[0]
    capacity, units = kept[2].shape[2:]
    any_spec = pl.BlockSpec(memory_space=pl.ANY)
    block = jax.ShapeDtypeStruct((tokens, width), BF16)
    deep = local * capacity + 2 * share + padded
    flops = group * 2 * tokens * width * (local * capacity * 3 + 5 * share) + (
        group * 2 * width * local * capacity * units * 5
    )
    step = at // group
    wide_units = -(-units // 128) * 128
    fore = 2 * (-(-share // 64) * 64) + 128
    results = pl.pallas_call(
        functools.partial(experts_kernel, at, group, local, experts, len(given)),
        grid=(1,),
        out_shape=(block,) * group + tuple(jax.ShapeDtypeStruct(k.shape, k.dtype) for k in kept),
        in_specs=[pl.BlockSpec(memory_space=pltpu.SMEM)]
        + [any_spec] * (group + 1)
        + [
            pl.BlockSpec((group, local, tokens), lambda i: (step, 0, 0)),
            pl.BlockSpec((group, tokens, local), lambda i: (step, 0, 0)),
            pl.BlockSpec((padded, width), lambda i: (0, 0)),
        ]
        + [any_spec] * (3 + len(given)),
        out_specs=(any_spec,) * (group + len(kept)),
        input_output_aliases={8 + group + i: group + i for i in range(len(given))},
        scratch_shapes=[
            pltpu.VMEM((group, tokens, width), BF16),
            pltpu.VMEM((group, tokens, width), BF16),
            pltpu.VMEM((fore, width), BF16),
            pltpu.VMEM((local, 2 * wide_units, width), BF16),
            pltpu.VMEM((local, wide_units, width), BF16),
            pltpu.VMEM((share, width), BF16),
            pltpu.VMEM((group, tokens, width), BF16),
            pltpu.VMEM((group, tokens, deep), BF16),
            pltpu.VMEM((group, deep, width), BF16),
            pltpu.SemaphoreType.DMA((2 * group + 3 + 3 * local,)),
            pltpu.SemaphoreType.DMA((8, max(2 * local, group))),
        ]
        + [
            pltpu.VMEM(k.shape[:1] + (group,) + k.shape[2:], BF16) for k in kept[:4]
        ]
        + [pltpu.VMEM((group,) + k.shape[1:], BF16) for k in kept[4:]],
        compiler_params=pltpu.CompilerParams(vmem_limit_bytes=VMEM_LIMIT),
        cost_estimate=pl.CostEstimate(flops=flops // 16, bytes_accessed=2**20, transcendentals=0),
        name="run_experts",
    )(place.reshape(1), *x_group, g_all, slot_rows, slot_cols, *weights, *given)
    return results[:group], results[group:]


def outputs_kernel(group, count, local, act, slot_col, sact, w_out, w_shared, *refs):
    out_refs, (outs, left, right, sems) = refs[:count], refs[count:]
    step = pl.program_id(0)
    slot = lax.rem(step, 2)
    capacity, units = act.shape[2:]
    tokens, share = sact.shape[1:]
    wide = local * capacity

    def store(at, b, into):
        return pltpu.make_async_copy(outs.at[into, b], out_refs[at * group + b], sems.at[into, b])

    @pl.when(step >= 2)
    def _():
        for b in range(group):
            store(0, b, slot).wait()

    for e in range(local):
        rows = dot(act[e].reshape(group * capacity, units), w_out[e], NN).astype(BF16)
        for b in range(group):
            right[b, e * capacity : (e + 1) * capacity] = rows[b * capacity : (b + 1) * capacity]
    slot_at = lax.broadcasted_iota(jnp.int32, (tokens, capacity), 1)
    for b in range(group):
        for e in range(local):
            picks = jnp.where(slot_at == slot_col[b, :, e : e + 1], 1.0, 0.0).astype(BF16)
            left[b, :, e * capacity : (e + 1) * capacity] = picks
        left[b, :, wide : wide + share] = sact[b]
        right[b, wide : wide + share] = w_shared[0]
        outs[slot, b] = dot(left[b], right[b], NN).astype(BF16)
    for at in range(count // group):

        @pl.when(step == at)
        def _():
            for b in range(group):
                store(at, b, at % 2).start()

    @pl.when(step == count // group - 1)
    def _():
        for b in range(group):
            for into in range(2):
                store(0, b, into).wait()


def expert_grads_kernel(rows_x, rows_g, act, dpair, in_ref, out_ref):
    rows = rows_x.shape[1] * rows_x.shape[2]
    x = rows_x[0].reshape(rows, -1)
    for c in range(2):
        in_ref[0, c] = dot(dpair[c].reshape(rows, -1), x, TN)
    out_ref[0] = dot(act[0].reshape(rows, -1), rows_g[0].reshape(rows, -1), TN)


def grads_of_experts(rows_x, rows_g, act, dpair):
    local, count, capacity, width = rows_x.shape
    units = act.shape[3]
    tile = min(width, 1024)
    return pl.pallas_call(
        expert_grads_kernel,
        grid=(local, width // tile),
        out_shape=(
            jax.ShapeDtypeStruct((local, 2, units, width), F32),
            jax.ShapeDtypeStruct((local, units, width), F32),
        ),
        in_specs=[
            pl.BlockSpec((1, count, capacity, tile), lambda e, i: (e, 0, 0, i)),
            pl.BlockSpec((1, count, capacity, tile), lambda e, i: (e, 0, 0, i)),
            pl.BlockSpec((1, count, capacity, units), lambda e, i: (e, 0, 0, 0)),
            pl.BlockSpec((2, count, capacity, units), lambda e, i: (e, 0, 0, 0)),
        ],
        out_specs=(
            pl.BlockSpec((1, 2, units, tile), lambda e, i: (e, 0, 0, i)),
            pl.BlockSpec((1, units, tile), lambda e, i: (e, 0, i)),
        ),
        compiler_params=pltpu.CompilerParams(vmem_limit_bytes=VMEM_LIMIT),
        cost_estimate=pl.CostEstimate(flops=0, bytes_accessed=2**20, transcendentals=0),
        name="grads_of_experts",
    )(rows_x, rows_g, act, dpair)


def run_outputs(act, slot_cols, sact, w_out, w_shared):
    local, count, capacity, units = act.shape
    tokens, share = sact.shape[1:]
    width = w_out.shape[2]
    group = 2
    deep = local * capacity + share
    return pl.pallas_call(
        functools.partial(outputs_kernel, group, count, local),
        grid=(count // group,),
        out_shape=(jax.ShapeDtypeStruct((tokens, width), BF16),) * count,
        in_specs=[
            pl.BlockSpec((local, group, capacity, units), lambda i: (0, i, 0, 0)),
            pl.BlockSpec((group, tokens, local), lambda i: (i, 0, 0)),
            pl.BlockSpec((group, tokens, share), lambda i: (i, 0, 0)),
            pl.BlockSpec((local, units, width), lambda i: (0, 0, 0)),
            pl.BlockSpec((1, share, width), lambda i: (2, 0, 0)),
        ],
        out_specs=(pl.BlockSpec(memory_space=pl.ANY),) * count,
        scratch_shapes=[
            pltpu.VMEM((2, group, tokens, width), BF16),
            pltpu.VMEM((group, tokens, deep), BF16),
            pltpu.VMEM((group, deep, width), BF16),
            pltpu.SemaphoreType.DMA((2, group)),
        ],
        compiler_params=pltpu.CompilerParams(vmem_limit_bytes=VMEM_LIMIT),
        cost_estimate=pl.CostEstimate(
            flops=count * width // 8 * (local * capacity * (units + tokens) + tokens * share),
            bytes_accessed=2**20,
            transcendentals=0,
        ),
        name="run_outputs",
    )(act, slot_cols, sact, w_out, w_shared)


def weight_parts_kernel(count, place_ref, x, raw, out_part, ends, *refs):
    part_refs, (part, sems) = refs[:count], refs[count:]
    place = place_ref[0]
    width = part.shape[2]
    q_rows, out_rows, end_rows = x.shape[1] // count, out_part.shape[0] // count, ends.shape[0] // count

    def store(j):
        return pltpu.make_async_copy(part.at[j % 2], part_refs[j], sems.at[j % 2])

    for j in range(count):
        if j >= 2:
            store(j - 2).wait()
        to = place ^ j
        columns = x[:, pl.ds(pl.multiple_of(to * q_rows, q_rows), q_rows)]
        grad = dot(columns, raw[...], TN).astype(BF16)
        for c in range(3):
            part[j % 2, c * q_rows : (c + 1) * q_rows] = grad[:, c * width : (c + 1) * width]
        rows = out_part[pl.ds(pl.multiple_of(to * out_rows, out_rows), out_rows)]
        at = 3 * q_rows
        for k in range(out_part.shape[1] // width):
            part[j % 2, at : at + out_rows] = rows[:, k * width : (k + 1) * width]
            at += out_rows
        part[j % 2, at:] = ends[pl.ds(pl.multiple_of(to * end_rows, end_rows), end_rows)]
        store(j).start()
    for j in range(count - 2, count):
        store(j).wait()


def weight_parts(place, x, raw, out_part, ends, count):
    tokens, size = x.shape
    width = ends.shape[1]
    rows = (3 * size + out_part.size // width + ends.shape[0]) // count
    return pl.pallas_call(
        functools.partial(weight_parts_kernel, count),
        out_shape=[jax.ShapeDtypeStruct((rows, width), BF16)] * count,
        in_specs=[pl.BlockSpec(memory_space=pltpu.SMEM)]
        + [pl.BlockSpec(memory_space=pltpu.VMEM)] * 4,
        out_specs=[pl.BlockSpec(memory_space=pl.ANY)] * count,
        scratch_shapes=[
            pltpu.VMEM((2, rows, width), BF16),
            pltpu.SemaphoreType.DMA((2,)),
        ],
        compiler_params=pltpu.CompilerParams(vmem_limit_bytes=VMEM_LIMIT),
        cost_estimate=pl.CostEstimate(flops=0, bytes_accessed=2**20, transcendentals=0),
        name="weight_parts",
    )(place.reshape(1), x, raw, out_part, ends)


def assemble_kernel(plan, count, place_ref, *refs):
    block_refs, refs = refs[:count], refs[count:]
    out_refs, (low, wide, in_sems, out_sems) = refs[:-4], refs[-4:]
    place = place_ref[0]

    def load(j):
        return pltpu.make_async_copy(block_refs[j], low.at[j % 2], in_sems.at[j % 2])

    def stores(j):
        return [
            pltpu.make_async_copy(
                wide.at[j % 2, pl.ds(first, rows)],
                out_refs[which].at[
                    pl.ds(pl.multiple_of(base + (place ^ j) * rows, 8), rows),
                    pl.ds(column, wide.shape[2]),
                ],
                out_sems.at[j % 2, i],
            )
            for i, (which, first, rows, base, column) in enumerate(plan)
        ]

    load(0).start()
    for j in range(count):
        if j + 1 < count:
            load(j + 1).start()
        load(j).wait()
        if j >= 2:
            for copy in stores(j - 2):
                copy.wait()
        wide[j % 2] = low[j % 2].astype(F32)
        for copy in stores(j):
            copy.start()
    for j in range(max(0, count - 2), count):
        for copy in stores(j):
            copy.wait()


def assemble(place, blocks, shapes, plan):
    count = len(blocks)
    rows, width = blocks[0].shape
    any_spec = pl.BlockSpec(memory_space=pl.ANY)
    return pl.pallas_call(
        functools.partial(assemble_kernel, plan, count),
        out_shape=[jax.ShapeDtypeStruct(shape, F32) for shape in shapes],
        in_specs=[pl.BlockSpec(memory_space=pltpu.SMEM)] + [any_spec] * count,
        out_specs=[any_spec] * len(shapes),
        scratch_shapes=[
            pltpu.VMEM((2, rows, width), BF16),
            pltpu.VMEM((2, rows, width), F32),
            pltpu.SemaphoreType.DMA((2,)),
            pltpu.SemaphoreType.DMA((2, len(plan))),
        ],
        compiler_params=pltpu.CompilerParams(vmem_limit_bytes=VMEM_LIMIT),
        cost_estimate=pl.CostEstimate(flops=0, bytes_accessed=2**20, transcendentals=0),
        name="assemble",
    )(place.reshape(1), *blocks)


def shared_grads_kernel(count, place_ref, *refs):
    x_refs, g_all, refs = refs[:count], refs[count], refs[count + 1 :]
    (sact, sdpair, dl, grads_ref, router_ref, xs, gs, grads, router, sems) = refs
    at = pl.program_id(0)
    slot = lax.rem(at, 2)

    def load(j, into):
        return (
            pltpu.make_async_copy(x_refs[j], xs.at[into], sems.at[0, into]),
            pltpu.make_async_copy(g_all.at[place_ref[0] ^ j], gs.at[into], sems.at[1, into]),
        )

    @pl.when(at == 0)
    def _():
        for copy in load(0, 0):
            copy.start()
        grads[...] = jnp.zeros_like(grads)
        router[...] = jnp.zeros_like(router)

    for j in range(1, count):

        @pl.when(at == j - 1)
        def _():
            for copy in load(j, j % 2):
                copy.start()

    for copy in load(0, slot):
        copy.wait()
    x, g = xs[slot], gs[slot]
    grads[0] += dot(sdpair[0, 0], x, TN)
    grads[1] += dot(sdpair[0, 1], x, TN)
    grads[2] += dot(sact[0], g, TN)
    router[...] += dot(dl[0], x, TN)

    @pl.when(at == count - 1)
    def _():
        grads_ref[...] = grads[...].astype(BF16)
        router_ref[...] = router[...]


def shared_grads(place, x_blocks, g_all, sact, sdpair, dl):
    count = len(x_blocks)
    tokens, width = x_blocks[0].shape
    share, padded = sact.shape[2], dl.shape[2]
    any_spec = pl.BlockSpec(memory_space=pl.ANY)
    return pl.pallas_call(
        functools.partial(shared_grads_kernel, count),
        grid=(count,),
        out_shape=(
            jax.ShapeDtypeStruct((3, share, width), BF16),
            jax.ShapeDtypeStruct((padded, width), F32),
        ),
        in_specs=[pl.BlockSpec(memory_space=pltpu.SMEM)]
        + [any_spec] * (count + 1)
        + [
            pl.BlockSpec((1, tokens, share), lambda j: (j, 0, 0)),
            pl.BlockSpec((1, 2, tokens, share), lambda j: (j, 0, 0, 0)),
            pl.BlockSpec((1, tokens, padded), lambda j: (j, 0, 0)),
        ],
        out_specs=(
            pl.BlockSpec((3, share, width), lambda j: (0, 0, 0)),
            pl.BlockSpec((padded, width), lambda j: (0, 0)),
        ),
        scratch_shapes=[
            pltpu.VMEM((2, tokens, width), BF16),
            pltpu.VMEM((2, tokens, width), BF16),
            pltpu.VMEM((3, share, width), F32),
            pltpu.VMEM((padded, width), F32),
            pltpu.SemaphoreType.DMA((2, 2)),
        ],
        compiler_params=pltpu.CompilerParams(vmem_limit_bytes=VMEM_LIMIT),
        cost_estimate=pl.CostEstimate(
            flops=count * tokens * width * share,
            bytes_accessed=2**20,
            transcendentals=0,
        ),
        name="shared_grads",
    )(place.reshape(1), *x_blocks, g_all, sact, sdpair, dl)


def on_device(
    hidden_in,
    cotangent,
    gain_attn,
    qkv_weight,
    qkv_bias,
    out_weight,
    gain_ffn,
    router_weight,
    routes,
    shared_gate,
    shared_in,
    shared_out,
    expert_in,
    expert_out,
):
    tokens, width = hidden_in.shape
    ctx_count = lax.axis_size("ctx")
    heads_local = qkv_weight.shape[2] // HD
    local = expert_in.shape[0]
    experts = local * ctx_count
    top_count = routes.shape[1]
    capacity = 3 * tokens * top_count // (2 * experts)
    place = lax.axis_index("ctx")
    order = jnp.arange(ctx_count, dtype=jnp.int32) ^ place
    score_scale = 1.0 / math.sqrt(HD)
    query_pos = place * tokens + jnp.arange(tokens, dtype=jnp.int32)
    cosine, sine = rotary_tables(query_pos, HD)

    x_full = hidden_in.astype(F32)
    inv_one = lax.rsqrt(jnp.mean(x_full * x_full, axis=-1, keepdims=True) + EPS)
    normed_one = x_full * inv_one
    x_one = (normed_one * gain_attn).astype(BF16)
    projected = (
        jnp.einsum("td,dcf->ctf", x_one, qkv_weight, preferred_element_type=F32)
        + qkv_bias[:, None]
    )
    shaped = projected.reshape(3, tokens, heads_local, HD).transpose(0, 2, 1, 3)
    query = rotate(shaped[0], cosine, sine).astype(BF16)
    key_local = rotate(shaped[1], cosine, sine).astype(BF16)
    value_local = shaped[2].astype(BF16)
    kv_rows = heads_local * tokens
    route_rows = -(-tokens * top_count // HD)
    behind = jnp.pad(
        routes.T.astype(BF16).reshape(route_rows, HD), ((0, -route_rows % 16), (0, 0))
    )
    kv_local = jnp.stack(
        [
            jnp.concatenate([key_local.reshape(kv_rows, HD), behind], axis=0),
            jnp.concatenate([value_local.reshape(kv_rows, HD), behind], axis=0),
        ]
    )
    share = shared_out.shape[0] // ctx_count
    piece = shared_out.shape[1]
    shared_send = jnp.concatenate(
        [
            shared_in.transpose(1, 2, 0).reshape(2, ctx_count, share, piece),
            shared_out.reshape(1, ctx_count, share, piece),
        ],
        axis=0,
    ).transpose(1, 0, 2, 3)
    kv_blocks = gather_end(gather_start(kv_local), shared_send)
    g_all = lax.all_gather(after(cotangent, kv_blocks[2 % ctx_count], kv_blocks[4 % ctx_count]), "ctx", axis=0)
    shared_got = lax.all_to_all(shared_send, "ctx", split_axis=0, concat_axis=0, tiled=True)

    half_rows = out_weight.shape[0] // 2
    core = place % 2
    out_mine = lax.all_gather(
        lax.dynamic_slice_in_dim(out_weight, core * half_rows, half_rows, 0), "tp", axis=0
    )

    routes_all = jnp.stack([b[0, kv_rows : kv_rows + route_rows] for b in kv_blocks])
    routes_all = routes_all.reshape(ctx_count, 1, top_count, tokens)
    own_experts = (place * local + jnp.arange(local, dtype=jnp.int32)).astype(BF16)
    hit = jnp.any(routes_all == own_experts[None, :, None, None], axis=2)
    token_at = jnp.arange(tokens, dtype=jnp.int32)
    earlier = (token_at[:, None] <= token_at[None, :]).astype(BF16)
    rank = dot(hit.astype(BF16).reshape(-1, tokens), earlier, NN).reshape(hit.shape) - 1.0
    slot_rows = jnp.where(hit, rank, -1.0).astype(jnp.int32)
    slot_cols = slot_rows.transpose(0, 2, 1)
    padded = -(-(experts + 1) // 8) * 8
    w_router = jnp.concatenate(
        [
            router_weight.T,
            shared_gate[None],
            jnp.zeros((padded - experts - 1, width), BF16),
        ],
        axis=0,
    )
    w_in = expert_in.transpose(0, 2, 3, 1)

    attended, lse = attend(place, query, kv_blocks)
    att = attended.astype(BF16).transpose(1, 0, 2).reshape(tokens, heads_local * HD)
    att_blocks = gather_tp(att)
    att_all = jnp.concatenate(att_blocks, axis=1)
    shared_got = after(shared_got, *att_blocks[1:])
    shared_w = shared_got.transpose(1, 2, 0, 3).reshape(3, share, width)
    whole_share = -(-share // 16) * 16
    if whole_share > share:
        shared_w = jnp.pad(shared_w, ((0, 0), (0, whole_share - share), (0, 0)))
    out_mine = after(out_mine, attended)
    out_other = swap(out_mine, 1)
    out_full = arrange(place, out_mine, out_other)
    att_all = after(att_all, out_full, slot_rows, slot_cols, w_router, w_in)
    hidden = x_full + dot(att_all, out_full, NN)
    inv_two = lax.rsqrt(jnp.mean(hidden * hidden, axis=-1, keepdims=True) + EPS)
    normed_two = hidden * inv_two
    x_two = (normed_two * gain_ffn).astype(BF16)

    units, group = expert_out.shape[1], 2
    kept = [
        jax.ShapeDtypeStruct(shape, BF16)
        for shape in (
            (local, ctx_count, capacity, width),
            (local, ctx_count, capacity, width),
            (local, ctx_count, capacity, units),
            (2 * local, ctx_count, capacity, units),
            (ctx_count, tokens, whole_share),
            (ctx_count, 2, tokens, whole_share),
            (ctx_count, tokens, padded),
        )
    ]
    weights = (w_router, w_in, expert_out, shared_w)
    got = gather_start(x_two)
    x_blocks = [got[0], got[1]]
    dxs = []
    early = None
    for at in range(0, ctx_count, group):
        if at == 4 and ctx_count == 8:
            pair_two = pair_sum(dxs, 2)
            early = (pair_two, pair_two[: tokens // 2].astype(BF16))
        if at == 6 and ctx_count == 8:
            x_blocks[6] = after(x_blocks[6], early[1])
        dx, kept = run_experts(
            at,
            experts,
            place,
            x_blocks[at : at + group],
            g_all,
            slot_rows,
            slot_cols,
            weights,
            kept,
        )
        dxs += dx
        if at == 0:
            x_blocks = x_blocks[:2] + gather_end(got, dx[0])[2:]
    grad_x_part = scatter_ctx(dxs, early)
    outs = run_outputs(kept[2], slot_cols, kept[4], expert_out, shared_w)
    grad_x_low = grad_x_part.astype(BF16)
    out_hops, out_stay = scatter_start(after(outs, grad_x_low))
    kept = after(kept, grad_x_low, outs[0])
    rows_x, rows_g, act_low, dpair, s_act, s_dpair, low_logits = kept
    shared_low, router_part = shared_grads(place, x_blocks, g_all, s_act, s_dpair, low_logits)
    out_hops = after(out_hops, shared_low)
    expert_grads = grads_of_experts(rows_x, rows_g, act_low, dpair)
    grad_expert_in, grad_expert_out = expert_grads
    gain_ffn_part = jnp.sum(grad_x_part * normed_two, axis=0)
    small = jnp.concatenate([router_part, gain_ffn_part[None]], axis=0).astype(BF16)
    small_rows = padded + 1
    half = tokens // 2
    second = jnp.concatenate(
        [grad_x_low[half:], jnp.pad(small, ((0, -small_rows % 16), (0, 0)))], axis=0
    )
    first = lax.psum(grad_x_low[:half], "tp")
    out_part = scatter_end((out_hops, out_stay), first)
    second = lax.psum(after(second, first), "tp")
    small = second[half : half + small_rows].astype(F32)
    shared_back = lax.all_to_all(
        shared_low[:, :share].reshape(3, share, ctx_count, piece).transpose(2, 0, 1, 3),
        "ctx",
        split_axis=0,
        concat_axis=0,
        tiled=True,
    )
    shared_back = shared_back.astype(F32)
    grad_shared_in = shared_back[:, :2].transpose(3, 1, 0, 2).reshape(shared_in.shape)
    grad_shared_out = shared_back[:, 2].reshape(shared_out.shape)
    summed = jnp.concatenate([first, second[:half]], axis=0)
    summed = after(summed, grad_shared_in, grad_shared_out, *expert_grads, out_part)
    summed = summed.astype(F32)
    grad_y = cotangent.astype(F32)
    grad_normed_two = summed * gain_ffn
    grad_hidden = grad_y + inv_two * (
        grad_normed_two
        - normed_two * jnp.mean(grad_normed_two * normed_two, axis=-1, keepdims=True)
    )
    grad_hidden_low = grad_hidden.astype(BF16)
    out_weight_part = dot(att, grad_hidden_low, (((0,), (0,)), ((), ())))
    grad_att = (
        dot(grad_hidden_low, out_weight, (((1,), (1,)), ((), ())))
        .astype(BF16)
        .reshape(tokens, heads_local, HD)
        .transpose(1, 0, 2)
    )
    delta = jnp.sum(grad_att.astype(F32) * attended, axis=-1)
    delta = jnp.broadcast_to(delta[:, None], lse.shape)
    grad_query, grad_pairs = attend_back(place, query, grad_att, lse, delta, kv_blocks)
    ffn_total = sum_tp_start(out_part)
    grad_pairs = after(grad_pairs, ffn_total)
    ffn_low = sum_tp_end(after(ffn_total, grad_query))
    grad_kv = scatter_ctx([grad_pairs[j] for j in range(ctx_count)])
    grad_kv = after(grad_kv, ffn_low)

    def raw_part(value):
        return value.astype(BF16).transpose(1, 0, 2).reshape(tokens, heads_local * HD)

    raw = [
        raw_part(rotate(grad_query, cosine, -sine)),
        raw_part(rotate(grad_kv[0], cosine, -sine)),
        raw_part(grad_kv[1]),
    ]
    raw = jnp.concatenate(raw, axis=1)
    grad_x_one_part = jnp.einsum(
        "tcf,dcf->td",
        raw.reshape(tokens, 3, -1),
        qkv_weight,
        preferred_element_type=F32,
    )
    grad_x_low = grad_x_one_part.astype(BF16)
    half_way = sum_tp_start(grad_x_low)
    grad_x_one = sum_tp_end(half_way)
    x_one = after(x_one, grad_x_low)
    gain_attn_part = jnp.sum(grad_x_one_part * normed_one, axis=0)
    gain_sum = sum_tp_small(gain_attn_part[None])
    head_width = heads_local * HD
    gain_rows = width // head_width
    ends = jnp.concatenate(
        [jnp.sum(raw.astype(F32), axis=0).reshape(3, -1)]
        + [gain_sum.reshape(gain_rows, -1), small.reshape((padded + 1) * gain_rows, -1)],
        axis=0,
    )
    ends = jnp.pad(ends, ((0, -ends.shape[0] % (16 * ctx_count)), (0, 0))).astype(BF16)
    turns = width // head_width
    sums = sum_ctx(
        weight_parts(place, x_one, raw, out_weight_part.astype(BF16), ends, ctx_count), half_way
    )
    q_rows = width // ctx_count
    out_rows = out_weight.shape[0] // ctx_count
    plan = [(0, c * q_rows, q_rows, c * width, 0) for c in range(3)] + [
        (1, 3 * q_rows + k * out_rows, out_rows, 0, k * head_width) for k in range(turns)
    ]
    qkv_grad, out_weight_grad = assemble(
        place, sums, [(3 * width, head_width), out_weight.shape], plan
    )
    qkv_grad = qkv_grad.reshape(3, width, head_width).transpose(1, 0, 2)
    ends = relative(jnp.stack([b[3 * q_rows + turns * out_rows :] for b in sums]))
    ends = ends.reshape(-1, head_width).astype(F32)
    small = ends[3 + gain_rows : 3 + (padded + 2) * gain_rows].reshape(padded + 1, width)
    grad_x_one = after(grad_x_one, sums[2]).astype(F32)
    grad_normed_one = grad_x_one * gain_attn
    grad_input = grad_hidden + inv_one * (
        grad_normed_one
        - normed_one * jnp.mean(grad_normed_one * normed_one, axis=-1, keepdims=True)
    )
    block_out = (hidden + ffn_low.astype(F32)).astype(BF16)
    return (
        block_out,
        grad_input,
        ends[3 : 3 + gain_rows].reshape(-1),
        qkv_grad,
        ends[:3],
        out_weight_grad,
        small[padded],
        small[:experts].T,
        small[experts],
        grad_shared_in,
        grad_shared_out,
        grad_expert_in.transpose(0, 3, 1, 2),
        grad_expert_out,
    )


def solution(mesh):
    return jax.shard_map(
        on_device,
        mesh=mesh,
        in_specs=(
            P("ctx", None),
            P("ctx", None),
            P(),
            P(None, None, "tp"),
            P(None, "tp"),
            P("tp", None),
            P(),
            P(),
            P("ctx", None),
            P(),
            P("ctx", None, "tp"),
            P("tp", "ctx"),
            P("ctx", None, None, "tp"),
            P("ctx", "tp", None),
        ),
        out_specs=(
            P("ctx", None),
            P("ctx", None),
            P(),
            P(None, None, "tp"),
            P(None, "tp"),
            P("tp", None),
            P(),
            P(),
            P(),
            P("ctx", None, "tp"),
            P("tp", "ctx"),
            P("ctx", None, None, "tp"),
            P("ctx", "tp", None),
        ),
        check_vma=False,
    )
```

```python
import functools
import math

import jax
import jax.numpy as jnp
from jax import lax
from jax.experimental import pallas as pl
from jax.experimental.pallas import tpu as pltpu
from jax.sharding import PartitionSpec as P

HD = 128
EPS = 1e-06
THETA = 1000000.0
NEG = -1e30
F32 = jnp.float32
BF16 = jnp.bfloat16


def rotary_tables(positions, width):
    half_width = width // 2
    freqs = THETA ** (-(jnp.arange(half_width, dtype=F32) * 2.0) / width)
    angles = positions.astype(F32)[:, None] * freqs[None, :]
    return (jnp.cos(angles), jnp.sin(angles))


def rotate(values, cosine, sine):
    half_width = values.shape[-1] // 2
    first, second = values[..., :half_width], values[..., half_width:]
    return jnp.concatenate(
        [first * cosine - second * sine, second * cosine + first * sine], axis=-1
    )


def dot(a, b, dims):
    return lax.dot_general(a, b, dims, preferred_element_type=F32)


def swap(value, bits):
    count = lax.axis_size("ctx")
    return lax.ppermute(value, "ctx", [(i, i ^ bits) for i in range(count)])


def relative(natural):
    count = natural.shape[0]
    order = jnp.arange(count, dtype=jnp.int32) ^ lax.axis_index("ctx")
    return natural[order]


def nothing_kernel(*refs):
    pass


def after(values, *others):
    single = not isinstance(values, (list, tuple))
    values = [values] if single else list(values)
    any_spec = pl.BlockSpec(memory_space=pl.ANY)
    results = pl.pallas_call(
        nothing_kernel,
        out_shape=[jax.ShapeDtypeStruct(v.shape, v.dtype) for v in values],
        in_specs=[any_spec] * (len(values) + len(others)),
        out_specs=[any_spec] * len(values),
        input_output_aliases={i: i for i in range(len(values))},
        name="after",
    )(*values, *others)
    return results[0] if single else results


def gather_start(own):
    if lax.axis_size("ctx") != 8:
        return relative(lax.all_gather(own, "ctx", axis=0))
    return [own, swap(own, 1), swap(own, 2), swap(own, 4)]


def gather_end(got, *others):
    if lax.axis_size("ctx") != 8:
        return [got[j] for j in range(lax.axis_size("ctx"))]
    own, b1, b2, b4 = got
    if others:
        b2, b4 = after((b2, b4), *others)
    half = own.shape[0] // 2
    via_x, via_y = swap(b4[:half], 2), swap(b2[half:], 4)
    b3, b5 = swap(b2, 1), swap(b4, 1)
    b6 = jnp.concatenate([via_x, via_y], axis=0)
    return [own, b1, b2, b3, b4, b5, b6, swap(b6, 1)]


def gather_ctx(own, *others):
    return gather_end(gather_start(own), *others)


def pair_sum(parts, j):
    return parts[j].astype(F32) + swap(parts[j ^ 1], 1).astype(F32)


def scatter_ctx(parts, early=None):
    return scatter_end(scatter_middle(scatter_start(parts, early)))


def scatter_start(parts, early=None):
    if lax.axis_size("ctx") != 8:
        return [jnp.stack(parts)], None
    half = parts[0].shape[0] // 2
    pair = {j: pair_sum(parts, j) for j in (2, 4, 6, 0) if j != 2 or early is None}
    if early is None:
        early = (pair[2], pair[2][:half].astype(BF16))
    q6 = pair[6].astype(BF16)
    hops = [early[1], pair[4][half:].astype(BF16), q6[:half], q6[half:]]
    return hops, (early[0], pair[4], pair[0])


def scatter_middle(started):
    hops, stay = started
    if lax.axis_size("ctx") != 8:
        return hops, None
    two, four, zero = stay
    half = two.shape[0] // 2
    r2, r4 = swap(hops[0], 2), swap(hops[1], 4)
    via_x, via_y = swap(hops[2], 2), swap(hops[3], 4)
    r4a = (four[:half] + via_x.astype(F32)).astype(BF16)
    r2b = (two[half:] + via_y.astype(F32)).astype(BF16)
    return [r4a, r2b], (r2, r4, zero)


def scatter_end(started, *others):
    hops, stay = started
    if lax.axis_size("ctx") != 8:
        natural = relative(hops[0])
        flat = natural.reshape((-1,) + natural.shape[2:])
        return lax.psum_scatter(flat, "ctx", scatter_dimension=0, tiled=True).astype(F32)
    if others:
        hops = after(hops, *others)
    r2, r4, zero = stay
    r4a, r2b = swap(hops[0], 4), swap(hops[1], 2)
    low = r2.astype(F32) + r4a.astype(F32)
    high = r2b.astype(F32) + r4.astype(F32)
    return zero + jnp.concatenate([low, high], axis=0)


def sum_ctx(parts, *others):
    own = scatter_end(scatter_middle(scatter_start(parts)), *others)
    return gather_ctx(own.astype(BF16))


def shards(value):
    count = lax.axis_size("ctx")
    rows = value.shape[0] // count
    place = lax.axis_index("ctx")
    return [lax.dynamic_slice_in_dim(value, (place ^ j) * rows, rows, 0) for j in range(count)]


def gather_tp(own):
    count = lax.axis_size("tp")
    return [own] + [
        lax.ppermute(own, "tp", [(i, i ^ k) for i in range(count)]) for k in range(1, count)
    ]


NT = (((1,), (1,)), ((), ()))
NN = (((1,), (0,)), ((), ()))
TN = (((0,), (0,)), ((), ()))
VMEM_LIMIT = 60 * 1024 * 1024


def sum_tp_start(value):
    pieces = value.astype(BF16).reshape(lax.axis_size("tp"), -1, value.shape[1])
    got = lax.all_to_all(pieces, "tp", split_axis=0, concat_axis=0, tiled=True)
    return jnp.sum(got.astype(F32), axis=0).astype(BF16)


def sum_tp_end(total):
    count, at = lax.axis_size("tp"), lax.axis_index("tp")
    blocks = jnp.stack(gather_tp(total))
    blocks = blocks[jnp.arange(count, dtype=jnp.int32) ^ at]
    return blocks.reshape(-1, total.shape[1])


def sum_tp_small(value):
    count, bits = lax.axis_size("tp"), 1
    while bits < count:
        value = value + lax.ppermute(value, "tp", [(i, i ^ bits) for i in range(count)])
        bits *= 2
    return value


def columns_kernel(count, places, *refs):
    block_refs, (mine, other) = refs[:count], refs[count:]
    core, at = places[0], places[1]
    width = mine.shape[1] // count
    for k in range(count):
        to = pl.ds(pl.multiple_of((at ^ k) * width, width), width)
        mine[:, to] = block_refs[k][:, pl.ds(pl.multiple_of(core * width, width), width)]
        other[:, to] = block_refs[k][:, pl.ds(pl.multiple_of((1 - core) * width, width), width)]


def columns(place, blocks):
    count = len(blocks)
    rows, width = blocks[0].shape
    vmem = pl.BlockSpec(memory_space=pltpu.VMEM)
    half = jax.ShapeDtypeStruct((rows, count * width // 2), blocks[0].dtype)
    return pl.pallas_call(
        functools.partial(columns_kernel, count),
        out_shape=(half, half),
        in_specs=[pl.BlockSpec(memory_space=pltpu.SMEM)] + [vmem] * count,
        out_specs=(vmem, vmem),
        compiler_params=pltpu.CompilerParams(vmem_limit_bytes=VMEM_LIMIT),
        cost_estimate=pl.CostEstimate(flops=0, bytes_accessed=2**20, transcendentals=0),
        name="columns",
    )(jnp.stack([place % 2, lax.axis_index("tp")]), *blocks)


def attend_kernel(factor, count, place_ref, q_ref, *refs):
    kv_refs, (att_ref, lse_ref, kv, sems) = refs[:count], refs[count:]
    rows = kv.shape[2]
    copies = [
        pltpu.make_async_copy(kv_refs[j].at[:, pl.ds(0, rows)], kv.at[j], sems.at[j])
        for j in range(count)
    ]
    for copy in copies:
        copy.start()
    for copy in copies:
        copy.wait()
    place = place_ref[0]
    heads, tokens, _ = q_ref.shape

    def one_head(head, _):
        query = q_ref[head]
        here = pl.ds(pl.multiple_of(head * tokens, tokens), tokens)

        def scores(j):
            return dot(kv[j, 0, here], query, NT) * factor

        key_at = lax.broadcasted_iota(jnp.int32, (tokens, tokens), 0)
        query_at = lax.broadcasted_iota(jnp.int32, (tokens, tokens), 1)
        first = jnp.where(key_at <= query_at, scores(0), NEG)
        top = jnp.max(first, axis=0, keepdims=True)
        exps = jnp.exp2(first - top)
        total = jnp.sum(exps, axis=0, keepdims=True)
        acc = dot(kv[0, 1, here], exps.astype(BF16), TN)

        def earlier(i, carry):
            top, total, acc = carry
            j = place ^ i
            now = scores(j)
            higher = jnp.maximum(top, jnp.max(now, axis=0, keepdims=True))
            exps = jnp.exp2(now - higher)
            keep = jnp.exp2(top - higher)
            total = total * keep + jnp.sum(exps, axis=0, keepdims=True)
            acc = acc * keep + dot(kv[j, 1, here], exps.astype(BF16), TN)
            return higher, total, acc

        top, total, acc = lax.fori_loop(0, place, earlier, (top, total, acc))
        att_ref[head] = (acc / total).T
        lse_ref[head] = jnp.broadcast_to(top + jnp.log2(total), lse_ref.shape[1:])
        return 0

    lax.fori_loop(0, heads, one_head, 0)


def attend(place, query, kv_blocks):
    heads, tokens, size = query.shape
    count = len(kv_blocks)
    factor = math.log2(math.e) / math.sqrt(size)
    flops = 4 * count * heads * tokens * tokens * size
    return pl.pallas_call(
        functools.partial(attend_kernel, factor, count),
        out_shape=(
            jax.ShapeDtypeStruct((heads, tokens, size), F32),
            jax.ShapeDtypeStruct((heads, 8, tokens), F32),
        ),
        in_specs=[
            pl.BlockSpec(memory_space=pltpu.SMEM),
            pl.BlockSpec(memory_space=pltpu.VMEM),
        ]
        + [pl.BlockSpec(memory_space=pl.ANY)] * count,
        out_specs=(pl.BlockSpec(memory_space=pltpu.VMEM),) * 2,
        scratch_shapes=[
            pltpu.VMEM((count, 2, heads * tokens, size), BF16),
            pltpu.SemaphoreType.DMA((count,)),
        ],
        compiler_params=pltpu.CompilerParams(vmem_limit_bytes=VMEM_LIMIT),
        cost_estimate=pl.CostEstimate(
            flops=flops // 16, bytes_accessed=2**20, transcendentals=0
        ),
        name="attend",
    )(place.reshape(1), query, *kv_blocks)


def attend_back_kernel(factor, scale, count, place_ref, q_ref, do_ref, lse_ref, delta_ref, *refs):
    kv_refs, (dq_ref, dkv_ref, kv, dkv, dq, sems, out_sems) = refs[:count], refs[count:]
    rows = kv.shape[2]
    copies = [
        pltpu.make_async_copy(kv_refs[j].at[:, pl.ds(0, rows)], kv.at[j], sems.at[j])
        for j in range(count)
    ]
    for copy in copies:
        copy.start()
    for copy in copies:
        copy.wait()
    place = place_ref[0]
    heads, tokens, _ = q_ref.shape

    def out_copy(j):
        return pltpu.make_async_copy(dkv.at[j], dkv_ref.at[j], out_sems.at[j])

    def one_block(j, masked):
        def one_head(head, _):
            query, do = q_ref[head], do_ref[head]
            here = pl.ds(pl.multiple_of(head * tokens, tokens), tokens)
            key, value = kv[j, 0, here], kv[j, 1, here]
            scores = dot(key, query, NT) * factor
            probs = jnp.exp2(scores - lse_ref[head, :1])
            if masked:
                key_at = lax.broadcasted_iota(jnp.int32, (tokens, tokens), 0)
                query_at = lax.broadcasted_iota(jnp.int32, (tokens, tokens), 1)
                probs = jnp.where(key_at <= query_at, probs, 0.0)
            dprob = dot(value, do, NT)
            dscore = (probs * (dprob - delta_ref[head, :1])).astype(BF16)
            dkv[j, 0, head] = (dot(dscore, query, NN) * scale).astype(BF16)
            dkv[j, 1, head] = dot(probs.astype(BF16), do, NN).astype(BF16)
            part = dot(key, dscore, TN)
            dq[head] = part if masked else dq[head] + part
            return 0

        lax.fori_loop(0, heads, one_head, 0)
        out_copy(j).start()

    one_block(0, True)

    def earlier(i, _):
        one_block(place ^ i, False)
        return 0

    def later(i, _):
        j = place ^ i
        dkv[j] = jnp.zeros(dkv.shape[1:], BF16)
        out_copy(j).start()
        return 0

    lax.fori_loop(0, place, earlier, 0)
    lax.fori_loop(place + 1, count, later, 0)
    for head in range(heads):
        dq_ref[head] = dq[head].T * scale
    for j in range(count):
        out_copy(j).wait()


def attend_back(place, query, do, lse, delta, kv_blocks):
    heads, tokens, size = query.shape
    count = len(kv_blocks)
    scale = 1.0 / math.sqrt(size)
    factor = math.log2(math.e) * scale
    return pl.pallas_call(
        functools.partial(attend_back_kernel, factor, scale, count),
        out_shape=(
            jax.ShapeDtypeStruct((heads, tokens, size), F32),
            jax.ShapeDtypeStruct((count, 2, heads, tokens, size), BF16),
        ),
        in_specs=[pl.BlockSpec(memory_space=pltpu.SMEM)]
        + [pl.BlockSpec(memory_space=pltpu.VMEM)] * 4
        + [pl.BlockSpec(memory_space=pl.ANY)] * count,
        out_specs=(pl.BlockSpec(memory_space=pltpu.VMEM), pl.BlockSpec(memory_space=pl.ANY)),
        scratch_shapes=[
            pltpu.VMEM((count, 2, heads * tokens, size), BF16),
            pltpu.VMEM((count, 2, heads, tokens, size), BF16),
            pltpu.VMEM((heads, size, tokens), F32),
            pltpu.SemaphoreType.DMA((count,)),
            pltpu.SemaphoreType.DMA((count,)),
        ],
        compiler_params=pltpu.CompilerParams(vmem_limit_bytes=VMEM_LIMIT),
        cost_estimate=pl.CostEstimate(
            flops=count * heads * tokens * tokens * size,
            bytes_accessed=2**20,
            transcendentals=0,
        ),
        name="attend_back",
    )(place.reshape(1), query, do, lse, delta, *kv_blocks)


def swiglu_back(one, two, dact, gate):
    sig = 1.0 / (1.0 + jnp.exp(-one))
    silu = one * sig
    act = silu * two
    prod = act * dact
    dgate = gate * dact
    d_one = (dgate * two * sig * (1.0 + one * (1.0 - sig))).astype(BF16)
    d_two = (dgate * silu).astype(BF16)
    return (gate * act).astype(BF16), d_one, d_two, prod


def experts_kernel(at, group, local, experts, given, place_ref, *refs):
    x_refs, g_all, refs = refs[:group], refs[group], refs[group + 1 :]
    (slot_row, slot_col, w_router, w_in, w_out, w_shared), refs = refs[:6], refs[6 + given :]
    dx_refs, refs = refs[:group], refs[group:]
    kept_refs, refs = refs[:7], refs[7:]
    (xs, gs, first_w, in_w, out_w, shared_w, dxs, left, right, sems, out_sems), stage = refs[:11], refs[11:]
    rows_x, rows_g, act_s, dpair_s, sact_s, sdpair_s, dl_s = stage
    tokens, width = xs.shape[1:]
    capacity, units = act_s.shape[2:]
    wide = local * capacity
    share = sact_s.shape[2]
    third = first_w.shape[0] - 128
    second = third // 2
    padded = w_router.shape[0]
    most = out_w.shape[1]

    loads = [pltpu.make_async_copy(x_refs[b], xs.at[b], sems.at[b]) for b in range(group)]
    fore_loads = [
        pltpu.make_async_copy(
            w_shared.at[c], first_w.at[pl.ds(c * second, share)], sems.at[2 * group + c]
        )
        for c in range(2)
    ]
    loads += [
        pltpu.make_async_copy(g_all.at[place_ref[0] ^ (at + b)], gs.at[b], sems.at[group + b])
        for b in range(group)
    ]
    base = 2 * group + 2
    more = [
        [
            pltpu.make_async_copy(
                w_in.at[e, c], in_w.at[e, pl.ds(c * most, units)], sems.at[base + 3 * e + c]
            )
            for c in range(2)
        ]
        + [
            pltpu.make_async_copy(
                w_out.at[e], out_w.at[e, pl.ds(0, units)], sems.at[base + 3 * e + 2]
            )
        ]
        for e in range(local)
    ]
    last = pltpu.make_async_copy(w_shared.at[2], shared_w, sems.at[base + 3 * local])
    for copy in loads[:group] + fore_loads:
        copy.start()
    first_w[third : third + padded] = w_router[...]
    first_w[third + padded :] = jnp.zeros((128 - padded, width), BF16)
    if second > share:
        for c in range(2):
            gap = jnp.zeros((second - share, width), BF16)
            first_w[c * second + share : (c + 1) * second] = gap
    if most > units:
        gap = jnp.zeros((most - units, width), BF16)
        for e in range(local):
            in_w[e, units:most] = gap
            in_w[e, most + units :] = gap
            out_w[e, units:] = gap

    sent = []

    def send(copy):
        copy.start()
        sent.append(copy)

    for copy in loads[:group] + fore_loads:
        copy.wait()
    for copy in loads[group:] + more[0]:
        copy.start()
    x = xs[...].reshape(group * tokens, width)
    fore = dot(x, first_w[...], NT)
    s_one, s_two = fore[:, :share], fore[:, second : second + share]
    s_gate = 1.0 / (1.0 + jnp.exp(-fore[:, third + experts : third + experts + 1]))
    row_at = lax.broadcasted_iota(jnp.int32, (padded, tokens), 0)
    slot_at = lax.broadcasted_iota(jnp.int32, (capacity, tokens), 0)
    probs, change, hits = [], [], []
    for b in range(group):
        logits = fore[b * tokens : (b + 1) * tokens, third:].T[:padded]
        shown = jnp.where(row_at < experts, logits, NEG)
        exps = jnp.exp(shown - jnp.max(shown, axis=0, keepdims=True))
        soft = exps / jnp.sum(exps, axis=0, keepdims=True)
        probs.append(jnp.where(row_at == experts, 1.0 / (1.0 + jnp.exp(-logits)), soft))
        change.append(jnp.zeros((padded, tokens), F32))
        picks = jnp.concatenate(
            [
                jnp.where(slot_at == slot_row[b, e : e + 1, :], 1.0, 0.0).astype(BF16)
                for e in range(local)
            ],
            axis=0,
        )
        rows = dot(picks, xs[b], NN).astype(BF16)
        for e in range(local):
            rows_x[e, b] = rows[e * capacity : (e + 1) * capacity]
        loads[group + b].wait()
        if b == group - 1:
            for e in range(1, local):
                for copy in more[e]:
                    copy.start()
            last.start()
        rows = dot(picks, gs[b], NN).astype(BF16)
        for e in range(local):
            rows_g[e, b] = rows[e * capacity : (e + 1) * capacity]
    def send_all(i, lead):
        for e in range(lead):
            send(
                pltpu.make_async_copy(
                    stage[i].at[e], kept_refs[i].at[e, pl.ds(at, group)], out_sems.at[i, e]
                )
            )

    send_all(0, local)
    send_all(1, local)
    is_expert = row_at < experts
    for e in range(local):
        chosen = row_at == place_ref[0] * local + e
        gates, owns, hits = [], [], []
        for b in range(group):
            own = jnp.sum(jnp.where(chosen, probs[b], 0.0), axis=0, keepdims=True)
            hit = slot_at == slot_row[b, e : e + 1, :]
            gates.append(jnp.sum(jnp.where(hit, own, 0.0), axis=1, keepdims=True))
            owns.append(own)
            hits.append(hit)
        for copy in more[e]:
            copy.wait()
        pair = dot(rows_x[e].reshape(group * capacity, width), in_w[e], NT)
        dact = dot(rows_g[e].reshape(group * capacity, width), out_w[e], NT)
        act, d_one, d_two, prod = swiglu_back(
            pair[:, :most], pair[:, most:], dact, jnp.concatenate(gates, axis=0)
        )
        act_s[e] = act[:, :units].reshape(group, capacity, units)
        dpair_s[2 * e] = d_one[:, :units].reshape(group, capacity, units)
        dpair_s[2 * e + 1] = d_two[:, :units].reshape(group, capacity, units)
        row_dot = jnp.sum(prod, axis=1, keepdims=True)
        drow = dot(jnp.concatenate([d_one, d_two], axis=1), in_w[e], NN).astype(BF16)
        for b in range(group):
            rows = slice(b * capacity, (b + 1) * capacity)
            found = jnp.sum(jnp.where(hits[b], row_dot[rows], 0.0), axis=0, keepdims=True)
            change[b] += (found * owns[b]) * (
                jnp.where(chosen, 1.0, 0.0) - jnp.where(is_expert, probs[b], 0.0)
            )
            right[b, e * capacity : (e + 1) * capacity] = drow[rows]
    send_all(2, local)
    send_all(3, 2 * local)
    last.wait()
    g = gs[...].reshape(group * tokens, width)
    s_dact = dot(g, shared_w[...], NT)
    act, d_one, d_two, prod = swiglu_back(s_one, s_two, s_dact, s_gate)
    sact_s[...] = act.reshape(group, tokens, share)
    sdpair_s[:, 0] = d_one.reshape(group, tokens, share)
    sdpair_s[:, 1] = d_two.reshape(group, tokens, share)
    dslogit = jnp.sum(prod, axis=1, keepdims=True) * s_gate * (1.0 - s_gate)
    lane_at = lax.broadcasted_iota(jnp.int32, (tokens, 128), 1)
    rest = jnp.zeros((128 - padded, tokens), F32)
    deep = wide + 2 * share
    column_at = lax.broadcasted_iota(jnp.int32, (tokens, capacity), 1)
    stores = []
    for b in range(group):
        rows = slice(b * tokens, (b + 1) * tokens)
        columns = jnp.concatenate([change[b], rest], axis=0).T
        columns = jnp.where(lane_at == experts, dslogit[rows], columns)[:, :padded].astype(BF16)
        dl_s[b] = columns
        left[b, :, deep : deep + padded] = columns
        right[b, deep : deep + padded] = w_router[...]
        for e in range(local):
            picks = jnp.where(column_at == slot_col[b, :, e : e + 1], 1.0, 0.0).astype(BF16)
            left[b, :, e * capacity : (e + 1) * capacity] = picks
        left[b, :, wide : wide + share] = d_one[rows]
        left[b, :, wide + share : wide + 2 * share] = d_two[rows]
        right[b, wide : wide + share] = first_w[:share]
        right[b, wide + share : wide + 2 * share] = first_w[second : second + share]
        dxs[b] = dot(left[b], right[b], NN).astype(BF16)
        send(pltpu.make_async_copy(dxs.at[b], dx_refs[b], out_sems.at[7, b]))
    for i in range(4, 7):
        send(pltpu.make_async_copy(stage[i], kept_refs[i].at[pl.ds(at, group)], out_sems.at[i, 0]))
    for copy in sent:
        copy.wait()


def run_experts(at, experts, place, x_group, g_all, slot_rows, slot_cols, weights, kept):
    given = kept if at else []
    group = len(x_group)
    tokens, width = x_group[0].shape
    w_router, w_in, w_out, w_shared = weights
    local = w_out.shape[0]
    share = w_shared.shape[1]
    padded = w_router.shape[0]
    capacity, units = kept[2].shape[2:]
    any_spec = pl.BlockSpec(memory_space=pl.ANY)
    block = jax.ShapeDtypeStruct((tokens, width), BF16)
    deep = local * capacity + 2 * share + padded
    flops = group * 2 * tokens * width * (local * capacity * 3 + 5 * share) + (
        group * 2 * width * local * capacity * units * 5
    )
    step = at // group
    wide_units = -(-units // 128) * 128
    fore = 2 * (-(-share // 64) * 64) + 128
    results = pl.pallas_call(
        functools.partial(experts_kernel, at, group, local, experts, len(given)),
        grid=(1,),
        out_shape=(block,) * group + tuple(jax.ShapeDtypeStruct(k.shape, k.dtype) for k in kept),
        in_specs=[pl.BlockSpec(memory_space=pltpu.SMEM)]
        + [any_spec] * (group + 1)
        + [
            pl.BlockSpec((group, local, tokens), lambda i: (step, 0, 0)),
            pl.BlockSpec((group, tokens, local), lambda i: (step, 0, 0)),
            pl.BlockSpec((padded, width), lambda i: (0, 0)),
        ]
        + [any_spec] * (3 + len(given)),
        out_specs=(any_spec,) * (group + len(kept)),
        input_output_aliases={8 + group + i: group + i for i in range(len(given))},
        scratch_shapes=[
            pltpu.VMEM((group, tokens, width), BF16),
            pltpu.VMEM((group, tokens, width), BF16),
            pltpu.VMEM((fore, width), BF16),
            pltpu.VMEM((local, 2 * wide_units, width), BF16),
            pltpu.VMEM((local, wide_units, width), BF16),
            pltpu.VMEM((share, width), BF16),
            pltpu.VMEM((group, tokens, width), BF16),
            pltpu.VMEM((group, tokens, deep), BF16),
            pltpu.VMEM((group, deep, width), BF16),
            pltpu.SemaphoreType.DMA((2 * group + 3 + 3 * local,)),
            pltpu.SemaphoreType.DMA((8, max(2 * local, group))),
        ]
        + [
            pltpu.VMEM(k.shape[:1] + (group,) + k.shape[2:], BF16) for k in kept[:4]
        ]
        + [pltpu.VMEM((group,) + k.shape[1:], BF16) for k in kept[4:]],
        compiler_params=pltpu.CompilerParams(vmem_limit_bytes=VMEM_LIMIT),
        cost_estimate=pl.CostEstimate(flops=flops // 16, bytes_accessed=2**20, transcendentals=0),
        name="run_experts",
    )(place.reshape(1), *x_group, g_all, slot_rows, slot_cols, *weights, *given)
    return results[:group], results[group:]


def outputs_kernel(group, count, local, act, slot_col, sact, w_out, w_shared, *refs):
    out_refs, (outs, left, right, sems) = refs[:count], refs[count:]
    step = pl.program_id(0)
    slot = lax.rem(step, 2)
    capacity, units = act.shape[2:]
    tokens, share = sact.shape[1:]
    wide = local * capacity

    def store(at, b, into):
        return pltpu.make_async_copy(outs.at[into, b], out_refs[at * group + b], sems.at[into, b])

    @pl.when(step >= 2)
    def _():
        for b in range(group):
            store(0, b, slot).wait()

    for e in range(local):
        rows = dot(act[e].reshape(group * capacity, units), w_out[e], NN).astype(BF16)
        for b in range(group):
            right[b, e * capacity : (e + 1) * capacity] = rows[b * capacity : (b + 1) * capacity]
    slot_at = lax.broadcasted_iota(jnp.int32, (tokens, capacity), 1)
    for b in range(group):
        for e in range(local):
            picks = jnp.where(slot_at == slot_col[b, :, e : e + 1], 1.0, 0.0).astype(BF16)
            left[b, :, e * capacity : (e + 1) * capacity] = picks
        left[b, :, wide : wide + share] = sact[b]
        right[b, wide : wide + share] = w_shared[0]
        outs[slot, b] = dot(left[b], right[b], NN).astype(BF16)
    for at in range(count // group):

        @pl.when(step == at)
        def _():
            for b in range(group):
                store(at, b, at % 2).start()

    @pl.when(step == count // group - 1)
    def _():
        for b in range(group):
            for into in range(2):
                store(0, b, into).wait()


def expert_grads_kernel(rows_x, rows_g, act, dpair, in_ref, out_ref):
    rows = rows_x.shape[1] * rows_x.shape[2]
    x = rows_x[0].reshape(rows, -1)
    for c in range(2):
        in_ref[0, c] = dot(dpair[c].reshape(rows, -1), x, TN)
    out_ref[0] = dot(act[0].reshape(rows, -1), rows_g[0].reshape(rows, -1), TN)


def grads_of_experts(rows_x, rows_g, act, dpair):
    local, count, capacity, width = rows_x.shape
    units = act.shape[3]
    tile = min(width, 1024)
    return pl.pallas_call(
        expert_grads_kernel,
        grid=(local, width // tile),
        out_shape=(
            jax.ShapeDtypeStruct((local, 2, units, width), F32),
            jax.ShapeDtypeStruct((local, units, width), F32),
        ),
        in_specs=[
            pl.BlockSpec((1, count, capacity, tile), lambda e, i: (e, 0, 0, i)),
            pl.BlockSpec((1, count, capacity, tile), lambda e, i: (e, 0, 0, i)),
            pl.BlockSpec((1, count, capacity, units), lambda e, i: (e, 0, 0, 0)),
            pl.BlockSpec((2, count, capacity, units), lambda e, i: (e, 0, 0, 0)),
        ],
        out_specs=(
            pl.BlockSpec((1, 2, units, tile), lambda e, i: (e, 0, 0, i)),
            pl.BlockSpec((1, units, tile), lambda e, i: (e, 0, i)),
        ),
        compiler_params=pltpu.CompilerParams(vmem_limit_bytes=VMEM_LIMIT),
        cost_estimate=pl.CostEstimate(flops=0, bytes_accessed=2**20, transcendentals=0),
        name="grads_of_experts",
    )(rows_x, rows_g, act, dpair)


def run_outputs(act, slot_cols, sact, w_out, w_shared):
    local, count, capacity, units = act.shape
    tokens, share = sact.shape[1:]
    width = w_out.shape[2]
    group = 2
    deep = local * capacity + share
    return pl.pallas_call(
        functools.partial(outputs_kernel, group, count, local),
        grid=(count // group,),
        out_shape=(jax.ShapeDtypeStruct((tokens, width), BF16),) * count,
        in_specs=[
            pl.BlockSpec((local, group, capacity, units), lambda i: (0, i, 0, 0)),
            pl.BlockSpec((group, tokens, local), lambda i: (i, 0, 0)),
            pl.BlockSpec((group, tokens, share), lambda i: (i, 0, 0)),
            pl.BlockSpec((local, units, width), lambda i: (0, 0, 0)),
            pl.BlockSpec((1, share, width), lambda i: (2, 0, 0)),
        ],
        out_specs=(pl.BlockSpec(memory_space=pl.ANY),) * count,
        scratch_shapes=[
            pltpu.VMEM((2, group, tokens, width), BF16),
            pltpu.VMEM((group, tokens, deep), BF16),
            pltpu.VMEM((group, deep, width), BF16),
            pltpu.SemaphoreType.DMA((2, group)),
        ],
        compiler_params=pltpu.CompilerParams(vmem_limit_bytes=VMEM_LIMIT),
        cost_estimate=pl.CostEstimate(
            flops=count * width // 8 * (local * capacity * (units + tokens) + tokens * share),
            bytes_accessed=2**20,
            transcendentals=0,
        ),
        name="run_outputs",
    )(act, slot_cols, sact, w_out, w_shared)


def weight_parts_kernel(count, place_ref, x, raw, out_part, ends, *refs):
    part_refs, (part, sems) = refs[:count], refs[count:]
    place = place_ref[0]
    width = part.shape[2]
    q_rows, out_rows, end_rows = x.shape[1] // count, out_part.shape[0] // count, ends.shape[0] // count

    def store(j):
        return pltpu.make_async_copy(part.at[j % 2], part_refs[j], sems.at[j % 2])

    for j in range(count):
        if j >= 2:
            store(j - 2).wait()
        to = place ^ j
        columns = x[:, pl.ds(pl.multiple_of(to * q_rows, q_rows), q_rows)]
        grad = dot(columns, raw[...], TN).astype(BF16)
        for c in range(3):
            part[j % 2, c * q_rows : (c + 1) * q_rows] = grad[:, c * width : (c + 1) * width]
        rows = out_part[pl.ds(pl.multiple_of(to * out_rows, out_rows), out_rows)]
        at = 3 * q_rows
        for k in range(out_part.shape[1] // width):
            part[j % 2, at : at + out_rows] = rows[:, k * width : (k + 1) * width]
            at += out_rows
        part[j % 2, at:] = ends[pl.ds(pl.multiple_of(to * end_rows, end_rows), end_rows)]
        store(j).start()
    for j in range(count - 2, count):
        store(j).wait()


def weight_parts(place, x, raw, out_part, ends, count):
    tokens, size = x.shape
    width = ends.shape[1]
    rows = (3 * size + out_part.size // width + ends.shape[0]) // count
    return pl.pallas_call(
        functools.partial(weight_parts_kernel, count),
        out_shape=[jax.ShapeDtypeStruct((rows, width), BF16)] * count,
        in_specs=[pl.BlockSpec(memory_space=pltpu.SMEM)]
        + [pl.BlockSpec(memory_space=pltpu.VMEM)] * 4,
        out_specs=[pl.BlockSpec(memory_space=pl.ANY)] * count,
        scratch_shapes=[
            pltpu.VMEM((2, rows, width), BF16),
            pltpu.SemaphoreType.DMA((2,)),
        ],
        compiler_params=pltpu.CompilerParams(vmem_limit_bytes=VMEM_LIMIT),
        cost_estimate=pl.CostEstimate(flops=0, bytes_accessed=2**20, transcendentals=0),
        name="weight_parts",
    )(place.reshape(1), x, raw, out_part, ends)


def assemble_kernel(plan, count, place_ref, *refs):
    block_refs, refs = refs[:count], refs[count:]
    out_refs, (low, wide, in_sems, out_sems) = refs[:-4], refs[-4:]
    place = place_ref[0]

    def load(j):
        return pltpu.make_async_copy(block_refs[j], low.at[j % 2], in_sems.at[j % 2])

    def stores(j):
        return [
            pltpu.make_async_copy(
                wide.at[j % 2, pl.ds(first, rows)],
                out_refs[which].at[
                    pl.ds(pl.multiple_of(base + (place ^ j) * rows, 8), rows),
                    pl.ds(column, wide.shape[2]),
                ],
                out_sems.at[j % 2, i],
            )
            for i, (which, first, rows, base, column) in enumerate(plan)
        ]

    load(0).start()
    for j in range(count):
        if j + 1 < count:
            load(j + 1).start()
        load(j).wait()
        if j >= 2:
            for copy in stores(j - 2):
                copy.wait()
        wide[j % 2] = low[j % 2].astype(F32)
        for copy in stores(j):
            copy.start()
    for j in range(max(0, count - 2), count):
        for copy in stores(j):
            copy.wait()


def assemble(place, blocks, shapes, plan):
    count = len(blocks)
    rows, width = blocks[0].shape
    any_spec = pl.BlockSpec(memory_space=pl.ANY)
    return pl.pallas_call(
        functools.partial(assemble_kernel, plan, count),
        out_shape=[jax.ShapeDtypeStruct(shape, F32) for shape in shapes],
        in_specs=[pl.BlockSpec(memory_space=pltpu.SMEM)] + [any_spec] * count,
        out_specs=[any_spec] * len(shapes),
        scratch_shapes=[
            pltpu.VMEM((2, rows, width), BF16),
            pltpu.VMEM((2, rows, width), F32),
            pltpu.SemaphoreType.DMA((2,)),
            pltpu.SemaphoreType.DMA((2, len(plan))),
        ],
        compiler_params=pltpu.CompilerParams(vmem_limit_bytes=VMEM_LIMIT),
        cost_estimate=pl.CostEstimate(flops=0, bytes_accessed=2**20, transcendentals=0),
        name="assemble",
    )(place.reshape(1), *blocks)


def shared_grads_kernel(count, place_ref, *refs):
    x_refs, g_all, refs = refs[:count], refs[count], refs[count + 1 :]
    (sact, sdpair, dl, grads_ref, router_ref, xs, gs, grads, router, sems) = refs
    at = pl.program_id(0)
    slot = lax.rem(at, 2)

    def load(j, into):
        return (
            pltpu.make_async_copy(x_refs[j], xs.at[into], sems.at[0, into]),
            pltpu.make_async_copy(g_all.at[place_ref[0] ^ j], gs.at[into], sems.at[1, into]),
        )

    @pl.when(at == 0)
    def _():
        for copy in load(0, 0):
            copy.start()
        grads[...] = jnp.zeros_like(grads)
        router[...] = jnp.zeros_like(router)

    for j in range(1, count):

        @pl.when(at == j - 1)
        def _():
            for copy in load(j, j % 2):
                copy.start()

    for copy in load(0, slot):
        copy.wait()
    x, g = xs[slot], gs[slot]
    grads[0] += dot(sdpair[0, 0], x, TN)
    grads[1] += dot(sdpair[0, 1], x, TN)
    grads[2] += dot(sact[0], g, TN)
    router[...] += dot(dl[0], x, TN)

    @pl.when(at == count - 1)
    def _():
        grads_ref[...] = grads[...].astype(BF16)
        router_ref[...] = router[...]


def shared_grads(place, x_blocks, g_all, sact, sdpair, dl):
    count = len(x_blocks)
    tokens, width = x_blocks[0].shape
    share, padded = sact.shape[2], dl.shape[2]
    any_spec = pl.BlockSpec(memory_space=pl.ANY)
    return pl.pallas_call(
        functools.partial(shared_grads_kernel, count),
        grid=(count,),
        out_shape=(
            jax.ShapeDtypeStruct((3, share, width), BF16),
            jax.ShapeDtypeStruct((padded, width), F32),
        ),
        in_specs=[pl.BlockSpec(memory_space=pltpu.SMEM)]
        + [any_spec] * (count + 1)
        + [
            pl.BlockSpec((1, tokens, share), lambda j: (j, 0, 0)),
            pl.BlockSpec((1, 2, tokens, share), lambda j: (j, 0, 0, 0)),
            pl.BlockSpec((1, tokens, padded), lambda j: (j, 0, 0)),
        ],
        out_specs=(
            pl.BlockSpec((3, share, width), lambda j: (0, 0, 0)),
            pl.BlockSpec((padded, width), lambda j: (0, 0)),
        ),
        scratch_shapes=[
            pltpu.VMEM((2, tokens, width), BF16),
            pltpu.VMEM((2, tokens, width), BF16),
            pltpu.VMEM((3, share, width), F32),
            pltpu.VMEM((padded, width), F32),
            pltpu.SemaphoreType.DMA((2, 2)),
        ],
        compiler_params=pltpu.CompilerParams(vmem_limit_bytes=VMEM_LIMIT),
        cost_estimate=pl.CostEstimate(
            flops=count * tokens * width * share,
            bytes_accessed=2**20,
            transcendentals=0,
        ),
        name="shared_grads",
    )(place.reshape(1), *x_blocks, g_all, sact, sdpair, dl)


def on_device(
    hidden_in,
    cotangent,
    gain_attn,
    qkv_weight,
    qkv_bias,
    out_weight,
    gain_ffn,
    router_weight,
    routes,
    shared_gate,
    shared_in,
    shared_out,
    expert_in,
    expert_out,
):
    tokens, width = hidden_in.shape
    ctx_count = lax.axis_size("ctx")
    heads_local = qkv_weight.shape[2] // HD
    local = expert_in.shape[0]
    experts = local * ctx_count
    top_count = routes.shape[1]
    capacity = 3 * tokens * top_count // (2 * experts)
    place = lax.axis_index("ctx")
    order = jnp.arange(ctx_count, dtype=jnp.int32) ^ place
    score_scale = 1.0 / math.sqrt(HD)
    query_pos = place * tokens + jnp.arange(tokens, dtype=jnp.int32)
    cosine, sine = rotary_tables(query_pos, HD)

    x_full = hidden_in.astype(F32)
    inv_one = lax.rsqrt(jnp.mean(x_full * x_full, axis=-1, keepdims=True) + EPS)
    normed_one = x_full * inv_one
    x_one = (normed_one * gain_attn).astype(BF16)
    projected = (
        jnp.einsum("td,dcf->ctf", x_one, qkv_weight, preferred_element_type=F32)
        + qkv_bias[:, None]
    )
    shaped = projected.reshape(3, tokens, heads_local, HD).transpose(0, 2, 1, 3)
    query = rotate(shaped[0], cosine, sine).astype(BF16)
    key_local = rotate(shaped[1], cosine, sine).astype(BF16)
    value_local = shaped[2].astype(BF16)
    kv_rows = heads_local * tokens
    route_rows = -(-tokens * top_count // HD)
    behind = jnp.pad(
        routes.T.astype(BF16).reshape(route_rows, HD), ((0, -route_rows % 16), (0, 0))
    )
    kv_local = jnp.stack(
        [
            jnp.concatenate([key_local.reshape(kv_rows, HD), behind], axis=0),
            jnp.concatenate([value_local.reshape(kv_rows, HD), behind], axis=0),
        ]
    )
    share = shared_out.shape[0] // ctx_count
    piece = shared_out.shape[1]
    shared_send = jnp.concatenate(
        [
            shared_in.transpose(1, 2, 0).reshape(2, ctx_count, share, piece),
            shared_out.reshape(1, ctx_count, share, piece),
        ],
        axis=0,
    ).transpose(1, 0, 2, 3)
    kv_blocks = gather_end(gather_start(kv_local), shared_send)
    g_all = lax.all_gather(after(cotangent, kv_blocks[2 % ctx_count], kv_blocks[4 % ctx_count]), "ctx", axis=0)
    shared_got = lax.all_to_all(shared_send, "ctx", split_axis=0, concat_axis=0, tiled=True)

    half_rows = out_weight.shape[0] // 2
    core = place % 2
    out_mine = lax.all_gather(
        lax.dynamic_slice_in_dim(out_weight, core * half_rows, half_rows, 0), "tp", axis=0
    )

    routes_all = jnp.stack([b[0, kv_rows : kv_rows + route_rows] for b in kv_blocks])
    routes_all = routes_all.reshape(ctx_count, 1, top_count, tokens)
    own_experts = (place * local + jnp.arange(local, dtype=jnp.int32)).astype(BF16)
    hit = jnp.any(routes_all == own_experts[None, :, None, None], axis=2)
    token_at = jnp.arange(tokens, dtype=jnp.int32)
    earlier = (token_at[:, None] <= token_at[None, :]).astype(BF16)
    rank = dot(hit.astype(BF16).reshape(-1, tokens), earlier, NN).reshape(hit.shape) - 1.0
    slot_rows = jnp.where(hit, rank, -1.0).astype(jnp.int32)
    slot_cols = slot_rows.transpose(0, 2, 1)
    padded = -(-(experts + 1) // 8) * 8
    w_router = jnp.concatenate(
        [
            router_weight.T,
            shared_gate[None],
            jnp.zeros((padded - experts - 1, width), BF16),
        ],
        axis=0,
    )
    w_in = expert_in.transpose(0, 2, 3, 1)

    attended, lse = attend(place, query, kv_blocks)
    att = attended.astype(BF16).transpose(1, 0, 2).reshape(tokens, heads_local * HD)
    att = after(att, shared_got)
    out_mine = after(out_mine, attended)
    out_other = swap(out_mine, 1)
    att_mine, att_other = columns(place, gather_tp(att))
    att_mine = after(att_mine, slot_rows, slot_cols, w_router, w_in)
    rows = out_mine.shape[0] * half_rows
    hidden = x_full + (
        dot(att_mine, out_mine.reshape(rows, width), NN)
        + dot(att_other, out_other.reshape(rows, width), NN)
    )
    shared_w = shared_got.transpose(1, 2, 0, 3).reshape(3, share, width)
    whole_share = -(-share // 16) * 16
    if whole_share > share:
        shared_w = jnp.pad(shared_w, ((0, 0), (0, whole_share - share), (0, 0)))
    inv_two = lax.rsqrt(jnp.mean(hidden * hidden, axis=-1, keepdims=True) + EPS)
    normed_two = hidden * inv_two
    x_two = (normed_two * gain_ffn).astype(BF16)

    units, group = expert_out.shape[1], 2
    kept = [
        jax.ShapeDtypeStruct(shape, BF16)
        for shape in (
            (local, ctx_count, capacity, width),
            (local, ctx_count, capacity, width),
            (local, ctx_count, capacity, units),
            (2 * local, ctx_count, capacity, units),
            (ctx_count, tokens, whole_share),
            (ctx_count, 2, tokens, whole_share),
            (ctx_count, tokens, padded),
        )
    ]
    weights = (w_router, w_in, expert_out, shared_w)
    got = gather_start(x_two)
    x_blocks = [got[0], got[1]]
    dxs = []
    early = None
    for at in range(0, ctx_count, group):
        if at == 4 and ctx_count == 8:
            pair_two = pair_sum(dxs, 2)
            early = (pair_two, pair_two[: tokens // 2].astype(BF16))
        if at == 6 and ctx_count == 8:
            x_blocks[6] = after(x_blocks[6], early[1])
        dx, kept = run_experts(
            at,
            experts,
            place,
            x_blocks[at : at + group],
            g_all,
            slot_rows,
            slot_cols,
            weights,
            kept,
        )
        dxs += dx
        if at == 0:
            x_blocks = x_blocks[:2] + gather_end(got, dx[0])[2:]
    grad_x_part = scatter_ctx(dxs, early)
    outs = run_outputs(kept[2], slot_cols, kept[4], expert_out, shared_w)
    grad_x_low = grad_x_part.astype(BF16)
    out_middle = scatter_middle(scatter_start(after(outs, grad_x_low)))
    kept = after(kept, outs[0], *out_middle[0])
    rows_x, rows_g, act_low, dpair, s_act, s_dpair, low_logits = kept
    shared_low, router_part = shared_grads(place, x_blocks, g_all, s_act, s_dpair, low_logits)
    expert_grads = grads_of_experts(rows_x, rows_g, act_low, dpair)
    grad_expert_in, grad_expert_out = expert_grads
    gain_ffn_part = jnp.sum(grad_x_part * normed_two, axis=0)
    small = sum_tp_small(jnp.concatenate([router_part, gain_ffn_part[None]], axis=0))
    half = tokens // 2
    first = lax.psum(grad_x_low[:half], "tp")
    second = lax.psum(after(grad_x_low[half:], first, *out_middle[0]), "tp")
    out_part = scatter_end(out_middle)

    shared_back = lax.all_to_all(
        shared_low[:, :share].reshape(3, share, ctx_count, piece).transpose(2, 0, 1, 3),
        "ctx",
        split_axis=0,
        concat_axis=0,
        tiled=True,
    )
    shared_back = shared_back.astype(F32)
    grad_shared_in = shared_back[:, :2].transpose(3, 1, 0, 2).reshape(shared_in.shape)
    grad_shared_out = shared_back[:, 2].reshape(shared_out.shape)
    summed = jnp.concatenate([first, second], axis=0)
    summed = after(summed, grad_shared_in, grad_shared_out, *expert_grads, out_part)
    summed = summed.astype(F32)
    grad_y = cotangent.astype(F32)
    grad_normed_two = summed * gain_ffn
    grad_hidden = grad_y + inv_two * (
        grad_normed_two
        - normed_two * jnp.mean(grad_normed_two * normed_two, axis=-1, keepdims=True)
    )
    grad_hidden_low = grad_hidden.astype(BF16)
    out_weight_part = dot(att, grad_hidden_low, (((0,), (0,)), ((), ())))
    grad_att = (
        dot(grad_hidden_low, out_weight, (((1,), (1,)), ((), ())))
        .astype(BF16)
        .reshape(tokens, heads_local, HD)
        .transpose(1, 0, 2)
    )
    delta = jnp.sum(grad_att.astype(F32) * attended, axis=-1)
    delta = jnp.broadcast_to(delta[:, None], lse.shape)
    grad_query, grad_pairs = attend_back(place, query, grad_att, lse, delta, kv_blocks)
    ffn_total = sum_tp_start(out_part)
    grad_pairs = after(grad_pairs, ffn_total, small)
    ffn_low = sum_tp_end(after(ffn_total, grad_query))
    grad_kv = scatter_ctx([grad_pairs[j] for j in range(ctx_count)])
    grad_kv = after(grad_kv, ffn_low)

    def raw_part(value):
        return value.astype(BF16).transpose(1, 0, 2).reshape(tokens, heads_local * HD)

    raw = [
        raw_part(rotate(grad_query, cosine, -sine)),
        raw_part(rotate(grad_kv[0], cosine, -sine)),
        raw_part(grad_kv[1]),
    ]
    raw = jnp.concatenate(raw, axis=1)
    grad_x_one_part = jnp.einsum(
        "tcf,dcf->td",
        raw.reshape(tokens, 3, -1),
        qkv_weight,
        preferred_element_type=F32,
    )
    grad_x_low = grad_x_one_part.astype(BF16)
    half_way = sum_tp_start(grad_x_low)
    grad_x_one = sum_tp_end(half_way)
    x_one = after(x_one, grad_x_low)
    gain_attn_part = jnp.sum(grad_x_one_part * normed_one, axis=0)
    gain_sum = sum_tp_small(gain_attn_part[None])
    head_width = heads_local * HD
    gain_rows = width // head_width
    ends = jnp.concatenate(
        [jnp.sum(raw.astype(F32), axis=0).reshape(3, -1)]
        + [gain_sum.reshape(gain_rows, -1), small.reshape((padded + 1) * gain_rows, -1)],
        axis=0,
    )
    ends = jnp.pad(ends, ((0, -ends.shape[0] % (16 * ctx_count)), (0, 0))).astype(BF16)
    turns = width // head_width
    sums = sum_ctx(
        weight_parts(place, x_one, raw, out_weight_part.astype(BF16), ends, ctx_count), half_way
    )
    q_rows = width // ctx_count
    out_rows = out_weight.shape[0] // ctx_count
    plan = [(0, c * q_rows, q_rows, c * width, 0) for c in range(3)] + [
        (1, 3 * q_rows + k * out_rows, out_rows, 0, k * head_width) for k in range(turns)
    ]
    qkv_grad, out_weight_grad = assemble(
        place, sums, [(3 * width, head_width), out_weight.shape], plan
    )
    qkv_grad = qkv_grad.reshape(3, width, head_width).transpose(1, 0, 2)
    ends = relative(jnp.stack([b[3 * q_rows + turns * out_rows :] for b in sums]))
    ends = ends.reshape(-1, head_width).astype(F32)
    small = ends[3 + gain_rows : 3 + (padded + 2) * gain_rows].reshape(padded + 1, width)
    grad_x_one = after(grad_x_one, sums[2]).astype(F32)
    grad_normed_one = grad_x_one * gain_attn
    grad_input = grad_hidden + inv_one * (
        grad_normed_one
        - normed_one * jnp.mean(grad_normed_one * normed_one, axis=-1, keepdims=True)
    )
    block_out = (hidden + ffn_low.astype(F32)).astype(BF16)
    return (
        block_out,
        grad_input,
        ends[3 : 3 + gain_rows].reshape(-1),
        qkv_grad,
        ends[:3],
        out_weight_grad,
        small[padded],
        small[:experts].T,
        small[experts],
        grad_shared_in,
        grad_shared_out,
        grad_expert_in.transpose(0, 3, 1, 2),
        grad_expert_out,
    )


def solution(mesh):
    return jax.shard_map(
        on_device,
        mesh=mesh,
        in_specs=(
            P("ctx", None),
            P("ctx", None),
            P(),
            P(None, None, "tp"),
            P(None, "tp"),
            P("tp", None),
            P(),
            P(),
            P("ctx", None),
            P(),
            P("ctx", None, "tp"),
            P("tp", "ctx"),
            P("ctx", None, None, "tp"),
            P("ctx", "tp", None),
        ),
        out_specs=(
            P("ctx", None),
            P("ctx", None),
            P(),
            P(None, None, "tp"),
            P(None, "tp"),
            P("tp", None),
            P(),
            P(),
            P(),
            P("ctx", None, "tp"),
            P("tp", "ctx"),
            P("ctx", None, None, "tp"),
            P("ctx", "tp", None),
        ),
        check_vma=False,
    )
```

```python
import functools
import math

import jax
import jax.numpy as jnp
from jax import lax
from jax.experimental import pallas as pl
from jax.experimental.pallas import tpu as pltpu
from jax.sharding import PartitionSpec as P

HD = 128
EPS = 1e-06
THETA = 1000000.0
NEG = -1e30
F32 = jnp.float32
BF16 = jnp.bfloat16


def rotary_tables(positions, width):
    half_width = width // 2
    freqs = THETA ** (-(jnp.arange(half_width, dtype=F32) * 2.0) / width)
    angles = positions.astype(F32)[:, None] * freqs[None, :]
    return (jnp.cos(angles), jnp.sin(angles))


def rotate(values, cosine, sine):
    half_width = values.shape[-1] // 2
    first, second = values[..., :half_width], values[..., half_width:]
    return jnp.concatenate(
        [first * cosine - second * sine, second * cosine + first * sine], axis=-1
    )


def dot(a, b, dims):
    return lax.dot_general(a, b, dims, preferred_element_type=F32)


def swap(value, bits):
    count = lax.axis_size("ctx")
    return lax.ppermute(value, "ctx", [(i, i ^ bits) for i in range(count)])


def relative(natural):
    count = natural.shape[0]
    order = jnp.arange(count, dtype=jnp.int32) ^ lax.axis_index("ctx")
    return natural[order]


def nothing_kernel(*refs):
    pass


def after(values, *others):
    single = not isinstance(values, (list, tuple))
    values = [values] if single else list(values)
    any_spec = pl.BlockSpec(memory_space=pl.ANY)
    results = pl.pallas_call(
        nothing_kernel,
        out_shape=[jax.ShapeDtypeStruct(v.shape, v.dtype) for v in values],
        in_specs=[any_spec] * (len(values) + len(others)),
        out_specs=[any_spec] * len(values),
        input_output_aliases={i: i for i in range(len(values))},
        name="after",
    )(*values, *others)
    return results[0] if single else results


def gather_start(own):
    if lax.axis_size("ctx") != 8:
        return relative(lax.all_gather(own, "ctx", axis=0))
    return [own, swap(own, 1), swap(own, 2), swap(own, 4)]


def gather_end(got, *others):
    if lax.axis_size("ctx") != 8:
        return [got[j] for j in range(lax.axis_size("ctx"))]
    own, b1, b2, b4 = got
    if others:
        b2, b4 = after((b2, b4), *others)
    half = own.shape[0] // 2
    via_x, via_y = swap(b4[:half], 2), swap(b2[half:], 4)
    b3, b5 = swap(b2, 1), swap(b4, 1)
    b6 = jnp.concatenate([via_x, via_y], axis=0)
    return [own, b1, b2, b3, b4, b5, b6, swap(b6, 1)]


def gather_ctx(own, *others):
    return gather_end(gather_start(own), *others)


def pair_sum(parts, j):
    return parts[j].astype(F32) + swap(parts[j ^ 1], 1).astype(F32)


def scatter_ctx(parts, early=None):
    return scatter_end(scatter_middle(scatter_start(parts, early)))


def scatter_start(parts, early=None):
    if lax.axis_size("ctx") != 8:
        return [jnp.stack(parts)], None
    half = parts[0].shape[0] // 2
    pair = {j: pair_sum(parts, j) for j in (2, 4, 6, 0) if j != 2 or early is None}
    if early is None:
        early = (pair[2], pair[2][:half].astype(BF16))
    q6 = pair[6].astype(BF16)
    hops = [early[1], pair[4][half:].astype(BF16), q6[:half], q6[half:]]
    return hops, (early[0], pair[4], pair[0])


def scatter_middle(started):
    hops, stay = started
    if lax.axis_size("ctx") != 8:
        return hops, None
    two, four, zero = stay
    half = two.shape[0] // 2
    r2, r4 = swap(hops[0], 2), swap(hops[1], 4)
    via_x, via_y = swap(hops[2], 2), swap(hops[3], 4)
    r4a = (four[:half] + via_x.astype(F32)).astype(BF16)
    r2b = (two[half:] + via_y.astype(F32)).astype(BF16)
    return [r4a, r2b], (r2, r4, zero)


def scatter_end(started, *others):
    hops, stay = started
    if lax.axis_size("ctx") != 8:
        natural = relative(hops[0])
        flat = natural.reshape((-1,) + natural.shape[2:])
        return lax.psum_scatter(flat, "ctx", scatter_dimension=0, tiled=True).astype(F32)
    if others:
        hops = after(hops, *others)
    r2, r4, zero = stay
    r4a, r2b = swap(hops[0], 4), swap(hops[1], 2)
    low = r2.astype(F32) + r4a.astype(F32)
    high = r2b.astype(F32) + r4.astype(F32)
    return zero + jnp.concatenate([low, high], axis=0)


def sum_ctx(parts, *others):
    own = scatter_end(scatter_middle(scatter_start(parts)), *others)
    return gather_ctx(own.astype(BF16))


def shards(value):
    count = lax.axis_size("ctx")
    rows = value.shape[0] // count
    place = lax.axis_index("ctx")
    return [lax.dynamic_slice_in_dim(value, (place ^ j) * rows, rows, 0) for j in range(count)]


def gather_tp(own):
    count = lax.axis_size("tp")
    return [own] + [
        lax.ppermute(own, "tp", [(i, i ^ k) for i in range(count)]) for k in range(1, count)
    ]


NT = (((1,), (1,)), ((), ()))
NN = (((1,), (0,)), ((), ()))
TN = (((0,), (0,)), ((), ()))
VMEM_LIMIT = 60 * 1024 * 1024


def sum_tp_start(*values):
    pieces = [v.astype(BF16).reshape(lax.axis_size("tp"), -1, v.shape[1]) for v in values]
    pieces = jnp.concatenate(pieces, axis=1)
    got = lax.all_to_all(pieces, "tp", split_axis=0, concat_axis=0, tiled=True)
    return jnp.sum(got.astype(F32), axis=0).astype(BF16)


def sum_tp_end(total):
    count, at = lax.axis_size("tp"), lax.axis_index("tp")
    blocks = jnp.stack(gather_tp(total))
    blocks = blocks[jnp.arange(count, dtype=jnp.int32) ^ at]
    return blocks


def sum_tp_small(value):
    count, bits = lax.axis_size("tp"), 1
    while bits < count:
        value = value + lax.ppermute(value, "tp", [(i, i ^ bits) for i in range(count)])
        bits *= 2
    return value


def columns_kernel(count, places, *refs):
    block_refs, (mine, other) = refs[:count], refs[count:]
    core, at = places[0], places[1]
    width = mine.shape[1] // count
    for k in range(count):
        to = pl.ds(pl.multiple_of((at ^ k) * width, width), width)
        mine[:, to] = block_refs[k][:, pl.ds(pl.multiple_of(core * width, width), width)]
        other[:, to] = block_refs[k][:, pl.ds(pl.multiple_of((1 - core) * width, width), width)]


def columns(place, blocks):
    count = len(blocks)
    rows, width = blocks[0].shape
    vmem = pl.BlockSpec(memory_space=pltpu.VMEM)
    half = jax.ShapeDtypeStruct((rows, count * width // 2), blocks[0].dtype)
    return pl.pallas_call(
        functools.partial(columns_kernel, count),
        out_shape=(half, half),
        in_specs=[pl.BlockSpec(memory_space=pltpu.SMEM)] + [vmem] * count,
        out_specs=(vmem, vmem),
        compiler_params=pltpu.CompilerParams(vmem_limit_bytes=VMEM_LIMIT),
        cost_estimate=pl.CostEstimate(flops=0, bytes_accessed=2**20, transcendentals=0),
        name="columns",
    )(jnp.stack([place % 2, lax.axis_index("tp")]), *blocks)


def attend_kernel(factor, count, place_ref, q_ref, *refs):
    kv_refs, (att_ref, lse_ref, kv, sems) = refs[:count], refs[count:]
    rows = kv.shape[2]
    copies = [
        pltpu.make_async_copy(kv_refs[j].at[:, pl.ds(0, rows)], kv.at[j], sems.at[j])
        for j in range(count)
    ]
    for copy in copies:
        copy.start()
    for copy in copies:
        copy.wait()
    place = place_ref[0]
    heads, tokens, _ = q_ref.shape

    def one_head(head, _):
        query = q_ref[head]
        here = pl.ds(pl.multiple_of(head * tokens, tokens), tokens)

        def scores(j):
            return dot(kv[j, 0, here], query, NT) * factor

        key_at = lax.broadcasted_iota(jnp.int32, (tokens, tokens), 0)
        query_at = lax.broadcasted_iota(jnp.int32, (tokens, tokens), 1)
        first = jnp.where(key_at <= query_at, scores(0), NEG)
        top = jnp.max(first, axis=0, keepdims=True)
        exps = jnp.exp2(first - top)
        total = jnp.sum(exps, axis=0, keepdims=True)
        acc = dot(kv[0, 1, here], exps.astype(BF16), TN)

        def earlier(i, carry):
            top, total, acc = carry
            j = place ^ i
            now = scores(j)
            higher = jnp.maximum(top, jnp.max(now, axis=0, keepdims=True))
            exps = jnp.exp2(now - higher)
            keep = jnp.exp2(top - higher)
            total = total * keep + jnp.sum(exps, axis=0, keepdims=True)
            acc = acc * keep + dot(kv[j, 1, here], exps.astype(BF16), TN)
            return higher, total, acc

        top, total, acc = lax.fori_loop(0, place, earlier, (top, total, acc))
        att_ref[head] = (acc / total).T
        lse_ref[head] = jnp.broadcast_to(top + jnp.log2(total), lse_ref.shape[1:])
        return 0

    lax.fori_loop(0, heads, one_head, 0)


def attend(place, query, kv_blocks):
    heads, tokens, size = query.shape
    count = len(kv_blocks)
    factor = math.log2(math.e) / math.sqrt(size)
    flops = 4 * count * heads * tokens * tokens * size
    return pl.pallas_call(
        functools.partial(attend_kernel, factor, count),
        out_shape=(
            jax.ShapeDtypeStruct((heads, tokens, size), F32),
            jax.ShapeDtypeStruct((heads, 8, tokens), F32),
        ),
        in_specs=[
            pl.BlockSpec(memory_space=pltpu.SMEM),
            pl.BlockSpec(memory_space=pltpu.VMEM),
        ]
        + [pl.BlockSpec(memory_space=pl.ANY)] * count,
        out_specs=(pl.BlockSpec(memory_space=pltpu.VMEM),) * 2,
        scratch_shapes=[
            pltpu.VMEM((count, 2, heads * tokens, size), BF16),
            pltpu.SemaphoreType.DMA((count,)),
        ],
        compiler_params=pltpu.CompilerParams(vmem_limit_bytes=VMEM_LIMIT),
        cost_estimate=pl.CostEstimate(
            flops=flops // 16, bytes_accessed=2**20, transcendentals=0
        ),
        name="attend",
    )(place.reshape(1), query, *kv_blocks)


def attend_back_kernel(factor, scale, count, place_ref, q_ref, do_ref, lse_ref, delta_ref, *refs):
    kv_refs, (dq_ref, dkv_ref, kv, dkv, dq, sems, out_sems) = refs[:count], refs[count:]
    rows = kv.shape[2]
    copies = [
        pltpu.make_async_copy(kv_refs[j].at[:, pl.ds(0, rows)], kv.at[j], sems.at[j])
        for j in range(count)
    ]
    for copy in copies:
        copy.start()
    for copy in copies:
        copy.wait()
    place = place_ref[0]
    heads, tokens, _ = q_ref.shape

    def out_copy(j):
        return pltpu.make_async_copy(dkv.at[j], dkv_ref.at[j], out_sems.at[j])

    def one_block(j, masked):
        def one_head(head, _):
            query, do = q_ref[head], do_ref[head]
            here = pl.ds(pl.multiple_of(head * tokens, tokens), tokens)
            key, value = kv[j, 0, here], kv[j, 1, here]
            scores = dot(key, query, NT) * factor
            probs = jnp.exp2(scores - lse_ref[head, :1])
            if masked:
                key_at = lax.broadcasted_iota(jnp.int32, (tokens, tokens), 0)
                query_at = lax.broadcasted_iota(jnp.int32, (tokens, tokens), 1)
                probs = jnp.where(key_at <= query_at, probs, 0.0)
            dprob = dot(value, do, NT)
            dscore = (probs * (dprob - delta_ref[head, :1])).astype(BF16)
            dkv[j, 0, head] = (dot(dscore, query, NN) * scale).astype(BF16)
            dkv[j, 1, head] = dot(probs.astype(BF16), do, NN).astype(BF16)
            part = dot(key, dscore, TN)
            dq[head] = part if masked else dq[head] + part
            return 0

        lax.fori_loop(0, heads, one_head, 0)
        out_copy(j).start()

    one_block(0, True)

    def earlier(i, _):
        one_block(place ^ i, False)
        return 0

    def later(i, _):
        j = place ^ i
        dkv[j] = jnp.zeros(dkv.shape[1:], BF16)
        out_copy(j).start()
        return 0

    lax.fori_loop(0, place, earlier, 0)
    lax.fori_loop(place + 1, count, later, 0)
    for head in range(heads):
        dq_ref[head] = dq[head].T * scale
    for j in range(count):
        out_copy(j).wait()


def attend_back(place, query, do, lse, delta, kv_blocks):
    heads, tokens, size = query.shape
    count = len(kv_blocks)
    scale = 1.0 / math.sqrt(size)
    factor = math.log2(math.e) * scale
    return pl.pallas_call(
        functools.partial(attend_back_kernel, factor, scale, count),
        out_shape=(
            jax.ShapeDtypeStruct((heads, tokens, size), F32),
            jax.ShapeDtypeStruct((count, 2, heads, tokens, size), BF16),
        ),
        in_specs=[pl.BlockSpec(memory_space=pltpu.SMEM)]
        + [pl.BlockSpec(memory_space=pltpu.VMEM)] * 4
        + [pl.BlockSpec(memory_space=pl.ANY)] * count,
        out_specs=(pl.BlockSpec(memory_space=pltpu.VMEM), pl.BlockSpec(memory_space=pl.ANY)),
        scratch_shapes=[
            pltpu.VMEM((count, 2, heads * tokens, size), BF16),
            pltpu.VMEM((count, 2, heads, tokens, size), BF16),
            pltpu.VMEM((heads, size, tokens), F32),
            pltpu.SemaphoreType.DMA((count,)),
            pltpu.SemaphoreType.DMA((count,)),
        ],
        compiler_params=pltpu.CompilerParams(vmem_limit_bytes=VMEM_LIMIT),
        cost_estimate=pl.CostEstimate(
            flops=count * heads * tokens * tokens * size,
            bytes_accessed=2**20,
            transcendentals=0,
        ),
        name="attend_back",
    )(place.reshape(1), query, do, lse, delta, *kv_blocks)


def swiglu_back(one, two, dact, gate):
    sig = 1.0 / (1.0 + jnp.exp(-one))
    silu = one * sig
    act = silu * two
    prod = act * dact
    dgate = gate * dact
    d_one = (dgate * two * sig * (1.0 + one * (1.0 - sig))).astype(BF16)
    d_two = (dgate * silu).astype(BF16)
    return (gate * act).astype(BF16), d_one, d_two, prod


def experts_kernel(at, group, local, experts, given, near, place_ref, *refs):
    x_refs, refs = refs[:group], refs[group:]
    if near:
        g_refs, refs = refs[:group], refs[group:]
    else:
        g_refs = [refs[0].at[place_ref[0] ^ (at + b)] for b in range(group)]
        refs = refs[1:]
    (slot_row, slot_col, w_router, w_in, w_out, w_shared), refs = refs[:6], refs[6 + given :]
    dx_refs, refs = refs[:group], refs[group:]
    kept_refs, refs = refs[:7], refs[7:]
    (xs, gs, first_w, in_w, out_w, shared_w, dxs, left, right, sems, out_sems), stage = refs[:11], refs[11:]
    rows_x, rows_g, act_s, dpair_s, sact_s, sdpair_s, dl_s = stage
    tokens, width = xs.shape[1:]
    capacity, units = act_s.shape[2:]
    wide = local * capacity
    share = sact_s.shape[2]
    third = first_w.shape[0] - 128
    second = third // 2
    padded = w_router.shape[0]
    most = out_w.shape[1]

    loads = [pltpu.make_async_copy(x_refs[b], xs.at[b], sems.at[b]) for b in range(group)]
    fore_loads = [
        pltpu.make_async_copy(
            w_shared.at[c], first_w.at[pl.ds(c * second, share)], sems.at[2 * group + c]
        )
        for c in range(2)
    ]
    loads += [
        pltpu.make_async_copy(g_refs[b], gs.at[b], sems.at[group + b]) for b in range(group)
    ]
    base = 2 * group + 2
    more = [
        [
            pltpu.make_async_copy(
                w_in.at[e, c], in_w.at[e, pl.ds(c * most, units)], sems.at[base + 3 * e + c]
            )
            for c in range(2)
        ]
        + [
            pltpu.make_async_copy(
                w_out.at[e], out_w.at[e, pl.ds(0, units)], sems.at[base + 3 * e + 2]
            )
        ]
        for e in range(local)
    ]
    last = pltpu.make_async_copy(w_shared.at[2], shared_w, sems.at[base + 3 * local])
    for copy in loads[:group] + fore_loads:
        copy.start()
    first_w[third : third + padded] = w_router[...]
    first_w[third + padded :] = jnp.zeros((128 - padded, width), BF16)
    if second > share:
        for c in range(2):
            gap = jnp.zeros((second - share, width), BF16)
            first_w[c * second + share : (c + 1) * second] = gap
    if most > units:
        gap = jnp.zeros((most - units, width), BF16)
        for e in range(local):
            in_w[e, units:most] = gap
            in_w[e, most + units :] = gap
            out_w[e, units:] = gap

    sent = []

    def send(copy):
        copy.start()
        sent.append(copy)

    for copy in loads[:group] + fore_loads:
        copy.wait()
    for copy in loads[group:] + more[0]:
        copy.start()
    x = xs[...].reshape(group * tokens, width)
    fore = dot(x, first_w[...], NT)
    s_one, s_two = fore[:, :share], fore[:, second : second + share]
    s_gate = 1.0 / (1.0 + jnp.exp(-fore[:, third + experts : third + experts + 1]))
    row_at = lax.broadcasted_iota(jnp.int32, (padded, tokens), 0)
    slot_at = lax.broadcasted_iota(jnp.int32, (capacity, tokens), 0)
    probs, change, hits = [], [], []
    for b in range(group):
        logits = fore[b * tokens : (b + 1) * tokens, third:].T[:padded]
        shown = jnp.where(row_at < experts, logits, NEG)
        exps = jnp.exp(shown - jnp.max(shown, axis=0, keepdims=True))
        soft = exps / jnp.sum(exps, axis=0, keepdims=True)
        probs.append(jnp.where(row_at == experts, 1.0 / (1.0 + jnp.exp(-logits)), soft))
        change.append(jnp.zeros((padded, tokens), F32))
        picks = jnp.concatenate(
            [
                jnp.where(slot_at == slot_row[b, e : e + 1, :], 1.0, 0.0).astype(BF16)
                for e in range(local)
            ],
            axis=0,
        )
        rows = dot(picks, xs[b], NN).astype(BF16)
        for e in range(local):
            rows_x[e, b] = rows[e * capacity : (e + 1) * capacity]
        loads[group + b].wait()
        if b == group - 1:
            for e in range(1, local):
                for copy in more[e]:
                    copy.start()
            last.start()
        rows = dot(picks, gs[b], NN).astype(BF16)
        for e in range(local):
            rows_g[e, b] = rows[e * capacity : (e + 1) * capacity]
    def send_all(i, lead):
        for e in range(lead):
            send(
                pltpu.make_async_copy(
                    stage[i].at[e], kept_refs[i].at[e, pl.ds(at, group)], out_sems.at[i, e]
                )
            )

    send_all(0, local)
    send_all(1, local)
    is_expert = row_at < experts
    for e in range(local):
        chosen = row_at == place_ref[0] * local + e
        gates, owns, hits = [], [], []
        for b in range(group):
            own = jnp.sum(jnp.where(chosen, probs[b], 0.0), axis=0, keepdims=True)
            hit = slot_at == slot_row[b, e : e + 1, :]
            gates.append(jnp.sum(jnp.where(hit, own, 0.0), axis=1, keepdims=True))
            owns.append(own)
            hits.append(hit)
        for copy in more[e]:
            copy.wait()
        pair = dot(rows_x[e].reshape(group * capacity, width), in_w[e], NT)
        dact = dot(rows_g[e].reshape(group * capacity, width), out_w[e], NT)
        act, d_one, d_two, prod = swiglu_back(
            pair[:, :most], pair[:, most:], dact, jnp.concatenate(gates, axis=0)
        )
        act_s[e] = act[:, :units].reshape(group, capacity, units)
        dpair_s[2 * e] = d_one[:, :units].reshape(group, capacity, units)
        dpair_s[2 * e + 1] = d_two[:, :units].reshape(group, capacity, units)
        row_dot = jnp.sum(prod, axis=1, keepdims=True)
        drow = dot(jnp.concatenate([d_one, d_two], axis=1), in_w[e], NN).astype(BF16)
        for b in range(group):
            rows = slice(b * capacity, (b + 1) * capacity)
            found = jnp.sum(jnp.where(hits[b], row_dot[rows], 0.0), axis=0, keepdims=True)
            change[b] += (found * owns[b]) * (
                jnp.where(chosen, 1.0, 0.0) - jnp.where(is_expert, probs[b], 0.0)
            )
            right[b, e * capacity : (e + 1) * capacity] = drow[rows]
    send_all(2, local)
    send_all(3, 2 * local)
    last.wait()
    g = gs[...].reshape(group * tokens, width)
    s_dact = dot(g, shared_w[...], NT)
    act, d_one, d_two, prod = swiglu_back(s_one, s_two, s_dact, s_gate)
    sact_s[...] = act.reshape(group, tokens, share)
    sdpair_s[:, 0] = d_one.reshape(group, tokens, share)
    sdpair_s[:, 1] = d_two.reshape(group, tokens, share)
    dslogit = jnp.sum(prod, axis=1, keepdims=True) * s_gate * (1.0 - s_gate)
    lane_at = lax.broadcasted_iota(jnp.int32, (tokens, 128), 1)
    rest = jnp.zeros((128 - padded, tokens), F32)
    deep = wide + 2 * share
    column_at = lax.broadcasted_iota(jnp.int32, (tokens, capacity), 1)
    stores = []
    for b in range(group):
        rows = slice(b * tokens, (b + 1) * tokens)
        columns = jnp.concatenate([change[b], rest], axis=0).T
        columns = jnp.where(lane_at == experts, dslogit[rows], columns)[:, :padded].astype(BF16)
        dl_s[b] = columns
        left[b, :, deep : deep + padded] = columns
        right[b, deep : deep + padded] = w_router[...]
        for e in range(local):
            picks = jnp.where(column_at == slot_col[b, :, e : e + 1], 1.0, 0.0).astype(BF16)
            left[b, :, e * capacity : (e + 1) * capacity] = picks
        left[b, :, wide : wide + share] = d_one[rows]
        left[b, :, wide + share : wide + 2 * share] = d_two[rows]
        right[b, wide : wide + share] = first_w[:share]
        right[b, wide + share : wide + 2 * share] = first_w[second : second + share]
        dxs[b] = dot(left[b], right[b], NN).astype(BF16)
        send(pltpu.make_async_copy(dxs.at[b], dx_refs[b], out_sems.at[7, b]))
    for i in range(4, 7):
        send(pltpu.make_async_copy(stage[i], kept_refs[i].at[pl.ds(at, group)], out_sems.at[i, 0]))
    for copy in sent:
        copy.wait()


def run_experts(at, experts, place, x_group, g_group, slot_rows, slot_cols, weights, kept):
    given = kept if at else []
    group = len(x_group)
    near = len(g_group) == group
    tokens, width = x_group[0].shape
    w_router, w_in, w_out, w_shared = weights
    local = w_out.shape[0]
    share = w_shared.shape[1]
    padded = w_router.shape[0]
    capacity, units = kept[2].shape[2:]
    any_spec = pl.BlockSpec(memory_space=pl.ANY)
    block = jax.ShapeDtypeStruct((tokens, width), BF16)
    deep = local * capacity + 2 * share + padded
    flops = group * 2 * tokens * width * (local * capacity * 3 + 5 * share) + (
        group * 2 * width * local * capacity * units * 5
    )
    step = at // group
    wide_units = -(-units // 128) * 128
    fore = 2 * (-(-share // 64) * 64) + 128
    results = pl.pallas_call(
        functools.partial(experts_kernel, at, group, local, experts, len(given), near),
        grid=(1,),
        out_shape=(block,) * group + tuple(jax.ShapeDtypeStruct(k.shape, k.dtype) for k in kept),
        in_specs=[pl.BlockSpec(memory_space=pltpu.SMEM)]
        + [any_spec] * (group + len(g_group))
        + [
            pl.BlockSpec((group, local, tokens), lambda i: (step, 0, 0)),
            pl.BlockSpec((group, tokens, local), lambda i: (step, 0, 0)),
            pl.BlockSpec((padded, width), lambda i: (0, 0)),
        ]
        + [any_spec] * (3 + len(given)),
        out_specs=(any_spec,) * (group + len(kept)),
        input_output_aliases={7 + group + len(g_group) + i: group + i for i in range(len(given))},
        scratch_shapes=[
            pltpu.VMEM((group, tokens, width), BF16),
            pltpu.VMEM((group, tokens, width), BF16),
            pltpu.VMEM((fore, width), BF16),
            pltpu.VMEM((local, 2 * wide_units, width), BF16),
            pltpu.VMEM((local, wide_units, width), BF16),
            pltpu.VMEM((share, width), BF16),
            pltpu.VMEM((group, tokens, width), BF16),
            pltpu.VMEM((group, tokens, deep), BF16),
            pltpu.VMEM((group, deep, width), BF16),
            pltpu.SemaphoreType.DMA((2 * group + 3 + 3 * local,)),
            pltpu.SemaphoreType.DMA((8, max(2 * local, group))),
        ]
        + [
            pltpu.VMEM(k.shape[:1] + (group,) + k.shape[2:], BF16) for k in kept[:4]
        ]
        + [pltpu.VMEM((group,) + k.shape[1:], BF16) for k in kept[4:]],
        compiler_params=pltpu.CompilerParams(vmem_limit_bytes=VMEM_LIMIT),
        cost_estimate=pl.CostEstimate(flops=flops // 16, bytes_accessed=2**20, transcendentals=0),
        name="run_experts",
    )(place.reshape(1), *x_group, *g_group, slot_rows, slot_cols, *weights, *given)
    return results[:group], results[group:]


def outputs_kernel(group, count, local, act, slot_col, sact, w_out, w_shared, *refs):
    out_refs, (outs, left, right, sems) = refs[:count], refs[count:]
    step = pl.program_id(0)
    slot = lax.rem(step, 2)
    capacity, units = act.shape[2:]
    tokens, share = sact.shape[1:]
    wide = local * capacity

    def store(at, b, into):
        return pltpu.make_async_copy(outs.at[into, b], out_refs[at * group + b], sems.at[into, b])

    @pl.when(step >= 2)
    def _():
        for b in range(group):
            store(0, b, slot).wait()

    for e in range(local):
        rows = dot(act[e].reshape(group * capacity, units), w_out[e], NN).astype(BF16)
        for b in range(group):
            right[b, e * capacity : (e + 1) * capacity] = rows[b * capacity : (b + 1) * capacity]
    slot_at = lax.broadcasted_iota(jnp.int32, (tokens, capacity), 1)
    for b in range(group):
        for e in range(local):
            picks = jnp.where(slot_at == slot_col[b, :, e : e + 1], 1.0, 0.0).astype(BF16)
            left[b, :, e * capacity : (e + 1) * capacity] = picks
        left[b, :, wide : wide + share] = sact[b]
        right[b, wide : wide + share] = w_shared[0]
        outs[slot, b] = dot(left[b], right[b], NN).astype(BF16)
    for at in range(count // group):

        @pl.when(step == at)
        def _():
            for b in range(group):
                store(at, b, at % 2).start()

    @pl.when(step == count // group - 1)
    def _():
        for b in range(group):
            for into in range(2):
                store(0, b, into).wait()


def expert_grads_kernel(rows_x, rows_g, act, dpair, in_ref, out_ref):
    rows = rows_x.shape[1] * rows_x.shape[2]
    x = rows_x[0].reshape(rows, -1)
    for c in range(2):
        in_ref[0, c] = dot(dpair[c].reshape(rows, -1), x, TN)
    out_ref[0] = dot(act[0].reshape(rows, -1), rows_g[0].reshape(rows, -1), TN)


def grads_of_experts(rows_x, rows_g, act, dpair):
    local, count, capacity, width = rows_x.shape
    units = act.shape[3]
    tile = min(width, 1024)
    return pl.pallas_call(
        expert_grads_kernel,
        grid=(local, width // tile),
        out_shape=(
            jax.ShapeDtypeStruct((local, 2, units, width), F32),
            jax.ShapeDtypeStruct((local, units, width), F32),
        ),
        in_specs=[
            pl.BlockSpec((1, count, capacity, tile), lambda e, i: (e, 0, 0, i)),
            pl.BlockSpec((1, count, capacity, tile), lambda e, i: (e, 0, 0, i)),
            pl.BlockSpec((1, count, capacity, units), lambda e, i: (e, 0, 0, 0)),
            pl.BlockSpec((2, count, capacity, units), lambda e, i: (e, 0, 0, 0)),
        ],
        out_specs=(
            pl.BlockSpec((1, 2, units, tile), lambda e, i: (e, 0, 0, i)),
            pl.BlockSpec((1, units, tile), lambda e, i: (e, 0, i)),
        ),
        compiler_params=pltpu.CompilerParams(vmem_limit_bytes=VMEM_LIMIT),
        cost_estimate=pl.CostEstimate(flops=0, bytes_accessed=2**20, transcendentals=0),
        name="grads_of_experts",
    )(rows_x, rows_g, act, dpair)


def run_outputs(act, slot_cols, sact, w_out, w_shared):
    local, count, capacity, units = act.shape
    tokens, share = sact.shape[1:]
    width = w_out.shape[2]
    group = 2
    deep = local * capacity + share
    return pl.pallas_call(
        functools.partial(outputs_kernel, group, count, local),
        grid=(count // group,),
        out_shape=(jax.ShapeDtypeStruct((tokens, width), BF16),) * count,
        in_specs=[
            pl.BlockSpec((local, group, capacity, units), lambda i: (0, i, 0, 0)),
            pl.BlockSpec((group, tokens, local), lambda i: (i, 0, 0)),
            pl.BlockSpec((group, tokens, share), lambda i: (i, 0, 0)),
            pl.BlockSpec((local, units, width), lambda i: (0, 0, 0)),
            pl.BlockSpec((1, share, width), lambda i: (2, 0, 0)),
        ],
        out_specs=(pl.BlockSpec(memory_space=pl.ANY),) * count,
        scratch_shapes=[
            pltpu.VMEM((2, group, tokens, width), BF16),
            pltpu.VMEM((group, tokens, deep), BF16),
            pltpu.VMEM((group, deep, width), BF16),
            pltpu.SemaphoreType.DMA((2, group)),
        ],
        compiler_params=pltpu.CompilerParams(vmem_limit_bytes=VMEM_LIMIT),
        cost_estimate=pl.CostEstimate(
            flops=count * width // 8 * (local * capacity * (units + tokens) + tokens * share),
            bytes_accessed=2**20,
            transcendentals=0,
        ),
        name="run_outputs",
    )(act, slot_cols, sact, w_out, w_shared)


def weight_parts_kernel(count, place_ref, x, raw, out_part, ends, *refs):
    part_refs, (part, sems) = refs[:count], refs[count:]
    place = place_ref[0]
    width = part.shape[2]
    q_rows, out_rows, end_rows = x.shape[1] // count, out_part.shape[0] // count, ends.shape[0] // count

    def store(j):
        return pltpu.make_async_copy(part.at[j % 2], part_refs[j], sems.at[j % 2])

    for j in range(count):
        if j >= 2:
            store(j - 2).wait()
        to = place ^ j
        columns = x[:, pl.ds(pl.multiple_of(to * q_rows, q_rows), q_rows)]
        grad = dot(columns, raw[...], TN).astype(BF16)
        for c in range(3):
            part[j % 2, c * q_rows : (c + 1) * q_rows] = grad[:, c * width : (c + 1) * width]
        rows = out_part[pl.ds(pl.multiple_of(to * out_rows, out_rows), out_rows)]
        at = 3 * q_rows
        for k in range(out_part.shape[1] // width):
            part[j % 2, at : at + out_rows] = rows[:, k * width : (k + 1) * width]
            at += out_rows
        part[j % 2, at:] = ends[pl.ds(pl.multiple_of(to * end_rows, end_rows), end_rows)]
        store(j).start()
    for j in range(count - 2, count):
        store(j).wait()


def weight_parts(place, x, raw, out_part, ends, count):
    tokens, size = x.shape
    width = ends.shape[1]
    rows = (3 * size + out_part.size // width + ends.shape[0]) // count
    return pl.pallas_call(
        functools.partial(weight_parts_kernel, count),
        out_shape=[jax.ShapeDtypeStruct((rows, width), BF16)] * count,
        in_specs=[pl.BlockSpec(memory_space=pltpu.SMEM)]
        + [pl.BlockSpec(memory_space=pltpu.VMEM)] * 4,
        out_specs=[pl.BlockSpec(memory_space=pl.ANY)] * count,
        scratch_shapes=[
            pltpu.VMEM((2, rows, width), BF16),
            pltpu.SemaphoreType.DMA((2,)),
        ],
        compiler_params=pltpu.CompilerParams(vmem_limit_bytes=VMEM_LIMIT),
        cost_estimate=pl.CostEstimate(flops=0, bytes_accessed=2**20, transcendentals=0),
        name="weight_parts",
    )(place.reshape(1), x, raw, out_part, ends)


def assemble_kernel(plan, count, place_ref, *refs):
    block_refs, refs = refs[:count], refs[count:]
    out_refs, (low, wide, in_sems, out_sems) = refs[:-4], refs[-4:]
    place = place_ref[0]

    def load(j):
        return pltpu.make_async_copy(block_refs[j], low.at[j % 2], in_sems.at[j % 2])

    def stores(j):
        return [
            pltpu.make_async_copy(
                wide.at[j % 2, pl.ds(first, rows)],
                out_refs[which].at[
                    pl.ds(pl.multiple_of(base + (place ^ j) * rows, 8), rows),
                    pl.ds(column, wide.shape[2]),
                ],
                out_sems.at[j % 2, i],
            )
            for i, (which, first, rows, base, column) in enumerate(plan)
        ]

    load(0).start()
    for j in range(count):
        if j + 1 < count:
            load(j + 1).start()
        load(j).wait()
        if j >= 2:
            for copy in stores(j - 2):
                copy.wait()
        wide[j % 2] = low[j % 2].astype(F32)
        for copy in stores(j):
            copy.start()
    for j in range(max(0, count - 2), count):
        for copy in stores(j):
            copy.wait()


def assemble(place, blocks, shapes, plan):
    count = len(blocks)
    rows, width = blocks[0].shape
    any_spec = pl.BlockSpec(memory_space=pl.ANY)
    return pl.pallas_call(
        functools.partial(assemble_kernel, plan, count),
        out_shape=[jax.ShapeDtypeStruct(shape, F32) for shape in shapes],
        in_specs=[pl.BlockSpec(memory_space=pltpu.SMEM)] + [any_spec] * count,
        out_specs=[any_spec] * len(shapes),
        scratch_shapes=[
            pltpu.VMEM((2, rows, width), BF16),
            pltpu.VMEM((2, rows, width), F32),
            pltpu.SemaphoreType.DMA((2,)),
            pltpu.SemaphoreType.DMA((2, len(plan))),
        ],
        compiler_params=pltpu.CompilerParams(vmem_limit_bytes=VMEM_LIMIT),
        cost_estimate=pl.CostEstimate(flops=0, bytes_accessed=2**20, transcendentals=0),
        name="assemble",
    )(place.reshape(1), *blocks)


def shared_grads_kernel(count, place_ref, *refs):
    x_refs, g_all, refs = refs[:count], refs[count], refs[count + 1 :]
    (sact, sdpair, dl, grads_ref, router_ref, xs, gs, grads, router, sems) = refs
    at = pl.program_id(0)
    slot = lax.rem(at, 2)

    def load(j, into):
        return (
            pltpu.make_async_copy(x_refs[j], xs.at[into], sems.at[0, into]),
            pltpu.make_async_copy(g_all.at[place_ref[0] ^ j], gs.at[into], sems.at[1, into]),
        )

    @pl.when(at == 0)
    def _():
        for copy in load(0, 0):
            copy.start()
        grads[...] = jnp.zeros_like(grads)
        router[...] = jnp.zeros_like(router)

    for j in range(1, count):

        @pl.when(at == j - 1)
        def _():
            for copy in load(j, j % 2):
                copy.start()

    for copy in load(0, slot):
        copy.wait()
    x, g = xs[slot], gs[slot]
    grads[0] += dot(sdpair[0, 0], x, TN)
    grads[1] += dot(sdpair[0, 1], x, TN)
    grads[2] += dot(sact[0], g, TN)
    router[...] += dot(dl[0], x, TN)

    @pl.when(at == count - 1)
    def _():
        grads_ref[...] = grads[...].astype(BF16)
        router_ref[...] = router[...]


def shared_grads(place, x_blocks, g_all, sact, sdpair, dl):
    count = len(x_blocks)
    tokens, width = x_blocks[0].shape
    share, padded = sact.shape[2], dl.shape[2]
    any_spec = pl.BlockSpec(memory_space=pl.ANY)
    return pl.pallas_call(
        functools.partial(shared_grads_kernel, count),
        grid=(count,),
        out_shape=(
            jax.ShapeDtypeStruct((3, share, width), BF16),
            jax.ShapeDtypeStruct((padded, width), F32),
        ),
        in_specs=[pl.BlockSpec(memory_space=pltpu.SMEM)]
        + [any_spec] * (count + 1)
        + [
            pl.BlockSpec((1, tokens, share), lambda j: (j, 0, 0)),
            pl.BlockSpec((1, 2, tokens, share), lambda j: (j, 0, 0, 0)),
            pl.BlockSpec((1, tokens, padded), lambda j: (j, 0, 0)),
        ],
        out_specs=(
            pl.BlockSpec((3, share, width), lambda j: (0, 0, 0)),
            pl.BlockSpec((padded, width), lambda j: (0, 0)),
        ),
        scratch_shapes=[
            pltpu.VMEM((2, tokens, width), BF16),
            pltpu.VMEM((2, tokens, width), BF16),
            pltpu.VMEM((3, share, width), F32),
            pltpu.VMEM((padded, width), F32),
            pltpu.SemaphoreType.DMA((2, 2)),
        ],
        compiler_params=pltpu.CompilerParams(vmem_limit_bytes=VMEM_LIMIT),
        cost_estimate=pl.CostEstimate(
            flops=count * tokens * width * share,
            bytes_accessed=2**20,
            transcendentals=0,
        ),
        name="shared_grads",
    )(place.reshape(1), *x_blocks, g_all, sact, sdpair, dl)


def on_device(
    hidden_in,
    cotangent,
    gain_attn,
    qkv_weight,
    qkv_bias,
    out_weight,
    gain_ffn,
    router_weight,
    routes,
    shared_gate,
    shared_in,
    shared_out,
    expert_in,
    expert_out,
):
    tokens, width = hidden_in.shape
    ctx_count = lax.axis_size("ctx")
    heads_local = qkv_weight.shape[2] // HD
    local = expert_in.shape[0]
    experts = local * ctx_count
    top_count = routes.shape[1]
    capacity = 3 * tokens * top_count // (2 * experts)
    place = lax.axis_index("ctx")
    order = jnp.arange(ctx_count, dtype=jnp.int32) ^ place
    score_scale = 1.0 / math.sqrt(HD)
    query_pos = place * tokens + jnp.arange(tokens, dtype=jnp.int32)
    cosine, sine = rotary_tables(query_pos, HD)

    x_full = hidden_in.astype(F32)
    inv_one = lax.rsqrt(jnp.mean(x_full * x_full, axis=-1, keepdims=True) + EPS)
    normed_one = x_full * inv_one
    x_one = (normed_one * gain_attn).astype(BF16)
    projected = (
        jnp.einsum("td,dcf->ctf", x_one, qkv_weight, preferred_element_type=F32)
        + qkv_bias[:, None]
    )
    shaped = projected.reshape(3, tokens, heads_local, HD).transpose(0, 2, 1, 3)
    query = rotate(shaped[0], cosine, sine).astype(BF16)
    key_local = rotate(shaped[1], cosine, sine).astype(BF16)
    value_local = shaped[2].astype(BF16)
    kv_rows = heads_local * tokens
    route_rows = -(-tokens * top_count // HD)
    behind = jnp.pad(
        routes.T.astype(BF16).reshape(route_rows, HD), ((0, -route_rows % 16), (0, 0))
    )
    kv_local = jnp.stack(
        [
            jnp.concatenate([key_local.reshape(kv_rows, HD), behind], axis=0),
            jnp.concatenate([value_local.reshape(kv_rows, HD), behind], axis=0),
        ]
    )
    share = shared_out.shape[0] // ctx_count
    piece = shared_out.shape[1]
    shared_send = jnp.concatenate(
        [
            shared_in.transpose(1, 2, 0).reshape(2, ctx_count, share, piece),
            shared_out.reshape(1, ctx_count, share, piece),
        ],
        axis=0,
    ).transpose(1, 0, 2, 3)
    shared_got = lax.all_to_all(shared_send, "ctx", split_axis=0, concat_axis=0, tiled=True)
    kv_blocks = gather_ctx(after(kv_local, shared_got))
    g_all = lax.all_gather(after(cotangent, kv_blocks[2 % ctx_count], kv_blocks[4 % ctx_count]), "ctx", axis=0)

    half_rows = out_weight.shape[0] // 2
    core = place % 2
    out_mine = lax.all_gather(
        lax.dynamic_slice_in_dim(out_weight, core * half_rows, half_rows, 0), "tp", axis=0
    )

    routes_all = jnp.stack([b[0, kv_rows : kv_rows + route_rows] for b in kv_blocks])
    routes_all = routes_all.reshape(ctx_count, 1, top_count, tokens)
    own_experts = (place * local + jnp.arange(local, dtype=jnp.int32)).astype(BF16)
    hit = jnp.any(routes_all == own_experts[None, :, None, None], axis=2)
    token_at = jnp.arange(tokens, dtype=jnp.int32)
    earlier = (token_at[:, None] <= token_at[None, :]).astype(BF16)
    rank = dot(hit.astype(BF16).reshape(-1, tokens), earlier, NN).reshape(hit.shape) - 1.0
    slot_rows = jnp.where(hit, rank, -1.0).astype(jnp.int32)
    slot_cols = slot_rows.transpose(0, 2, 1)
    padded = -(-(experts + 1) // 8) * 8
    w_router = jnp.concatenate(
        [
            router_weight.T,
            shared_gate[None],
            jnp.zeros((padded - experts - 1, width), BF16),
        ],
        axis=0,
    )
    w_in = expert_in.transpose(0, 2, 3, 1)

    attended, lse = attend(place, query, kv_blocks)
    att = attended.astype(BF16).transpose(1, 0, 2).reshape(tokens, heads_local * HD)
    out_mine = after(out_mine, attended)
    out_other = swap(out_mine, 1)
    att_mine, att_other = columns(place, gather_tp(att))
    att_mine = after(att_mine, slot_rows, slot_cols, w_router, w_in)
    rows = out_mine.shape[0] * half_rows
    hidden = x_full + (
        dot(att_mine, out_mine.reshape(rows, width), NN)
        + dot(att_other, out_other.reshape(rows, width), NN)
    )
    shared_w = shared_got.transpose(1, 2, 0, 3).reshape(3, share, width)
    whole_share = -(-share // 16) * 16
    if whole_share > share:
        shared_w = jnp.pad(shared_w, ((0, 0), (0, whole_share - share), (0, 0)))
    inv_two = lax.rsqrt(jnp.mean(hidden * hidden, axis=-1, keepdims=True) + EPS)
    normed_two = hidden * inv_two
    x_two = (normed_two * gain_ffn).astype(BF16)

    units, group = expert_out.shape[1], 2
    kept = [
        jax.ShapeDtypeStruct(shape, BF16)
        for shape in (
            (local, ctx_count, capacity, width),
            (local, ctx_count, capacity, width),
            (local, ctx_count, capacity, units),
            (2 * local, ctx_count, capacity, units),
            (ctx_count, tokens, whole_share),
            (ctx_count, 2, tokens, whole_share),
            (ctx_count, tokens, padded),
        )
    ]
    weights = (w_router, w_in, expert_out, shared_w)
    g_near = [cotangent, swap(cotangent, 1)]
    got = gather_start(x_two)
    x_blocks = [got[0], got[1]]
    dxs = []
    early = None
    for at in range(0, ctx_count, group):
        if at == 4 and ctx_count == 8:
            pair_two = pair_sum(dxs, 2)
            early = (pair_two, pair_two[: tokens // 2].astype(BF16))
        if at == 6 and ctx_count == 8:
            x_blocks[6] = after(x_blocks[6], early[1])
        dx, kept = run_experts(
            at,
            experts,
            place,
            x_blocks[at : at + group],
            g_near if at == 0 else [g_all],
            slot_rows,
            slot_cols,
            weights,
            kept,
        )
        dxs += dx
        if at == 0:
            x_blocks = x_blocks[:2] + gather_end(got, dx[0])[2:]
    grad_x_part = scatter_ctx(dxs, early)
    outs = run_outputs(kept[2], slot_cols, kept[4], expert_out, shared_w)
    grad_x_low = grad_x_part.astype(BF16)
    out_middle = scatter_middle(scatter_start(after(outs, grad_x_low)))
    kept = after(kept, outs[0], *out_middle[0])
    rows_x, rows_g, act_low, dpair, s_act, s_dpair, low_logits = kept
    shared_low, router_part = shared_grads(place, x_blocks, g_all, s_act, s_dpair, low_logits)
    expert_grads = grads_of_experts(rows_x, rows_g, act_low, dpair)
    grad_expert_in, grad_expert_out = expert_grads
    gain_ffn_part = jnp.sum(grad_x_part * normed_two, axis=0)
    small_rows = padded + 1
    small_part = jnp.concatenate([router_part, gain_ffn_part[None]], axis=0)
    small_part = jnp.pad(small_part, ((0, -small_rows % (8 * lax.axis_size("tp"))), (0, 0)))
    half = tokens // 2
    first = lax.psum(grad_x_low[:half], "tp")
    second = lax.psum(after(grad_x_low[half:], first, *out_middle[0]), "tp")
    out_part = scatter_end(out_middle)

    shared_back = lax.all_to_all(
        shared_low[:, :share].reshape(3, share, ctx_count, piece).transpose(2, 0, 1, 3),
        "ctx",
        split_axis=0,
        concat_axis=0,
        tiled=True,
    )
    shared_wide = shared_back.astype(F32)
    grad_shared_in = shared_wide[:, :2].transpose(3, 1, 0, 2).reshape(shared_in.shape)
    grad_shared_out = shared_wide[:, 2].reshape(shared_out.shape)
    summed = jnp.concatenate([first, second], axis=0)
    summed = after(summed, shared_low, *expert_grads, out_part)
    summed = summed.astype(F32)
    grad_y = cotangent.astype(F32)
    grad_normed_two = summed * gain_ffn
    grad_hidden = grad_y + inv_two * (
        grad_normed_two
        - normed_two * jnp.mean(grad_normed_two * normed_two, axis=-1, keepdims=True)
    )
    grad_hidden_low = grad_hidden.astype(BF16)
    out_weight_part = dot(att, grad_hidden_low, (((0,), (0,)), ((), ())))
    grad_att = (
        dot(grad_hidden_low, out_weight, (((1,), (1,)), ((), ())))
        .astype(BF16)
        .reshape(tokens, heads_local, HD)
        .transpose(1, 0, 2)
    )
    delta = jnp.sum(grad_att.astype(F32) * attended, axis=-1)
    delta = jnp.broadcast_to(delta[:, None], lse.shape)
    grad_query, grad_pairs = attend_back(place, query, grad_att, lse, delta, kv_blocks)
    ffn_total = sum_tp_start(out_part, small_part)
    grad_pairs = after(grad_pairs, ffn_total, shared_back)
    kv_middle = scatter_middle(scatter_start([grad_pairs[j] for j in range(ctx_count)]))
    ffn_low = sum_tp_end(after(ffn_total, *kv_middle[0]))
    own_rows = tokens // lax.axis_size("tp")
    small = ffn_low[:, own_rows:].reshape(-1, width)[:small_rows].astype(F32)
    ffn_low = ffn_low[:, :own_rows].reshape(tokens, width)
    grad_kv = scatter_end(kv_middle)
    grad_kv = after(grad_kv, grad_shared_in, grad_shared_out)

    def raw_part(value):
        return value.astype(BF16).transpose(1, 0, 2).reshape(tokens, heads_local * HD)

    raw = [
        raw_part(rotate(grad_query, cosine, -sine)),
        raw_part(rotate(grad_kv[0], cosine, -sine)),
        raw_part(grad_kv[1]),
    ]
    raw = jnp.concatenate(raw, axis=1)
    grad_x_one_part = jnp.einsum(
        "tcf,dcf->td",
        raw.reshape(tokens, 3, -1),
        qkv_weight,
        preferred_element_type=F32,
    )
    grad_x_low = grad_x_one_part.astype(BF16)
    half_way = sum_tp_start(grad_x_low)
    grad_x_one = sum_tp_end(half_way).reshape(tokens, width)
    x_one = after(x_one, grad_x_low)
    gain_attn_part = jnp.sum(grad_x_one_part * normed_one, axis=0)
    gain_sum = sum_tp_small(gain_attn_part[None])
    head_width = heads_local * HD
    gain_rows = width // head_width
    ends = jnp.concatenate(
        [jnp.sum(raw.astype(F32), axis=0).reshape(3, -1)]
        + [gain_sum.reshape(gain_rows, -1), small.reshape((padded + 1) * gain_rows, -1)],
        axis=0,
    )
    ends = jnp.pad(ends, ((0, -ends.shape[0] % (16 * ctx_count)), (0, 0))).astype(BF16)
    turns = width // head_width
    sums = sum_ctx(
        weight_parts(place, x_one, raw, out_weight_part.astype(BF16), ends, ctx_count), half_way
    )
    q_rows = width // ctx_count
    out_rows = out_weight.shape[0] // ctx_count
    plan = [(0, c * q_rows, q_rows, c * width, 0) for c in range(3)] + [
        (1, 3 * q_rows + k * out_rows, out_rows, 0, k * head_width) for k in range(turns)
    ]
    qkv_grad, out_weight_grad = assemble(
        place, sums, [(3 * width, head_width), out_weight.shape], plan
    )
    qkv_grad = qkv_grad.reshape(3, width, head_width).transpose(1, 0, 2)
    ends = relative(jnp.stack([b[3 * q_rows + turns * out_rows :] for b in sums]))
    ends = ends.reshape(-1, head_width).astype(F32)
    small = ends[3 + gain_rows : 3 + (padded + 2) * gain_rows].reshape(padded + 1, width)
    grad_x_one = after(grad_x_one, sums[2]).astype(F32)
    grad_normed_one = grad_x_one * gain_attn
    grad_input = grad_hidden + inv_one * (
        grad_normed_one
        - normed_one * jnp.mean(grad_normed_one * normed_one, axis=-1, keepdims=True)
    )
    block_out = (hidden + ffn_low.astype(F32)).astype(BF16)
    return (
        block_out,
        grad_input,
        ends[3 : 3 + gain_rows].reshape(-1),
        qkv_grad,
        ends[:3],
        out_weight_grad,
        small[padded],
        small[:experts].T,
        small[experts],
        grad_shared_in,
        grad_shared_out,
        grad_expert_in.transpose(0, 3, 1, 2),
        grad_expert_out,
    )


def solution(mesh):
    return jax.shard_map(
        on_device,
        mesh=mesh,
        in_specs=(
            P("ctx", None),
            P("ctx", None),
            P(),
            P(None, None, "tp"),
            P(None, "tp"),
            P("tp", None),
            P(),
            P(),
            P("ctx", None),
            P(),
            P("ctx", None, "tp"),
            P("tp", "ctx"),
            P("ctx", None, None, "tp"),
            P("ctx", "tp", None),
        ),
        out_specs=(
            P("ctx", None),
            P("ctx", None),
            P(),
            P(None, None, "tp"),
            P(None, "tp"),
            P("tp", None),
            P(),
            P(),
            P(),
            P("ctx", None, "tp"),
            P("tp", "ctx"),
            P("ctx", None, None, "tp"),
            P("ctx", "tp", None),
        ),
        check_vma=False,
    )
```

```python
import functools
import math

import jax
import jax.numpy as jnp
from jax import lax
from jax.experimental import pallas as pl
from jax.experimental.pallas import tpu as pltpu
from jax.sharding import PartitionSpec as P

HD = 128
EPS = 1e-06
THETA = 1000000.0
NEG = -1e30
F32 = jnp.float32
BF16 = jnp.bfloat16


def rotary_tables(positions, width):
    half_width = width // 2
    freqs = THETA ** (-(jnp.arange(half_width, dtype=F32) * 2.0) / width)
    angles = positions.astype(F32)[:, None] * freqs[None, :]
    return (jnp.cos(angles), jnp.sin(angles))


def rotate(values, cosine, sine):
    half_width = values.shape[-1] // 2
    first, second = values[..., :half_width], values[..., half_width:]
    return jnp.concatenate(
        [first * cosine - second * sine, second * cosine + first * sine], axis=-1
    )


def dot(a, b, dims):
    return lax.dot_general(a, b, dims, preferred_element_type=F32)


def swap(value, bits):
    count = lax.axis_size("ctx")
    return lax.ppermute(value, "ctx", [(i, i ^ bits) for i in range(count)])


def relative(natural):
    count = natural.shape[0]
    order = jnp.arange(count, dtype=jnp.int32) ^ lax.axis_index("ctx")
    return natural[order]


def nothing_kernel(*refs):
    pass


def after(values, *others):
    single = not isinstance(values, (list, tuple))
    values = [values] if single else list(values)
    any_spec = pl.BlockSpec(memory_space=pl.ANY)
    results = pl.pallas_call(
        nothing_kernel,
        out_shape=[jax.ShapeDtypeStruct(v.shape, v.dtype) for v in values],
        in_specs=[any_spec] * (len(values) + len(others)),
        out_specs=[any_spec] * len(values),
        input_output_aliases={i: i for i in range(len(values))},
        name="after",
    )(*values, *others)
    return results[0] if single else results


def gather_start(own):
    if lax.axis_size("ctx") != 8:
        return relative(lax.all_gather(own, "ctx", axis=0))
    return [own, swap(own, 1), swap(own, 2), swap(own, 4)]


def gather_end(got, *others):
    if lax.axis_size("ctx") != 8:
        return [got[j] for j in range(lax.axis_size("ctx"))]
    own, b1, b2, b4 = got
    if others:
        b2, b4 = after((b2, b4), *others)
    half = own.shape[0] // 2
    via_x, via_y = swap(b4[:half], 2), swap(b2[half:], 4)
    b3, b5 = swap(b2, 1), swap(b4, 1)
    b6 = jnp.concatenate([via_x, via_y], axis=0)
    return [own, b1, b2, b3, b4, b5, b6, swap(b6, 1)]


def gather_ctx(own, *others):
    return gather_end(gather_start(own), *others)


def pair_sum(parts, j):
    return parts[j].astype(F32) + swap(parts[j ^ 1], 1).astype(F32)


def scatter_ctx(parts, early=None):
    return scatter_end(scatter_middle(scatter_start(parts, early)))


def scatter_start(parts, early=None):
    if lax.axis_size("ctx") != 8:
        return [jnp.stack(parts)], None
    half = parts[0].shape[0] // 2
    pair = {j: pair_sum(parts, j) for j in (2, 4, 6, 0) if j != 2 or early is None}
    if early is None:
        early = (pair[2], pair[2][:half].astype(BF16))
    q6 = pair[6].astype(BF16)
    hops = [early[1], pair[4][half:].astype(BF16), q6[:half], q6[half:]]
    return hops, (early[0], pair[4], pair[0])


def scatter_middle(started):
    hops, stay = started
    if lax.axis_size("ctx") != 8:
        return hops, None
    two, four, zero = stay
    half = two.shape[0] // 2
    r2, r4 = swap(hops[0], 2), swap(hops[1], 4)
    via_x, via_y = swap(hops[2], 2), swap(hops[3], 4)
    r4a = (four[:half] + via_x.astype(F32)).astype(BF16)
    r2b = (two[half:] + via_y.astype(F32)).astype(BF16)
    return [r4a, r2b], (r2, r4, zero)


def scatter_end(started, *others):
    hops, stay = started
    if lax.axis_size("ctx") != 8:
        natural = relative(hops[0])
        flat = natural.reshape((-1,) + natural.shape[2:])
        return lax.psum_scatter(flat, "ctx", scatter_dimension=0, tiled=True).astype(F32)
    if others:
        hops = after(hops, *others)
    r2, r4, zero = stay
    r4a, r2b = swap(hops[0], 4), swap(hops[1], 2)
    low = r2.astype(F32) + r4a.astype(F32)
    high = r2b.astype(F32) + r4.astype(F32)
    return zero + jnp.concatenate([low, high], axis=0)


def sum_ctx(parts, *others):
    own = scatter_end(scatter_middle(scatter_start(parts)), *others)
    return gather_ctx(own.astype(BF16))


def shards(value):
    count = lax.axis_size("ctx")
    rows = value.shape[0] // count
    place = lax.axis_index("ctx")
    return [lax.dynamic_slice_in_dim(value, (place ^ j) * rows, rows, 0) for j in range(count)]


def gather_tp(own):
    count = lax.axis_size("tp")
    return [own] + [
        lax.ppermute(own, "tp", [(i, i ^ k) for i in range(count)]) for k in range(1, count)
    ]


NT = (((1,), (1,)), ((), ()))
NN = (((1,), (0,)), ((), ()))
TN = (((0,), (0,)), ((), ()))
VMEM_LIMIT = 60 * 1024 * 1024


def sum_tp_start(*values):
    pieces = [v.astype(BF16).reshape(lax.axis_size("tp"), -1, v.shape[1]) for v in values]
    pieces = jnp.concatenate(pieces, axis=1)
    got = lax.all_to_all(pieces, "tp", split_axis=0, concat_axis=0, tiled=True)
    return jnp.sum(got.astype(F32), axis=0).astype(BF16)


def sum_tp_end(total):
    count, at = lax.axis_size("tp"), lax.axis_index("tp")
    blocks = jnp.stack(gather_tp(total))
    blocks = blocks[jnp.arange(count, dtype=jnp.int32) ^ at]
    return blocks


def sum_tp_small(value):
    count, bits = lax.axis_size("tp"), 1
    while bits < count:
        value = value + lax.ppermute(value, "tp", [(i, i ^ bits) for i in range(count)])
        bits *= 2
    return value


def columns_kernel(count, places, *refs):
    block_refs, (mine, other) = refs[:count], refs[count:]
    core, at = places[0], places[1]
    width = mine.shape[1] // count
    for k in range(count):
        to = pl.ds(pl.multiple_of((at ^ k) * width, width), width)
        mine[:, to] = block_refs[k][:, pl.ds(pl.multiple_of(core * width, width), width)]
        other[:, to] = block_refs[k][:, pl.ds(pl.multiple_of((1 - core) * width, width), width)]


def columns(place, blocks):
    count = len(blocks)
    rows, width = blocks[0].shape
    vmem = pl.BlockSpec(memory_space=pltpu.VMEM)
    half = jax.ShapeDtypeStruct((rows, count * width // 2), blocks[0].dtype)
    return pl.pallas_call(
        functools.partial(columns_kernel, count),
        out_shape=(half, half),
        in_specs=[pl.BlockSpec(memory_space=pltpu.SMEM)] + [vmem] * count,
        out_specs=(vmem, vmem),
        compiler_params=pltpu.CompilerParams(vmem_limit_bytes=VMEM_LIMIT),
        cost_estimate=pl.CostEstimate(flops=0, bytes_accessed=2**20, transcendentals=0),
        name="columns",
    )(jnp.stack([place % 2, lax.axis_index("tp")]), *blocks)


def attend_kernel(factor, count, place_ref, q_ref, *refs):
    kv_refs, (att_ref, lse_ref, kv, sems) = refs[:count], refs[count:]
    rows = kv.shape[2]
    copies = [
        pltpu.make_async_copy(kv_refs[j].at[:, pl.ds(0, rows)], kv.at[j], sems.at[j])
        for j in range(count)
    ]
    for copy in copies:
        copy.start()
    for copy in copies:
        copy.wait()
    place = place_ref[0]
    heads, tokens, _ = q_ref.shape

    def one_head(head, _):
        query = q_ref[head]
        here = pl.ds(pl.multiple_of(head * tokens, tokens), tokens)

        def scores(j):
            return dot(kv[j, 0, here], query, NT) * factor

        key_at = lax.broadcasted_iota(jnp.int32, (tokens, tokens), 0)
        query_at = lax.broadcasted_iota(jnp.int32, (tokens, tokens), 1)
        first = jnp.where(key_at <= query_at, scores(0), NEG)
        top = jnp.max(first, axis=0, keepdims=True)
        exps = jnp.exp2(first - top)
        total = jnp.sum(exps, axis=0, keepdims=True)
        acc = dot(kv[0, 1, here], exps.astype(BF16), TN)

        def earlier(i, carry):
            top, total, acc = carry
            j = place ^ i
            now = scores(j)
            higher = jnp.maximum(top, jnp.max(now, axis=0, keepdims=True))
            exps = jnp.exp2(now - higher)
            keep = jnp.exp2(top - higher)
            total = total * keep + jnp.sum(exps, axis=0, keepdims=True)
            acc = acc * keep + dot(kv[j, 1, here], exps.astype(BF16), TN)
            return higher, total, acc

        top, total, acc = lax.fori_loop(0, place, earlier, (top, total, acc))
        att_ref[head] = (acc / total).T
        lse_ref[head] = jnp.broadcast_to(top + jnp.log2(total), lse_ref.shape[1:])
        return 0

    lax.fori_loop(0, heads, one_head, 0)


def attend(place, query, kv_blocks):
    heads, tokens, size = query.shape
    count = len(kv_blocks)
    factor = math.log2(math.e) / math.sqrt(size)
    flops = 4 * count * heads * tokens * tokens * size
    return pl.pallas_call(
        functools.partial(attend_kernel, factor, count),
        out_shape=(
            jax.ShapeDtypeStruct((heads, tokens, size), F32),
            jax.ShapeDtypeStruct((heads, 8, tokens), F32),
        ),
        in_specs=[
            pl.BlockSpec(memory_space=pltpu.SMEM),
            pl.BlockSpec(memory_space=pltpu.VMEM),
        ]
        + [pl.BlockSpec(memory_space=pl.ANY)] * count,
        out_specs=(pl.BlockSpec(memory_space=pltpu.VMEM),) * 2,
        scratch_shapes=[
            pltpu.VMEM((count, 2, heads * tokens, size), BF16),
            pltpu.SemaphoreType.DMA((count,)),
        ],
        compiler_params=pltpu.CompilerParams(vmem_limit_bytes=VMEM_LIMIT),
        cost_estimate=pl.CostEstimate(
            flops=flops // 16, bytes_accessed=2**20, transcendentals=0
        ),
        name="attend",
    )(place.reshape(1), query, *kv_blocks)


def attend_back_kernel(factor, scale, count, place_ref, q_ref, do_ref, lse_ref, delta_ref, *refs):
    kv_refs, (dq_ref, dkv_ref, kv, dkv, dq, sems, out_sems) = refs[:count], refs[count:]
    rows = kv.shape[2]
    copies = [
        pltpu.make_async_copy(kv_refs[j].at[:, pl.ds(0, rows)], kv.at[j], sems.at[j])
        for j in range(count)
    ]
    for copy in copies:
        copy.start()
    for copy in copies:
        copy.wait()
    place = place_ref[0]
    heads, tokens, _ = q_ref.shape

    def out_copy(j):
        return pltpu.make_async_copy(dkv.at[j], dkv_ref.at[j], out_sems.at[j])

    def one_block(j, masked):
        def one_head(head, _):
            query, do = q_ref[head], do_ref[head]
            here = pl.ds(pl.multiple_of(head * tokens, tokens), tokens)
            key, value = kv[j, 0, here], kv[j, 1, here]
            scores = dot(key, query, NT) * factor
            probs = jnp.exp2(scores - lse_ref[head, :1])
            if masked:
                key_at = lax.broadcasted_iota(jnp.int32, (tokens, tokens), 0)
                query_at = lax.broadcasted_iota(jnp.int32, (tokens, tokens), 1)
                probs = jnp.where(key_at <= query_at, probs, 0.0)
            dprob = dot(value, do, NT)
            dscore = (probs * (dprob - delta_ref[head, :1])).astype(BF16)
            dkv[j, 0, head] = (dot(dscore, query, NN) * scale).astype(BF16)
            dkv[j, 1, head] = dot(probs.astype(BF16), do, NN).astype(BF16)
            part = dot(key, dscore, TN)
            dq[head] = part if masked else dq[head] + part
            return 0

        lax.fori_loop(0, heads, one_head, 0)
        out_copy(j).start()

    one_block(0, True)

    def earlier(i, _):
        one_block(place ^ i, False)
        return 0

    def later(i, _):
        j = place ^ i
        dkv[j] = jnp.zeros(dkv.shape[1:], BF16)
        out_copy(j).start()
        return 0

    lax.fori_loop(0, place, earlier, 0)
    lax.fori_loop(place + 1, count, later, 0)
    for head in range(heads):
        dq_ref[head] = dq[head].T * scale
    for j in range(count):
        out_copy(j).wait()


def attend_back(place, query, do, lse, delta, kv_blocks):
    heads, tokens, size = query.shape
    count = len(kv_blocks)
    scale = 1.0 / math.sqrt(size)
    factor = math.log2(math.e) * scale
    return pl.pallas_call(
        functools.partial(attend_back_kernel, factor, scale, count),
        out_shape=(
            jax.ShapeDtypeStruct((heads, tokens, size), F32),
            jax.ShapeDtypeStruct((count, 2, heads, tokens, size), BF16),
        ),
        in_specs=[pl.BlockSpec(memory_space=pltpu.SMEM)]
        + [pl.BlockSpec(memory_space=pltpu.VMEM)] * 4
        + [pl.BlockSpec(memory_space=pl.ANY)] * count,
        out_specs=(pl.BlockSpec(memory_space=pltpu.VMEM), pl.BlockSpec(memory_space=pl.ANY)),
        scratch_shapes=[
            pltpu.VMEM((count, 2, heads * tokens, size), BF16),
            pltpu.VMEM((count, 2, heads, tokens, size), BF16),
            pltpu.VMEM((heads, size, tokens), F32),
            pltpu.SemaphoreType.DMA((count,)),
            pltpu.SemaphoreType.DMA((count,)),
        ],
        compiler_params=pltpu.CompilerParams(vmem_limit_bytes=VMEM_LIMIT),
        cost_estimate=pl.CostEstimate(
            flops=count * heads * tokens * tokens * size,
            bytes_accessed=2**20,
            transcendentals=0,
        ),
        name="attend_back",
    )(place.reshape(1), query, do, lse, delta, *kv_blocks)


def swiglu_back(one, two, dact, gate):
    sig = 1.0 / (1.0 + jnp.exp(-one))
    silu = one * sig
    act = silu * two
    prod = act * dact
    dgate = gate * dact
    d_one = (dgate * two * sig * (1.0 + one * (1.0 - sig))).astype(BF16)
    d_two = (dgate * silu).astype(BF16)
    return (gate * act).astype(BF16), d_one, d_two, prod


def experts_kernel(at, group, local, experts, given, near, place_ref, *refs):
    x_refs, refs = refs[:group], refs[group:]
    if near:
        g_refs, refs = refs[:group], refs[group:]
    else:
        g_refs = [refs[0].at[place_ref[0] ^ (at + b)] for b in range(group)]
        refs = refs[1:]
    (slot_row, slot_col, w_router, w_in, w_out, w_shared), refs = refs[:6], refs[6 + given :]
    dx_refs, refs = refs[:group], refs[group:]
    kept_refs, refs = refs[:7], refs[7:]
    (xs, gs, first_w, in_w, out_w, shared_w, dxs, left, right, sems, out_sems), stage = refs[:11], refs[11:]
    rows_x, rows_g, act_s, dpair_s, sact_s, sdpair_s, dl_s = stage
    tokens, width = xs.shape[1:]
    capacity, units = act_s.shape[2:]
    wide = local * capacity
    share = sact_s.shape[2]
    third = first_w.shape[0] - 128
    second = third // 2
    padded = w_router.shape[0]
    most = out_w.shape[1]

    loads = [pltpu.make_async_copy(x_refs[b], xs.at[b], sems.at[b]) for b in range(group)]
    fore_loads = [
        pltpu.make_async_copy(
            w_shared.at[c], first_w.at[pl.ds(c * second, share)], sems.at[2 * group + c]
        )
        for c in range(2)
    ]
    loads += [
        pltpu.make_async_copy(g_refs[b], gs.at[b], sems.at[group + b]) for b in range(group)
    ]
    base = 2 * group + 2
    more = [
        [
            pltpu.make_async_copy(
                w_in.at[e, c], in_w.at[e, pl.ds(c * most, units)], sems.at[base + 3 * e + c]
            )
            for c in range(2)
        ]
        + [
            pltpu.make_async_copy(
                w_out.at[e], out_w.at[e, pl.ds(0, units)], sems.at[base + 3 * e + 2]
            )
        ]
        for e in range(local)
    ]
    last = pltpu.make_async_copy(w_shared.at[2], shared_w, sems.at[base + 3 * local])
    for copy in loads[:group] + fore_loads:
        copy.start()
    first_w[third : third + padded] = w_router[...]
    first_w[third + padded :] = jnp.zeros((128 - padded, width), BF16)
    if second > share:
        for c in range(2):
            gap = jnp.zeros((second - share, width), BF16)
            first_w[c * second + share : (c + 1) * second] = gap
    if most > units:
        gap = jnp.zeros((most - units, width), BF16)
        for e in range(local):
            in_w[e, units:most] = gap
            in_w[e, most + units :] = gap
            out_w[e, units:] = gap

    sent = []

    def send(copy):
        copy.start()
        sent.append(copy)

    for copy in loads[:group] + fore_loads:
        copy.wait()
    for copy in loads[group:] + more[0]:
        copy.start()
    x = xs[...].reshape(group * tokens, width)
    fore = dot(x, first_w[...], NT)
    s_one, s_two = fore[:, :share], fore[:, second : second + share]
    s_gate = 1.0 / (1.0 + jnp.exp(-fore[:, third + experts : third + experts + 1]))
    row_at = lax.broadcasted_iota(jnp.int32, (padded, tokens), 0)
    slot_at = lax.broadcasted_iota(jnp.int32, (capacity, tokens), 0)
    probs, change, hits = [], [], []
    for b in range(group):
        logits = fore[b * tokens : (b + 1) * tokens, third:].T[:padded]
        shown = jnp.where(row_at < experts, logits, NEG)
        exps = jnp.exp(shown - jnp.max(shown, axis=0, keepdims=True))
        soft = exps / jnp.sum(exps, axis=0, keepdims=True)
        probs.append(jnp.where(row_at == experts, 1.0 / (1.0 + jnp.exp(-logits)), soft))
        change.append(jnp.zeros((padded, tokens), F32))
        picks = jnp.concatenate(
            [
                jnp.where(slot_at == slot_row[b, e : e + 1, :], 1.0, 0.0).astype(BF16)
                for e in range(local)
            ],
            axis=0,
        )
        rows = dot(picks, xs[b], NN).astype(BF16)
        for e in range(local):
            rows_x[e, b] = rows[e * capacity : (e + 1) * capacity]
        loads[group + b].wait()
        if b == group - 1:
            for e in range(1, local):
                for copy in more[e]:
                    copy.start()
            last.start()
        rows = dot(picks, gs[b], NN).astype(BF16)
        for e in range(local):
            rows_g[e, b] = rows[e * capacity : (e + 1) * capacity]
    def send_all(i, lead):
        for e in range(lead):
            send(
                pltpu.make_async_copy(
                    stage[i].at[e], kept_refs[i].at[e, pl.ds(at, group)], out_sems.at[i, e]
                )
            )

    send_all(0, local)
    send_all(1, local)
    is_expert = row_at < experts
    for e in range(local):
        chosen = row_at == place_ref[0] * local + e
        gates, owns, hits = [], [], []
        for b in range(group):
            own = jnp.sum(jnp.where(chosen, probs[b], 0.0), axis=0, keepdims=True)
            hit = slot_at == slot_row[b, e : e + 1, :]
            gates.append(jnp.sum(jnp.where(hit, own, 0.0), axis=1, keepdims=True))
            owns.append(own)
            hits.append(hit)
        for copy in more[e]:
            copy.wait()
        pair = dot(rows_x[e].reshape(group * capacity, width), in_w[e], NT)
        dact = dot(rows_g[e].reshape(group * capacity, width), out_w[e], NT)
        act, d_one, d_two, prod = swiglu_back(
            pair[:, :most], pair[:, most:], dact, jnp.concatenate(gates, axis=0)
        )
        act_s[e] = act[:, :units].reshape(group, capacity, units)
        dpair_s[2 * e] = d_one[:, :units].reshape(group, capacity, units)
        dpair_s[2 * e + 1] = d_two[:, :units].reshape(group, capacity, units)
        row_dot = jnp.sum(prod, axis=1, keepdims=True)
        drow = dot(jnp.concatenate([d_one, d_two], axis=1), in_w[e], NN).astype(BF16)
        for b in range(group):
            rows = slice(b * capacity, (b + 1) * capacity)
            found = jnp.sum(jnp.where(hits[b], row_dot[rows], 0.0), axis=0, keepdims=True)
            change[b] += (found * owns[b]) * (
                jnp.where(chosen, 1.0, 0.0) - jnp.where(is_expert, probs[b], 0.0)
            )
            right[b, e * capacity : (e + 1) * capacity] = drow[rows]
    send_all(2, local)
    send_all(3, 2 * local)
    last.wait()
    g = gs[...].reshape(group * tokens, width)
    s_dact = dot(g, shared_w[...], NT)
    act, d_one, d_two, prod = swiglu_back(s_one, s_two, s_dact, s_gate)
    sact_s[...] = act.reshape(group, tokens, share)
    sdpair_s[:, 0] = d_one.reshape(group, tokens, share)
    sdpair_s[:, 1] = d_two.reshape(group, tokens, share)
    dslogit = jnp.sum(prod, axis=1, keepdims=True) * s_gate * (1.0 - s_gate)
    lane_at = lax.broadcasted_iota(jnp.int32, (tokens, 128), 1)
    rest = jnp.zeros((128 - padded, tokens), F32)
    deep = wide + 2 * share
    column_at = lax.broadcasted_iota(jnp.int32, (tokens, capacity), 1)
    stores = []
    for b in range(group):
        rows = slice(b * tokens, (b + 1) * tokens)
        columns = jnp.concatenate([change[b], rest], axis=0).T
        columns = jnp.where(lane_at == experts, dslogit[rows], columns)[:, :padded].astype(BF16)
        dl_s[b] = columns
        left[b, :, deep : deep + padded] = columns
        right[b, deep : deep + padded] = w_router[...]
        for e in range(local):
            picks = jnp.where(column_at == slot_col[b, :, e : e + 1], 1.0, 0.0).astype(BF16)
            left[b, :, e * capacity : (e + 1) * capacity] = picks
        left[b, :, wide : wide + share] = d_one[rows]
        left[b, :, wide + share : wide + 2 * share] = d_two[rows]
        right[b, wide : wide + share] = first_w[:share]
        right[b, wide + share : wide + 2 * share] = first_w[second : second + share]
        dxs[b] = dot(left[b], right[b], NN).astype(BF16)
        send(pltpu.make_async_copy(dxs.at[b], dx_refs[b], out_sems.at[7, b]))
    for i in range(4, 7):
        send(pltpu.make_async_copy(stage[i], kept_refs[i].at[pl.ds(at, group)], out_sems.at[i, 0]))
    for copy in sent:
        copy.wait()


def run_experts(at, experts, place, x_group, g_group, slot_rows, slot_cols, weights, kept):
    given = kept if at else []
    group = len(x_group)
    near = len(g_group) == group
    tokens, width = x_group[0].shape
    w_router, w_in, w_out, w_shared = weights
    local = w_out.shape[0]
    share = w_shared.shape[1]
    padded = w_router.shape[0]
    capacity, units = kept[2].shape[2:]
    any_spec = pl.BlockSpec(memory_space=pl.ANY)
    block = jax.ShapeDtypeStruct((tokens, width), BF16)
    deep = local * capacity + 2 * share + padded
    flops = group * 2 * tokens * width * (local * capacity * 3 + 5 * share) + (
        group * 2 * width * local * capacity * units * 5
    )
    step = at // group
    wide_units = -(-units // 128) * 128
    fore = 2 * (-(-share // 64) * 64) + 128
    results = pl.pallas_call(
        functools.partial(experts_kernel, at, group, local, experts, len(given), near),
        grid=(1,),
        out_shape=(block,) * group + tuple(jax.ShapeDtypeStruct(k.shape, k.dtype) for k in kept),
        in_specs=[pl.BlockSpec(memory_space=pltpu.SMEM)]
        + [any_spec] * (group + len(g_group))
        + [
            pl.BlockSpec((group, local, tokens), lambda i: (step, 0, 0)),
            pl.BlockSpec((group, tokens, local), lambda i: (step, 0, 0)),
            pl.BlockSpec((padded, width), lambda i: (0, 0)),
        ]
        + [any_spec] * (3 + len(given)),
        out_specs=(any_spec,) * (group + len(kept)),
        input_output_aliases={7 + group + len(g_group) + i: group + i for i in range(len(given))},
        scratch_shapes=[
            pltpu.VMEM((group, tokens, width), BF16),
            pltpu.VMEM((group, tokens, width), BF16),
            pltpu.VMEM((fore, width), BF16),
            pltpu.VMEM((local, 2 * wide_units, width), BF16),
            pltpu.VMEM((local, wide_units, width), BF16),
            pltpu.VMEM((share, width), BF16),
            pltpu.VMEM((group, tokens, width), BF16),
            pltpu.VMEM((group, tokens, deep), BF16),
            pltpu.VMEM((group, deep, width), BF16),
            pltpu.SemaphoreType.DMA((2 * group + 3 + 3 * local,)),
            pltpu.SemaphoreType.DMA((8, max(2 * local, group))),
        ]
        + [
            pltpu.VMEM(k.shape[:1] + (group,) + k.shape[2:], BF16) for k in kept[:4]
        ]
        + [pltpu.VMEM((group,) + k.shape[1:], BF16) for k in kept[4:]],
        compiler_params=pltpu.CompilerParams(vmem_limit_bytes=VMEM_LIMIT),
        cost_estimate=pl.CostEstimate(flops=flops // 16, bytes_accessed=2**20, transcendentals=0),
        name="run_experts",
    )(place.reshape(1), *x_group, *g_group, slot_rows, slot_cols, *weights, *given)
    return results[:group], results[group:]


def outputs_kernel(group, count, local, act, slot_col, sact, w_out, w_shared, *refs):
    out_refs, (outs, left, right, sems) = refs[:count], refs[count:]
    step = pl.program_id(0)
    slot = lax.rem(step, 2)
    capacity, units = act.shape[2:]
    tokens, share = sact.shape[1:]
    wide = local * capacity

    def store(at, b, into):
        return pltpu.make_async_copy(outs.at[into, b], out_refs[at * group + b], sems.at[into, b])

    @pl.when(step >= 2)
    def _():
        for b in range(group):
            store(0, b, slot).wait()

    for e in range(local):
        rows = dot(act[e].reshape(group * capacity, units), w_out[e], NN).astype(BF16)
        for b in range(group):
            right[b, e * capacity : (e + 1) * capacity] = rows[b * capacity : (b + 1) * capacity]
    slot_at = lax.broadcasted_iota(jnp.int32, (tokens, capacity), 1)
    for b in range(group):
        for e in range(local):
            picks = jnp.where(slot_at == slot_col[b, :, e : e + 1], 1.0, 0.0).astype(BF16)
            left[b, :, e * capacity : (e + 1) * capacity] = picks
        left[b, :, wide : wide + share] = sact[b]
        right[b, wide : wide + share] = w_shared[0]
        outs[slot, b] = dot(left[b], right[b], NN).astype(BF16)
    for at in range(count // group):

        @pl.when(step == at)
        def _():
            for b in range(group):
                store(at, b, at % 2).start()

    @pl.when(step == count // group - 1)
    def _():
        for b in range(group):
            for into in range(2):
                store(0, b, into).wait()


def expert_grads_kernel(rows_x, rows_g, act, dpair, in_ref, out_ref):
    rows = rows_x.shape[1] * rows_x.shape[2]
    x = rows_x[0].reshape(rows, -1)
    for c in range(2):
        in_ref[0, c] = dot(dpair[c].reshape(rows, -1), x, TN)
    out_ref[0] = dot(act[0].reshape(rows, -1), rows_g[0].reshape(rows, -1), TN)


def grads_of_experts(rows_x, rows_g, act, dpair):
    local, count, capacity, width = rows_x.shape
    units = act.shape[3]
    tile = min(width, 1024)
    return pl.pallas_call(
        expert_grads_kernel,
        grid=(local, width // tile),
        out_shape=(
            jax.ShapeDtypeStruct((local, 2, units, width), F32),
            jax.ShapeDtypeStruct((local, units, width), F32),
        ),
        in_specs=[
            pl.BlockSpec((1, count, capacity, tile), lambda e, i: (e, 0, 0, i)),
            pl.BlockSpec((1, count, capacity, tile), lambda e, i: (e, 0, 0, i)),
            pl.BlockSpec((1, count, capacity, units), lambda e, i: (e, 0, 0, 0)),
            pl.BlockSpec((2, count, capacity, units), lambda e, i: (e, 0, 0, 0)),
        ],
        out_specs=(
            pl.BlockSpec((1, 2, units, tile), lambda e, i: (e, 0, 0, i)),
            pl.BlockSpec((1, units, tile), lambda e, i: (e, 0, i)),
        ),
        compiler_params=pltpu.CompilerParams(vmem_limit_bytes=VMEM_LIMIT),
        cost_estimate=pl.CostEstimate(flops=0, bytes_accessed=2**20, transcendentals=0),
        name="grads_of_experts",
    )(rows_x, rows_g, act, dpair)


def run_outputs(act, slot_cols, sact, w_out, w_shared):
    local, count, capacity, units = act.shape
    tokens, share = sact.shape[1:]
    width = w_out.shape[2]
    group = 2
    deep = local * capacity + share
    return pl.pallas_call(
        functools.partial(outputs_kernel, group, count, local),
        grid=(count // group,),
        out_shape=(jax.ShapeDtypeStruct((tokens, width), BF16),) * count,
        in_specs=[
            pl.BlockSpec((local, group, capacity, units), lambda i: (0, i, 0, 0)),
            pl.BlockSpec((group, tokens, local), lambda i: (i, 0, 0)),
            pl.BlockSpec((group, tokens, share), lambda i: (i, 0, 0)),
            pl.BlockSpec((local, units, width), lambda i: (0, 0, 0)),
            pl.BlockSpec((1, share, width), lambda i: (2, 0, 0)),
        ],
        out_specs=(pl.BlockSpec(memory_space=pl.ANY),) * count,
        scratch_shapes=[
            pltpu.VMEM((2, group, tokens, width), BF16),
            pltpu.VMEM((group, tokens, deep), BF16),
            pltpu.VMEM((group, deep, width), BF16),
            pltpu.SemaphoreType.DMA((2, group)),
        ],
        compiler_params=pltpu.CompilerParams(vmem_limit_bytes=VMEM_LIMIT),
        cost_estimate=pl.CostEstimate(
            flops=count * width // 8 * (local * capacity * (units + tokens) + tokens * share),
            bytes_accessed=2**20,
            transcendentals=0,
        ),
        name="run_outputs",
    )(act, slot_cols, sact, w_out, w_shared)


def weight_parts_kernel(count, place_ref, x, raw, out_part, ends, *refs):
    part_refs, (part, sems) = refs[:count], refs[count:]
    place = place_ref[0]
    width = part.shape[2]
    q_rows, out_rows, end_rows = x.shape[1] // count, out_part.shape[0] // count, ends.shape[0] // count

    def store(j):
        return pltpu.make_async_copy(part.at[j % 2], part_refs[j], sems.at[j % 2])

    for j in range(count):
        if j >= 2:
            store(j - 2).wait()
        to = place ^ j
        columns = x[:, pl.ds(pl.multiple_of(to * q_rows, q_rows), q_rows)]
        grad = dot(columns, raw[...], TN).astype(BF16)
        for c in range(3):
            part[j % 2, c * q_rows : (c + 1) * q_rows] = grad[:, c * width : (c + 1) * width]
        rows = out_part[pl.ds(pl.multiple_of(to * out_rows, out_rows), out_rows)]
        at = 3 * q_rows
        for k in range(out_part.shape[1] // width):
            part[j % 2, at : at + out_rows] = rows[:, k * width : (k + 1) * width]
            at += out_rows
        part[j % 2, at:] = ends[pl.ds(pl.multiple_of(to * end_rows, end_rows), end_rows)]
        store(j).start()
    for j in range(count - 2, count):
        store(j).wait()


def weight_parts(place, x, raw, out_part, ends, count):
    tokens, size = x.shape
    width = ends.shape[1]
    rows = (3 * size + out_part.size // width + ends.shape[0]) // count
    return pl.pallas_call(
        functools.partial(weight_parts_kernel, count),
        out_shape=[jax.ShapeDtypeStruct((rows, width), BF16)] * count,
        in_specs=[pl.BlockSpec(memory_space=pltpu.SMEM)]
        + [pl.BlockSpec(memory_space=pltpu.VMEM)] * 4,
        out_specs=[pl.BlockSpec(memory_space=pl.ANY)] * count,
        scratch_shapes=[
            pltpu.VMEM((2, rows, width), BF16),
            pltpu.SemaphoreType.DMA((2,)),
        ],
        compiler_params=pltpu.CompilerParams(vmem_limit_bytes=VMEM_LIMIT),
        cost_estimate=pl.CostEstimate(flops=0, bytes_accessed=2**20, transcendentals=0),
        name="weight_parts",
    )(place.reshape(1), x, raw, out_part, ends)


def assemble_kernel(plan, count, place_ref, *refs):
    block_refs, refs = refs[:count], refs[count:]
    out_refs, (low, wide, in_sems, out_sems) = refs[:-4], refs[-4:]
    place = place_ref[0]

    def load(j):
        return pltpu.make_async_copy(block_refs[j], low.at[j % 2], in_sems.at[j % 2])

    def stores(j):
        return [
            pltpu.make_async_copy(
                wide.at[j % 2, pl.ds(first, rows)],
                out_refs[which].at[
                    pl.ds(pl.multiple_of(base + (place ^ j) * rows, 8), rows),
                    pl.ds(column, wide.shape[2]),
                ],
                out_sems.at[j % 2, i],
            )
            for i, (which, first, rows, base, column) in enumerate(plan)
        ]

    load(0).start()
    for j in range(count):
        if j + 1 < count:
            load(j + 1).start()
        load(j).wait()
        if j >= 2:
            for copy in stores(j - 2):
                copy.wait()
        wide[j % 2] = low[j % 2].astype(F32)
        for copy in stores(j):
            copy.start()
    for j in range(max(0, count - 2), count):
        for copy in stores(j):
            copy.wait()


def assemble(place, blocks, shapes, plan):
    count = len(blocks)
    rows, width = blocks[0].shape
    any_spec = pl.BlockSpec(memory_space=pl.ANY)
    return pl.pallas_call(
        functools.partial(assemble_kernel, plan, count),
        out_shape=[jax.ShapeDtypeStruct(shape, F32) for shape in shapes],
        in_specs=[pl.BlockSpec(memory_space=pltpu.SMEM)] + [any_spec] * count,
        out_specs=[any_spec] * len(shapes),
        scratch_shapes=[
            pltpu.VMEM((2, rows, width), BF16),
            pltpu.VMEM((2, rows, width), F32),
            pltpu.SemaphoreType.DMA((2,)),
            pltpu.SemaphoreType.DMA((2, len(plan))),
        ],
        compiler_params=pltpu.CompilerParams(vmem_limit_bytes=VMEM_LIMIT),
        cost_estimate=pl.CostEstimate(flops=0, bytes_accessed=2**20, transcendentals=0),
        name="assemble",
    )(place.reshape(1), *blocks)


def shared_grads_kernel(count, place_ref, *refs):
    x_refs, g_all, refs = refs[:count], refs[count], refs[count + 1 :]
    (sact, sdpair, dl, grads_ref, router_ref, xs, gs, grads, router, sems) = refs
    at = pl.program_id(0)
    slot = lax.rem(at, 2)

    def load(j, into):
        return (
            pltpu.make_async_copy(x_refs[j], xs.at[into], sems.at[0, into]),
            pltpu.make_async_copy(g_all.at[place_ref[0] ^ j], gs.at[into], sems.at[1, into]),
        )

    @pl.when(at == 0)
    def _():
        for copy in load(0, 0):
            copy.start()
        grads[...] = jnp.zeros_like(grads)
        router[...] = jnp.zeros_like(router)

    for j in range(1, count):

        @pl.when(at == j - 1)
        def _():
            for copy in load(j, j % 2):
                copy.start()

    for copy in load(0, slot):
        copy.wait()
    x, g = xs[slot], gs[slot]
    grads[0] += dot(sdpair[0, 0], x, TN)
    grads[1] += dot(sdpair[0, 1], x, TN)
    grads[2] += dot(sact[0], g, TN)
    router[...] += dot(dl[0], x, TN)

    @pl.when(at == count - 1)
    def _():
        grads_ref[...] = grads[...].astype(BF16)
        router_ref[...] = router[...]


def shared_grads(place, x_blocks, g_all, sact, sdpair, dl):
    count = len(x_blocks)
    tokens, width = x_blocks[0].shape
    share, padded = sact.shape[2], dl.shape[2]
    any_spec = pl.BlockSpec(memory_space=pl.ANY)
    return pl.pallas_call(
        functools.partial(shared_grads_kernel, count),
        grid=(count,),
        out_shape=(
            jax.ShapeDtypeStruct((3, share, width), BF16),
            jax.ShapeDtypeStruct((padded, width), F32),
        ),
        in_specs=[pl.BlockSpec(memory_space=pltpu.SMEM)]
        + [any_spec] * (count + 1)
        + [
            pl.BlockSpec((1, tokens, share), lambda j: (j, 0, 0)),
            pl.BlockSpec((1, 2, tokens, share), lambda j: (j, 0, 0, 0)),
            pl.BlockSpec((1, tokens, padded), lambda j: (j, 0, 0)),
        ],
        out_specs=(
            pl.BlockSpec((3, share, width), lambda j: (0, 0, 0)),
            pl.BlockSpec((padded, width), lambda j: (0, 0)),
        ),
        scratch_shapes=[
            pltpu.VMEM((2, tokens, width), BF16),
            pltpu.VMEM((2, tokens, width), BF16),
            pltpu.VMEM((3, share, width), F32),
            pltpu.VMEM((padded, width), F32),
            pltpu.SemaphoreType.DMA((2, 2)),
        ],
        compiler_params=pltpu.CompilerParams(vmem_limit_bytes=VMEM_LIMIT),
        cost_estimate=pl.CostEstimate(
            flops=count * tokens * width * share,
            bytes_accessed=2**20,
            transcendentals=0,
        ),
        name="shared_grads",
    )(place.reshape(1), *x_blocks, g_all, sact, sdpair, dl)


def on_device(
    hidden_in,
    cotangent,
    gain_attn,
    qkv_weight,
    qkv_bias,
    out_weight,
    gain_ffn,
    router_weight,
    routes,
    shared_gate,
    shared_in,
    shared_out,
    expert_in,
    expert_out,
):
    tokens, width = hidden_in.shape
    ctx_count = lax.axis_size("ctx")
    heads_local = qkv_weight.shape[2] // HD
    local = expert_in.shape[0]
    experts = local * ctx_count
    top_count = routes.shape[1]
    capacity = 3 * tokens * top_count // (2 * experts)
    place = lax.axis_index("ctx")
    order = jnp.arange(ctx_count, dtype=jnp.int32) ^ place
    score_scale = 1.0 / math.sqrt(HD)
    query_pos = place * tokens + jnp.arange(tokens, dtype=jnp.int32)
    cosine, sine = rotary_tables(query_pos, HD)

    x_full = hidden_in.astype(F32)
    inv_one = lax.rsqrt(jnp.mean(x_full * x_full, axis=-1, keepdims=True) + EPS)
    normed_one = x_full * inv_one
    x_one = (normed_one * gain_attn).astype(BF16)
    projected = (
        jnp.einsum("td,dcf->ctf", x_one, qkv_weight, preferred_element_type=F32)
        + qkv_bias[:, None]
    )
    shaped = projected.reshape(3, tokens, heads_local, HD).transpose(0, 2, 1, 3)
    query = rotate(shaped[0], cosine, sine).astype(BF16)
    key_local = rotate(shaped[1], cosine, sine).astype(BF16)
    value_local = shaped[2].astype(BF16)
    kv_rows = heads_local * tokens
    route_rows = -(-tokens * top_count // HD)
    behind = jnp.pad(
        routes.T.astype(BF16).reshape(route_rows, HD), ((0, -route_rows % 16), (0, 0))
    )
    kv_local = jnp.stack(
        [
            jnp.concatenate([key_local.reshape(kv_rows, HD), behind], axis=0),
            jnp.concatenate([value_local.reshape(kv_rows, HD), behind], axis=0),
        ]
    )
    share = shared_out.shape[0] // ctx_count
    piece = shared_out.shape[1]
    shared_send = jnp.concatenate(
        [
            shared_in.transpose(1, 2, 0).reshape(2, ctx_count, share, piece),
            shared_out.reshape(1, ctx_count, share, piece),
        ],
        axis=0,
    ).transpose(1, 0, 2, 3)
    shared_got = lax.all_to_all(shared_send, "ctx", split_axis=0, concat_axis=0, tiled=True)
    kv_blocks = gather_ctx(after(kv_local, shared_got))
    g_all = lax.all_gather(after(cotangent, kv_blocks[2 % ctx_count], kv_blocks[4 % ctx_count]), "ctx", axis=0)

    half_rows = out_weight.shape[0] // 2
    core = place % 2
    out_mine = lax.all_gather(
        lax.dynamic_slice_in_dim(out_weight, core * half_rows, half_rows, 0), "tp", axis=0
    )

    routes_all = jnp.stack([b[0, kv_rows : kv_rows + route_rows] for b in kv_blocks])
    routes_all = routes_all.reshape(ctx_count, 1, top_count, tokens)
    own_experts = (place * local + jnp.arange(local, dtype=jnp.int32)).astype(BF16)
    hit = jnp.any(routes_all == own_experts[None, :, None, None], axis=2)
    token_at = jnp.arange(tokens, dtype=jnp.int32)
    earlier = (token_at[:, None] <= token_at[None, :]).astype(BF16)
    rank = dot(hit.astype(BF16).reshape(-1, tokens), earlier, NN).reshape(hit.shape) - 1.0
    slot_rows = jnp.where(hit, rank, -1.0).astype(jnp.int32)
    slot_cols = slot_rows.transpose(0, 2, 1)
    padded = -(-(experts + 1) // 8) * 8
    w_router = jnp.concatenate(
        [
            router_weight.T,
            shared_gate[None],
            jnp.zeros((padded - experts - 1, width), BF16),
        ],
        axis=0,
    )
    w_in = expert_in.transpose(0, 2, 3, 1)

    attended, lse = attend(place, query, kv_blocks)
    att = attended.astype(BF16).transpose(1, 0, 2).reshape(tokens, heads_local * HD)
    out_mine = after(out_mine, attended)
    out_other = swap(out_mine, 1)
    att_mine, att_other = columns(place, gather_tp(att))
    att_mine = after(att_mine, slot_rows, slot_cols, w_router, w_in)
    rows = out_mine.shape[0] * half_rows
    hidden = x_full + (
        dot(att_mine, out_mine.reshape(rows, width), NN)
        + dot(att_other, out_other.reshape(rows, width), NN)
    )
    shared_w = shared_got.transpose(1, 2, 0, 3).reshape(3, share, width)
    whole_share = -(-share // 16) * 16
    if whole_share > share:
        shared_w = jnp.pad(shared_w, ((0, 0), (0, whole_share - share), (0, 0)))
    inv_two = lax.rsqrt(jnp.mean(hidden * hidden, axis=-1, keepdims=True) + EPS)
    normed_two = hidden * inv_two
    x_two = (normed_two * gain_ffn).astype(BF16)

    units, group = expert_out.shape[1], 2
    kept = [
        jax.ShapeDtypeStruct(shape, BF16)
        for shape in (
            (local, ctx_count, capacity, width),
            (local, ctx_count, capacity, width),
            (local, ctx_count, capacity, units),
            (2 * local, ctx_count, capacity, units),
            (ctx_count, tokens, whole_share),
            (ctx_count, 2, tokens, whole_share),
            (ctx_count, tokens, padded),
        )
    ]
    weights = (w_router, w_in, expert_out, shared_w)
    g_near = [cotangent, swap(cotangent, 1)]
    got = gather_start(x_two)
    x_blocks = [got[0], got[1]]
    dxs = []
    early = None
    for at in range(0, ctx_count, group):
        if at == 4 and ctx_count == 8:
            pair_two = pair_sum(dxs, 2)
            early = (pair_two, pair_two[: tokens // 2].astype(BF16))
        if at == 6 and ctx_count == 8:
            x_blocks[6] = after(x_blocks[6], early[1])
        dx, kept = run_experts(
            at,
            experts,
            place,
            x_blocks[at : at + group],
            g_near if at == 0 else [g_all],
            slot_rows,
            slot_cols,
            weights,
            kept,
        )
        dxs += dx
        if at == 0:
            x_blocks = x_blocks[:2] + gather_end(got, dx[0])[2:]
    grad_x_part = scatter_ctx(dxs, early)
    outs = run_outputs(kept[2], slot_cols, kept[4], expert_out, shared_w)
    grad_x_low = grad_x_part.astype(BF16)
    out_middle = scatter_middle(scatter_start(after(outs, grad_x_low)))
    kept = after(kept, outs[0], *out_middle[0])
    rows_x, rows_g, act_low, dpair, s_act, s_dpair, low_logits = kept
    shared_low, router_part = shared_grads(place, x_blocks, g_all, s_act, s_dpair, low_logits)
    expert_grads = grads_of_experts(rows_x, rows_g, act_low, dpair)
    grad_expert_in, grad_expert_out = expert_grads
    gain_ffn_part = jnp.sum(grad_x_part * normed_two, axis=0)
    small_rows = padded + 1
    small_part = jnp.concatenate([router_part, gain_ffn_part[None]], axis=0)
    small_part = jnp.pad(small_part, ((0, -small_rows % (8 * lax.axis_size("tp"))), (0, 0)))
    half = tokens // 2
    first = lax.psum(grad_x_low[:half], "tp")
    second = lax.psum(after(grad_x_low[half:], first, *out_middle[0]), "tp")
    out_part = scatter_end(out_middle)

    shared_back = lax.all_to_all(
        shared_low[:, :share].reshape(3, share, ctx_count, piece).transpose(2, 0, 1, 3),
        "ctx",
        split_axis=0,
        concat_axis=0,
        tiled=True,
    )
    shared_wide = shared_back.astype(F32)
    grad_shared_in = shared_wide[:, :2].transpose(3, 1, 0, 2).reshape(shared_in.shape)
    grad_shared_out = shared_wide[:, 2].reshape(shared_out.shape)
    summed = jnp.concatenate([first, second], axis=0)
    summed = after(summed, shared_back, *expert_grads, out_part)
    summed = summed.astype(F32)
    grad_y = cotangent.astype(F32)
    grad_normed_two = summed * gain_ffn
    grad_hidden = grad_y + inv_two * (
        grad_normed_two
        - normed_two * jnp.mean(grad_normed_two * normed_two, axis=-1, keepdims=True)
    )
    grad_hidden_low = grad_hidden.astype(BF16)
    out_weight_part = dot(att, grad_hidden_low, (((0,), (0,)), ((), ())))
    grad_att = (
        dot(grad_hidden_low, out_weight, (((1,), (1,)), ((), ())))
        .astype(BF16)
        .reshape(tokens, heads_local, HD)
        .transpose(1, 0, 2)
    )
    delta = jnp.sum(grad_att.astype(F32) * attended, axis=-1)
    delta = jnp.broadcast_to(delta[:, None], lse.shape)
    grad_query, grad_pairs = attend_back(place, query, grad_att, lse, delta, kv_blocks)
    ffn_total = sum_tp_start(out_part, small_part)
    grad_pairs = after(grad_pairs, ffn_total)
    kv_middle = scatter_middle(scatter_start([grad_pairs[j] for j in range(ctx_count)]))
    ffn_low = sum_tp_end(after(ffn_total, *kv_middle[0]))
    own_rows = tokens // lax.axis_size("tp")
    small = ffn_low[:, own_rows:].reshape(-1, width)[:small_rows].astype(F32)
    ffn_low = ffn_low[:, :own_rows].reshape(tokens, width)
    grad_kv = scatter_end(kv_middle)
    grad_kv = after(grad_kv, grad_shared_in, grad_shared_out)

    def raw_part(value):
        return value.astype(BF16).transpose(1, 0, 2).reshape(tokens, heads_local * HD)

    raw = [
        raw_part(rotate(grad_query, cosine, -sine)),
        raw_part(rotate(grad_kv[0], cosine, -sine)),
        raw_part(grad_kv[1]),
    ]
    raw = jnp.concatenate(raw, axis=1)
    grad_x_one_part = jnp.einsum(
        "tcf,dcf->td",
        raw.reshape(tokens, 3, -1),
        qkv_weight,
        preferred_element_type=F32,
    )
    grad_x_low = grad_x_one_part.astype(BF16)
    half_way = sum_tp_start(grad_x_low)
    grad_x_one = sum_tp_end(half_way).reshape(tokens, width)
    x_one = after(x_one, grad_x_low)
    gain_attn_part = jnp.sum(grad_x_one_part * normed_one, axis=0)
    gain_sum = sum_tp_small(gain_attn_part[None])
    head_width = heads_local * HD
    gain_rows = width // head_width
    ends = jnp.concatenate(
        [jnp.sum(raw.astype(F32), axis=0).reshape(3, -1)]
        + [gain_sum.reshape(gain_rows, -1), small.reshape((padded + 1) * gain_rows, -1)],
        axis=0,
    )
    ends = jnp.pad(ends, ((0, -ends.shape[0] % (16 * ctx_count)), (0, 0))).astype(BF16)
    turns = width // head_width
    sums = sum_ctx(
        weight_parts(place, x_one, raw, out_weight_part.astype(BF16), ends, ctx_count), half_way
    )
    q_rows = width // ctx_count
    out_rows = out_weight.shape[0] // ctx_count
    plan = [(0, c * q_rows, q_rows, c * width, 0) for c in range(3)] + [
        (1, 3 * q_rows + k * out_rows, out_rows, 0, k * head_width) for k in range(turns)
    ]
    qkv_grad, out_weight_grad = assemble(
        place, sums, [(3 * width, head_width), out_weight.shape], plan
    )
    qkv_grad = qkv_grad.reshape(3, width, head_width).transpose(1, 0, 2)
    ends = relative(jnp.stack([b[3 * q_rows + turns * out_rows :] for b in sums]))
    ends = ends.reshape(-1, head_width).astype(F32)
    small = ends[3 + gain_rows : 3 + (padded + 2) * gain_rows].reshape(padded + 1, width)
    grad_x_one = after(grad_x_one, sums[2]).astype(F32)
    grad_normed_one = grad_x_one * gain_attn
    grad_input = grad_hidden + inv_one * (
        grad_normed_one
        - normed_one * jnp.mean(grad_normed_one * normed_one, axis=-1, keepdims=True)
    )
    block_out = (hidden + ffn_low.astype(F32)).astype(BF16)
    return (
        block_out,
        grad_input,
        ends[3 : 3 + gain_rows].reshape(-1),
        qkv_grad,
        ends[:3],
        out_weight_grad,
        small[padded],
        small[:experts].T,
        small[experts],
        grad_shared_in,
        grad_shared_out,
        grad_expert_in.transpose(0, 3, 1, 2),
        grad_expert_out,
    )


def solution(mesh):
    return jax.shard_map(
        on_device,
        mesh=mesh,
        in_specs=(
            P("ctx", None),
            P("ctx", None),
            P(),
            P(None, None, "tp"),
            P(None, "tp"),
            P("tp", None),
            P(),
            P(),
            P("ctx", None),
            P(),
            P("ctx", None, "tp"),
            P("tp", "ctx"),
            P("ctx", None, None, "tp"),
            P("ctx", "tp", None),
        ),
        out_specs=(
            P("ctx", None),
            P("ctx", None),
            P(),
            P(None, None, "tp"),
            P(None, "tp"),
            P("tp", None),
            P(),
            P(),
            P(),
            P("ctx", None, "tp"),
            P("tp", "ctx"),
            P("ctx", None, None, "tp"),
            P("ctx", "tp", None),
        ),
        check_vma=False,
    )
```

```python
import functools
import math

import jax
import jax.numpy as jnp
from jax import lax
from jax.experimental import pallas as pl
from jax.experimental.pallas import tpu as pltpu
from jax.sharding import PartitionSpec as P

HD = 128
EPS = 1e-06
THETA = 1000000.0
NEG = -1e30
F32 = jnp.float32
BF16 = jnp.bfloat16


def rotary_tables(positions, width):
    half_width = width // 2
    freqs = THETA ** (-(jnp.arange(half_width, dtype=F32) * 2.0) / width)
    angles = positions.astype(F32)[:, None] * freqs[None, :]
    return (jnp.cos(angles), jnp.sin(angles))


def rotate(values, cosine, sine):
    half_width = values.shape[-1] // 2
    first, second = values[..., :half_width], values[..., half_width:]
    return jnp.concatenate(
        [first * cosine - second * sine, second * cosine + first * sine], axis=-1
    )


def dot(a, b, dims):
    return lax.dot_general(a, b, dims, preferred_element_type=F32)


def swap(value, bits):
    count = lax.axis_size("ctx")
    return lax.ppermute(value, "ctx", [(i, i ^ bits) for i in range(count)])


def relative(natural):
    count = natural.shape[0]
    order = jnp.arange(count, dtype=jnp.int32) ^ lax.axis_index("ctx")
    return natural[order]


def nothing_kernel(*refs):
    pass


def after(values, *others):
    single = not isinstance(values, (list, tuple))
    values = [values] if single else list(values)
    any_spec = pl.BlockSpec(memory_space=pl.ANY)
    results = pl.pallas_call(
        nothing_kernel,
        out_shape=[jax.ShapeDtypeStruct(v.shape, v.dtype) for v in values],
        in_specs=[any_spec] * (len(values) + len(others)),
        out_specs=[any_spec] * len(values),
        input_output_aliases={i: i for i in range(len(values))},
        name="after",
    )(*values, *others)
    return results[0] if single else results


def gather_start(own):
    if lax.axis_size("ctx") != 8:
        return relative(lax.all_gather(own, "ctx", axis=0))
    return [own, swap(own, 1), swap(own, 2), swap(own, 4)]


def gather_end(got, *others):
    if lax.axis_size("ctx") != 8:
        return [got[j] for j in range(lax.axis_size("ctx"))]
    own, b1, b2, b4 = got
    if others:
        b2, b4 = after((b2, b4), *others)
    half = own.shape[0] // 2
    via_x, via_y = swap(b4[:half], 2), swap(b2[half:], 4)
    b3, b5 = swap(b2, 1), swap(b4, 1)
    b6 = jnp.concatenate([via_x, via_y], axis=0)
    return [own, b1, b2, b3, b4, b5, b6, swap(b6, 1)]


def gather_ctx(own, *others):
    return gather_end(gather_start(own), *others)


def pair_sum(parts, j):
    return parts[j].astype(F32) + swap(parts[j ^ 1], 1).astype(F32)


def scatter_ctx(parts, early=None):
    return scatter_end(scatter_middle(scatter_start(parts, early)))


def scatter_start(parts, early=None):
    if lax.axis_size("ctx") != 8:
        return [jnp.stack(parts)], None
    half = parts[0].shape[0] // 2
    pair = {j: pair_sum(parts, j) for j in (2, 4, 6, 0) if j != 2 or early is None}
    if early is None:
        early = (pair[2], pair[2][:half].astype(BF16))
    q6 = pair[6].astype(BF16)
    hops = [early[1], pair[4][half:].astype(BF16), q6[:half], q6[half:]]
    return hops, (early[0], pair[4], pair[0])


def scatter_middle(started):
    hops, stay = started
    if lax.axis_size("ctx") != 8:
        return hops, None
    two, four, zero = stay
    half = two.shape[0] // 2
    r2, r4 = swap(hops[0], 2), swap(hops[1], 4)
    via_x, via_y = swap(hops[2], 2), swap(hops[3], 4)
    r4a = (four[:half] + via_x.astype(F32)).astype(BF16)
    r2b = (two[half:] + via_y.astype(F32)).astype(BF16)
    return [r4a, r2b], (r2, r4, zero)


def scatter_end(started, *others):
    hops, stay = started
    if lax.axis_size("ctx") != 8:
        natural = relative(hops[0])
        flat = natural.reshape((-1,) + natural.shape[2:])
        return lax.psum_scatter(flat, "ctx", scatter_dimension=0, tiled=True).astype(F32)
    if others:
        hops = after(hops, *others)
    r2, r4, zero = stay
    r4a, r2b = swap(hops[0], 4), swap(hops[1], 2)
    low = r2.astype(F32) + r4a.astype(F32)
    high = r2b.astype(F32) + r4.astype(F32)
    return zero + jnp.concatenate([low, high], axis=0)


def sum_ctx(parts, *others):
    hops, stay = scatter_start(parts)
    own = scatter_end(scatter_middle((after(hops, *others), stay)))
    return gather_ctx(own.astype(BF16))


def shards(value):
    count = lax.axis_size("ctx")
    rows = value.shape[0] // count
    place = lax.axis_index("ctx")
    return [lax.dynamic_slice_in_dim(value, (place ^ j) * rows, rows, 0) for j in range(count)]


def gather_tp(own):
    count = lax.axis_size("tp")
    return [own] + [
        lax.ppermute(own, "tp", [(i, i ^ k) for i in range(count)]) for k in range(1, count)
    ]


NT = (((1,), (1,)), ((), ()))
NN = (((1,), (0,)), ((), ()))
TN = (((0,), (0,)), ((), ()))
VMEM_LIMIT = 60 * 1024 * 1024


def sum_tp_start(*values):
    pieces = [v.astype(BF16).reshape(lax.axis_size("tp"), -1, v.shape[1]) for v in values]
    pieces = jnp.concatenate(pieces, axis=1)
    got = lax.all_to_all(pieces, "tp", split_axis=0, concat_axis=0, tiled=True)
    return jnp.sum(got.astype(F32), axis=0).astype(BF16)


def sum_tp_end(total):
    count, at = lax.axis_size("tp"), lax.axis_index("tp")
    blocks = jnp.stack(gather_tp(total))
    blocks = blocks[jnp.arange(count, dtype=jnp.int32) ^ at]
    return blocks


def sum_tp_small(value):
    count, bits = lax.axis_size("tp"), 1
    while bits < count:
        value = value + lax.ppermute(value, "tp", [(i, i ^ bits) for i in range(count)])
        bits *= 2
    return value


def columns_kernel(count, places, *refs):
    block_refs, (mine, other) = refs[:count], refs[count:]
    core, at = places[0], places[1]
    width = mine.shape[1] // count
    for k in range(count):
        to = pl.ds(pl.multiple_of((at ^ k) * width, width), width)
        mine[:, to] = block_refs[k][:, pl.ds(pl.multiple_of(core * width, width), width)]
        other[:, to] = block_refs[k][:, pl.ds(pl.multiple_of((1 - core) * width, width), width)]


def columns(place, blocks):
    count = len(blocks)
    rows, width = blocks[0].shape
    vmem = pl.BlockSpec(memory_space=pltpu.VMEM)
    half = jax.ShapeDtypeStruct((rows, count * width // 2), blocks[0].dtype)
    return pl.pallas_call(
        functools.partial(columns_kernel, count),
        out_shape=(half, half),
        in_specs=[pl.BlockSpec(memory_space=pltpu.SMEM)] + [vmem] * count,
        out_specs=(vmem, vmem),
        compiler_params=pltpu.CompilerParams(vmem_limit_bytes=VMEM_LIMIT),
        cost_estimate=pl.CostEstimate(flops=0, bytes_accessed=2**20, transcendentals=0),
        name="columns",
    )(jnp.stack([place % 2, lax.axis_index("tp")]), *blocks)


def attend_kernel(factor, count, place_ref, q_ref, *refs):
    kv_refs, (att_ref, lse_ref, kv, sems) = refs[:count], refs[count:]
    rows = kv.shape[2]
    copies = [
        pltpu.make_async_copy(kv_refs[j].at[:, pl.ds(0, rows)], kv.at[j], sems.at[j])
        for j in range(count)
    ]
    for copy in copies:
        copy.start()
    for copy in copies:
        copy.wait()
    place = place_ref[0]
    heads, tokens, _ = q_ref.shape

    def one_head(head, _):
        query = q_ref[head]
        here = pl.ds(pl.multiple_of(head * tokens, tokens), tokens)

        def scores(j):
            return dot(kv[j, 0, here], query, NT) * factor

        key_at = lax.broadcasted_iota(jnp.int32, (tokens, tokens), 0)
        query_at = lax.broadcasted_iota(jnp.int32, (tokens, tokens), 1)
        first = jnp.where(key_at <= query_at, scores(0), NEG)
        top = jnp.max(first, axis=0, keepdims=True)
        exps = jnp.exp2(first - top)
        total = jnp.sum(exps, axis=0, keepdims=True)
        acc = dot(kv[0, 1, here], exps.astype(BF16), TN)

        def earlier(i, carry):
            top, total, acc = carry
            j = place ^ i
            now = scores(j)
            higher = jnp.maximum(top, jnp.max(now, axis=0, keepdims=True))
            exps = jnp.exp2(now - higher)
            keep = jnp.exp2(top - higher)
            total = total * keep + jnp.sum(exps, axis=0, keepdims=True)
            acc = acc * keep + dot(kv[j, 1, here], exps.astype(BF16), TN)
            return higher, total, acc

        top, total, acc = lax.fori_loop(0, place, earlier, (top, total, acc))
        att_ref[head] = (acc / total).T
        lse_ref[head] = jnp.broadcast_to(top + jnp.log2(total), lse_ref.shape[1:])
        return 0

    lax.fori_loop(0, heads, one_head, 0)


def attend(place, query, kv_blocks):
    heads, tokens, size = query.shape
    count = len(kv_blocks)
    factor = math.log2(math.e) / math.sqrt(size)
    flops = 4 * count * heads * tokens * tokens * size
    return pl.pallas_call(
        functools.partial(attend_kernel, factor, count),
        out_shape=(
            jax.ShapeDtypeStruct((heads, tokens, size), F32),
            jax.ShapeDtypeStruct((heads, 8, tokens), F32),
        ),
        in_specs=[
            pl.BlockSpec(memory_space=pltpu.SMEM),
            pl.BlockSpec(memory_space=pltpu.VMEM),
        ]
        + [pl.BlockSpec(memory_space=pl.ANY)] * count,
        out_specs=(pl.BlockSpec(memory_space=pltpu.VMEM),) * 2,
        scratch_shapes=[
            pltpu.VMEM((count, 2, heads * tokens, size), BF16),
            pltpu.SemaphoreType.DMA((count,)),
        ],
        compiler_params=pltpu.CompilerParams(vmem_limit_bytes=VMEM_LIMIT),
        cost_estimate=pl.CostEstimate(
            flops=flops // 16, bytes_accessed=2**20, transcendentals=0
        ),
        name="attend",
    )(place.reshape(1), query, *kv_blocks)


def attend_back_kernel(factor, scale, count, place_ref, q_ref, do_ref, lse_ref, delta_ref, *refs):
    kv_refs, (dq_ref, dkv_ref, kv, dkv, dq, sems, out_sems) = refs[:count], refs[count:]
    rows = kv.shape[2]
    copies = [
        pltpu.make_async_copy(kv_refs[j].at[:, pl.ds(0, rows)], kv.at[j], sems.at[j])
        for j in range(count)
    ]
    for copy in copies:
        copy.start()
    for copy in copies:
        copy.wait()
    place = place_ref[0]
    heads, tokens, _ = q_ref.shape

    def out_copy(j):
        return pltpu.make_async_copy(dkv.at[j], dkv_ref.at[j], out_sems.at[j])

    def one_block(j, masked):
        def one_head(head, _):
            query, do = q_ref[head], do_ref[head]
            here = pl.ds(pl.multiple_of(head * tokens, tokens), tokens)
            key, value = kv[j, 0, here], kv[j, 1, here]
            scores = dot(key, query, NT) * factor
            probs = jnp.exp2(scores - lse_ref[head, :1])
            if masked:
                key_at = lax.broadcasted_iota(jnp.int32, (tokens, tokens), 0)
                query_at = lax.broadcasted_iota(jnp.int32, (tokens, tokens), 1)
                probs = jnp.where(key_at <= query_at, probs, 0.0)
            dprob = dot(value, do, NT)
            dscore = (probs * (dprob - delta_ref[head, :1])).astype(BF16)
            dkv[j, 0, head] = (dot(dscore, query, NN) * scale).astype(BF16)
            dkv[j, 1, head] = dot(probs.astype(BF16), do, NN).astype(BF16)
            part = dot(key, dscore, TN)
            dq[head] = part if masked else dq[head] + part
            return 0

        lax.fori_loop(0, heads, one_head, 0)
        out_copy(j).start()

    one_block(0, True)

    def earlier(i, _):
        one_block(place ^ i, False)
        return 0

    def later(i, _):
        j = place ^ i
        dkv[j] = jnp.zeros(dkv.shape[1:], BF16)
        out_copy(j).start()
        return 0

    lax.fori_loop(0, place, earlier, 0)
    lax.fori_loop(place + 1, count, later, 0)
    for head in range(heads):
        dq_ref[head] = dq[head].T * scale
    for j in range(count):
        out_copy(j).wait()


def attend_back(place, query, do, lse, delta, kv_blocks):
    heads, tokens, size = query.shape
    count = len(kv_blocks)
    scale = 1.0 / math.sqrt(size)
    factor = math.log2(math.e) * scale
    return pl.pallas_call(
        functools.partial(attend_back_kernel, factor, scale, count),
        out_shape=(
            jax.ShapeDtypeStruct((heads, tokens, size), F32),
            jax.ShapeDtypeStruct((count, 2, heads, tokens, size), BF16),
        ),
        in_specs=[pl.BlockSpec(memory_space=pltpu.SMEM)]
        + [pl.BlockSpec(memory_space=pltpu.VMEM)] * 4
        + [pl.BlockSpec(memory_space=pl.ANY)] * count,
        out_specs=(pl.BlockSpec(memory_space=pltpu.VMEM), pl.BlockSpec(memory_space=pl.ANY)),
        scratch_shapes=[
            pltpu.VMEM((count, 2, heads * tokens, size), BF16),
            pltpu.VMEM((count, 2, heads, tokens, size), BF16),
            pltpu.VMEM((heads, size, tokens), F32),
            pltpu.SemaphoreType.DMA((count,)),
            pltpu.SemaphoreType.DMA((count,)),
        ],
        compiler_params=pltpu.CompilerParams(vmem_limit_bytes=VMEM_LIMIT),
        cost_estimate=pl.CostEstimate(
            flops=count * heads * tokens * tokens * size,
            bytes_accessed=2**20,
            transcendentals=0,
        ),
        name="attend_back",
    )(place.reshape(1), query, do, lse, delta, *kv_blocks)


def swiglu_back(one, two, dact, gate):
    sig = 1.0 / (1.0 + jnp.exp(-one))
    silu = one * sig
    act = silu * two
    prod = act * dact
    dgate = gate * dact
    d_one = (dgate * two * sig * (1.0 + one * (1.0 - sig))).astype(BF16)
    d_two = (dgate * silu).astype(BF16)
    return (gate * act).astype(BF16), d_one, d_two, prod


def experts_kernel(at, group, local, experts, given, near, place_ref, *refs):
    x_refs, refs = refs[:group], refs[group:]
    if near:
        g_refs, refs = refs[:group], refs[group:]
    else:
        g_refs = [refs[0].at[place_ref[0] ^ (at + b)] for b in range(group)]
        refs = refs[1:]
    (slot_row, slot_col, w_router, w_in, w_out, w_shared), refs = refs[:6], refs[6 + given :]
    dx_refs, refs = refs[:group], refs[group:]
    kept_refs, refs = refs[:7], refs[7:]
    (xs, gs, first_w, in_w, out_w, shared_w, dxs, left, right, sems, out_sems), stage = refs[:11], refs[11:]
    rows_x, rows_g, act_s, dpair_s, sact_s, sdpair_s, dl_s = stage
    tokens, width = xs.shape[1:]
    capacity, units = act_s.shape[2:]
    wide = local * capacity
    share = sact_s.shape[2]
    third = first_w.shape[0] - 128
    second = third // 2
    padded = w_router.shape[0]
    most = out_w.shape[1]

    loads = [pltpu.make_async_copy(x_refs[b], xs.at[b], sems.at[b]) for b in range(group)]
    fore_loads = [
        pltpu.make_async_copy(
            w_shared.at[c], first_w.at[pl.ds(c * second, share)], sems.at[2 * group + c]
        )
        for c in range(2)
    ]
    loads += [
        pltpu.make_async_copy(g_refs[b], gs.at[b], sems.at[group + b]) for b in range(group)
    ]
    base = 2 * group + 2
    more = [
        [
            pltpu.make_async_copy(
                w_in.at[e, c], in_w.at[e, pl.ds(c * most, units)], sems.at[base + 3 * e + c]
            )
            for c in range(2)
        ]
        + [
            pltpu.make_async_copy(
                w_out.at[e], out_w.at[e, pl.ds(0, units)], sems.at[base + 3 * e + 2]
            )
        ]
        for e in range(local)
    ]
    last = pltpu.make_async_copy(w_shared.at[2], shared_w, sems.at[base + 3 * local])
    for copy in loads[:group] + fore_loads:
        copy.start()
    first_w[third : third + padded] = w_router[...]
    first_w[third + padded :] = jnp.zeros((128 - padded, width), BF16)
    if second > share:
        for c in range(2):
            gap = jnp.zeros((second - share, width), BF16)
            first_w[c * second + share : (c + 1) * second] = gap
    if most > units:
        gap = jnp.zeros((most - units, width), BF16)
        for e in range(local):
            in_w[e, units:most] = gap
            in_w[e, most + units :] = gap
            out_w[e, units:] = gap

    sent = []

    def send(copy):
        copy.start()
        sent.append(copy)

    for copy in loads[:group] + fore_loads:
        copy.wait()
    for copy in loads[group:] + more[0]:
        copy.start()
    x = xs[...].reshape(group * tokens, width)
    fore = dot(x, first_w[...], NT)
    s_one, s_two = fore[:, :share], fore[:, second : second + share]
    s_gate = 1.0 / (1.0 + jnp.exp(-fore[:, third + experts : third + experts + 1]))
    row_at = lax.broadcasted_iota(jnp.int32, (padded, tokens), 0)
    slot_at = lax.broadcasted_iota(jnp.int32, (capacity, tokens), 0)
    probs, change, hits = [], [], []
    for b in range(group):
        logits = fore[b * tokens : (b + 1) * tokens, third:].T[:padded]
        shown = jnp.where(row_at < experts, logits, NEG)
        exps = jnp.exp(shown - jnp.max(shown, axis=0, keepdims=True))
        soft = exps / jnp.sum(exps, axis=0, keepdims=True)
        probs.append(jnp.where(row_at == experts, 1.0 / (1.0 + jnp.exp(-logits)), soft))
        change.append(jnp.zeros((padded, tokens), F32))
        picks = jnp.concatenate(
            [
                jnp.where(slot_at == slot_row[b, e : e + 1, :], 1.0, 0.0).astype(BF16)
                for e in range(local)
            ],
            axis=0,
        )
        rows = dot(picks, xs[b], NN).astype(BF16)
        for e in range(local):
            rows_x[e, b] = rows[e * capacity : (e + 1) * capacity]
        loads[group + b].wait()
        if b == group - 1:
            for e in range(1, local):
                for copy in more[e]:
                    copy.start()
            last.start()
        rows = dot(picks, gs[b], NN).astype(BF16)
        for e in range(local):
            rows_g[e, b] = rows[e * capacity : (e + 1) * capacity]
    def send_all(i, lead):
        for e in range(lead):
            send(
                pltpu.make_async_copy(
                    stage[i].at[e], kept_refs[i].at[e, pl.ds(at, group)], out_sems.at[i, e]
                )
            )

    send_all(0, local)
    send_all(1, local)
    is_expert = row_at < experts
    for e in range(local):
        chosen = row_at == place_ref[0] * local + e
        gates, owns, hits = [], [], []
        for b in range(group):
            own = jnp.sum(jnp.where(chosen, probs[b], 0.0), axis=0, keepdims=True)
            hit = slot_at == slot_row[b, e : e + 1, :]
            gates.append(jnp.sum(jnp.where(hit, own, 0.0), axis=1, keepdims=True))
            owns.append(own)
            hits.append(hit)
        for copy in more[e]:
            copy.wait()
        pair = dot(rows_x[e].reshape(group * capacity, width), in_w[e], NT)
        dact = dot(rows_g[e].reshape(group * capacity, width), out_w[e], NT)
        act, d_one, d_two, prod = swiglu_back(
            pair[:, :most], pair[:, most:], dact, jnp.concatenate(gates, axis=0)
        )
        act_s[e] = act[:, :units].reshape(group, capacity, units)
        dpair_s[2 * e] = d_one[:, :units].reshape(group, capacity, units)
        dpair_s[2 * e + 1] = d_two[:, :units].reshape(group, capacity, units)
        row_dot = jnp.sum(prod, axis=1, keepdims=True)
        drow = dot(jnp.concatenate([d_one, d_two], axis=1), in_w[e], NN).astype(BF16)
        for b in range(group):
            rows = slice(b * capacity, (b + 1) * capacity)
            found = jnp.sum(jnp.where(hits[b], row_dot[rows], 0.0), axis=0, keepdims=True)
            change[b] += (found * owns[b]) * (
                jnp.where(chosen, 1.0, 0.0) - jnp.where(is_expert, probs[b], 0.0)
            )
            right[b, e * capacity : (e + 1) * capacity] = drow[rows]
    send_all(2, local)
    send_all(3, 2 * local)
    last.wait()
    g = gs[...].reshape(group * tokens, width)
    s_dact = dot(g, shared_w[...], NT)
    act, d_one, d_two, prod = swiglu_back(s_one, s_two, s_dact, s_gate)
    sact_s[...] = act.reshape(group, tokens, share)
    sdpair_s[:, 0] = d_one.reshape(group, tokens, share)
    sdpair_s[:, 1] = d_two.reshape(group, tokens, share)
    dslogit = jnp.sum(prod, axis=1, keepdims=True) * s_gate * (1.0 - s_gate)
    lane_at = lax.broadcasted_iota(jnp.int32, (tokens, 128), 1)
    rest = jnp.zeros((128 - padded, tokens), F32)
    deep = wide + 2 * share
    column_at = lax.broadcasted_iota(jnp.int32, (tokens, capacity), 1)
    stores = []
    for b in range(group):
        rows = slice(b * tokens, (b + 1) * tokens)
        columns = jnp.concatenate([change[b], rest], axis=0).T
        columns = jnp.where(lane_at == experts, dslogit[rows], columns)[:, :padded].astype(BF16)
        dl_s[b] = columns
        left[b, :, deep : deep + padded] = columns
        right[b, deep : deep + padded] = w_router[...]
        for e in range(local):
            picks = jnp.where(column_at == slot_col[b, :, e : e + 1], 1.0, 0.0).astype(BF16)
            left[b, :, e * capacity : (e + 1) * capacity] = picks
        left[b, :, wide : wide + share] = d_one[rows]
        left[b, :, wide + share : wide + 2 * share] = d_two[rows]
        right[b, wide : wide + share] = first_w[:share]
        right[b, wide + share : wide + 2 * share] = first_w[second : second + share]
        dxs[b] = dot(left[b], right[b], NN).astype(BF16)
        send(pltpu.make_async_copy(dxs.at[b], dx_refs[b], out_sems.at[7, b]))
    for i in range(4, 7):
        send(pltpu.make_async_copy(stage[i], kept_refs[i].at[pl.ds(at, group)], out_sems.at[i, 0]))
    for copy in sent:
        copy.wait()


def run_experts(at, experts, place, x_group, g_group, slot_rows, slot_cols, weights, kept):
    given = kept if at else []
    group = len(x_group)
    near = len(g_group) == group
    tokens, width = x_group[0].shape
    w_router, w_in, w_out, w_shared = weights
    local = w_out.shape[0]
    share = w_shared.shape[1]
    padded = w_router.shape[0]
    capacity, units = kept[2].shape[2:]
    any_spec = pl.BlockSpec(memory_space=pl.ANY)
    block = jax.ShapeDtypeStruct((tokens, width), BF16)
    deep = local * capacity + 2 * share + padded
    flops = group * 2 * tokens * width * (local * capacity * 3 + 5 * share) + (
        group * 2 * width * local * capacity * units * 5
    )
    step = at // group
    wide_units = -(-units // 128) * 128
    fore = 2 * (-(-share // 64) * 64) + 128
    results = pl.pallas_call(
        functools.partial(experts_kernel, at, group, local, experts, len(given), near),
        grid=(1,),
        out_shape=(block,) * group + tuple(jax.ShapeDtypeStruct(k.shape, k.dtype) for k in kept),
        in_specs=[pl.BlockSpec(memory_space=pltpu.SMEM)]
        + [any_spec] * (group + len(g_group))
        + [
            pl.BlockSpec((group, local, tokens), lambda i: (step, 0, 0)),
            pl.BlockSpec((group, tokens, local), lambda i: (step, 0, 0)),
            pl.BlockSpec((padded, width), lambda i: (0, 0)),
        ]
        + [any_spec] * (3 + len(given)),
        out_specs=(any_spec,) * (group + len(kept)),
        input_output_aliases={7 + group + len(g_group) + i: group + i for i in range(len(given))},
        scratch_shapes=[
            pltpu.VMEM((group, tokens, width), BF16),
            pltpu.VMEM((group, tokens, width), BF16),
            pltpu.VMEM((fore, width), BF16),
            pltpu.VMEM((local, 2 * wide_units, width), BF16),
            pltpu.VMEM((local, wide_units, width), BF16),
            pltpu.VMEM((share, width), BF16),
            pltpu.VMEM((group, tokens, width), BF16),
            pltpu.VMEM((group, tokens, deep), BF16),
            pltpu.VMEM((group, deep, width), BF16),
            pltpu.SemaphoreType.DMA((2 * group + 3 + 3 * local,)),
            pltpu.SemaphoreType.DMA((8, max(2 * local, group))),
        ]
        + [
            pltpu.VMEM(k.shape[:1] + (group,) + k.shape[2:], BF16) for k in kept[:4]
        ]
        + [pltpu.VMEM((group,) + k.shape[1:], BF16) for k in kept[4:]],
        compiler_params=pltpu.CompilerParams(vmem_limit_bytes=VMEM_LIMIT),
        cost_estimate=pl.CostEstimate(flops=flops // 16, bytes_accessed=2**20, transcendentals=0),
        name="run_experts",
    )(place.reshape(1), *x_group, *g_group, slot_rows, slot_cols, *weights, *given)
    return results[:group], results[group:]


def outputs_kernel(group, count, local, act, slot_col, sact, w_out, w_shared, *refs):
    out_refs, (outs, left, right, sems) = refs[:count], refs[count:]
    step = pl.program_id(0)
    slot = lax.rem(step, 2)
    capacity, units = act.shape[2:]
    tokens, share = sact.shape[1:]
    wide = local * capacity

    def store(at, b, into):
        return pltpu.make_async_copy(outs.at[into, b], out_refs[at * group + b], sems.at[into, b])

    @pl.when(step >= 2)
    def _():
        for b in range(group):
            store(0, b, slot).wait()

    for e in range(local):
        rows = dot(act[e].reshape(group * capacity, units), w_out[e], NN).astype(BF16)
        for b in range(group):
            right[b, e * capacity : (e + 1) * capacity] = rows[b * capacity : (b + 1) * capacity]
    slot_at = lax.broadcasted_iota(jnp.int32, (tokens, capacity), 1)
    for b in range(group):
        for e in range(local):
            picks = jnp.where(slot_at == slot_col[b, :, e : e + 1], 1.0, 0.0).astype(BF16)
            left[b, :, e * capacity : (e + 1) * capacity] = picks
        left[b, :, wide : wide + share] = sact[b]
        right[b, wide : wide + share] = w_shared[0]
        outs[slot, b] = dot(left[b], right[b], NN).astype(BF16)
    for at in range(count // group):

        @pl.when(step == at)
        def _():
            for b in range(group):
                store(at, b, at % 2).start()

    @pl.when(step == count // group - 1)
    def _():
        for b in range(group):
            for into in range(2):
                store(0, b, into).wait()


def expert_grads_kernel(rows_x, rows_g, act, dpair, in_ref, out_ref):
    rows = rows_x.shape[1] * rows_x.shape[2]
    x = rows_x[0].reshape(rows, -1)
    for c in range(2):
        in_ref[0, c] = dot(dpair[c].reshape(rows, -1), x, TN)
    out_ref[0] = dot(act[0].reshape(rows, -1), rows_g[0].reshape(rows, -1), TN)


def grads_of_experts(rows_x, rows_g, act, dpair):
    local, count, capacity, width = rows_x.shape
    units = act.shape[3]
    tile = min(width, 1024)
    return pl.pallas_call(
        expert_grads_kernel,
        grid=(local, width // tile),
        out_shape=(
            jax.ShapeDtypeStruct((local, 2, units, width), F32),
            jax.ShapeDtypeStruct((local, units, width), F32),
        ),
        in_specs=[
            pl.BlockSpec((1, count, capacity, tile), lambda e, i: (e, 0, 0, i)),
            pl.BlockSpec((1, count, capacity, tile), lambda e, i: (e, 0, 0, i)),
            pl.BlockSpec((1, count, capacity, units), lambda e, i: (e, 0, 0, 0)),
            pl.BlockSpec((2, count, capacity, units), lambda e, i: (e, 0, 0, 0)),
        ],
        out_specs=(
            pl.BlockSpec((1, 2, units, tile), lambda e, i: (e, 0, 0, i)),
            pl.BlockSpec((1, units, tile), lambda e, i: (e, 0, i)),
        ),
        compiler_params=pltpu.CompilerParams(vmem_limit_bytes=VMEM_LIMIT),
        cost_estimate=pl.CostEstimate(flops=0, bytes_accessed=2**20, transcendentals=0),
        name="grads_of_experts",
    )(rows_x, rows_g, act, dpair)


def run_outputs(act, slot_cols, sact, w_out, w_shared):
    local, count, capacity, units = act.shape
    tokens, share = sact.shape[1:]
    width = w_out.shape[2]
    group = 2
    deep = local * capacity + share
    return pl.pallas_call(
        functools.partial(outputs_kernel, group, count, local),
        grid=(count // group,),
        out_shape=(jax.ShapeDtypeStruct((tokens, width), BF16),) * count,
        in_specs=[
            pl.BlockSpec((local, group, capacity, units), lambda i: (0, i, 0, 0)),
            pl.BlockSpec((group, tokens, local), lambda i: (i, 0, 0)),
            pl.BlockSpec((group, tokens, share), lambda i: (i, 0, 0)),
            pl.BlockSpec((local, units, width), lambda i: (0, 0, 0)),
            pl.BlockSpec((1, share, width), lambda i: (2, 0, 0)),
        ],
        out_specs=(pl.BlockSpec(memory_space=pl.ANY),) * count,
        scratch_shapes=[
            pltpu.VMEM((2, group, tokens, width), BF16),
            pltpu.VMEM((group, tokens, deep), BF16),
            pltpu.VMEM((group, deep, width), BF16),
            pltpu.SemaphoreType.DMA((2, group)),
        ],
        compiler_params=pltpu.CompilerParams(vmem_limit_bytes=VMEM_LIMIT),
        cost_estimate=pl.CostEstimate(
            flops=count * width // 8 * (local * capacity * (units + tokens) + tokens * share),
            bytes_accessed=2**20,
            transcendentals=0,
        ),
        name="run_outputs",
    )(act, slot_cols, sact, w_out, w_shared)


def weight_parts_kernel(count, place_ref, x, raw, out_part, ends, *refs):
    part_refs, (part, sems) = refs[:count], refs[count:]
    place = place_ref[0]
    width = part.shape[2]
    q_rows, out_rows, end_rows = x.shape[1] // count, out_part.shape[0] // count, ends.shape[0] // count

    def store(j):
        return pltpu.make_async_copy(part.at[j % 2], part_refs[j], sems.at[j % 2])

    for j in range(count):
        if j >= 2:
            store(j - 2).wait()
        to = place ^ j
        columns = x[:, pl.ds(pl.multiple_of(to * q_rows, q_rows), q_rows)]
        grad = dot(columns, raw[...], TN).astype(BF16)
        for c in range(3):
            part[j % 2, c * q_rows : (c + 1) * q_rows] = grad[:, c * width : (c + 1) * width]
        rows = out_part[pl.ds(pl.multiple_of(to * out_rows, out_rows), out_rows)]
        at = 3 * q_rows
        for k in range(out_part.shape[1] // width):
            part[j % 2, at : at + out_rows] = rows[:, k * width : (k + 1) * width]
            at += out_rows
        part[j % 2, at:] = ends[pl.ds(pl.multiple_of(to * end_rows, end_rows), end_rows)]
        store(j).start()
    for j in range(count - 2, count):
        store(j).wait()


def weight_parts(place, x, raw, out_part, ends, count):
    tokens, size = x.shape
    width = ends.shape[1]
    rows = (3 * size + out_part.size // width + ends.shape[0]) // count
    return pl.pallas_call(
        functools.partial(weight_parts_kernel, count),
        out_shape=[jax.ShapeDtypeStruct((rows, width), BF16)] * count,
        in_specs=[pl.BlockSpec(memory_space=pltpu.SMEM)]
        + [pl.BlockSpec(memory_space=pltpu.VMEM)] * 4,
        out_specs=[pl.BlockSpec(memory_space=pl.ANY)] * count,
        scratch_shapes=[
            pltpu.VMEM((2, rows, width), BF16),
            pltpu.SemaphoreType.DMA((2,)),
        ],
        compiler_params=pltpu.CompilerParams(vmem_limit_bytes=VMEM_LIMIT),
        cost_estimate=pl.CostEstimate(flops=0, bytes_accessed=2**20, transcendentals=0),
        name="weight_parts",
    )(place.reshape(1), x, raw, out_part, ends)


def assemble_kernel(plan, count, place_ref, *refs):
    block_refs, refs = refs[:count], refs[count:]
    out_refs, (low, wide, in_sems, out_sems) = refs[:-4], refs[-4:]
    place = place_ref[0]

    def load(j):
        return pltpu.make_async_copy(block_refs[j], low.at[j % 2], in_sems.at[j % 2])

    def stores(j):
        return [
            pltpu.make_async_copy(
                wide.at[j % 2, pl.ds(first, rows)],
                out_refs[which].at[
                    pl.ds(pl.multiple_of(base + (place ^ j) * rows, 8), rows),
                    pl.ds(column, wide.shape[2]),
                ],
                out_sems.at[j % 2, i],
            )
            for i, (which, first, rows, base, column) in enumerate(plan)
        ]

    load(0).start()
    for j in range(count):
        if j + 1 < count:
            load(j + 1).start()
        load(j).wait()
        if j >= 2:
            for copy in stores(j - 2):
                copy.wait()
        wide[j % 2] = low[j % 2].astype(F32)
        for copy in stores(j):
            copy.start()
    for j in range(max(0, count - 2), count):
        for copy in stores(j):
            copy.wait()


def assemble(place, blocks, shapes, plan):
    count = len(blocks)
    rows, width = blocks[0].shape
    any_spec = pl.BlockSpec(memory_space=pl.ANY)
    return pl.pallas_call(
        functools.partial(assemble_kernel, plan, count),
        out_shape=[jax.ShapeDtypeStruct(shape, F32) for shape in shapes],
        in_specs=[pl.BlockSpec(memory_space=pltpu.SMEM)] + [any_spec] * count,
        out_specs=[any_spec] * len(shapes),
        scratch_shapes=[
            pltpu.VMEM((2, rows, width), BF16),
            pltpu.VMEM((2, rows, width), F32),
            pltpu.SemaphoreType.DMA((2,)),
            pltpu.SemaphoreType.DMA((2, len(plan))),
        ],
        compiler_params=pltpu.CompilerParams(vmem_limit_bytes=VMEM_LIMIT),
        cost_estimate=pl.CostEstimate(flops=0, bytes_accessed=2**20, transcendentals=0),
        name="assemble",
    )(place.reshape(1), *blocks)


def shared_grads_kernel(count, place_ref, *refs):
    x_refs, g_all, refs = refs[:count], refs[count], refs[count + 1 :]
    (sact, sdpair, dl, grads_ref, router_ref, xs, gs, grads, router, sems) = refs
    at = pl.program_id(0)
    slot = lax.rem(at, 2)

    def load(j, into):
        return (
            pltpu.make_async_copy(x_refs[j], xs.at[into], sems.at[0, into]),
            pltpu.make_async_copy(g_all.at[place_ref[0] ^ j], gs.at[into], sems.at[1, into]),
        )

    @pl.when(at == 0)
    def _():
        for copy in load(0, 0):
            copy.start()
        grads[...] = jnp.zeros_like(grads)
        router[...] = jnp.zeros_like(router)

    for j in range(1, count):

        @pl.when(at == j - 1)
        def _():
            for copy in load(j, j % 2):
                copy.start()

    for copy in load(0, slot):
        copy.wait()
    x, g = xs[slot], gs[slot]
    grads[0] += dot(sdpair[0, 0], x, TN)
    grads[1] += dot(sdpair[0, 1], x, TN)
    grads[2] += dot(sact[0], g, TN)
    router[...] += dot(dl[0], x, TN)

    @pl.when(at == count - 1)
    def _():
        grads_ref[...] = grads[...].astype(BF16)
        router_ref[...] = router[...]


def shared_grads(place, x_blocks, g_all, sact, sdpair, dl):
    count = len(x_blocks)
    tokens, width = x_blocks[0].shape
    share, padded = sact.shape[2], dl.shape[2]
    any_spec = pl.BlockSpec(memory_space=pl.ANY)
    return pl.pallas_call(
        functools.partial(shared_grads_kernel, count),
        grid=(count,),
        out_shape=(
            jax.ShapeDtypeStruct((3, share, width), BF16),
            jax.ShapeDtypeStruct((padded, width), F32),
        ),
        in_specs=[pl.BlockSpec(memory_space=pltpu.SMEM)]
        + [any_spec] * (count + 1)
        + [
            pl.BlockSpec((1, tokens, share), lambda j: (j, 0, 0)),
            pl.BlockSpec((1, 2, tokens, share), lambda j: (j, 0, 0, 0)),
            pl.BlockSpec((1, tokens, padded), lambda j: (j, 0, 0)),
        ],
        out_specs=(
            pl.BlockSpec((3, share, width), lambda j: (0, 0, 0)),
            pl.BlockSpec((padded, width), lambda j: (0, 0)),
        ),
        scratch_shapes=[
            pltpu.VMEM((2, tokens, width), BF16),
            pltpu.VMEM((2, tokens, width), BF16),
            pltpu.VMEM((3, share, width), F32),
            pltpu.VMEM((padded, width), F32),
            pltpu.SemaphoreType.DMA((2, 2)),
        ],
        compiler_params=pltpu.CompilerParams(vmem_limit_bytes=VMEM_LIMIT),
        cost_estimate=pl.CostEstimate(
            flops=count * tokens * width * share,
            bytes_accessed=2**20,
            transcendentals=0,
        ),
        name="shared_grads",
    )(place.reshape(1), *x_blocks, g_all, sact, sdpair, dl)


def on_device(
    hidden_in,
    cotangent,
    gain_attn,
    qkv_weight,
    qkv_bias,
    out_weight,
    gain_ffn,
    router_weight,
    routes,
    shared_gate,
    shared_in,
    shared_out,
    expert_in,
    expert_out,
):
    tokens, width = hidden_in.shape
    ctx_count = lax.axis_size("ctx")
    heads_local = qkv_weight.shape[2] // HD
    local = expert_in.shape[0]
    experts = local * ctx_count
    top_count = routes.shape[1]
    capacity = 3 * tokens * top_count // (2 * experts)
    place = lax.axis_index("ctx")
    order = jnp.arange(ctx_count, dtype=jnp.int32) ^ place
    score_scale = 1.0 / math.sqrt(HD)
    query_pos = place * tokens + jnp.arange(tokens, dtype=jnp.int32)
    cosine, sine = rotary_tables(query_pos, HD)

    x_full = hidden_in.astype(F32)
    inv_one = lax.rsqrt(jnp.mean(x_full * x_full, axis=-1, keepdims=True) + EPS)
    normed_one = x_full * inv_one
    x_one = (normed_one * gain_attn).astype(BF16)
    projected = (
        jnp.einsum("td,dcf->ctf", x_one, qkv_weight, preferred_element_type=F32)
        + qkv_bias[:, None]
    )
    shaped = projected.reshape(3, tokens, heads_local, HD).transpose(0, 2, 1, 3)
    query = rotate(shaped[0], cosine, sine).astype(BF16)
    key_local = rotate(shaped[1], cosine, sine).astype(BF16)
    value_local = shaped[2].astype(BF16)
    kv_rows = heads_local * tokens
    route_rows = -(-tokens * top_count // HD)
    behind = jnp.pad(
        routes.T.astype(BF16).reshape(route_rows, HD), ((0, -route_rows % 16), (0, 0))
    )
    kv_local = jnp.stack(
        [
            jnp.concatenate([key_local.reshape(kv_rows, HD), behind], axis=0),
            jnp.concatenate([value_local.reshape(kv_rows, HD), behind], axis=0),
        ]
    )
    share = shared_out.shape[0] // ctx_count
    piece = shared_out.shape[1]
    shared_send = jnp.concatenate(
        [
            shared_in.transpose(1, 2, 0).reshape(2, ctx_count, share, piece),
            shared_out.reshape(1, ctx_count, share, piece),
        ],
        axis=0,
    ).transpose(1, 0, 2, 3)
    shared_got = lax.all_to_all(shared_send, "ctx", split_axis=0, concat_axis=0, tiled=True)
    kv_blocks = gather_ctx(after(kv_local, shared_got))
    g_all = lax.all_gather(after(cotangent, kv_blocks[2 % ctx_count], kv_blocks[4 % ctx_count]), "ctx", axis=0)

    half_rows = out_weight.shape[0] // 2
    core = place % 2
    out_mine = lax.all_gather(
        lax.dynamic_slice_in_dim(out_weight, core * half_rows, half_rows, 0), "tp", axis=0
    )

    routes_all = jnp.stack([b[0, kv_rows : kv_rows + route_rows] for b in kv_blocks])
    routes_all = routes_all.reshape(ctx_count, 1, top_count, tokens)
    own_experts = (place * local + jnp.arange(local, dtype=jnp.int32)).astype(BF16)
    hit = jnp.any(routes_all == own_experts[None, :, None, None], axis=2)
    token_at = jnp.arange(tokens, dtype=jnp.int32)
    earlier = (token_at[:, None] <= token_at[None, :]).astype(BF16)
    rank = dot(hit.astype(BF16).reshape(-1, tokens), earlier, NN).reshape(hit.shape) - 1.0
    slot_rows = jnp.where(hit, rank, -1.0).astype(jnp.int32)
    slot_cols = slot_rows.transpose(0, 2, 1)
    padded = -(-(experts + 1) // 8) * 8
    w_router = jnp.concatenate(
        [
            router_weight.T,
            shared_gate[None],
            jnp.zeros((padded - experts - 1, width), BF16),
        ],
        axis=0,
    )
    w_in = expert_in.transpose(0, 2, 3, 1)

    attended, lse = attend(place, query, kv_blocks)
    att = attended.astype(BF16).transpose(1, 0, 2).reshape(tokens, heads_local * HD)
    out_mine = after(out_mine, attended)
    out_other = swap(out_mine, 1)
    att_mine, att_other = columns(place, gather_tp(att))
    att_mine = after(att_mine, slot_rows, slot_cols, w_router, w_in)
    rows = out_mine.shape[0] * half_rows
    hidden = x_full + (
        dot(att_mine, out_mine.reshape(rows, width), NN)
        + dot(att_other, out_other.reshape(rows, width), NN)
    )
    shared_w = shared_got.transpose(1, 2, 0, 3).reshape(3, share, width)
    whole_share = -(-share // 16) * 16
    if whole_share > share:
        shared_w = jnp.pad(shared_w, ((0, 0), (0, whole_share - share), (0, 0)))
    inv_two = lax.rsqrt(jnp.mean(hidden * hidden, axis=-1, keepdims=True) + EPS)
    normed_two = hidden * inv_two
    x_two = (normed_two * gain_ffn).astype(BF16)

    units, group = expert_out.shape[1], 2
    kept = [
        jax.ShapeDtypeStruct(shape, BF16)
        for shape in (
            (local, ctx_count, capacity, width),
            (local, ctx_count, capacity, width),
            (local, ctx_count, capacity, units),
            (2 * local, ctx_count, capacity, units),
            (ctx_count, tokens, whole_share),
            (ctx_count, 2, tokens, whole_share),
            (ctx_count, tokens, padded),
        )
    ]
    weights = (w_router, w_in, expert_out, shared_w)
    g_near = [cotangent, swap(cotangent, 1)]
    got = gather_start(x_two)
    x_blocks = [got[0], got[1]]
    dxs = []
    early = None
    for at in range(0, ctx_count, group):
        if at == 4 and ctx_count == 8:
            pair_two = pair_sum(dxs, 2)
            early = (pair_two, pair_two[: tokens // 2].astype(BF16))
        if at == 6 and ctx_count == 8:
            x_blocks[6] = after(x_blocks[6], early[1])
        dx, kept = run_experts(
            at,
            experts,
            place,
            x_blocks[at : at + group],
            g_near if at == 0 else [g_all],
            slot_rows,
            slot_cols,
            weights,
            kept,
        )
        dxs += dx
        if at == 0:
            x_blocks = x_blocks[:2] + gather_end(got, dx[0])[2:]
    grad_x_part = scatter_ctx(dxs, early)
    outs = run_outputs(kept[2], slot_cols, kept[4], expert_out, shared_w)
    grad_x_low = grad_x_part.astype(BF16)
    out_middle = scatter_middle(scatter_start(after(outs, grad_x_low)))
    kept = after(kept, outs[0], *out_middle[0])
    rows_x, rows_g, act_low, dpair, s_act, s_dpair, low_logits = kept
    shared_low, router_part = shared_grads(place, x_blocks, g_all, s_act, s_dpair, low_logits)
    expert_grads = grads_of_experts(rows_x, rows_g, act_low, dpair)
    grad_expert_in, grad_expert_out = expert_grads
    gain_ffn_part = jnp.sum(grad_x_part * normed_two, axis=0)
    small_rows = padded + 1
    small_part = jnp.concatenate([router_part, gain_ffn_part[None]], axis=0)
    small_part = jnp.pad(small_part, ((0, -small_rows % (8 * lax.axis_size("tp"))), (0, 0)))
    half = tokens // 2
    first = lax.psum(grad_x_low[:half], "tp")
    second = lax.psum(after(grad_x_low[half:], first, *out_middle[0]), "tp")
    out_part = scatter_end(out_middle)

    shared_back = lax.all_to_all(
        shared_low[:, :share].reshape(3, share, ctx_count, piece).transpose(2, 0, 1, 3),
        "ctx",
        split_axis=0,
        concat_axis=0,
        tiled=True,
    )
    shared_wide = shared_back.astype(F32)
    grad_shared_in = shared_wide[:, :2].transpose(3, 1, 0, 2).reshape(shared_in.shape)
    grad_shared_out = shared_wide[:, 2].reshape(shared_out.shape)
    summed = jnp.concatenate([first, second], axis=0)
    summed = after(summed, shared_back, *expert_grads, out_part)
    summed = summed.astype(F32)
    grad_y = cotangent.astype(F32)
    grad_normed_two = summed * gain_ffn
    grad_hidden = grad_y + inv_two * (
        grad_normed_two
        - normed_two * jnp.mean(grad_normed_two * normed_two, axis=-1, keepdims=True)
    )
    grad_hidden_low = grad_hidden.astype(BF16)
    out_weight_part = dot(att, grad_hidden_low, (((0,), (0,)), ((), ())))
    grad_att = (
        dot(grad_hidden_low, out_weight, (((1,), (1,)), ((), ())))
        .astype(BF16)
        .reshape(tokens, heads_local, HD)
        .transpose(1, 0, 2)
    )
    delta = jnp.sum(grad_att.astype(F32) * attended, axis=-1)
    delta = jnp.broadcast_to(delta[:, None], lse.shape)
    grad_query, grad_pairs = attend_back(place, query, grad_att, lse, delta, kv_blocks)
    ffn_total = sum_tp_start(out_part, small_part)
    grad_pairs = after(grad_pairs, ffn_total)
    kv_middle = scatter_middle(scatter_start([grad_pairs[j] for j in range(ctx_count)]))
    ffn_low = sum_tp_end(after(ffn_total, *kv_middle[0]))
    own_rows = tokens // lax.axis_size("tp")
    small = ffn_low[:, own_rows:].reshape(-1, width)[:small_rows].astype(F32)
    ffn_low = ffn_low[:, :own_rows].reshape(tokens, width)
    grad_kv = scatter_end(kv_middle)
    grad_kv = after(grad_kv, grad_shared_in, grad_shared_out)

    def raw_part(value):
        return value.astype(BF16).transpose(1, 0, 2).reshape(tokens, heads_local * HD)

    raw = [
        raw_part(rotate(grad_query, cosine, -sine)),
        raw_part(rotate(grad_kv[0], cosine, -sine)),
        raw_part(grad_kv[1]),
    ]
    raw = jnp.concatenate(raw, axis=1)
    grad_x_one_part = jnp.einsum(
        "tcf,dcf->td",
        raw.reshape(tokens, 3, -1),
        qkv_weight,
        preferred_element_type=F32,
    )
    grad_x_low = grad_x_one_part.astype(BF16)
    half_way = sum_tp_start(grad_x_low)
    grad_x_one = sum_tp_end(half_way).reshape(tokens, width)
    x_one = after(x_one, grad_x_low)
    gain_attn_part = jnp.sum(grad_x_one_part * normed_one, axis=0)
    gain_sum = sum_tp_small(gain_attn_part[None])
    head_width = heads_local * HD
    gain_rows = width // head_width
    ends = jnp.concatenate(
        [jnp.sum(raw.astype(F32), axis=0).reshape(3, -1)]
        + [gain_sum.reshape(gain_rows, -1), small.reshape((padded + 1) * gain_rows, -1)],
        axis=0,
    )
    ends = jnp.pad(ends, ((0, -ends.shape[0] % (16 * ctx_count)), (0, 0))).astype(BF16)
    turns = width // head_width
    sums = sum_ctx(
        weight_parts(place, x_one, raw, out_weight_part.astype(BF16), ends, ctx_count), half_way
    )
    q_rows = width // ctx_count
    out_rows = out_weight.shape[0] // ctx_count
    plan = [(0, c * q_rows, q_rows, c * width, 0) for c in range(3)] + [
        (1, 3 * q_rows + k * out_rows, out_rows, 0, k * head_width) for k in range(turns)
    ]
    qkv_grad, out_weight_grad = assemble(
        place, sums, [(3 * width, head_width), out_weight.shape], plan
    )
    qkv_grad = qkv_grad.reshape(3, width, head_width).transpose(1, 0, 2)
    ends = relative(jnp.stack([b[3 * q_rows + turns * out_rows :] for b in sums]))
    ends = ends.reshape(-1, head_width).astype(F32)
    small = ends[3 + gain_rows : 3 + (padded + 2) * gain_rows].reshape(padded + 1, width)
    grad_x_one = after(grad_x_one, sums[2]).astype(F32)
    grad_normed_one = grad_x_one * gain_attn
    grad_input = grad_hidden + inv_one * (
        grad_normed_one
        - normed_one * jnp.mean(grad_normed_one * normed_one, axis=-1, keepdims=True)
    )
    block_out = (hidden + ffn_low.astype(F32)).astype(BF16)
    return (
        block_out,
        grad_input,
        ends[3 : 3 + gain_rows].reshape(-1),
        qkv_grad,
        ends[:3],
        out_weight_grad,
        small[padded],
        small[:experts].T,
        small[experts],
        grad_shared_in,
        grad_shared_out,
        grad_expert_in.transpose(0, 3, 1, 2),
        grad_expert_out,
    )


def solution(mesh):
    return jax.shard_map(
        on_device,
        mesh=mesh,
        in_specs=(
            P("ctx", None),
            P("ctx", None),
            P(),
            P(None, None, "tp"),
            P(None, "tp"),
            P("tp", None),
            P(),
            P(),
            P("ctx", None),
            P(),
            P("ctx", None, "tp"),
            P("tp", "ctx"),
            P("ctx", None, None, "tp"),
            P("ctx", "tp", None),
        ),
        out_specs=(
            P("ctx", None),
            P("ctx", None),
            P(),
            P(None, None, "tp"),
            P(None, "tp"),
            P("tp", None),
            P(),
            P(),
            P(),
            P("ctx", None, "tp"),
            P("tp", "ctx"),
            P("ctx", None, None, "tp"),
            P("ctx", "tp", None),
        ),
        check_vma=False,
    )
```
